32 devices in a mesh: section: 2 (over x), dp: 8 (over z, y), mp: 2 (over core).
Axes of the slice: x: 2, y: 2, z: 4, core: 2. Of those that a mesh axis runs over, the one named last changes fastest.
Arguments:
- embeds: bfloat16 [2, 1024, 3, 1024], P(None, ('dp', 'mp')), may hold values from -6 to 6
- lengths: int32 [2, 8, 4], P(None, 'dp'), may hold values from 1 to 96, 128 in all within a row
- norm_gains: float32 [2, 2, 1024], P('section'), may hold values from 0.1 to 1.9
- w_qkv: bfloat16 [2, 1024, 3, 1024], P('section', None, None, 'mp'), may hold values from -0.1875 to 0.1875
- w_out: bfloat16 [2, 1024, 1024], P('section', 'mp'), may hold values from -0.375 to 0.375
- w_up: bfloat16 [2, 1024, 4096], P('section', None, 'mp'), may hold values from -0.1875 to 0.1875
- w_down: bfloat16 [2, 4096, 1024], P('section', 'mp'), may hold values from -0.09375 to 0.09375
- cotangent: bfloat16 [2, 1024, 3, 1024], P(None, ('dp', 'mp')), may hold values from -6 to 6
Outputs:
- local_out: bfloat16 [2, 1024, 3, 1024], P(None, ('dp', 'mp'))
- grad_embeds: bfloat16 [2, 1024, 3, 1024], P(None, ('dp', 'mp'))
- grad_gains: float32 [2, 2, 1024], P('section')
- grad_qkv: float32 [2, 1024, 3, 1024], P('section', 'dp', None, 'mp')
- grad_out: float32 [2, 1024, 1024], P('section', 'mp', 'dp')
- grad_up: float32 [2, 1024, 4096], P('section', 'dp', 'mp')
- grad_down: float32 [2, 4096, 1024], P('section', 'mp', 'dp')
The draws below stay inside these ranges and needn't reach their ends.
Inputs may be any that keep to these rules, and one draw needn't show every extreme that they name: Each row's 4 document lengths are positive and add up to 128; the longest is 96.
All inputs are finite; a program needn't handle non-finite values.
Results may differ from the reference program's by a relative error of at most 0.014.
Values may be sent and summed in bfloat16 or wider, within the bound.
A program may use at most 192 MiB of HBM per device.

```python
import math
import jax
import jax.numpy as jnp
import numpy as np
from jax import lax

D = 1024
HEADS = 16
HEAD_DIM = 64
FF = 4096
FR_ROW = 128
MB = 2
NDOC = 4
LONGEST = 96
SEQ_FRAMES = 1024
N_DP = 8


def block_levels(rng, extent, cuts, least, high):
    level = 1.0
    for dim, parts in cuts:
        draws = jax.random.uniform(jax.random.fold_in(jax.random.fold_in(rng, 6), dim), (parts,), jnp.float32, least / len(cuts), high / len(cuts))
        level = level * jnp.repeat(jnp.exp(draws), extent[dim] // parts).reshape((-1,) + (1,) * (len(extent) - 1 - dim))
    return level


def profile(amount, total, bound, skew):
    loads = [(1 << 20) // math.isqrt(grade ** skew) + 1 for grade in range(2, amount + 1)]
    surplus, holding = total - bound - (amount - 1), [1] * (amount - 1)
    while surplus > 0:
        free = [i for i in range(amount - 1) if holding[i] < bound]
        pool, left = sum([loads[i] for i in free]), surplus
        for i in free:
            addition = min(bound - holding[i], max(1, left * loads[i] // pool), surplus)
            holding[i] = holding[i] + addition
            surplus = surplus - addition
    return np.array([bound] + holding)


def ragged_sizes(own_key, amount, total, most, lean):
    if amount == 2:
        one = jax.random.randint(own_key, (), max(1, total - most), min(most, total - 1) + 1)
        return jnp.stack([one, total - one])
    tallies = jnp.asarray(profile(amount, total, most, lean), jnp.int32)
    twos = (amount - 1) // 2
    giver, sink = tallies[1:1 + 2 * twos:2], tallies[2:2 + 2 * twos:2]
    margin = jnp.minimum(giver - 1, most - sink)
    moved = jax.random.randint(jax.random.fold_in(own_key, 1), (twos,), 0, 1 << 20) % (margin + 1)
    tallies = tallies.at[1:1 + 2 * twos:2].set(giver - moved).at[2:2 + 2 * twos:2].set(sink + moved)
    return tallies[jax.random.permutation(jax.random.fold_in(own_key, 2), amount)]


def scatter_about(key, shape, width, bound, split=(), kind=jnp.bfloat16):
    drawn = jax.random.normal(key, shape, jnp.float32) * width
    if len(split) > 0:
        drawn = block_levels(key, shape, split, -0.22, 0.18) * drawn
    return jnp.clip(drawn, min=-bound, max=bound).astype(kind)


def setup_inputs(seed: int = 0) -> dict:
    splits = jax.random.split(jax.random.key(seed), 9)
    embeds = scatter_about(splits[0], (MB, SEQ_FRAMES, 3, D), 1.0, 6.0, ((1, 16),))
    lengths = jax.vmap(lambda own: ragged_sizes(own, NDOC, FR_ROW, LONGEST, 2))(jax.random.split(splits[1], MB * N_DP)).reshape((MB, N_DP, NDOC)).astype(jnp.int32)
    norm_gains = jnp.clip(1.0 + 0.18 * jax.random.normal(splits[2], (2, 2, D), jnp.float32), 0.1, 1.9)
    w_qkv = scatter_about(splits[3], (2, D, 3, D), D ** -0.5, 0.1875, ((0, 2), (3, 2)))
    w_out = scatter_about(splits[4], (2, D, D), (D // 4) ** -0.5, 0.375, ((0, 2), (1, 2)))
    w_up = scatter_about(splits[5], (2, D, FF), D ** -0.5, 0.1875, ((0, 2), (2, 2)))
    w_down = scatter_about(splits[6], (2, FF, D), FF ** -0.5, 0.09375, ((0, 2), (1, 2)))
    cotangent = scatter_about(splits[7], (MB, SEQ_FRAMES, 3, D), 1.0, 6.0, ((1, 16),))
    return {"embeds": embeds, "lengths": lengths, "norm_gains": norm_gains, "w_qkv": w_qkv, "w_out": w_out, "w_up": w_up, "w_down": w_down, "cotangent": cotangent}


@jax.custom_vjp
def low(v):
    return lax.optimization_barrier(v.astype(jnp.bfloat16)).astype(jnp.float32)

@jax.custom_vjp
def low_back(v):
    return v

def low_keep(v):
    return (low(v), None)

def low_pass(kept, grad):
    return (grad,)

def back_keep(v):
    return (v, None)

def back_low(kept, grad):
    return (low(grad),)
low.defvjp(low_keep, low_pass)
low_back.defvjp(back_keep, back_low)
norm_eps = 1e-05
masked_fill = -1e+30
rotary_base = 10000.0

def rms_scale(values, gain_row):
    return values * lax.rsqrt(lax.optimization_barrier(jnp.mean(values * values, axis=-1, keepdims=True)) + norm_eps) * gain_row

def rotate(values, cos_tab, sin_tab):
    half_dim = values.shape[-1] // 2
    first_half = values[..., :half_dim]
    second_half = values[..., half_dim:]
    cos_rows = cos_tab[:, None, :]
    sin_rows = sin_tab[:, None, :]
    return jnp.concatenate([first_half * cos_rows - second_half * sin_rows, second_half * cos_rows + first_half * sin_rows], axis=-1)

def global_context(length_row, frames):
    doc_ends = jnp.cumsum(length_row)
    places = jnp.arange(frames, dtype=jnp.int32)
    passed = (places[:, None] >= doc_ends[None, :]).astype(jnp.int32)
    segment = lax.optimization_barrier(jnp.sum(passed, axis=1))
    offsets = places - lax.optimization_barrier(jnp.sum(passed * length_row[None, :], axis=1))
    allowed = (segment[:, None] == segment[None, :]) & (places[None, :] <= places[:, None])
    half_dim = HEAD_DIM // 2
    frequency = jnp.exp(jnp.arange(half_dim, dtype=jnp.float32) * (-2.0 * math.log(rotary_base) / HEAD_DIM))
    angles = offsets.astype(jnp.float32)[:, None] * frequency[None, :]
    return (allowed, jnp.cos(angles), jnp.sin(angles))

def matmul_high(left, right):
    return jnp.dot(left, right, precision=lax.Precision.HIGHEST, preferred_element_type=jnp.float32)

def global_attend(projected, context):
    allowed, cos_tab, sin_tab = context
    attn_scale = 1.0 / math.sqrt(HEAD_DIM)
    query_rows = low(rotate(projected[:, 0], cos_tab, sin_tab))
    key_rows = low(rotate(projected[:, 1], cos_tab, sin_tab))
    value_rows = low(projected[:, 2])
    scores = low_back(jnp.einsum('qhd,khd->hqk', query_rows, key_rows, precision=lax.Precision.HIGHEST) * attn_scale)
    weights_low = low(jax.nn.softmax(jnp.where(allowed[None], scores, masked_fill), axis=-1))
    return jnp.einsum('hqk,khd->qhd', weights_low, value_rows, precision=lax.Precision.HIGHEST)

def local_attend(projected, context):
    allowed = context
    attn_scale = 1.0 / math.sqrt(HEAD_DIM)
    row_total = projected.shape[0]
    qkv_parts = projected.reshape(row_total // 3, 3, 3, HEADS, HEAD_DIM)
    query_rows = low(qkv_parts[:, :, 0])
    key_rows = low(qkv_parts[:, :, 1])
    value_rows = low(qkv_parts[:, :, 2])
    scores = low_back(jnp.einsum('fihd,fjhd->fhij', query_rows, key_rows, precision=lax.Precision.HIGHEST) * attn_scale)
    weights_low = low(jax.nn.softmax(jnp.where(allowed[None, None], scores, masked_fill), axis=-1))
    mixed_rows = jnp.einsum('fhij,fjhd->fihd', weights_low, value_rows, precision=lax.Precision.HIGHEST)
    return mixed_rows.reshape(row_total, HEADS, HEAD_DIM)

def block_forward(frame_rows, gain_pair, w_qkv, w_out, w_up, w_down, attend, context):
    row_total = frame_rows.shape[0]
    normed = low(rms_scale(frame_rows, gain_pair[0]))
    projected = low_back(matmul_high(normed, w_qkv.reshape(D, 3 * D))).reshape(row_total, 3, HEADS, HEAD_DIM)
    mixed_rows = low(low_back(attend(projected, context).reshape(row_total, D)))
    middle = frame_rows + low_back(matmul_high(mixed_rows, w_out))
    normed_mid = low(rms_scale(middle, gain_pair[1]))
    hidden = low(jax.nn.gelu(low_back(matmul_high(normed_mid, w_up))))
    return middle + low_back(matmul_high(hidden, w_down))

def row_pass(embed_row, length_row, params):
    norm_gains, w_qkv, w_out, w_up, w_down = params
    context = global_context(length_row, FR_ROW)
    frame_in = lax.optimization_barrier(jnp.sum(embed_row, axis=1))
    global_out = block_forward(frame_in, norm_gains[0], w_qkv[0], w_out[0], w_up[0], w_down[0], global_attend, context)
    sent_rows = low_back(low(global_out))
    local_in = (embed_row + sent_rows[:, None, :]).reshape(FR_ROW * 3, D)
    local_allowed = jnp.tril(jnp.ones((3, 3), dtype=jnp.bool_))
    final = block_forward(local_in, norm_gains[1], w_qkv[1], w_out[1], w_up[1], w_down[1], local_attend, local_allowed)
    return final.reshape(FR_ROW, 3, D)

def add_pair(left, right):
    return left + right

def reference(embeds, lengths, norm_gains, w_qkv, w_out, w_up, w_down, cotangent):
    row_count = MB * N_DP
    embed_rows = embeds.astype(jnp.float32).reshape(row_count, FR_ROW, 3, D)
    length_rows = lengths.reshape(row_count, NDOC)
    cot_rows = cotangent.astype(jnp.float32).reshape(row_count, FR_ROW, 3, D)
    params = (norm_gains.astype(jnp.float32), w_qkv.astype(jnp.float32), w_out.astype(jnp.float32), w_up.astype(jnp.float32), w_down.astype(jnp.float32))

    def one_row(totals, row_data):
        embed_row, length_row, cot_row = row_data

        def forward(embed_value, param_value):
            return row_pass(embed_value, length_row, param_value)
        out_row, pullback = jax.vjp(forward, embed_row, params)
        grad_embed, grad_params = pullback(cot_row)
        totals = jax.tree.map(add_pair, totals, grad_params)
        return (totals, (out_row.astype(jnp.bfloat16), grad_embed.astype(jnp.bfloat16)))
    zero_totals = jax.tree.map(jnp.zeros_like, params)
    totals, (out_rows, grad_rows) = lax.scan(one_row, zero_totals, (embed_rows, length_rows, cot_rows))
    grad_gains, grad_qkv, grad_out, grad_up, grad_down = totals
    local_out = out_rows.reshape(MB, N_DP * FR_ROW, 3, D)
    grad_embeds = grad_rows.reshape(MB, N_DP * FR_ROW, 3, D)
    return (local_out, grad_embeds, grad_gains, grad_qkv, grad_out, grad_up, grad_down)
```

```python
import functools
import math

import jax
import jax.numpy as jnp
from jax import lax
from jax.experimental import pallas as pl
from jax.experimental.pallas import tpu as pltpu
from jax.sharding import PartitionSpec as P

HEAD_DIM = 64


norm_eps = 1e-05
masked_fill = -1e30
rotary_base = 10000.0


def passed_along(value, axis, steps):
    count = lax.axis_size(axis)
    leading, last = (max(0, -steps), min(count, count - steps))
    return lax.ppermute(value, axis, [(source, source + steps) for source in range(leading, last)])


def rms_scale(values, gain_row):
    return (
        values * lax.rsqrt(jnp.mean(values * values, axis=-1, keepdims=True) + norm_eps) * gain_row
    )


def rotate(values, cos_tab, sin_tab):
    half_dim = values.shape[-1] // 2
    first_half = values[..., :half_dim]
    second_half = values[..., half_dim:]
    cos_rows = cos_tab[:, None, :]
    sin_rows = sin_tab[:, None, :]
    return jnp.concatenate(
        [
            first_half * cos_rows - second_half * sin_rows,
            second_half * cos_rows + first_half * sin_rows,
        ],
        axis=-1,
    )


def global_context(length_row, frames):
    doc_ends = jnp.cumsum(length_row)
    places = jnp.arange(frames, dtype=jnp.int32)
    passed = (places[:, None] >= doc_ends[None, :]).astype(jnp.int32)
    segment = jnp.sum(passed, axis=1)
    offsets = places - jnp.sum(passed * length_row[None, :], axis=1)
    allowed = (segment[:, None] == segment[None, :]) & (places[None, :] <= places[:, None])
    half_dim = HEAD_DIM // 2
    frequency = jnp.exp(
        jnp.arange(half_dim, dtype=jnp.float32) * (-2.0 * math.log(rotary_base) / HEAD_DIM)
    )
    angles = offsets.astype(jnp.float32)[:, None] * frequency[None, :]
    return (allowed, jnp.cos(angles), jnp.sin(angles))


def global_attend(projected, context):
    allowed, cos_tab, sin_tab = context
    attn_scale = 1.0 / math.sqrt(HEAD_DIM)
    row_total, _, local_width = projected.shape
    head_count = local_width // HEAD_DIM
    query_rows = rotate(
        projected[:, 0].reshape(row_total, head_count, HEAD_DIM), cos_tab, sin_tab
    ).astype(jnp.bfloat16)
    key_rows = rotate(
        projected[:, 1].reshape(row_total, head_count, HEAD_DIM), cos_tab, sin_tab
    ).astype(jnp.bfloat16)
    value_rows = projected[:, 2].reshape(row_total, head_count, HEAD_DIM).astype(jnp.bfloat16)
    scores = (
        jnp.einsum("qhd,khd->hqk", query_rows, key_rows, preferred_element_type=jnp.float32)
        * attn_scale
    )
    scores = jnp.where(allowed[None], scores, masked_fill)
    score_peak = jnp.max(scores, axis=-1, keepdims=True)
    exp_scores = jnp.exp(scores - score_peak)
    row_sums = jnp.sum(exp_scores, axis=-1, keepdims=True)
    weights_low = (exp_scores / row_sums).astype(jnp.bfloat16)
    mixed_rows = jnp.einsum(
        "hqk,khd->qhd", weights_low, value_rows, preferred_element_type=jnp.float32
    )
    log_total = score_peak + jnp.log(row_sums)
    return (
        mixed_rows.reshape(row_total, local_width).astype(jnp.bfloat16),
        (query_rows, key_rows, value_rows, log_total),
    )


def global_attend_back(attn_saved, context, grad_mixed):
    query_rows, key_rows, value_rows, log_total = attn_saved
    allowed, cos_tab, sin_tab = context
    attn_scale = 1.0 / math.sqrt(HEAD_DIM)
    row_total, head_count, _ = query_rows.shape
    grad_heads = grad_mixed.reshape(row_total, head_count, HEAD_DIM)
    scores = (
        jnp.einsum("qhd,khd->hqk", query_rows, key_rows, preferred_element_type=jnp.float32)
        * attn_scale
    )
    prob_rows = jnp.where(allowed[None], jnp.exp(scores - log_total), 0.0)
    grad_values = jnp.einsum(
        "hqk,qhd->khd",
        prob_rows.astype(jnp.bfloat16),
        grad_heads,
        preferred_element_type=jnp.float32,
    )
    grad_probs = jnp.einsum(
        "qhd,khd->hqk", grad_heads, value_rows, preferred_element_type=jnp.float32
    )
    grad_scores = (
        prob_rows * (grad_probs - jnp.sum(grad_probs * prob_rows, axis=-1, keepdims=True))
    ).astype(jnp.bfloat16)
    grad_query = (
        jnp.einsum("hqk,khd->qhd", grad_scores, key_rows, preferred_element_type=jnp.float32)
        * attn_scale
    )
    grad_keys = (
        jnp.einsum("hqk,qhd->khd", grad_scores, query_rows, preferred_element_type=jnp.float32)
        * attn_scale
    )
    grad_query = rotate(grad_query, cos_tab, -sin_tab)
    grad_keys = rotate(grad_keys, cos_tab, -sin_tab)
    stacked = jnp.stack([grad_query, grad_keys, grad_values], axis=1)
    return stacked.reshape(row_total, 3, head_count * HEAD_DIM).astype(jnp.bfloat16)


def local_attend(projected, context):
    attn_scale = 1.0 / math.sqrt(HEAD_DIM)
    row_total, _, local_width = projected.shape
    head_count = local_width // HEAD_DIM
    frames = row_total // 3
    qkv_parts = projected.reshape(frames, 3, 3, head_count, HEAD_DIM).astype(jnp.bfloat16)
    query_rows = qkv_parts[:, :, 0]
    key_rows = qkv_parts[:, :, 1]
    value_rows = qkv_parts[:, :, 2]
    scores = (
        jnp.einsum("fihd,fjhd->fhij", query_rows, key_rows, preferred_element_type=jnp.float32)
        * attn_scale
    )
    scores = jnp.where(context[None, None], scores, masked_fill)
    score_peak = jnp.max(scores, axis=-1, keepdims=True)
    exp_scores = jnp.exp(scores - score_peak)
    row_sums = jnp.sum(exp_scores, axis=-1, keepdims=True)
    weights_low = (exp_scores / row_sums).astype(jnp.bfloat16)
    mixed_rows = jnp.einsum(
        "fhij,fjhd->fihd", weights_low, value_rows, preferred_element_type=jnp.float32
    )
    log_total = score_peak + jnp.log(row_sums)
    return (
        mixed_rows.reshape(row_total, local_width).astype(jnp.bfloat16),
        (query_rows, key_rows, value_rows, log_total),
    )


def local_attend_back(attn_saved, context, grad_mixed):
    query_rows, key_rows, value_rows, log_total = attn_saved
    attn_scale = 1.0 / math.sqrt(HEAD_DIM)
    frames, _, head_count, _ = query_rows.shape
    grad_heads = grad_mixed.reshape(frames, 3, head_count, HEAD_DIM)
    scores = (
        jnp.einsum("fihd,fjhd->fhij", query_rows, key_rows, preferred_element_type=jnp.float32)
        * attn_scale
    )
    prob_rows = jnp.where(context[None, None], jnp.exp(scores - log_total), 0.0)
    grad_values = jnp.einsum(
        "fhij,fihd->fjhd",
        prob_rows.astype(jnp.bfloat16),
        grad_heads,
        preferred_element_type=jnp.float32,
    )
    grad_probs = jnp.einsum(
        "fihd,fjhd->fhij", grad_heads, value_rows, preferred_element_type=jnp.float32
    )
    grad_scores = (
        prob_rows * (grad_probs - jnp.sum(grad_probs * prob_rows, axis=-1, keepdims=True))
    ).astype(jnp.bfloat16)
    grad_query = (
        jnp.einsum("fhij,fjhd->fihd", grad_scores, key_rows, preferred_element_type=jnp.float32)
        * attn_scale
    )
    grad_keys = (
        jnp.einsum("fhij,fihd->fjhd", grad_scores, query_rows, preferred_element_type=jnp.float32)
        * attn_scale
    )
    stacked = jnp.stack([grad_query, grad_keys, grad_values], axis=2)
    return stacked.reshape(frames * 3, 3, head_count * HEAD_DIM).astype(jnp.bfloat16)


def gather_project(normed, weight, form):
    piece_rows = lax.all_gather(normed, "mp", axis=0, tiled=True)
    return (piece_rows, jnp.einsum(form, piece_rows, weight, preferred_element_type=jnp.float32))


def reduce_rows(left, weight, form, row_count):

    def partial_term(first_row, count_rows):
        return jnp.einsum(form, left, weight, preferred_element_type=jnp.float32)

    return lax.psum_scatter(
        partial_term(jnp.int32(0), row_count * lax.axis_size("mp")),
        "mp",
        scatter_dimension=0,
        tiled=True,
    )


def reduce_grads(left, weight, form, row_count):

    def partial_term(first_row, count_rows):
        return jnp.einsum(form, left, weight, preferred_element_type=jnp.float32)

    return lax.psum_scatter(
        partial_term(jnp.int32(0), row_count * lax.axis_size("mp")),
        "mp",
        scatter_dimension=0,
        tiled=True,
    )


def gather_grads(grad_low):
    return lax.all_gather(grad_low, "mp", axis=0, tiled=True)


def layer_forward(frame_rows, weights, attend, context):
    gain_pair, w_qkv, w_out, w_up, w_down = weights
    row_count = frame_rows.shape[0]
    normed = rms_scale(frame_rows, gain_pair[0]).astype(jnp.bfloat16)
    normed_all, projected = gather_project(normed, w_qkv, "nd,dce->nce")
    mixed_rows, attn_saved = attend(projected, context)
    attn_rows = reduce_rows(mixed_rows, w_out, "ne,ed->nd", row_count)
    middle = frame_rows + attn_rows
    normed_mid = rms_scale(middle, gain_pair[1]).astype(jnp.bfloat16)
    normed_mid_all, up_all = gather_project(normed_mid, w_up, "nd,de->ne")
    hidden = jax.nn.gelu(up_all).astype(jnp.bfloat16)
    down_rows = reduce_rows(hidden, w_down, "nf,fd->nd", row_count)
    record = (normed_all, attn_saved, mixed_rows, middle, normed_mid_all, up_all, hidden)
    return (middle + down_rows, attn_rows + down_rows, record)


def layer_backward(frame_rows, weights, attend_back, context, record, grad_result):
    gain_pair, w_qkv, w_out, w_up, w_down = weights
    normed_all, attn_saved, mixed_rows, middle, normed_mid_all, up_all, hidden = record
    row_count = frame_rows.shape[0]
    grad_down_all = gather_grads(grad_result.astype(jnp.bfloat16))
    grad_w_down = jnp.einsum("nf,nd->fd", hidden, grad_down_all, preferred_element_type=jnp.float32)
    grad_hidden = jnp.einsum("nd,fd->nf", grad_down_all, w_down, preferred_element_type=jnp.float32)
    _, gelu_back = jax.vjp(jax.nn.gelu, up_all)
    grad_up = gelu_back(grad_hidden)[0].astype(jnp.bfloat16)
    grad_w_up = jnp.einsum("nd,ne->de", normed_mid_all, grad_up, preferred_element_type=jnp.float32)
    grad_normed_mid = reduce_grads(grad_up, w_up, "ne,de->nd", row_count)
    _, mid_back = jax.vjp(rms_scale, middle, gain_pair[1])
    grad_middle_part, grad_gain_mid = mid_back(grad_normed_mid)
    grad_middle = grad_result + grad_middle_part
    grad_attn_all = gather_grads(grad_middle.astype(jnp.bfloat16))
    grad_w_out = jnp.einsum(
        "ne,nd->ed", mixed_rows, grad_attn_all, preferred_element_type=jnp.float32
    )
    grad_mixed = jnp.einsum(
        "nd,ed->ne", grad_attn_all, w_out, preferred_element_type=jnp.float32
    ).astype(jnp.bfloat16)
    grad_projected = attend_back(attn_saved, context, grad_mixed)
    grad_w_qkv = jnp.einsum(
        "nd,nce->dce", normed_all, grad_projected, preferred_element_type=jnp.float32
    )
    grad_normed = reduce_grads(grad_projected, w_qkv, "nce,dce->nd", row_count)
    _, first_back = jax.vjp(rms_scale, frame_rows, gain_pair[0])
    grad_rows_part, grad_gain_first = first_back(grad_normed)
    grad_frame_rows = grad_middle + grad_rows_part
    layer_grads = (
        jnp.stack([grad_gain_first, grad_gain_mid]),
        grad_w_qkv,
        grad_w_out,
        grad_w_up,
        grad_w_down,
    )
    return (grad_frame_rows, layer_grads)


def on_device(embeds, lengths, norm_gains, w_qkv, w_out, w_up, w_down, cotangent):
    weights = (norm_gains[0], w_qkv[0], w_out[0], w_up[0], w_down[0])
    micro_count = embeds.shape[0]
    shard_rows = embeds.shape[1]
    width = embeds.shape[-1]
    frames = shard_rows * lax.axis_size("mp")
    is_first = lax.axis_index("section") == 0
    local_allowed = jnp.tril(jnp.ones((3, 3), dtype=jnp.bool_))
    gain_total = jnp.zeros(norm_gains.shape[1:], jnp.float32)
    weight_totals = tuple((jnp.zeros(weight.shape, jnp.float32) for weight in weights[1:]))
    totals = (gain_total,) + weight_totals
    y_part = jnp.zeros(embeds.shape, jnp.float32)
    e_part = jnp.zeros(embeds.shape, jnp.float32)
    zero_send = jnp.zeros((shard_rows, width), jnp.bfloat16)

    def add_grads(running, layer_grads):
        run_gain, run_qkv, run_out, run_up, run_down = running
        part_gain, part_qkv, part_out, part_up, part_down = layer_grads
        return (
            run_gain + part_gain,
            run_qkv + part_qkv,
            run_out + part_out,
            run_up + part_up,
            run_down + part_down,
        )

    def global_forward(micro_index):
        context = global_context(lengths[micro_index, 0], frames)
        frame_in = jnp.sum(embeds[micro_index].astype(jnp.float32), axis=1)
        result, _, record = layer_forward(frame_in, weights, global_attend, context)
        return (frame_in, context, result, record)

    def pick(first_value, second_value):
        return jnp.where(is_first, first_value, second_value)

    carry_state = (totals, y_part, e_part)
    forward_recv = zero_send
    backward_recv = zero_send
    for tick_index in range(micro_count + 2):

        def first_section(state_in):
            running, y_state, e_state = state_in
            send_fwd = zero_send
            if tick_index < micro_count:
                _, _, result, _ = global_forward(tick_index)
                send_fwd = result.astype(jnp.bfloat16)
                joined = (
                    embeds[tick_index].astype(jnp.float32)
                    + send_fwd.astype(jnp.float32)[:, None, :]
                )
                y_state = y_state.at[tick_index].set(joined)
            if tick_index >= 2:
                micro_index = tick_index - 2
                frame_in, context, _, record = global_forward(micro_index)
                grad_frame, layer_grads = layer_backward(
                    frame_in,
                    weights,
                    global_attend_back,
                    context,
                    record,
                    backward_recv.astype(jnp.float32),
                )
                running = add_grads(running, layer_grads)
                e_state = e_state.at[micro_index].set(
                    jnp.broadcast_to(grad_frame[:, None, :], e_state.shape[1:])
                )
            return ((running, y_state, e_state), send_fwd, zero_send)

        def second_section(state_in):
            running, y_state, e_state = state_in
            send_back = zero_send
            if 1 <= tick_index <= micro_count:
                micro_index = tick_index - 1
                local_in = (
                    embeds[micro_index].astype(jnp.float32)
                    + forward_recv.astype(jnp.float32)[:, None, :]
                )
                local_in = local_in.reshape(shard_rows * 3, width)
                _, branches, record = layer_forward(local_in, weights, local_attend, local_allowed)
                grad_seed = (
                    cotangent[micro_index].astype(jnp.float32).reshape(shard_rows * 3, width)
                )
                grad_local, layer_grads = layer_backward(
                    local_in, weights, local_attend_back, local_allowed, record, grad_seed
                )
                running = add_grads(running, layer_grads)
                y_state = y_state.at[micro_index].set(branches.reshape(shard_rows, 3, width))
                grad_frames = grad_local.reshape(shard_rows, 3, width)
                e_state = e_state.at[micro_index].set(grad_frames)
                send_back = jnp.sum(grad_frames, axis=1).astype(jnp.bfloat16)
            return ((running, y_state, e_state), zero_send, send_back)

        first_result = first_section(carry_state)
        second_result = second_section(carry_state)
        carry_state, send_fwd, send_back = jax.tree.map(pick, first_result, second_result)
        if tick_index < micro_count:
            forward_recv = passed_along(send_fwd, "section", 1)
        if 1 <= tick_index <= micro_count:
            backward_recv = passed_along(send_back, "section", -1)
    totals, y_part, e_part = carry_state
    gain_total, grad_qkv, grad_out, grad_up, grad_down = totals
    grad_qkv, grad_out, grad_up, grad_down = (
        lax.psum_scatter(grad_qkv, "dp", scatter_dimension=0, tiled=True),
        lax.psum_scatter(grad_out, "dp", scatter_dimension=1, tiled=True),
        lax.psum_scatter(grad_up, "dp", scatter_dimension=0, tiled=True),
        lax.psum_scatter(grad_down, "dp", scatter_dimension=1, tiled=True),
    )
    gain_total = lax.psum(gain_total, ("dp", "mp"))
    y_sum, e_sum = (
        lax.psum(y_part.astype(jnp.bfloat16), "section").astype(jnp.float32),
        lax.psum(e_part.astype(jnp.bfloat16), "section").astype(jnp.float32),
    )
    return (
        y_sum.astype(jnp.bfloat16),
        e_sum.astype(jnp.bfloat16),
        gain_total[None],
        grad_qkv[None],
        grad_out[None],
        grad_up[None],
        grad_down[None],
    )


BF = jnp.bfloat16
F32 = jnp.float32
MESH = pl.DeviceIdType.MESH
SLOTS = 5
CHUNKS = 12
ROWS = 256


def dot_nn(left, right):
    return lax.dot_general(left, right, (((1,), (0,)), ((), ())), preferred_element_type=F32)


def dot_nt(left, right):
    return lax.dot_general(left, right, (((1,), (1,)), ((), ())), preferred_element_type=F32)


def dot_tn(left, right):
    return lax.dot_general(left, right, (((0,), (0,)), ((), ())), preferred_element_type=F32)


def gelu_parts(u):
    c0 = math.sqrt(2.0 / math.pi)
    inner = c0 * (u + 0.044715 * (u * u * u))
    return jnp.tanh(inner)


def loop(lower, upper, body, unroll=1):
    def step(i, carry):
        body(i)
        return carry

    lax.fori_loop(lower, upper, step, 0, unroll=unroll)


def body(
    emb, cot, lens, gains, wq_h, wo_h, wu_h, wd_h,
    lo_h, ge_h, gg_o, gq_o, go_o, gu_o, gd_o,
    wq, wo, wu, wd, em, gd, sr, xb, mid, ab, bm, qkv, ob, dob, up, hid, xs, xr, tb, ob1, ob2,
    cs, gga, ggr, gpart, rg, ry, rz,
    wsem, esem, exs, exr, csem, cxs, cxr, mps, mpr, hops, hopr, lol, los, lor, dls, dlr,
    gel, ges, ger, ggs, ggrs, gms, gmr, ysn, yrc, zrs, zrr, zls, zlr, ycr, rcr, lcr,
):
    s = lax.axis_index("section")
    d = lax.axis_index("dp")
    m = lax.axis_index("mp")
    y = lax.rem(d, 2)
    z = lax.div(d, 2)
    peer = (s, d, 1 - m)
    across = (1 - s, d, m)
    ypeer = (s, d + 1 - 2 * y, m)
    zup = (s, jnp.minimum(d + 2, 7), m)
    zdown = (s, jnp.maximum(d - 2, 0), m)
    nb = jnp.where(s == 0, 1, 3)
    frame = s == 0
    code = s == 1
    ga = em

    def remote(src, dst, ssem, rsem, to):
        return pltpu.make_async_remote_copy(
            src_ref=src, dst_ref=dst, send_sem=ssem, recv_sem=rsem, device_id=to, device_id_type=MESH
        )

    def local(src, dst, sem):
        return pltpu.make_async_copy(src, dst, sem)

    w_copies = [local(a, b, wsem.at[i]) for i, (a, b) in enumerate(((wq_h, wq), (wo_h, wo), (wu_h, wu), (wd_h, wd)))]
    e_local = [local(emb.at[:, c], em.at[c, :, m], esem.at[c]) for c in range(3)]
    c_local = [local(cot.at[:, c], gd.at[c, :, m], csem.at[c]) for c in range(3)]
    for cp in e_local:
        cp.start()
    w_copies[0].start()

    bar = pltpu.get_barrier_semaphore()
    pl.semaphore_signal(bar, 1, device_id=peer, device_id_type=MESH)
    pl.semaphore_signal(bar, 1, device_id=across, device_id_type=MESH)
    for t in range(1, 8):
        pl.semaphore_signal(bar, 1, device_id=(s, lax.rem(d + t, 8), m), device_id_type=MESH)
    pl.semaphore_wait(bar, 9)

    e_far = [remote(emb.at[:, c], em.at[c, :, m], exs.at[c], exr.at[c], peer) for c in range(3)]
    c_far = [remote(cot.at[:, c], gd.at[c, :, m], cxs.at[c], cxr.at[c], peer) for c in range(3)]
    for cp in e_far:
        cp.start()
    for cp in w_copies[1:]:
        cp.start()

    @pl.when(code)
    def _():
        for cp in c_local:
            cp.start()
        for cp in c_far:
            cp.start()

    gga[...] = jnp.zeros_like(gga)

    @pl.when(frame)
    def _():
        for mb in range(2):
            pos = lax.broadcasted_iota(jnp.int32, (128, 128), 0)
            lane = lax.broadcasted_iota(jnp.int32, (128, 128), 1)
            start = jnp.zeros((128, 128), jnp.int32)
            end = jnp.int32(0)
            for j in range(4):
                size = lens[mb, 0, j]
                end = end + size
                start = start + jnp.where(pos >= end, size, 0)
            half = lax.rem(lane, 32).astype(F32)
            freq = jnp.exp(half * (-2.0 * math.log(rotary_base) / HEAD_DIM))
            angle = (pos - start).astype(F32) * freq
            sine = jnp.sin(angle)
            cs[0, mb * 128 : mb * 128 + 128] = jnp.cos(angle)
            cs[1, mb * 128 : mb * 128 + 128] = jnp.where(lax.rem(lane, 64) < 32, -sine, sine)
            cs[2, mb * 128 : mb * 128 + 128] = start.astype(F32)

    for cp in e_local:
        cp.wait()
    for cp in e_far:
        cp.wait()

    @pl.when(frame)
    def _():
        def rows(i):
            mb, mh, r = lax.div(i, 8), lax.rem(lax.div(i, 4), 2), pl.multiple_of(lax.rem(i, 4) * 16, 16)
            total = (
                em[0, mb, mh, pl.ds(r, 16)].astype(F32)
                + em[1, mb, mh, pl.ds(r, 16)].astype(F32)
                + em[2, mb, mh, pl.ds(r, 16)].astype(F32)
            )
            xb[0, pl.ds(pl.multiple_of(i * 16, 16), 16)] = total

        loop(0, 16, rows)

    hop = [remote(sr.at[:, m], sr.at[:, m], hops.at[0], hopr.at[0], across),
           remote(sr.at[:, m], sr.at[:, m], hops.at[1], hopr.at[1], peer)]

    @pl.when(code)
    def _():
        hop[0].wait_recv()
        hop[1].start()
        hop[1].wait_recv()

        def rows(i):
            mb, mh, r = lax.div(i, 8), lax.rem(lax.div(i, 4), 2), pl.multiple_of(lax.rem(i, 4) * 16, 16)
            came = sr[mb, mh, pl.ds(r, 16)].astype(F32)
            for c in range(3):
                xb[c, pl.ds(pl.multiple_of(i * 16, 16), 16)] = em[c, mb, mh, pl.ds(r, 16)].astype(F32) + came

        loop(0, 16, rows)
        hop[1].wait_send()

    def norm_rows(src, dst, b, gain_row):
        gain = gains[0, pl.ds(gain_row, 1)]

        def rows(i):
            at = pl.ds(pl.multiple_of(i * 16, 16), 16)
            v = src[b, at]
            scale = lax.rsqrt(jnp.mean(v * v, axis=-1, keepdims=True) + norm_eps)
            dst[b, at] = (v * scale * gain).astype(BF)

        loop(0, 16, rows, unroll=2)

    def swap_halves(v):
        lane = lax.broadcasted_iota(jnp.int32, v.shape, 1)
        return jnp.where(lax.rem(lane, 64) < 32, pltpu.roll(v, 96, 1), pltpu.roll(v, 32, 1))

    def rope(v, sign):
        return v * cs[0] + swap_halves(v) * (sign * cs[1])

    def phase_a(b):
        norm_rows(xb, ab, b, 0)
        for c in range(3):
            t = dot_nn(ab[b], wq[c])
            if c == 2:
                qkv[b, c] = t.astype(BF)
            else:
                @pl.when(frame)
                def _():
                    for g in range(4):
                        qkv[b, c, :, g * 128 : g * 128 + 128] = rope(t[:, g * 128 : g * 128 + 128], 1.0).astype(BF)

                @pl.when(code)
                def _():
                    qkv[b, c] = t.astype(BF)

    w_copies[0].wait()
    loop(0, nb, phase_a)

    scale = 1.0 / math.sqrt(HEAD_DIM)

    def frame_probs(q, k, sel, allowed):
        scores = dot_nt(jnp.where(sel, q, jnp.zeros_like(q)), k) * scale
        scores = jnp.where(allowed, scores, masked_fill)
        e = jnp.exp(scores - jnp.max(scores, axis=-1, keepdims=True))
        return e / jnp.sum(e, axis=-1, keepdims=True)

    def frame_masks(mb):
        pos = lax.broadcasted_iota(jnp.int32, (128, 128), 0)
        lane = lax.broadcasted_iota(jnp.int32, (128, 128), 1)
        first = cs[2, mb * 128 : mb * 128 + 128]
        return (lane <= pos) & (lane.astype(F32) >= first), lane < 64

    @pl.when(frame)
    def _():
        def pair(g):
            cols = pl.ds(pl.multiple_of(g * 128, 128), 128)
            for mb in range(2):
                at = slice(mb * 128, mb * 128 + 128)
                allowed, low_half = frame_masks(mb)
                q, k, v = (qkv[0, c, at, cols] for c in range(3))
                p0 = frame_probs(q, k, low_half, allowed).astype(BF)
                p1 = frame_probs(q, k, ~low_half, allowed).astype(BF)
                ob[0, at, cols] = jnp.where(low_half, dot_nn(p0, v), dot_nn(p1, v)).astype(BF)

        loop(0, 4, pair)

    def head_sum(prod):
        r0 = lax.broadcasted_iota(jnp.int32, (256, 256), 0)
        r1 = lax.broadcasted_iota(jnp.int32, (256, 256), 1)
        ones = (lax.div(r0, 64) == lax.div(r1, 64)).astype(BF)
        return dot_nn(prod.astype(BF), ones)

    def code_probs(q, k):
        probs = []
        for i in range(3):
            sc = [head_sum(q[i] * k[j]) * scale for j in range(i + 1)]
            top = functools.reduce(jnp.maximum, sc)
            e = [jnp.exp(v - top) for v in sc]
            inv = 1.0 / functools.reduce(jnp.add, e)
            probs.append([v * inv for v in e])
        return probs

    @pl.when(code)
    def _():
        def part(i):
            at = pl.ds(pl.multiple_of(lax.div(i, 2) * 64, 64), 64)
            cols = pl.ds(pl.multiple_of(lax.rem(i, 2) * 256, 256), 256)
            q, k, v = ([qkv[b, c, at, cols].astype(F32) for b in range(3)] for c in range(3))
            probs = code_probs(q, k)
            for i3 in range(3):
                o = functools.reduce(jnp.add, [probs[i3][j].astype(BF).astype(F32) * v[j] for j in range(i3 + 1)])
                ob[i3, at, cols] = o.astype(BF)

        loop(0, 8, part)

    def exchange(slot, b, whole):
        mine = slice(None) if whole else 1 - m
        return remote(xs.at[b, :, mine], xr.at[slot, :, mine], mps.at[b], mpr.at[slot], peer)

    def put_xs(b, cols, t):
        xs[b, :, :, :, cols] = t.astype(BF).reshape(2, 2, 64, t.shape[-1])

    def phase_out(b):
        for n in range(2):
            put_xs(b, slice(n * 512, n * 512 + 512), dot_nn(ob[b], wo[:, n * 512 : n * 512 + 512]))
        exchange(b, b, True).start()

    w_copies[1].wait()
    loop(0, nb, phase_out)
    w_copies[2].wait()
    w_copies[3].wait()

    def at16(i):
        return lax.div(i, 8), lax.rem(lax.div(i, 4), 2), pl.ds(pl.multiple_of(lax.rem(i, 4) * 16, 16), 16)

    def summed(slot, b, i):
        mb, mh, r = at16(i)
        return xs[b, mb, mh, r].astype(F32) + xr[slot, mb, mh, r].astype(F32)

    def phase_ff(b):
        exchange(b, b, True).wait()
        gain = gains[0, 1:2]

        def rows(i):
            at = pl.ds(pl.multiple_of(i * 16, 16), 16)
            v = xb[b, at] + summed(b, b, i)
            mid[b, at] = v
            sc = lax.rsqrt(jnp.mean(v * v, axis=-1, keepdims=True) + norm_eps)
            bm[b, at] = (v * sc * gain).astype(BF)

        loop(0, 16, rows, unroll=2)
        for f in range(4):
            t = dot_nn(bm[b], wu[:, f * 512 : f * 512 + 512])
            for g in range(8):
                u = t[g * 32 : g * 32 + 32]
                up[f, b, g * 32 : g * 32 + 32] = u.astype(BF)
                hid[f, b, g * 32 : g * 32 + 32] = (0.5 * u * (1.0 + gelu_parts(u))).astype(BF)
        for n in range(2):
            cols = slice(n * 512, n * 512 + 512)
            t = dot_nn(hid[0, b], wd[0:512, cols])
            for f in range(1, 4):
                t = t + dot_nn(hid[f, b], wd[f * 512 : f * 512 + 512, cols])
            put_xs(b, cols, t)
        exchange(3 + b, b, False).start()

    loop(0, nb, phase_ff)

    def phase_res(b):
        exchange(3 + b, b, False).wait()

        def rows(i):
            mb, r = lax.div(i, 4), pl.multiple_of(lax.rem(i, 4) * 16, 16)
            row = pl.multiple_of(mb * 128 + m * 64 + r, 16)
            own = xs[b, mb, m, pl.ds(r, 16)].astype(F32) + xr[3 + b, mb, m, pl.ds(r, 16)].astype(F32)
            res = (mid[b, pl.ds(row, 16)] + own).astype(BF)

            @pl.when(frame)
            def _():
                sr[mb, m, pl.ds(r, 16)] = res

            @pl.when(code)
            def _():
                ob1[b, mb, pl.ds(r, 16)] = res

        loop(0, 8, rows, unroll=2)

    loop(0, nb, phase_res)

    lo_local = [local(ob1.at[c], lo_h.at[:, c], lol.at[c]) for c in range(3)]
    lo_far = [remote(ob1.at[c], lo_h.at[:, c], los.at[c], lor.at[c], across) for c in range(3)]
    hop2 = [remote(ob2.at[0], gd.at[0, :, m], hops.at[2], hopr.at[2], across),
            remote(gd.at[0, :, m], gd.at[0, :, m], hops.at[3], hopr.at[3], peer)]

    @pl.when(frame)
    def _():
        hop[0].start()
        hop2[0].wait_recv()
        hop2[1].start()
        hop2[1].wait_recv()
        hop[0].wait_send()
        hop2[1].wait_send()

    @pl.when(code)
    def _():
        for cp in lo_local + lo_far:
            cp.start()
        for cp in c_local:
            cp.wait()
        for cp in c_far:
            cp.wait()

    def flip(src_at):
        def one(b):
            at = pl.ds(pl.multiple_of(b * 256, 256), 256)
            t = src_at(b)
            for g in range(4):
                tb[g * 256 : g * 256 + 256, at] = t[:, g * 256 : g * 256 + 256].T

        loop(0, nb, one)

    def sends(slot):
        return remote(rg.at[slot, :, 1 - y], ry.at[slot], ysn.at[slot], yrc.at[slot], ypeer)

    def right(slot, k):
        return remote(rg.at[slot, k, y], rz.at[slot, k + 1], zrs.at[slot, k], zrr.at[slot, k], zup)

    def left(slot, k):
        return remote(rg.at[slot, k, y], rz.at[slot, k], zls.at[slot, k], zlr.at[slot, k], zdown)

    def free_slot(slot):
        sends(slot).wait_send()
        for k in range(4):
            @pl.when(k > z)
            def _():
                right(slot, k).wait_send()

            @pl.when(k < z)
            def _():
                left(slot, k).wait_send()

    def make_chunk(i, act3, act1):
        slot = lax.rem(i, SLOTS)

        @pl.when(i >= SLOTS)
        def _():
            free_slot(slot)

        def part(k):
            at = pl.ds(pl.multiple_of(k * 256, 256), 256)

            @pl.when(code)
            def _():
                rg[slot, k] = dot_nn(tb[at, :], act3()).astype(BF).reshape(2, 128, 512)

            @pl.when(frame)
            def _():
                rg[slot, k] = dot_nn(tb[at, 0:256], act1()).astype(BF).reshape(2, 128, 512)

        loop(0, 4, part)

        @pl.when(i >= SLOTS)
        def _():
            pl.semaphore_wait(ycr, 1)

        sends(slot).start()

    def add_into(slot, k, ref, idx):
        for g in range(4):
            at = slice(g * 32, g * 32 + 32)
            rg[slot, k, y, at] = (rg[slot, k, y, at].astype(F32) + ref[slot, idx, at].astype(F32)).astype(BF)

    def proc_y(i):
        slot = lax.rem(i, SLOTS)
        sends(slot).wait_recv()

        @pl.when(i >= SLOTS)
        def _():
            @pl.when(z < 3)
            def _():
                pl.semaphore_wait(rcr, 1)

            @pl.when(z > 0)
            def _():
                pl.semaphore_wait(lcr, 1)

        def up_first(t):
            k = 3 - t
            add_into(slot, k, ry, k)

            @pl.when((z == 0) & (k > 0))
            def _():
                right(slot, k).start()

        def down_first(t):
            add_into(slot, t, ry, t)

            @pl.when((z == 3) & (t < 3))
            def _():
                left(slot, t).start()

        @pl.when(z < 2)
        def _():
            loop(0, 4, up_first)

        @pl.when(z >= 2)
        def _():
            loop(0, 4, down_first)

        @pl.when(i + SLOTS < CHUNKS)
        def _():
            pl.semaphore_signal(ycr, 1, device_id=ypeer, device_id_type=MESH)

    def pass_right(slot, k):
        right(slot, k).wait_recv()
        add_into(slot, k, rz, k + 1)
        right(slot, k).start()

    def pass_left(slot, k):
        left(slot, k).wait_recv()
        add_into(slot, k, rz, k)
        left(slot, k).start()

    def fwd_z(i):
        slot = lax.rem(i, SLOTS)

        @pl.when(z == 1)
        def _():
            pass_right(slot, 3)
            pass_right(slot, 2)
            pass_left(slot, 0)

        @pl.when(z == 2)
        def _():
            pass_left(slot, 0)
            pass_left(slot, 1)
            pass_right(slot, 3)

    def finish(i):
        slot = lax.rem(i, SLOTS)

        @pl.when(z > 0)
        def _():
            right(slot, z).wait_recv()
            add_into(slot, z, rz, z + 1)

        @pl.when(z < 3)
        def _():
            left(slot, z).wait_recv()
            add_into(slot, z, rz, z)

        total = rg[slot, z, y].astype(F32)

        @pl.when(i < 4)
        def _():
            gd_o[pl.ds(pl.multiple_of(i * 512, 512), 512)] = total.T

        @pl.when((i >= 4) & (i < 8))
        def _():
            gu_o[:, pl.ds(pl.multiple_of((i - 4) * 512, 512), 512)] = total

        @pl.when(i == 8)
        def _():
            go_o[...] = total.T

        @pl.when(i > 8)
        def _():
            gq_o[i - 9] = total

        @pl.when(i + SLOTS < CHUNKS)
        def _():
            @pl.when(z > 0)
            def _():
                pl.semaphore_signal(rcr, 1, device_id=zdown, device_id_type=MESH)

            @pl.when(z < 3)
            def _():
                pl.semaphore_signal(lcr, 1, device_id=zup, device_id_type=MESH)

    flip(lambda b: gd[b].reshape(ROWS, 1024))
    loop(0, 4, lambda i: make_chunk(i, lambda: hid[i].reshape(768, 512), lambda: hid[i, 0]))

    def phase_dff(b):
        g_low = gd[b].reshape(ROWS, 1024)
        for f in range(4):
            t = dot_nt(g_low, wd[f * 512 : f * 512 + 512])
            for g in range(8):
                at = slice(g * 32, g * 32 + 32)
                u = up[f, b, at].astype(F32)
                th = gelu_parts(u)
                c0 = math.sqrt(2.0 / math.pi)
                slope = 0.5 * (1.0 + th) + 0.5 * u * (1.0 - th * th) * (c0 * (1.0 + 3.0 * 0.044715 * (u * u)))
                up[f, b, at] = (slope * t[g * 32 : g * 32 + 32]).astype(BF)
        for n in range(2):
            at = slice(n * 512, n * 512 + 512)
            t = dot_nt(up[0, b], wu[at, 0:512])
            for f in range(1, 4):
                t = t + dot_nt(up[f, b], wu[at, f * 512 : f * 512 + 512])
            put_xs(b, at, t)
        exchange(b, b, True).start()

    loop(0, nb, phase_dff)
    proc_y(0)

    def phase_dmid(b):
        exchange(b, b, True).wait()
        gain = gains[0, 1:2]

        def rows(i):
            mb, mh, r = at16(i)
            at = pl.ds(pl.multiple_of(i * 16, 16), 16)
            dbm = summed(b, b, i)
            v = mid[b, at]
            sc = lax.rsqrt(jnp.mean(v * v, axis=-1, keepdims=True) + norm_eps)
            u = dbm * gain
            vn = v * sc
            corr = jnp.mean(vn * u, axis=-1, keepdims=True)
            dm = gd[b, mb, mh, r].astype(F32) + sc * (u - vn * corr)
            mid[b, at] = dm
            ga[b, mb, mh, r] = dm.astype(BF)
            part = dbm * vn
            gga[1] = gga[1] + (part[0:8] + part[8:16])

        loop(0, 16, rows, unroll=2)
        dob[b] = dot_nt(ga[b].reshape(ROWS, 1024), wo[...]).astype(BF)

    loop(0, nb, phase_dmid)
    proc_y(1)
    fwd_z(0)

    @pl.when(frame)
    def _():
        def pair(g):
            cols = pl.ds(pl.multiple_of(g * 128, 128), 128)
            for mb in range(2):
                at = slice(mb * 128, mb * 128 + 128)
                allowed, low_half = frame_masks(mb)
                q, k, v = (qkv[0, c, at, cols] for c in range(3))
                do = dob[0, at, cols]
                dq, dk, dv = [], [], []
                for sel in (low_half, ~low_half):
                    p = frame_probs(q, k, sel, allowed)
                    dp = dot_nt(jnp.where(sel, do, jnp.zeros_like(do)), v)
                    ds = (p * (dp - jnp.sum(dp * p, axis=-1, keepdims=True))).astype(BF)
                    dv.append(dot_tn(p.astype(BF), do))
                    dq.append(dot_nn(ds, k))
                    dk.append(dot_tn(ds, q))
                co, si = cs[0, at], cs[1, at]
                for c, pr in ((0, dq), (1, dk)):
                    t = jnp.where(low_half, pr[0], pr[1]) * scale
                    qkv[0, c, at, cols] = (t * co - swap_halves(t) * si).astype(BF)
                qkv[0, 2, at, cols] = jnp.where(low_half, dv[0], dv[1]).astype(BF)

        loop(0, 4, pair)

    @pl.when(code)
    def _():
        def part(i):
            at = pl.ds(pl.multiple_of(lax.div(i, 2) * 64, 64), 64)
            cols = pl.ds(pl.multiple_of(lax.rem(i, 2) * 256, 256), 256)
            q, k, v = ([qkv[b, c, at, cols].astype(F32) for b in range(3)] for c in range(3))
            do = [dob[b, at, cols].astype(F32) for b in range(3)]
            probs = code_probs(q, k)
            dk = [0.0] * 3
            dv = [0.0] * 3
            for i3 in range(3):
                dp = [head_sum(do[i3] * v[j]) for j in range(i3 + 1)]
                mean = functools.reduce(jnp.add, [dp[j] * probs[i3][j] for j in range(i3 + 1)])
                dq = 0.0
                for j in range(i3 + 1):
                    ds = (probs[i3][j] * (dp[j] - mean)).astype(BF).astype(F32)
                    dq = dq + ds * k[j]
                    dk[j] = dk[j] + ds * q[i3]
                    dv[j] = dv[j] + probs[i3][j].astype(BF).astype(F32) * do[i3]
                qkv[i3, 0, at, cols] = (dq * scale).astype(BF)
            for j in range(3):
                qkv[j, 1, at, cols] = (dk[j] * scale).astype(BF)
                qkv[j, 2, at, cols] = dv[j].astype(BF)

        loop(0, 8, part)

    def phase_dqkv(b):
        for n in range(2):
            at = slice(n * 512, n * 512 + 512)
            t = dot_nt(qkv[b, 0], wq[0, at])
            for c in range(1, 3):
                t = t + dot_nt(qkv[b, c], wq[c, at])
            put_xs(b, at, t)
        exchange(3 + b, b, False).start()

    loop(0, nb, phase_dqkv)
    proc_y(2)
    fwd_z(1)
    finish(0)

    @pl.when(code)
    def _():
        for cp in lo_local:
            cp.wait()
        for cp in lo_far:
            cp.wait_send()

    def phase_dx(b):
        exchange(3 + b, b, False).wait()
        gain = gains[0, 0:1]

        def rows(i):
            mb, r = lax.div(i, 4), pl.multiple_of(lax.rem(i, 4) * 16, 16)
            row = pl.multiple_of(mb * 128 + m * 64 + r, 16)
            da = xs[b, mb, m, pl.ds(r, 16)].astype(F32) + xr[3 + b, mb, m, pl.ds(r, 16)].astype(F32)
            v = xb[b, pl.ds(row, 16)]
            sc = lax.rsqrt(jnp.mean(v * v, axis=-1, keepdims=True) + norm_eps)
            u = da * gain
            vn = v * sc
            corr = jnp.mean(vn * u, axis=-1, keepdims=True)
            mid[b, pl.ds(row, 16)] = mid[b, pl.ds(row, 16)] + sc * (u - vn * corr)
            part = da * vn
            gga[0] = gga[0] + (part[0:8] + part[8:16])

        loop(0, 8, rows, unroll=2)

    loop(0, nb, phase_dx)

    dl_far = [remote(ob1.at[c], ob1.at[c], dls.at[c], dlr.at[c], across) for c in range(3)]

    @pl.when(code)
    def _():
        def rows(i):
            mb, r = lax.div(i, 4), pl.multiple_of(lax.rem(i, 4) * 16, 16)
            row = pl.multiple_of(mb * 128 + m * 64 + r, 16)
            parts = [mid[c, pl.ds(row, 16)] for c in range(3)]
            ob2[0, mb, pl.ds(r, 16)] = (parts[0] + parts[1] + parts[2]).astype(BF)
            for c in range(3):
                ob1[c, mb, pl.ds(r, 16)] = parts[c].astype(BF)

        loop(0, 8, rows)
        hop2[0].start()
        for cp in dl_far:
            cp.start()

    gm = remote(gpart.at[0], gpart.at[1], gms, gmr, peer)
    own0 = jnp.sum(gga[0], axis=0, keepdims=True)
    own1 = jnp.sum(gga[1], axis=0, keepdims=True)
    gpart[0] = jnp.broadcast_to(own0, (8, 1024))
    gm.start()

    def tail(i):
        @pl.when(i == 4)
        def _():
            flip(lambda b: bm[b])

        @pl.when(i == 8)
        def _():
            flip(lambda b: ga[b].reshape(ROWS, 1024))

        @pl.when(i == 9)
        def _():
            flip(lambda b: ab[b])

        @pl.when(i < 8)
        def _():
            make_chunk(i, lambda: up[i - 4].reshape(768, 512), lambda: up[i - 4, 0])

        @pl.when(i == 8)
        def _():
            make_chunk(i, lambda: ob[...].reshape(768, 512), lambda: ob[0])

        @pl.when((i > 8) & (i < CHUNKS))
        def _():
            c = i - 9
            make_chunk(i, lambda: jnp.concatenate([qkv[0, c], qkv[1, c], qkv[2, c]], axis=0), lambda: qkv[0, c])

        @pl.when(i - 1 < CHUNKS)
        def _():
            proc_y(i - 1)

        @pl.when(i - 2 < CHUNKS)
        def _():
            fwd_z(i - 2)

        finish(i - 3)

    loop(4, CHUNKS + 3, tail)

    gm.wait()
    mine = jnp.concatenate(
        [own0 + gpart[1, 0:1], own1, jnp.zeros((6, 1024), F32)], axis=0
    )
    ggr[d] = mine
    g_far = []
    for t in range(1, 8):
        o = lax.rem(d + t, 8)
        g_far.append((remote(ggr.at[d], ggr.at[d], ggs.at[t], ggrs.at[d], (s, o, m)),
                      remote(ggr.at[d], ggr.at[o], ggs.at[t], ggrs.at[o], (s, o, m))))
    for cp, _ in g_far:
        cp.start()

    @pl.when(frame)
    def _():
        for c in range(3):
            dl_far[c].wait_recv()

        def rows(i):
            mb, r = lax.div(i, 4), pl.multiple_of(lax.rem(i, 4) * 16, 16)
            row = pl.multiple_of(mb * 128 + m * 64 + r, 16)
            dx = mid[0, pl.ds(row, 16)]
            for c in range(3):
                ob2[c, mb, pl.ds(r, 16)] = (ob1[c, mb, pl.ds(r, 16)].astype(F32) + dx).astype(BF)

        loop(0, 8, rows)

    ge_local = [local(ob2.at[c], ge_h.at[:, c], gel.at[c]) for c in range(3)]
    ge_far = [remote(ob2.at[c], ge_h.at[:, c], ges.at[c], ger.at[c], across) for c in range(3)]

    @pl.when(frame)
    def _():
        for cp in ge_local + ge_far:
            cp.start()
        for cp in ge_local:
            cp.wait()
        for cp in ge_far:
            cp.wait_send()
        for cp in lo_far:
            cp.wait_recv()

    @pl.when(code)
    def _():
        hop2[0].wait_send()
        for cp in dl_far:
            cp.wait_send()
        for cp in ge_far:
            cp.wait_recv()

    for cp, back in g_far:
        cp.wait_send()
        back.wait_recv()
    acc = ggr[0]
    for t in range(1, 8):
        acc = acc + ggr[t]
    gg_o[0] = acc[0:2]
    for t in range(CHUNKS - SLOTS, CHUNKS):
        free_slot(t % SLOTS)


def on_device_kernel(embeds, lengths, norm_gains, w_qkv, w_out, w_up, w_down, cotangent):
    anyspec = pl.BlockSpec(memory_space=pl.ANY)
    vm = pl.BlockSpec(memory_space=pltpu.VMEM)
    sd = jax.ShapeDtypeStruct
    V = pltpu.VMEM
    D = pltpu.SemaphoreType.DMA
    R = pltpu.SemaphoreType.REGULAR
    half = (2, 64, 1024)
    full = (2, 2, 64, 1024)
    scratch = [
        V((3, 1024, 512), BF), V((512, 1024), BF), V((1024, 2048), BF), V((2048, 1024), BF),
        V((3,) + full, BF), V((3,) + full, BF), V(full, BF),
        V((3, ROWS, 1024), F32), V((3, ROWS, 1024), F32), V((3, ROWS, 1024), BF), V((3, ROWS, 1024), BF),
        V((3, 3, ROWS, 512), BF), V((3, ROWS, 512), BF), V((3, ROWS, 512), BF),
        V((4, 3, ROWS, 512), BF), V((4, 3, ROWS, 512), BF),
        V((3,) + full, BF), V((6,) + full, BF), V((1024, 768), BF),
        V((3,) + half, BF), V((3,) + half, BF),
        V((3, ROWS, 128), F32), V((2, 8, 1024), F32), V((8, 8, 1024), F32), V((2, 8, 1024), F32),
        V((SLOTS, 4, 2, 128, 512), BF), V((SLOTS, 4, 128, 512), BF), V((SLOTS, 5, 128, 512), BF),
        D((4,)), D((3,)), D((3,)), D((3,)), D((3,)), D((3,)), D((3,)), D((3,)), D((6,)), D((4,)), D((4,)),
        D((3,)), D((3,)), D((3,)), D((3,)), D((3,)),
        D((3,)), D((3,)), D((3,)), D((8,)), D((8,)), D, D,
        D((SLOTS,)), D((SLOTS,)), D((SLOTS, 4)), D((SLOTS, 4)), D((SLOTS, 4)), D((SLOTS, 4)), R, R, R,
    ]
    outs = pl.pallas_call(
        body,
        out_shape=(
            sd((2, 3, 64, 1024), BF), sd((2, 3, 64, 1024), BF), sd((1, 2, 1024), F32),
            sd((3, 128, 512), F32), sd((512, 128), F32), sd((128, 2048), F32), sd((2048, 128), F32),
        ),
        in_specs=[anyspec, anyspec, pl.BlockSpec(memory_space=pltpu.SMEM), vm, anyspec, anyspec, anyspec, anyspec],
        out_specs=(anyspec, anyspec, vm, vm, vm, vm, vm),
        scratch_shapes=scratch,
        compiler_params=pltpu.CompilerParams(
            collective_id=0, has_side_effects=True, vmem_limit_bytes=60 * 2**20
        ),
        name="two_sections",
    )(
        jnp.transpose(embeds, (0, 2, 1, 3)), jnp.transpose(cotangent, (0, 2, 1, 3)), lengths, norm_gains,
        jnp.transpose(w_qkv[0], (1, 0, 2)), w_out[0], w_up[0], w_down[0],
    )
    lo, ge, gg, gq, go, gu, gdn = outs
    return (
        jnp.transpose(lo, (0, 2, 1, 3)), jnp.transpose(ge, (0, 2, 1, 3)), gg,
        jnp.transpose(gq, (1, 0, 2))[None], go[None], gu[None], gdn[None],
    )


def solution(mesh):
    fits = tuple(mesh.shape[name] for name in ("section", "dp", "mp")) == (2, 8, 2)
    return jax.shard_map(
        on_device_kernel if fits else on_device,
        mesh=mesh,
        in_specs=(
            P(None, ("dp", "mp"), None, None),
            P(None, "dp", None),
            P("section", None, None),
            P("section", None, None, "mp"),
            P("section", "mp", None),
            P("section", None, "mp"),
            P("section", "mp", None),
            P(None, ("dp", "mp"), None, None),
        ),
        out_specs=(
            P(None, ("dp", "mp"), None, None),
            P(None, ("dp", "mp"), None, None),
            P("section", None, None),
            P("section", "dp", None, "mp"),
            P("section", "mp", "dp"),
            P("section", "dp", "mp"),
            P("section", "mp", "dp"),
        ),
        check_vma=False,
    )
```

```python
import functools
import math

import jax
import jax.numpy as jnp
from jax import lax
from jax.experimental import pallas as pl
from jax.experimental.pallas import tpu as pltpu
from jax.sharding import PartitionSpec as P

HEAD_DIM = 64


norm_eps = 1e-05
masked_fill = -1e30
rotary_base = 10000.0


def passed_along(value, axis, steps):
    count = lax.axis_size(axis)
    leading, last = (max(0, -steps), min(count, count - steps))
    return lax.ppermute(value, axis, [(source, source + steps) for source in range(leading, last)])


def rms_scale(values, gain_row):
    return (
        values * lax.rsqrt(jnp.mean(values * values, axis=-1, keepdims=True) + norm_eps) * gain_row
    )


def rotate(values, cos_tab, sin_tab):
    half_dim = values.shape[-1] // 2
    first_half = values[..., :half_dim]
    second_half = values[..., half_dim:]
    cos_rows = cos_tab[:, None, :]
    sin_rows = sin_tab[:, None, :]
    return jnp.concatenate(
        [
            first_half * cos_rows - second_half * sin_rows,
            second_half * cos_rows + first_half * sin_rows,
        ],
        axis=-1,
    )


def global_context(length_row, frames):
    doc_ends = jnp.cumsum(length_row)
    places = jnp.arange(frames, dtype=jnp.int32)
    passed = (places[:, None] >= doc_ends[None, :]).astype(jnp.int32)
    segment = jnp.sum(passed, axis=1)
    offsets = places - jnp.sum(passed * length_row[None, :], axis=1)
    allowed = (segment[:, None] == segment[None, :]) & (places[None, :] <= places[:, None])
    half_dim = HEAD_DIM // 2
    frequency = jnp.exp(
        jnp.arange(half_dim, dtype=jnp.float32) * (-2.0 * math.log(rotary_base) / HEAD_DIM)
    )
    angles = offsets.astype(jnp.float32)[:, None] * frequency[None, :]
    return (allowed, jnp.cos(angles), jnp.sin(angles))


def global_attend(projected, context):
    allowed, cos_tab, sin_tab = context
    attn_scale = 1.0 / math.sqrt(HEAD_DIM)
    row_total, _, local_width = projected.shape
    head_count = local_width // HEAD_DIM
    query_rows = rotate(
        projected[:, 0].reshape(row_total, head_count, HEAD_DIM), cos_tab, sin_tab
    ).astype(jnp.bfloat16)
    key_rows = rotate(
        projected[:, 1].reshape(row_total, head_count, HEAD_DIM), cos_tab, sin_tab
    ).astype(jnp.bfloat16)
    value_rows = projected[:, 2].reshape(row_total, head_count, HEAD_DIM).astype(jnp.bfloat16)
    scores = (
        jnp.einsum("qhd,khd->hqk", query_rows, key_rows, preferred_element_type=jnp.float32)
        * attn_scale
    )
    scores = jnp.where(allowed[None], scores, masked_fill)
    score_peak = jnp.max(scores, axis=-1, keepdims=True)
    exp_scores = jnp.exp(scores - score_peak)
    row_sums = jnp.sum(exp_scores, axis=-1, keepdims=True)
    weights_low = (exp_scores / row_sums).astype(jnp.bfloat16)
    mixed_rows = jnp.einsum(
        "hqk,khd->qhd", weights_low, value_rows, preferred_element_type=jnp.float32
    )
    log_total = score_peak + jnp.log(row_sums)
    return (
        mixed_rows.reshape(row_total, local_width).astype(jnp.bfloat16),
        (query_rows, key_rows, value_rows, log_total),
    )


def global_attend_back(attn_saved, context, grad_mixed):
    query_rows, key_rows, value_rows, log_total = attn_saved
    allowed, cos_tab, sin_tab = context
    attn_scale = 1.0 / math.sqrt(HEAD_DIM)
    row_total, head_count, _ = query_rows.shape
    grad_heads = grad_mixed.reshape(row_total, head_count, HEAD_DIM)
    scores = (
        jnp.einsum("qhd,khd->hqk", query_rows, key_rows, preferred_element_type=jnp.float32)
        * attn_scale
    )
    prob_rows = jnp.where(allowed[None], jnp.exp(scores - log_total), 0.0)
    grad_values = jnp.einsum(
        "hqk,qhd->khd",
        prob_rows.astype(jnp.bfloat16),
        grad_heads,
        preferred_element_type=jnp.float32,
    )
    grad_probs = jnp.einsum(
        "qhd,khd->hqk", grad_heads, value_rows, preferred_element_type=jnp.float32
    )
    grad_scores = (
        prob_rows * (grad_probs - jnp.sum(grad_probs * prob_rows, axis=-1, keepdims=True))
    ).astype(jnp.bfloat16)
    grad_query = (
        jnp.einsum("hqk,khd->qhd", grad_scores, key_rows, preferred_element_type=jnp.float32)
        * attn_scale
    )
    grad_keys = (
        jnp.einsum("hqk,qhd->khd", grad_scores, query_rows, preferred_element_type=jnp.float32)
        * attn_scale
    )
    grad_query = rotate(grad_query, cos_tab, -sin_tab)
    grad_keys = rotate(grad_keys, cos_tab, -sin_tab)
    stacked = jnp.stack([grad_query, grad_keys, grad_values], axis=1)
    return stacked.reshape(row_total, 3, head_count * HEAD_DIM).astype(jnp.bfloat16)


def local_attend(projected, context):
    attn_scale = 1.0 / math.sqrt(HEAD_DIM)
    row_total, _, local_width = projected.shape
    head_count = local_width // HEAD_DIM
    frames = row_total // 3
    qkv_parts = projected.reshape(frames, 3, 3, head_count, HEAD_DIM).astype(jnp.bfloat16)
    query_rows = qkv_parts[:, :, 0]
    key_rows = qkv_parts[:, :, 1]
    value_rows = qkv_parts[:, :, 2]
    scores = (
        jnp.einsum("fihd,fjhd->fhij", query_rows, key_rows, preferred_element_type=jnp.float32)
        * attn_scale
    )
    scores = jnp.where(context[None, None], scores, masked_fill)
    score_peak = jnp.max(scores, axis=-1, keepdims=True)
    exp_scores = jnp.exp(scores - score_peak)
    row_sums = jnp.sum(exp_scores, axis=-1, keepdims=True)
    weights_low = (exp_scores / row_sums).astype(jnp.bfloat16)
    mixed_rows = jnp.einsum(
        "fhij,fjhd->fihd", weights_low, value_rows, preferred_element_type=jnp.float32
    )
    log_total = score_peak + jnp.log(row_sums)
    return (
        mixed_rows.reshape(row_total, local_width).astype(jnp.bfloat16),
        (query_rows, key_rows, value_rows, log_total),
    )


def local_attend_back(attn_saved, context, grad_mixed):
    query_rows, key_rows, value_rows, log_total = attn_saved
    attn_scale = 1.0 / math.sqrt(HEAD_DIM)
    frames, _, head_count, _ = query_rows.shape
    grad_heads = grad_mixed.reshape(frames, 3, head_count, HEAD_DIM)
    scores = (
        jnp.einsum("fihd,fjhd->fhij", query_rows, key_rows, preferred_element_type=jnp.float32)
        * attn_scale
    )
    prob_rows = jnp.where(context[None, None], jnp.exp(scores - log_total), 0.0)
    grad_values = jnp.einsum(
        "fhij,fihd->fjhd",
        prob_rows.astype(jnp.bfloat16),
        grad_heads,
        preferred_element_type=jnp.float32,
    )
    grad_probs = jnp.einsum(
        "fihd,fjhd->fhij", grad_heads, value_rows, preferred_element_type=jnp.float32
    )
    grad_scores = (
        prob_rows * (grad_probs - jnp.sum(grad_probs * prob_rows, axis=-1, keepdims=True))
    ).astype(jnp.bfloat16)
    grad_query = (
        jnp.einsum("fhij,fjhd->fihd", grad_scores, key_rows, preferred_element_type=jnp.float32)
        * attn_scale
    )
    grad_keys = (
        jnp.einsum("fhij,fihd->fjhd", grad_scores, query_rows, preferred_element_type=jnp.float32)
        * attn_scale
    )
    stacked = jnp.stack([grad_query, grad_keys, grad_values], axis=2)
    return stacked.reshape(frames * 3, 3, head_count * HEAD_DIM).astype(jnp.bfloat16)


def gather_project(normed, weight, form):
    piece_rows = lax.all_gather(normed, "mp", axis=0, tiled=True)
    return (piece_rows, jnp.einsum(form, piece_rows, weight, preferred_element_type=jnp.float32))


def reduce_rows(left, weight, form, row_count):

    def partial_term(first_row, count_rows):
        return jnp.einsum(form, left, weight, preferred_element_type=jnp.float32)

    return lax.psum_scatter(
        partial_term(jnp.int32(0), row_count * lax.axis_size("mp")),
        "mp",
        scatter_dimension=0,
        tiled=True,
    )


def reduce_grads(left, weight, form, row_count):

    def partial_term(first_row, count_rows):
        return jnp.einsum(form, left, weight, preferred_element_type=jnp.float32)

    return lax.psum_scatter(
        partial_term(jnp.int32(0), row_count * lax.axis_size("mp")),
        "mp",
        scatter_dimension=0,
        tiled=True,
    )


def gather_grads(grad_low):
    return lax.all_gather(grad_low, "mp", axis=0, tiled=True)


def layer_forward(frame_rows, weights, attend, context):
    gain_pair, w_qkv, w_out, w_up, w_down = weights
    row_count = frame_rows.shape[0]
    normed = rms_scale(frame_rows, gain_pair[0]).astype(jnp.bfloat16)
    normed_all, projected = gather_project(normed, w_qkv, "nd,dce->nce")
    mixed_rows, attn_saved = attend(projected, context)
    attn_rows = reduce_rows(mixed_rows, w_out, "ne,ed->nd", row_count)
    middle = frame_rows + attn_rows
    normed_mid = rms_scale(middle, gain_pair[1]).astype(jnp.bfloat16)
    normed_mid_all, up_all = gather_project(normed_mid, w_up, "nd,de->ne")
    hidden = jax.nn.gelu(up_all).astype(jnp.bfloat16)
    down_rows = reduce_rows(hidden, w_down, "nf,fd->nd", row_count)
    record = (normed_all, attn_saved, mixed_rows, middle, normed_mid_all, up_all, hidden)
    return (middle + down_rows, attn_rows + down_rows, record)


def layer_backward(frame_rows, weights, attend_back, context, record, grad_result):
    gain_pair, w_qkv, w_out, w_up, w_down = weights
    normed_all, attn_saved, mixed_rows, middle, normed_mid_all, up_all, hidden = record
    row_count = frame_rows.shape[0]
    grad_down_all = gather_grads(grad_result.astype(jnp.bfloat16))
    grad_w_down = jnp.einsum("nf,nd->fd", hidden, grad_down_all, preferred_element_type=jnp.float32)
    grad_hidden = jnp.einsum("nd,fd->nf", grad_down_all, w_down, preferred_element_type=jnp.float32)
    _, gelu_back = jax.vjp(jax.nn.gelu, up_all)
    grad_up = gelu_back(grad_hidden)[0].astype(jnp.bfloat16)
    grad_w_up = jnp.einsum("nd,ne->de", normed_mid_all, grad_up, preferred_element_type=jnp.float32)
    grad_normed_mid = reduce_grads(grad_up, w_up, "ne,de->nd", row_count)
    _, mid_back = jax.vjp(rms_scale, middle, gain_pair[1])
    grad_middle_part, grad_gain_mid = mid_back(grad_normed_mid)
    grad_middle = grad_result + grad_middle_part
    grad_attn_all = gather_grads(grad_middle.astype(jnp.bfloat16))
    grad_w_out = jnp.einsum(
        "ne,nd->ed", mixed_rows, grad_attn_all, preferred_element_type=jnp.float32
    )
    grad_mixed = jnp.einsum(
        "nd,ed->ne", grad_attn_all, w_out, preferred_element_type=jnp.float32
    ).astype(jnp.bfloat16)
    grad_projected = attend_back(attn_saved, context, grad_mixed)
    grad_w_qkv = jnp.einsum(
        "nd,nce->dce", normed_all, grad_projected, preferred_element_type=jnp.float32
    )
    grad_normed = reduce_grads(grad_projected, w_qkv, "nce,dce->nd", row_count)
    _, first_back = jax.vjp(rms_scale, frame_rows, gain_pair[0])
    grad_rows_part, grad_gain_first = first_back(grad_normed)
    grad_frame_rows = grad_middle + grad_rows_part
    layer_grads = (
        jnp.stack([grad_gain_first, grad_gain_mid]),
        grad_w_qkv,
        grad_w_out,
        grad_w_up,
        grad_w_down,
    )
    return (grad_frame_rows, layer_grads)


def on_device(embeds, lengths, norm_gains, w_qkv, w_out, w_up, w_down, cotangent):
    weights = (norm_gains[0], w_qkv[0], w_out[0], w_up[0], w_down[0])
    micro_count = embeds.shape[0]
    shard_rows = embeds.shape[1]
    width = embeds.shape[-1]
    frames = shard_rows * lax.axis_size("mp")
    is_first = lax.axis_index("section") == 0
    local_allowed = jnp.tril(jnp.ones((3, 3), dtype=jnp.bool_))
    gain_total = jnp.zeros(norm_gains.shape[1:], jnp.float32)
    weight_totals = tuple((jnp.zeros(weight.shape, jnp.float32) for weight in weights[1:]))
    totals = (gain_total,) + weight_totals
    y_part = jnp.zeros(embeds.shape, jnp.float32)
    e_part = jnp.zeros(embeds.shape, jnp.float32)
    zero_send = jnp.zeros((shard_rows, width), jnp.bfloat16)

    def add_grads(running, layer_grads):
        run_gain, run_qkv, run_out, run_up, run_down = running
        part_gain, part_qkv, part_out, part_up, part_down = layer_grads
        return (
            run_gain + part_gain,
            run_qkv + part_qkv,
            run_out + part_out,
            run_up + part_up,
            run_down + part_down,
        )

    def global_forward(micro_index):
        context = global_context(lengths[micro_index, 0], frames)
        frame_in = jnp.sum(embeds[micro_index].astype(jnp.float32), axis=1)
        result, _, record = layer_forward(frame_in, weights, global_attend, context)
        return (frame_in, context, result, record)

    def pick(first_value, second_value):
        return jnp.where(is_first, first_value, second_value)

    carry_state = (totals, y_part, e_part)
    forward_recv = zero_send
    backward_recv = zero_send
    for tick_index in range(micro_count + 2):

        def first_section(state_in):
            running, y_state, e_state = state_in
            send_fwd = zero_send
            if tick_index < micro_count:
                _, _, result, _ = global_forward(tick_index)
                send_fwd = result.astype(jnp.bfloat16)
                joined = (
                    embeds[tick_index].astype(jnp.float32)
                    + send_fwd.astype(jnp.float32)[:, None, :]
                )
                y_state = y_state.at[tick_index].set(joined)
            if tick_index >= 2:
                micro_index = tick_index - 2
                frame_in, context, _, record = global_forward(micro_index)
                grad_frame, layer_grads = layer_backward(
                    frame_in,
                    weights,
                    global_attend_back,
                    context,
                    record,
                    backward_recv.astype(jnp.float32),
                )
                running = add_grads(running, layer_grads)
                e_state = e_state.at[micro_index].set(
                    jnp.broadcast_to(grad_frame[:, None, :], e_state.shape[1:])
                )
            return ((running, y_state, e_state), send_fwd, zero_send)

        def second_section(state_in):
            running, y_state, e_state = state_in
            send_back = zero_send
            if 1 <= tick_index <= micro_count:
                micro_index = tick_index - 1
                local_in = (
                    embeds[micro_index].astype(jnp.float32)
                    + forward_recv.astype(jnp.float32)[:, None, :]
                )
                local_in = local_in.reshape(shard_rows * 3, width)
                _, branches, record = layer_forward(local_in, weights, local_attend, local_allowed)
                grad_seed = (
                    cotangent[micro_index].astype(jnp.float32).reshape(shard_rows * 3, width)
                )
                grad_local, layer_grads = layer_backward(
                    local_in, weights, local_attend_back, local_allowed, record, grad_seed
                )
                running = add_grads(running, layer_grads)
                y_state = y_state.at[micro_index].set(branches.reshape(shard_rows, 3, width))
                grad_frames = grad_local.reshape(shard_rows, 3, width)
                e_state = e_state.at[micro_index].set(grad_frames)
                send_back = jnp.sum(grad_frames, axis=1).astype(jnp.bfloat16)
            return ((running, y_state, e_state), zero_send, send_back)

        first_result = first_section(carry_state)
        second_result = second_section(carry_state)
        carry_state, send_fwd, send_back = jax.tree.map(pick, first_result, second_result)
        if tick_index < micro_count:
            forward_recv = passed_along(send_fwd, "section", 1)
        if 1 <= tick_index <= micro_count:
            backward_recv = passed_along(send_back, "section", -1)
    totals, y_part, e_part = carry_state
    gain_total, grad_qkv, grad_out, grad_up, grad_down = totals
    grad_qkv, grad_out, grad_up, grad_down = (
        lax.psum_scatter(grad_qkv, "dp", scatter_dimension=0, tiled=True),
        lax.psum_scatter(grad_out, "dp", scatter_dimension=1, tiled=True),
        lax.psum_scatter(grad_up, "dp", scatter_dimension=0, tiled=True),
        lax.psum_scatter(grad_down, "dp", scatter_dimension=1, tiled=True),
    )
    gain_total = lax.psum(gain_total, ("dp", "mp"))
    y_sum, e_sum = (
        lax.psum(y_part.astype(jnp.bfloat16), "section").astype(jnp.float32),
        lax.psum(e_part.astype(jnp.bfloat16), "section").astype(jnp.float32),
    )
    return (
        y_sum.astype(jnp.bfloat16),
        e_sum.astype(jnp.bfloat16),
        gain_total[None],
        grad_qkv[None],
        grad_out[None],
        grad_up[None],
        grad_down[None],
    )


BF = jnp.bfloat16
F32 = jnp.float32
MESH = pl.DeviceIdType.MESH
SLOTS = 4
CHUNKS = 12
ROWS = 256
UNROLL = 4


def dot_nn(left, right):
    return lax.dot_general(left, right, (((1,), (0,)), ((), ())), preferred_element_type=F32)


def dot_nt(left, right):
    return lax.dot_general(left, right, (((1,), (1,)), ((), ())), preferred_element_type=F32)


def dot_tn(left, right):
    return lax.dot_general(left, right, (((0,), (0,)), ((), ())), preferred_element_type=F32)


def gelu_tanh(u):
    c0 = math.sqrt(2.0 / math.pi)
    return jnp.tanh(u * (c0 + (c0 * 0.044715) * (u * u)))


def gelu_slope(u, th):
    c0 = math.sqrt(2.0 / math.pi)
    return 0.5 * (1.0 + th) + 0.5 * u * (1.0 - th * th) * (c0 + (3.0 * 0.044715 * c0) * (u * u))


def loop(lower, upper, step, unroll=1):
    def wrapped(i, carry):
        step(i)
        return carry

    lax.fori_loop(lower, upper, wrapped, 0, unroll=unroll)


def grouped(count, work, store, size=4):
    def group(g):
        done = [work(g * size + t) for t in range(size)]
        for t in range(size):
            store(g * size + t, *done[t])

    loop(0, count // size, group)


def by16(i):
    return pl.ds(pl.multiple_of(i * 16, 16), 16)


def by512(i):
    return pl.ds(pl.multiple_of(i * 512, 512), 512)


def halves16(i):
    return lax.div(i, 8), lax.rem(lax.div(i, 4), 2), pl.ds(pl.multiple_of(lax.rem(i, 4) * 16, 16), 16)


def own16(i, m):
    mb, r = lax.div(i, 4), pl.multiple_of(lax.rem(i, 4) * 16, 16)
    return mb, pl.ds(r, 16), pl.ds(pl.multiple_of(mb * 128 + m * 64 + r, 16), 16)


def swap_halves(v):
    lane = lax.broadcasted_iota(jnp.int32, v.shape, 1)
    return jnp.where(lax.rem(lane, 64) < 32, pltpu.roll(v, 96, 1), pltpu.roll(v, 32, 1))


def body(
    emb, cot, lens, gains, wq_h, wo_h, wu_h, wd_h,
    lo_h, ge_h, g_h, gg_o,
    wq, wo, wu, wd, em, gd, sr, xm, ab, bm, qk, ob, dob, uph, xs, xr, tb, ob1, ob2,
    cs, tabs, st, gga, ggr, gpart, rg, ryz,
    gsem, wsem, esem, exs, exr, csem, cxs, cxr, mps, mpr, hops, hopr, lol, los, lor, dls, dlr,
    gel, ges, ger, ggs, ggrs, gms, gmr, ysn, yrc, zrs, zrr, zls, zlr,
    sts, strc, xas, xar, xms, xmr, das, dar, dms, dmr, ycr, rcr, lcr,
):
    s = lax.axis_index("section")
    d = lax.axis_index("dp")
    m = lax.axis_index("mp")
    y = lax.rem(d, 2)
    z = lax.div(d, 2)
    peer = (s, d, 1 - m)
    across = (1 - s, d, m)
    ypeer = (s, d + 1 - 2 * y, m)
    zup = (s, jnp.minimum(d + 2, 7), m)
    zdown = (s, jnp.maximum(d - 2, 0), m)
    frame = s == 0
    code = s == 1
    scale = 1.0 / math.sqrt(HEAD_DIM)

    def remote(src, dst, ssem, rsem, to):
        return pltpu.make_async_remote_copy(
            src_ref=src, dst_ref=dst, send_sem=ssem, recv_sem=rsem, device_id=to, device_id_type=MESH
        )

    def local(src, dst, sem):
        return pltpu.make_async_copy(src, dst, sem)

    w_copies = [local(a, b, wsem.at[i]) for i, (a, b) in enumerate(((wq_h, wq), (wo_h, wo), (wu_h, wu), (wd_h, wd)))]
    e_local = [local(emb.at[:, c], em.at[c, :, m], esem.at[c]) for c in range(3)]
    c_local = [local(cot.at[:, c], gd.at[c, :, m], csem.at[c]) for c in range(3)]
    for cp in e_local:
        cp.start()
    w_copies[0].start()

    bar = pltpu.get_barrier_semaphore()
    pl.semaphore_signal(bar, 1, device_id=peer, device_id_type=MESH)
    pl.semaphore_signal(bar, 1, device_id=across, device_id_type=MESH)
    for t in range(1, 8):
        pl.semaphore_signal(bar, 1, device_id=(s, lax.rem(d + t, 8), m), device_id_type=MESH)
    with jax.named_scope("barrier"):
        pl.semaphore_wait(bar, 9)

    e_far = [remote(emb.at[:, c], em.at[c, :, m], exs.at[c], exr.at[c], peer) for c in range(3)]
    c_far = [remote(cot.at[:, c], gd.at[c, :, m], cxs.at[c], cxr.at[c], peer) for c in range(3)]
    for cp in e_far:
        cp.start()
    for cp in w_copies[1:]:
        cp.start()

    hop = [remote(sr.at[:, m], sr.at[:, m], hops.at[0], hopr.at[0], across),
           remote(sr.at[:, m], sr.at[:, m], hops.at[1], hopr.at[1], peer)]
    hop2 = [
        remote(ob2.at[0, :, :, c * 512 : c * 512 + 512],
               ryz.at[pl.ds(d * 4 + c * 2, 2), pl.ds(pl.multiple_of(m * 64, 64), 64)],
               hops.at[2 + c], hopr.at[2 + c], across)
        for c in range(2)
    ]
    lo_local = [local(ob1.at[c], lo_h.at[:, c], lol.at[c]) for c in range(3)]
    lo_far = [remote(ob1.at[c], lo_h.at[:, c], los.at[c], lor.at[c], across) for c in range(3)]
    dl_far = [remote(ob1.at[c], ob1.at[c], dls.at[c], dlr.at[c], across) for c in range(3)]
    ge_local = [local(ob2.at[c], ge_h.at[:, c], gel.at[c]) for c in range(3)]
    ge_far = [remote(ob2.at[c], ge_h.at[:, c], ges.at[c], ger.at[c], across) for c in range(3)]

    grads_out = local(xm, g_h, gsem)
    gga[...] = jnp.zeros_like(gga)

    def rms(v):
        return lax.rsqrt(jnp.mean(v * v, axis=-1, keepdims=True) + norm_eps)

    def exchange(recv_slot, send_slot, whole):
        mine = slice(None) if whole else 1 - m
        return remote(xs.at[send_slot, :, mine], xr.at[recv_slot, :, mine], mps.at[send_slot], mpr.at[recv_slot], peer)

    def put_xs(slot, cols, t):
        xs[slot, :, :, :, cols] = t.astype(BF).reshape(2, 2, 64, t.shape[-1])

    def summed(recv_slot, send_slot, i):
        mb, mh, r = halves16(i)
        return xs[send_slot, mb, mh, r].astype(F32) + xr[recv_slot, mb, mh, r].astype(F32)

    def summed_own(recv_slot, send_slot, i):
        mb, r, _ = own16(i, m)
        return xs[send_slot, mb, m, r].astype(F32) + xr[recv_slot, mb, m, r].astype(F32)

    def out_block(o, recv_slot, send_slot):
        for n in range(2):
            put_xs(send_slot, slice(n * 512, n * 512 + 512), dot_nn(o, wo[:, n * 512 : n * 512 + 512]))
        exchange(recv_slot, send_slot, True).start()

    def up_block(b_in, put):
        for f in range(4):
            t = dot_nn(b_in, wu[:, f * 512 : f * 512 + 512])
            for g in range(8):
                put(f, slice(g * 32, g * 32 + 32), t[g * 32 : g * 32 + 32])

    def down_block(get_hid, recv_slot, send_slot):
        for n in range(2):
            cols = slice(n * 512, n * 512 + 512)
            t = dot_nn(get_hid(0), wd[0:512, cols])
            for f in range(1, 4):
                t = t + dot_nn(get_hid(f), wd[f * 512 : f * 512 + 512, cols])
            put_xs(send_slot, cols, t)
        exchange(recv_slot, send_slot, False).start()

    def dff_block(g_low, page, put_hid, recv_slot, send_slot):
        for f in range(4):
            t = dot_nt(g_low, wd[f * 512 : f * 512 + 512])
            for g in range(8):
                at = slice(g * 32, g * 32 + 32)
                u = uph[page(f), at].astype(F32)
                th = gelu_tanh(u)
                if put_hid is not None:
                    put_hid(f, at, (0.5 * u * (1.0 + th)).astype(BF))
                uph[page(f), at] = (gelu_slope(u, th) * t[g * 32 : g * 32 + 32]).astype(BF)
        for n in range(2):
            at = slice(n * 512, n * 512 + 512)
            t = dot_nt(uph[page(0)], wu[at, 0:512])
            for f in range(1, 4):
                t = t + dot_nt(uph[page(f)], wu[at, f * 512 : f * 512 + 512])
            put_xs(send_slot, at, t)
        exchange(recv_slot, send_slot, True).start()

    def dqkv_block(page, recv_slot, send_slot):
        for n in range(2):
            at = slice(n * 512, n * 512 + 512)
            t = dot_nt(qk[page(0)], wq[0, at])
            for c in range(1, 3):
                t = t + dot_nt(qk[page(c)], wq[c, at])
            put_xs(send_slot, at, t)
        exchange(recv_slot, send_slot, False).start()

    def norm_back(v, grad, gain):
        sc = rms(v)
        u = grad * gain
        vn = v * sc
        corr = jnp.mean(vn * u, axis=-1, keepdims=True)
        return sc * (u - vn * corr), grad * vn

    def add_gain(row, part):
        gga[row] = gga[row] + (part[0:8] + part[8:16])

    def acc_at(i):
        t = lax.rem(i, 4)
        return lax.div(i, 4), pl.ds(pl.multiple_of(lax.div(t, 2) * 128, 128), 128), by512(lax.rem(t, 2))

    gm = remote(gpart.at[0], gpart.at[1], gms, gmr, peer)

    def gain_first():
        gpart[0] = jnp.broadcast_to(jnp.sum(gga[0], axis=0, keepdims=True), (8, 1024))
        gm.start()

    g_far = []
    for t in range(1, 8):
        o = lax.rem(d + t, 8)
        g_far.append((remote(ggr.at[d], ggr.at[d], ggs.at[t], ggrs.at[d], (s, o, m)),
                      remote(ggr.at[d], ggr.at[o], ggs.at[t], ggrs.at[o], (s, o, m))))

    def gain_second():
        gm.wait()
        own1 = jnp.sum(gga[1], axis=0, keepdims=True)
        ggr[d] = jnp.concatenate([gpart[0, 0:1] + gpart[1, 0:1], own1, jnp.zeros((6, 1024), F32)], axis=0)
        for cp, _ in g_far:
            cp.start()

    def gain_last():
        for cp, back in g_far:
            cp.wait_send()
            back.wait_recv()
        acc = ggr[0]
        for t in range(1, 8):
            acc = acc + ggr[t]
        gg_o[0] = acc[0:2]

    def low_lanes():
        return lax.broadcasted_iota(jnp.int32, (128, 128), 1) < 64

    def stack_heads(v):
        zero = jnp.zeros_like(v)
        return jnp.concatenate([jnp.where(low_lanes(), v, zero), jnp.where(low_lanes(), zero, v)], axis=0)

    def side_by_side(v):
        return jnp.concatenate([v[0:128], v[128:256]], axis=1)

    def frame_allowed(mb):
        pos = lax.broadcasted_iota(jnp.int32, (128, 128), 0)
        lane = lax.broadcasted_iota(jnp.int32, (128, 128), 1)
        one = (lane <= pos) & (lane.astype(F32) >= cs[2, mb * 128 : mb * 128 + 128])
        return jnp.concatenate([one, one], axis=0)

    def frame_probs(places, q2, k):
        allowed = [frame_allowed(mb) for mb in range(2)]
        sc = [dot_nt(a, b) * scale for a, b in zip(q2, k)]
        sc = [jnp.where(allowed[mb], v, masked_fill) for (mb, _, _), v in zip(places, sc)]
        top = [jnp.max(v, axis=-1, keepdims=True) for v in sc]
        e = [jnp.exp(v - t) for v, t in zip(sc, top)]
        inv = [1.0 / jnp.sum(v, axis=-1, keepdims=True) for v in e]
        return [v * t for v, t in zip(e, inv)]

    def frame_places(g):
        return [
            (mb, slice(mb * 128, mb * 128 + 128), pl.ds(pl.multiple_of((g * 2 + t) * 128, 128), 128))
            for mb in range(2) for t in range(2)
        ]

    def frame_attend(b):
        def part(g):
            places = frame_places(g)
            q2 = [stack_heads(qk[b * 3, at, cols]) for _, at, cols in places]
            k = [qk[b * 3 + 1, at, cols] for _, at, cols in places]
            v2 = [stack_heads(qk[b * 3 + 2, at, cols]) for _, at, cols in places]
            p = [side_by_side(v.astype(BF)) for v in frame_probs(places, q2, k)]
            o = [dot_nn(v, w) for v, w in zip(p, v2)]
            for (_, at, cols), v in zip(places, o):
                ob[b, at, cols] = v.astype(BF)

        loop(0, 2, part)

    def frame_attend_back(b, do_slot):
        def part(g):
            places = frame_places(g)
            q2 = [stack_heads(qk[b * 3, at, cols]) for _, at, cols in places]
            k = [qk[b * 3 + 1, at, cols] for _, at, cols in places]
            v = [qk[b * 3 + 2, at, cols] for _, at, cols in places]
            do2 = [stack_heads(dob[do_slot, at, cols]) for _, at, cols in places]
            p = frame_probs(places, q2, k)
            dp = [dot_nt(a, c) for a, c in zip(do2, v)]
            mean = [jnp.sum(a * c, axis=-1, keepdims=True) for a, c in zip(dp, p)]
            ds = [(c * (a - t)).astype(BF) for a, c, t in zip(dp, p, mean)]
            dv = [dot_tn(a.astype(BF), c) for a, c in zip(p, do2)]
            dk = [dot_tn(a, c) for a, c in zip(ds, q2)]
            dq = [dot_nn(side_by_side(a), stack_heads(c)) for a, c in zip(ds, k)]
            for i, (_, at, cols) in enumerate(places):
                co, si = cs[0, at], cs[1, at]
                for c, t in ((0, dq[i] * scale), (1, dk[i] * scale)):
                    qk[b * 3 + c, at, cols] = (t * co - swap_halves(t) * si).astype(BF)
                qk[b * 3 + 2, at, cols] = dv[i].astype(BF)

        loop(0, 2, part)

    def frame_tables(b):
        for mb in range(2):
            at = slice(mb * 128, mb * 128 + 128)
            pos = lax.broadcasted_iota(jnp.int32, (128, 128), 0)
            lane = lax.broadcasted_iota(jnp.int32, (128, 128), 1)
            start = jnp.broadcast_to(st[b, mb : mb + 1], (128, 128)).T
            hot = ((pos.astype(F32) - start) == lane.astype(F32)).astype(BF)
            for c in range(2):
                cs[c, at] = dot_nn(hot, tabs[c, 0]) + dot_nn(hot, tabs[c, 1]) + dot_nn(hot, tabs[c, 2])
            cs[2, at] = start

    def frame_qkv(a_slot, b):
        for c in range(3):
            t = dot_nn(ab[a_slot], wq[c])
            for g in range(4):
                v = t[:, g * 128 : g * 128 + 128]
                if c < 2:
                    v = v * cs[0] + swap_halves(v) * cs[1]
                qk[b * 3 + c, :, g * 128 : g * 128 + 128] = v.astype(BF)

    def px(b, i):
        mb, r = lax.div(i, 8), by16(lax.rem(i, 8))
        q, k = lax.div(b, 2), lax.rem(b, 2) * 2
        return jnp.concatenate([rg[q, k, mb, r], rg[q, k + 1, mb, r]], axis=1).astype(F32)

    def put_px(b, i, v):
        mb, r = lax.div(i, 8), by16(lax.rem(i, 8))
        q, k = lax.div(b, 2), lax.rem(b, 2) * 2
        rg[q, k, mb, r] = v[:, 0:512].astype(BF)
        rg[q, k + 1, mb, r] = v[:, 512:1024].astype(BF)

    def ds_rows(b, i):
        mb, r = lax.div(i, 8), by16(lax.rem(i, 8))
        return jnp.concatenate([ryz[b * 4 + mb, r], ryz[b * 4 + 2 + mb, r]], axis=1).astype(F32)

    def ds_all(b):
        return jnp.concatenate(
            [ryz[pl.ds(b * 4, 2)].reshape(ROWS, 512), ryz[pl.ds(b * 4 + 2, 2)].reshape(ROWS, 512)], axis=1
        )

    mrows = pl.ds(pl.multiple_of(m * 64, 64), 64)

    def px_ref(b):
        return rg.at[lax.div(b, 2), pl.ds(lax.rem(b, 2) * 2, 2), :, mrows]

    def ds_ref(b):
        return ryz.at[pl.ds(b * 4, 4), mrows]

    def block_of(i):
        j = lax.div(i, 2)
        low = jnp.where(j == 0, 1, jnp.where(j == 1, 0, j))
        high = jnp.where(j == 0, 2, jnp.where(j == 1, 3, 3 - j))
        zz = jnp.where(z == 0, j, jnp.where(z == 1, low, jnp.where(z == 2, high, 3 - j)))
        other = lax.rem(i, 2)
        return zz * 2 + jnp.where(other == 0, y, 1 - y), zz, other

    def spread(ref, sems, rsem, ms, mr, i, with_peer):
        b, zz, other = block_of(i)

        def go(direction, to):
            remote(ref(b), ref(b), sems.at[b, direction], rsem.at[b], to).start()

        @pl.when(other == 0)
        def _():
            go(2, ypeer)

            @pl.when((zz <= z) & (z < 3))
            def _():
                go(0, zup)

            @pl.when((zz >= z) & (z > 0))
            def _():
                go(1, zdown)

        if with_peer:
            remote(ref(b), ref(b), ms.at[b], mr.at[b], peer).start()

    def arrive(ref, sems, rsem, ms, mr, i):
        b, _, _ = block_of(i)
        remote(ref(b), ref(b), sems.at[b, 2], rsem.at[b], ypeer).wait_recv()
        spread(ref, sems, rsem, ms, mr, i, True)

    def drained(ref, sems, rsem, ms, mr, i, with_peer):
        b, zz, other = block_of(i)

        @pl.when(other == 0)
        def _():
            remote(ref(b), ref(b), sems.at[b, 2], rsem.at[b], ypeer).wait_send()

            @pl.when((zz <= z) & (z < 3))
            def _():
                remote(ref(b), ref(b), sems.at[b, 0], rsem.at[b], zup).wait_send()

            @pl.when((zz >= z) & (z > 0))
            def _():
                remote(ref(b), ref(b), sems.at[b, 1], rsem.at[b], zdown).wait_send()

        if with_peer:
            remote(ref(b), ref(b), ms.at[b], mr.at[b], peer).wait_send()

    xset = (px_ref, xas, xar, xms, xmr)
    dset = (ds_ref, das, dar, dms, dmr)

    def late(i):
        return jnp.where(i == 2, 3, jnp.where(i == 3, 6, jnp.where(i == 4, 5, 7)))

    def halves_in(which, i):
        ref, _, _, ms, mr = which
        b, _, _ = block_of(i)
        remote(ref(b), ref(b), ms.at[b], mr.at[b], peer).wait_recv()

    def ring(e):
        t = lax.rem(e, 4)
        return jnp.where(t < 2, t + 1, t + 2), 1 + lax.rem(e, 2)

    mine128 = pl.ds(pl.multiple_of(d * 128, 128), 128)

    def lanes(i):
        return pl.ds(pl.multiple_of(i * 128, 128), 128)

    def hid_at(f):
        return slice(f * 256, f * 256 + 256)

    def gd_slice(b):
        page = b * 4 + lax.div(d, 4) * 2
        cols = pl.ds(pl.multiple_of(lax.rem(d, 4) * 128, 128), 128)
        return ryz[pl.ds(page, 2), :, cols].reshape(ROWS, 128).T

    def put_tb(f, at, v):
        tb[f * 256 + at.start : f * 256 + at.stop, 0:512] = v

    def frame_grad(chunk, left, right, first):
        at = acc_at(chunk)
        t = dot_nn(left, right)
        xm[at] = t if first else xm[at] + t

    def frame_grads_down(b, first):
        left = gd_slice(b)
        for f in range(4):
            frame_grad(f, left, tb[hid_at(f), 0:512], first)

    def frame_grads_up(b, bm_slot, bm_cols, first):
        left = bm[bm_slot, :, bm_cols].T
        for f in range(4):
            frame_grad(4 + f, left, uph[f * 8 + b], first)

    def frame_grads_attend(b, ga_slot, a_slot, a_cols, first):
        frame_grad(8, gd[ga_slot, :, :, :, mine128].reshape(ROWS, 128).T, ob[b], first)
        left = ab[a_slot, :, a_cols].T
        for c in range(3):
            frame_grad(9 + c, left, qk[b * 3 + c], first)

    @pl.when(frame)
    def _():
        pos = lax.broadcasted_iota(jnp.int32, (128, 128), 0)
        lane = lax.broadcasted_iota(jnp.int32, (128, 128), 1)
        freq = jnp.exp(lax.rem(lane, 32).astype(F32) * (-2.0 * math.log(rotary_base) / HEAD_DIM))
        angle = pos.astype(F32) * freq
        sine = jnp.sin(angle)
        for c, v in enumerate((jnp.cos(angle), jnp.where(lax.rem(lane, 64) < 32, -sine, sine))):
            for t in range(3):
                term = v.astype(BF)
                tabs[c, t] = term
                v = v - term.astype(F32)
        place = lax.broadcasted_iota(jnp.int32, (8, 128), 1)
        rows = []
        for mb in range(2):
            start = jnp.zeros((8, 128), jnp.int32)
            end = jnp.int32(0)
            for j in range(4):
                size = lens[mb, 0, j]
                end = end + size
                start = start + jnp.where(place >= end, size, 0)
            rows.append(start)
        which = lax.broadcasted_iota(jnp.int32, (8, 128), 0)
        st[d] = jnp.where(which == 0, rows[0], rows[1]).astype(F32)
        for t in range(1, 8):
            o = lax.rem(d + t, 8)
            remote(st.at[d], st.at[d], sts.at[t], strc.at[d], (s, o, m)).start()
        frame_tables(d)

        with jax.named_scope("embeds_wait"):
            for cp in e_local:
                cp.wait()
            for cp in e_far:
                cp.wait()

        gain0 = gains[0, 0:1]
        gain1 = gains[0, 1:2]

        def x_own(i):
            mb, mh, r = halves16(i)
            return em[0, mb, mh, r].astype(F32) + em[1, mb, mh, r].astype(F32) + em[2, mb, mh, r].astype(F32)

        def rows_in(i):
            v = x_own(i)
            xm[2, by16(i)] = v
            ab[0, by16(i)] = (v * rms(v) * gain0).astype(BF)
            put_px(d, i, v)

        with jax.named_scope("own_qkv"):
            loop(0, 16, rows_in, unroll=UNROLL)
            spread(*xset, 0, False)
            w_copies[0].wait()
            frame_qkv(0, d)
        with jax.named_scope("own_attend"):
            frame_attend(d)
        w_copies[1].wait()
        with jax.named_scope("own_out"):
            out_block(ob[d], 0, 0)
            w_copies[2].wait()
            exchange(0, 0, True).wait()

        def rows_mid(i):
            v = xm[2, by16(i)] + summed(0, 0, i)
            return v, (v * rms(v) * gain1).astype(BF)

        def put_mid(i, v, w):
            xm[2, by16(i)] = v
            bm[0, by16(i)] = w

        def put_own(f, at, u):
            uph[f * 8 + d, at] = u.astype(BF)
            put_tb(f, at, (0.5 * u * (1.0 + gelu_tanh(u))).astype(BF))

        with jax.named_scope("own_ff"):
            grouped(16, rows_mid, put_mid)
            up_block(bm[0], put_own)
            w_copies[3].wait()
            down_block(lambda f: tb[hid_at(f), 0:512], 3, 0)
            exchange(3, 0, False).wait()

        def rows_res(i):
            mb, r, row = own16(i, m)
            sr[mb, m, r] = (xm[2, row] + summed_own(3, 0, i)).astype(BF)

        loop(0, 8, rows_res, unroll=UNROLL)
        hop[0].start()

        for t in range(1, 8):
            o = lax.rem(d + t, 8)
            remote(st.at[d], st.at[o], sts.at[t], strc.at[o], (s, o, m)).wait()

        def others_in(i):
            b, _, _ = block_of(i)
            halves_in(xset, i)
            frame_tables(b)

            def rows_norm(t):
                v = px(b, t)
                ab[2, by16(t)] = (v * rms(v) * gain0).astype(BF)

            loop(0, 16, rows_norm, unroll=UNROLL)
            ab[1, :, lanes(i)] = ab[2, :, mine128]
            frame_qkv(2, b)
            frame_attend(b)
            out_block(ob[b], *ring(i))

        def others_ff(i):
            b, _, _ = block_of(i)
            recv_slot, send_slot = ring(i)
            exchange(recv_slot, send_slot, True).wait()
            drained(*xset, i, True)

            def rows_m(t):
                v = px(b, t) + summed(recv_slot, send_slot, t)
                return v, (v * rms(v) * gain1).astype(BF)

            def put_m(t, v, w):
                put_px(b, t, v)
                bm[2, by16(t)] = w

            grouped(16, rows_m, put_m)
            bm[1, :, lanes(i)] = bm[2, :, mine128]

            def put_up(f, at, u):
                uph[f * 8 + b, at] = u.astype(BF)

            up_block(bm[2], put_up)

        with jax.named_scope("oth_arrive"):
            arrive(*xset, 1)
            arrive(*xset, 2)
            arrive(*xset, 4)

        def others(i):
            @pl.when((i > 1) & (i < 6))
            def _():
                with jax.named_scope("oth_arrive"):
                    arrive(*xset, late(i))

            @pl.when(i < 8)
            def _():
                with jax.named_scope("oth_in"):
                    others_in(i)

            @pl.when(i > 1)
            def _():
                with jax.named_scope("oth_ff"):
                    others_ff(i - 1)

        loop(1, 9, others)
        drained(*xset, 0, False)
        hop[0].wait_send()

        with jax.named_scope("d_sent_wait"):
            for cp in hop2:
                cp.wait_recv()
            spread(*dset, 0, True)
            halves_in(dset, 0)
        with jax.named_scope("own_dff"):
            dff_block(ds_all(d), lambda f: f * 8 + d, put_tb, 0, 0)
            frame_grads_down(d, True)
        arrive(*dset, 1)
        exchange(0, 0, True).wait()

        def rows_dmid(i):
            add, part = norm_back(xm[2, by16(i)], summed(0, 0, i), gain1)
            return ds_rows(d, i) + add, part

        def put_dmid(i, dm, part):
            mb, mh, r = halves16(i)
            xm[2, by16(i)] = dm
            gd[0, mb, mh, r] = dm.astype(BF)
            add_gain(1, part)

        with jax.named_scope("own_dmid"):
            grouped(16, rows_dmid, put_dmid)
            dob[0] = dot_nt(gd[0].reshape(ROWS, 1024), wo[...]).astype(BF)
        frame_tables(d)
        with jax.named_scope("own_attend_back"):
            frame_attend_back(d, 0)
        dqkv_block(lambda c: d * 3 + c, 3, 0)
        with jax.named_scope("own_grads"):
            frame_grads_up(d, 0, mine128, True)
        arrive(*dset, 2)
        exchange(3, 0, False).wait()

        def rows_dx(i):
            mb, r, row = own16(i, m)
            v = em[0, mb, m, r].astype(F32) + em[1, mb, m, r].astype(F32) + em[2, mb, m, r].astype(F32)
            add, part = norm_back(v, summed_own(3, 0, i), gain0)
            return xm[2, row] + add, part

        def put_dx(i, dv, part):
            xm[2, own16(i, m)[2]] = dv
            add_gain(0, part)

        grouped(8, rows_dx, put_dx)
        gain_first()
        for cp in dl_far:
            cp.wait_recv()

        def rows_ge(i):
            mb, r, row = own16(i, m)
            for c in range(3):
                ob2[c, mb, r] = (ob1[c, mb, r].astype(F32) + xm[2, row]).astype(BF)

        loop(0, 8, rows_ge, unroll=UNROLL)
        for cp in ge_local + ge_far:
            cp.start()
        gain_second()
        frame_grads_attend(d, 0, 0, mine128, True)

        def back_first(i):
            b, _, _ = block_of(i)
            halves_in(dset, i)
            dff_block(ds_all(b), lambda f: f * 8 + b, put_tb, *ring(i + 7))
            frame_grads_down(b, False)

        def back_second(i):
            b, _, _ = block_of(i)
            recv_slot, send_slot = ring(i + 7)
            exchange(recv_slot, send_slot, True).wait()

            def rows_dm(t):
                mb, mh, r = halves16(t)
                add, _ = norm_back(px(b, t), summed(recv_slot, send_slot, t), gain1)
                gd[1, mb, mh, r] = (ds_rows(b, t) + add).astype(BF)

            loop(0, 16, rows_dm, unroll=UNROLL)
            dob[1] = dot_nt(gd[1].reshape(ROWS, 1024), wo[...]).astype(BF)
            frame_tables(b)
            frame_attend_back(b, 1)
            frame_grads_up(b, 1, lanes(i), False)
            frame_grads_attend(b, 1, 1, lanes(i), False)

        with jax.named_scope("oth_arrive_d"):
            arrive(*dset, 4)

        def others_back(i):
            @pl.when((i > 1) & (i < 6))
            def _():
                with jax.named_scope("oth_arrive_d"):
                    arrive(*dset, late(i))

            @pl.when(i < 8)
            def _():
                with jax.named_scope("oth_dff"):
                    back_first(i)

            @pl.when(i > 1)
            def _():
                with jax.named_scope("oth_rest"):
                    back_second(i - 1)

        loop(1, 9, others_back)
        loop(0, 8, lambda i: drained(*dset, i, True))
        grads_out.start()
        gain_last()
        for cp in ge_local:
            cp.wait()
        for cp in ge_far:
            cp.wait_send()
        for cp in lo_far:
            cp.wait_recv()
        grads_out.wait()

    def head_sum(prod):
        r0 = lax.broadcasted_iota(jnp.int32, (256, 256), 0)
        r1 = lax.broadcasted_iota(jnp.int32, (256, 256), 1)
        ones = (lax.div(r0, 64) == lax.div(r1, 64)).astype(BF)
        return dot_nn(prod.astype(BF), ones)

    def code_probs(q, k):
        probs = []
        for i in range(3):
            sc = [head_sum(q[i] * k[j]) * scale for j in range(i + 1)]
            top = functools.reduce(jnp.maximum, sc)
            e = [jnp.exp(v - top) for v in sc]
            inv = 1.0 / functools.reduce(jnp.add, e)
            probs.append([v * inv for v in e])
        return probs

    def code_part(i):
        return (pl.ds(pl.multiple_of(lax.div(i, 2) * 64, 64), 64), pl.ds(pl.multiple_of(lax.rem(i, 2) * 256, 256), 256))

    def code_attend(i):
        at, cols = code_part(i)
        q, k, v = ([qk[c * 3 + b, at, cols].astype(F32) for b in range(3)] for c in range(3))
        probs = code_probs(q, k)
        for t in range(3):
            o = functools.reduce(jnp.add, [probs[t][j].astype(BF).astype(F32) * v[j] for j in range(t + 1)])
            ob[t, at, cols] = o.astype(BF)

    def code_attend_back(i):
        at, cols = code_part(i)
        q, k, v = ([qk[c * 3 + b, at, cols].astype(F32) for b in range(3)] for c in range(3))
        do = [dob[b, at, cols].astype(F32) for b in range(3)]
        probs = code_probs(q, k)
        dk = [0.0] * 3
        dv = [0.0] * 3
        for t in range(3):
            dp = [head_sum(do[t] * v[j]) for j in range(t + 1)]
            mean = functools.reduce(jnp.add, [dp[j] * probs[t][j] for j in range(t + 1)])
            dq = 0.0
            for j in range(t + 1):
                ds = (probs[t][j] * (dp[j] - mean)).astype(BF).astype(F32)
                dq = dq + ds * k[j]
                dk[j] = dk[j] + ds * q[t]
                dv[j] = dv[j] + probs[t][j].astype(BF).astype(F32) * do[t]
            qk[t, at, cols] = (dq * scale).astype(BF)
        for j in range(3):
            qk[3 + j, at, cols] = (dk[j] * scale).astype(BF)
            qk[6 + j, at, cols] = dv[j].astype(BF)

    def flip(get):
        def one(b):
            at = pl.ds(pl.multiple_of(b * 256, 256), 256)
            t = get(b)
            for g in range(4):
                tb[g * 256 : g * 256 + 256, at] = t[:, g * 256 : g * 256 + 256].T

        loop(0, 3, one)

    def ry(slot):
        return ryz.at[pl.ds(slot * 4, 4)]

    def rz(slot, idx):
        return SLOTS * 4 + slot * 5 + idx

    def sends(slot):
        return remote(rg.at[slot, :, 1 - y], ry(slot), ysn.at[slot], yrc.at[slot], ypeer)

    def right(slot, k):
        return remote(rg.at[slot, k, y], ryz.at[rz(slot, k + 1)], zrs.at[slot, k], zrr.at[slot, k], zup)

    def left(slot, k):
        return remote(rg.at[slot, k, y], ryz.at[rz(slot, k)], zls.at[slot, k], zlr.at[slot, k], zdown)

    def free_slot(slot):
        sends(slot).wait_send()
        for k in range(4):
            @pl.when(k > z)
            def _():
                right(slot, k).wait_send()

            @pl.when(k < z)
            def _():
                left(slot, k).wait_send()

    def make_chunk(i, act):
        slot = lax.rem(i, SLOTS)

        @pl.when(i >= SLOTS)
        def _():
            free_slot(slot)

        def part(k):
            at = pl.ds(pl.multiple_of(k * 256, 256), 256)
            rg[slot, k] = dot_nn(tb[at, :], act()).astype(BF).reshape(2, 128, 512)

        loop(0, 4, part)

        @pl.when(i >= SLOTS)
        def _():
            pl.semaphore_wait(ycr, 1)

        sends(slot).start()

    def add_into(slot, k, page):
        for g in range(4):
            at = slice(g * 32, g * 32 + 32)
            rg[slot, k, y, at] = (rg[slot, k, y, at].astype(F32) + ryz[page, at].astype(F32)).astype(BF)

    def proc_y(i):
        slot = lax.rem(i, SLOTS)
        sends(slot).wait_recv()

        @pl.when(i >= SLOTS)
        def _():
            @pl.when(z < 3)
            def _():
                pl.semaphore_wait(rcr, 1)

            @pl.when(z > 0)
            def _():
                pl.semaphore_wait(lcr, 1)

        def up_first(t):
            k = 3 - t
            add_into(slot, k, slot * 4 + k)

            @pl.when((z == 0) & (k > 0))
            def _():
                right(slot, k).start()

        def down_first(t):
            add_into(slot, t, slot * 4 + t)

            @pl.when((z == 3) & (t < 3))
            def _():
                left(slot, t).start()

        @pl.when(z < 2)
        def _():
            loop(0, 4, up_first)

        @pl.when(z >= 2)
        def _():
            loop(0, 4, down_first)

        @pl.when(i + SLOTS < CHUNKS)
        def _():
            pl.semaphore_signal(ycr, 1, device_id=ypeer, device_id_type=MESH)

    def pass_right(slot, k):
        right(slot, k).wait_recv()
        add_into(slot, k, rz(slot, k + 1))
        right(slot, k).start()

    def pass_left(slot, k):
        left(slot, k).wait_recv()
        add_into(slot, k, rz(slot, k))
        left(slot, k).start()

    def fwd_z(i):
        slot = lax.rem(i, SLOTS)

        @pl.when(z == 1)
        def _():
            pass_right(slot, 3)
            pass_right(slot, 2)
            pass_left(slot, 0)

        @pl.when(z == 2)
        def _():
            pass_left(slot, 0)
            pass_left(slot, 1)
            pass_right(slot, 3)

    def finish(i):
        slot = lax.rem(i, SLOTS)

        @pl.when(z > 0)
        def _():
            right(slot, z).wait_recv()
            add_into(slot, z, rz(slot, z + 1))

        @pl.when(z < 3)
        def _():
            left(slot, z).wait_recv()
            add_into(slot, z, rz(slot, z))

        total = rg[slot, z, y].astype(F32)

        xm[acc_at(i)] = total

        @pl.when(i + SLOTS < CHUNKS)
        def _():
            @pl.when(z > 0)
            def _():
                pl.semaphore_signal(rcr, 1, device_id=zdown, device_id_type=MESH)

            @pl.when(z < 3)
            def _():
                pl.semaphore_signal(lcr, 1, device_id=zup, device_id_type=MESH)

    @pl.when(code)
    def _():
        for cp in c_local:
            cp.start()
        for cp in c_far:
            cp.start()
        for cp in e_local:
            cp.wait()
        for cp in e_far:
            cp.wait()
        gain0 = gains[0, 0:1]
        gain1 = gains[0, 1:2]
        with jax.named_scope("sent_wait"):
            hop[0].wait_recv()
            hop[1].start()
            hop[1].wait_recv()

        def rows_in(i):
            mb, mh, r = halves16(i)
            came = sr[mb, mh, r].astype(F32)
            for c in range(3):
                v = em[c, mb, mh, r].astype(F32) + came
                xm[c, by16(i)] = v
                ab[c, by16(i)] = (v * rms(v) * gain0).astype(BF)

        with jax.named_scope("code_norm"):
            loop(0, 16, rows_in, unroll=UNROLL)

        def qkv_all(b):
            for c in range(3):
                qk[c * 3 + b] = dot_nn(ab[b], wq[c]).astype(BF)

        w_copies[0].wait()
        with jax.named_scope("code_qkv"):
            loop(0, 3, qkv_all)
        with jax.named_scope("code_attend"):
            loop(0, 8, code_attend)
        w_copies[1].wait()
        with jax.named_scope("code_out"):
            loop(0, 3, lambda b: out_block(ob[b], b, b))
        w_copies[2].wait()
        w_copies[3].wait()

        def ff(b):
            exchange(b, b, True).wait()

            def rows_mid(i):
                v = xm[b, by16(i)] + summed(b, b, i)
                return v, (v * rms(v) * gain1).astype(BF)

            def put_mid(i, v, w):
                xm[b, by16(i)] = v
                bm[b, by16(i)] = w

            grouped(16, rows_mid, put_mid)

            def put(f, at, u):
                uph[f * 3 + b, at] = u.astype(BF)
                uph[12 + f * 3 + b, at] = (0.5 * u * (1.0 + gelu_tanh(u))).astype(BF)

            up_block(bm[b], put)
            down_block(lambda f: uph[12 + f * 3 + b], 3 + b, b)

        with jax.named_scope("code_ff"):
            loop(0, 3, ff)

        def res(b):
            exchange(3 + b, b, False).wait()

            def rows_res(i):
                mb, r, row = own16(i, m)
                ob1[b, mb, r] = (xm[b, row] + summed_own(3 + b, b, i)).astype(BF)

            loop(0, 8, rows_res, unroll=UNROLL)

        loop(0, 3, res)
        for cp in lo_local + lo_far:
            cp.start()
        for cp in c_local:
            cp.wait()
        for cp in c_far:
            cp.wait()

        with jax.named_scope("code_grad_down"):
            flip(lambda b: gd[b].reshape(ROWS, 1024))
            loop(0, 4, lambda i: make_chunk(i, lambda: uph[pl.ds(12 + i * 3, 3)].reshape(768, 512)))

        def dff(b):
            dff_block(gd[b].reshape(ROWS, 1024), lambda f: f * 3 + b, None, b, b)

        with jax.named_scope("code_dff"):
            loop(0, 3, dff)
        def dmid(b):
            exchange(b, b, True).wait()

            def rows_dmid(i):
                mb, mh, r = halves16(i)
                add, part = norm_back(xm[b, by16(i)], summed(b, b, i), gain1)
                return gd[b, mb, mh, r].astype(F32) + add, part

            def put_dmid(i, dm, part):
                mb, mh, r = halves16(i)
                xm[b, by16(i)] = dm
                gd[b, mb, mh, r] = dm.astype(BF)
                add_gain(1, part)

            grouped(16, rows_dmid, put_dmid)
            dob[b] = dot_nt(gd[b].reshape(ROWS, 1024), wo[...]).astype(BF)

        with jax.named_scope("code_dmid"):
            loop(0, 3, dmid)
        with jax.named_scope("code_attend_back"):
            loop(0, 8, code_attend_back)
        with jax.named_scope("code_dqkv"):
            loop(0, 3, lambda b: dqkv_block(lambda c: c * 3 + b, 3 + b, b))
        for cp in lo_local:
            cp.wait()
        for cp in lo_far:
            cp.wait_send()

        def dx(b):
            exchange(3 + b, b, False).wait()

            def rows_dx(i):
                mb, r, row = own16(i, m)
                v = em[b, mb, m, r].astype(F32) + sr[mb, m, r].astype(F32)
                add, part = norm_back(v, summed_own(3 + b, b, i), gain0)
                return xm[b, row] + add, part

            def put_dx(i, dv, part):
                mb, r, row = own16(i, m)
                xm[b, row] = dv
                ob1[b, mb, r] = dv.astype(BF)
                add_gain(0, part)

            grouped(8, rows_dx, put_dx)

        with jax.named_scope("code_dx"):
            loop(0, 3, dx)

        def rows_ds(i):
            mb, r, row = own16(i, m)
            ob2[0, mb, r] = (xm[0, row] + xm[1, row] + xm[2, row]).astype(BF)

        loop(0, 8, rows_ds, unroll=UNROLL)
        for cp in hop2:
            cp.start()
        gain_first()
        with jax.named_scope("code_y2"):
            proc_y(0)
            proc_y(1)
            fwd_z(0)
            proc_y(2)
            fwd_z(1)
            gain_second()
            finish(0)
        for cp in hop2:
            cp.wait_send()
        for cp in dl_far:
            cp.start()

        def tail(i):
            @pl.when(i == 4)
            def _():
                flip(lambda b: bm[b])

            @pl.when(i == 8)
            def _():
                flip(lambda b: gd[b].reshape(ROWS, 1024))

            @pl.when(i == 9)
            def _():
                flip(lambda b: ab[b])

            @pl.when(i < 8)
            def _():
                make_chunk(i, lambda: uph[pl.ds((i - 4) * 3, 3)].reshape(768, 512))

            @pl.when(i == 8)
            def _():
                make_chunk(i, lambda: ob[0:3].reshape(768, 512))

            @pl.when((i > 8) & (i < CHUNKS))
            def _():
                make_chunk(i, lambda: qk[pl.ds((i - 9) * 3, 3)].reshape(768, 512))

            @pl.when(i - 1 < CHUNKS)
            def _():
                with jax.named_scope("tail_y"):
                    proc_y(i - 1)

            @pl.when(i - 2 < CHUNKS)
            def _():
                with jax.named_scope("tail_z"):
                    fwd_z(i - 2)

            with jax.named_scope("tail_finish"):
                finish(i - 3)

        loop(4, CHUNKS + 3, tail)
        grads_out.start()
        hop[1].wait_send()
        for cp in dl_far:
            cp.wait_send()
        gain_last()
        for cp in ge_far:
            cp.wait_recv()
        for t in range(CHUNKS - SLOTS, CHUNKS):
            free_slot(t % SLOTS)
        grads_out.wait()


def unpack(lo_i, ge_i, g_i, gg_i, lo_o, ge_o, gg_o, gq_o, go_o, gu_o, gd_o):
    lo_o[...] = lo_i[...]
    ge_o[...] = ge_i[...]
    gg_o[...] = gg_i[...]

    def chunk(i):
        rows, cols = (i % 4) // 2 * 128, i % 2 * 512
        return g_i[i // 4, rows : rows + 128, cols : cols + 512]

    for f in range(4):
        gd_o[f * 512 : f * 512 + 512] = chunk(f).T
        gu_o[:, f * 512 : f * 512 + 512] = chunk(4 + f)
    go_o[...] = chunk(8).T
    for c in range(3):
        gq_o[c] = chunk(9 + c)


def on_device_kernel(embeds, lengths, norm_gains, w_qkv, w_out, w_up, w_down, cotangent):
    anyspec = pl.BlockSpec(memory_space=pl.ANY)
    vm = pl.BlockSpec(memory_space=pltpu.VMEM)
    sd = jax.ShapeDtypeStruct
    V = pltpu.VMEM
    D = pltpu.SemaphoreType.DMA
    R = pltpu.SemaphoreType.REGULAR
    half = (2, 64, 1024)
    full = (2, 2, 64, 1024)
    scratch = [
        V((3, 1024, 512), BF), V((512, 1024), BF), V((1024, 2048), BF), V((2048, 1024), BF),
        V((3,) + full, BF), V((3,) + full, BF), V(full, BF),
        V((3, ROWS, 1024), F32), V((3, ROWS, 1024), BF), V((3, ROWS, 1024), BF),
        V((24, ROWS, 512), BF), V((8, ROWS, 512), BF), V((3, ROWS, 512), BF), V((32, ROWS, 512), BF),
        V((3,) + full, BF), V((6,) + full, BF), V((1024, 768), BF),
        V((3,) + half, BF), V((3,) + half, BF),
        V((3, ROWS, 128), F32), V((2, 3, 128, 128), BF), V((8, 8, 128), F32),
        V((2, 8, 1024), F32), V((8, 8, 1024), F32), V((2, 8, 1024), F32),
        V((SLOTS, 4, 2, 128, 512), BF), V((SLOTS * 9, 128, 512), BF),
        D, D((4,)), D((3,)), D((3,)), D((3,)), D((3,)), D((3,)), D((3,)), D((3,)), D((6,)), D((4,)), D((4,)),
        D((3,)), D((3,)), D((3,)), D((3,)), D((3,)),
        D((3,)), D((3,)), D((3,)), D((8,)), D((8,)), D, D,
        D((SLOTS,)), D((SLOTS,)), D((SLOTS, 4)), D((SLOTS, 4)), D((SLOTS, 4)), D((SLOTS, 4)),
        D((8,)), D((8,)), D((8, 3)), D((8,)), D((8,)), D((8,)), D((8, 3)), D((8,)), D((8,)), D((8,)),
        R, R, R,
    ]
    rows, gain = sd((2, 3, 64, 1024), BF), sd((1, 2, 1024), F32)
    grads = (sd((3, 128, 512), F32), sd((512, 128), F32), sd((128, 2048), F32), sd((2048, 128), F32))
    outs = pl.pallas_call(
        body,
        out_shape=(rows, rows, sd((3, ROWS, 1024), F32), gain),
        in_specs=[anyspec, anyspec, pl.BlockSpec(memory_space=pltpu.SMEM), vm, anyspec, anyspec, anyspec, anyspec],
        out_specs=(anyspec, anyspec, anyspec, vm),
        scratch_shapes=scratch,
        compiler_params=pltpu.CompilerParams(
            collective_id=0, has_side_effects=True, vmem_limit_bytes=61 * 2**20 - 2**19
        ),
        name="two_sections",
    )(
        jnp.transpose(embeds, (0, 2, 1, 3)), jnp.transpose(cotangent, (0, 2, 1, 3)), lengths, norm_gains,
        jnp.transpose(w_qkv[0], (1, 0, 2)), w_out[0], w_up[0], w_down[0],
    )
    outs = pl.pallas_call(
        unpack,
        out_shape=(rows, rows, gain) + grads,
        in_specs=[vm] * 4,
        out_specs=(vm,) * 7,
        compiler_params=pltpu.CompilerParams(vmem_limit_bytes=24 * 2**20),
        name="results",
    )(*outs)
    lo, ge, gg, gq, go, gu, gdn = outs
    return (
        jnp.transpose(lo, (0, 2, 1, 3)), jnp.transpose(ge, (0, 2, 1, 3)), gg,
        jnp.transpose(gq, (1, 0, 2))[None], go[None], gu[None], gdn[None],
    )


def solution(mesh):
    fits = tuple(mesh.shape[name] for name in ("section", "dp", "mp")) == (2, 8, 2)
    return jax.shard_map(
        on_device_kernel if fits else on_device,
        mesh=mesh,
        in_specs=(
            P(None, ("dp", "mp"), None, None),
            P(None, "dp", None),
            P("section", None, None),
            P("section", None, None, "mp"),
            P("section", "mp", None),
            P("section", None, "mp"),
            P("section", "mp", None),
            P(None, ("dp", "mp"), None, None),
        ),
        out_specs=(
            P(None, ("dp", "mp"), None, None),
            P(None, ("dp", "mp"), None, None),
            P("section", None, None),
            P("section", "dp", None, "mp"),
            P("section", "mp", "dp"),
            P("section", "dp", "mp"),
            P("section", "mp", "dp"),
        ),
        check_vma=False,
    )
```

```python
import functools
import math

import jax
import jax.numpy as jnp
from jax import lax
from jax.experimental import pallas as pl
from jax.experimental.pallas import tpu as pltpu
from jax.sharding import PartitionSpec as P

HEAD_DIM = 64


norm_eps = 1e-05
masked_fill = -1e30
rotary_base = 10000.0


def passed_along(value, axis, steps):
    count = lax.axis_size(axis)
    leading, last = (max(0, -steps), min(count, count - steps))
    return lax.ppermute(value, axis, [(source, source + steps) for source in range(leading, last)])


def rms_scale(values, gain_row):
    return (
        values * lax.rsqrt(jnp.mean(values * values, axis=-1, keepdims=True) + norm_eps) * gain_row
    )


def rotate(values, cos_tab, sin_tab):
    half_dim = values.shape[-1] // 2
    first_half = values[..., :half_dim]
    second_half = values[..., half_dim:]
    cos_rows = cos_tab[:, None, :]
    sin_rows = sin_tab[:, None, :]
    return jnp.concatenate(
        [
            first_half * cos_rows - second_half * sin_rows,
            second_half * cos_rows + first_half * sin_rows,
        ],
        axis=-1,
    )


def global_context(length_row, frames):
    doc_ends = jnp.cumsum(length_row)
    places = jnp.arange(frames, dtype=jnp.int32)
    passed = (places[:, None] >= doc_ends[None, :]).astype(jnp.int32)
    segment = jnp.sum(passed, axis=1)
    offsets = places - jnp.sum(passed * length_row[None, :], axis=1)
    allowed = (segment[:, None] == segment[None, :]) & (places[None, :] <= places[:, None])
    half_dim = HEAD_DIM // 2
    frequency = jnp.exp(
        jnp.arange(half_dim, dtype=jnp.float32) * (-2.0 * math.log(rotary_base) / HEAD_DIM)
    )
    angles = offsets.astype(jnp.float32)[:, None] * frequency[None, :]
    return (allowed, jnp.cos(angles), jnp.sin(angles))


def global_attend(projected, context):
    allowed, cos_tab, sin_tab = context
    attn_scale = 1.0 / math.sqrt(HEAD_DIM)
    row_total, _, local_width = projected.shape
    head_count = local_width // HEAD_DIM
    query_rows = rotate(
        projected[:, 0].reshape(row_total, head_count, HEAD_DIM), cos_tab, sin_tab
    ).astype(jnp.bfloat16)
    key_rows = rotate(
        projected[:, 1].reshape(row_total, head_count, HEAD_DIM), cos_tab, sin_tab
    ).astype(jnp.bfloat16)
    value_rows = projected[:, 2].reshape(row_total, head_count, HEAD_DIM).astype(jnp.bfloat16)
    scores = (
        jnp.einsum("qhd,khd->hqk", query_rows, key_rows, preferred_element_type=jnp.float32)
        * attn_scale
    )
    scores = jnp.where(allowed[None], scores, masked_fill)
    score_peak = jnp.max(scores, axis=-1, keepdims=True)
    exp_scores = jnp.exp(scores - score_peak)
    row_sums = jnp.sum(exp_scores, axis=-1, keepdims=True)
    weights_low = (exp_scores / row_sums).astype(jnp.bfloat16)
    mixed_rows = jnp.einsum(
        "hqk,khd->qhd", weights_low, value_rows, preferred_element_type=jnp.float32
    )
    log_total = score_peak + jnp.log(row_sums)
    return (
        mixed_rows.reshape(row_total, local_width).astype(jnp.bfloat16),
        (query_rows, key_rows, value_rows, log_total),
    )


def global_attend_back(attn_saved, context, grad_mixed):
    query_rows, key_rows, value_rows, log_total = attn_saved
    allowed, cos_tab, sin_tab = context
    attn_scale = 1.0 / math.sqrt(HEAD_DIM)
    row_total, head_count, _ = query_rows.shape
    grad_heads = grad_mixed.reshape(row_total, head_count, HEAD_DIM)
    scores = (
        jnp.einsum("qhd,khd->hqk", query_rows, key_rows, preferred_element_type=jnp.float32)
        * attn_scale
    )
    prob_rows = jnp.where(allowed[None], jnp.exp(scores - log_total), 0.0)
    grad_values = jnp.einsum(
        "hqk,qhd->khd",
        prob_rows.astype(jnp.bfloat16),
        grad_heads,
        preferred_element_type=jnp.float32,
    )
    grad_probs = jnp.einsum(
        "qhd,khd->hqk", grad_heads, value_rows, preferred_element_type=jnp.float32
    )
    grad_scores = (
        prob_rows * (grad_probs - jnp.sum(grad_probs * prob_rows, axis=-1, keepdims=True))
    ).astype(jnp.bfloat16)
    grad_query = (
        jnp.einsum("hqk,khd->qhd", grad_scores, key_rows, preferred_element_type=jnp.float32)
        * attn_scale
    )
    grad_keys = (
        jnp.einsum("hqk,qhd->khd", grad_scores, query_rows, preferred_element_type=jnp.float32)
        * attn_scale
    )
    grad_query = rotate(grad_query, cos_tab, -sin_tab)
    grad_keys = rotate(grad_keys, cos_tab, -sin_tab)
    stacked = jnp.stack([grad_query, grad_keys, grad_values], axis=1)
    return stacked.reshape(row_total, 3, head_count * HEAD_DIM).astype(jnp.bfloat16)


def local_attend(projected, context):
    attn_scale = 1.0 / math.sqrt(HEAD_DIM)
    row_total, _, local_width = projected.shape
    head_count = local_width // HEAD_DIM
    frames = row_total // 3
    qkv_parts = projected.reshape(frames, 3, 3, head_count, HEAD_DIM).astype(jnp.bfloat16)
    query_rows = qkv_parts[:, :, 0]
    key_rows = qkv_parts[:, :, 1]
    value_rows = qkv_parts[:, :, 2]
    scores = (
        jnp.einsum("fihd,fjhd->fhij", query_rows, key_rows, preferred_element_type=jnp.float32)
        * attn_scale
    )
    scores = jnp.where(context[None, None], scores, masked_fill)
    score_peak = jnp.max(scores, axis=-1, keepdims=True)
    exp_scores = jnp.exp(scores - score_peak)
    row_sums = jnp.sum(exp_scores, axis=-1, keepdims=True)
    weights_low = (exp_scores / row_sums).astype(jnp.bfloat16)
    mixed_rows = jnp.einsum(
        "fhij,fjhd->fihd", weights_low, value_rows, preferred_element_type=jnp.float32
    )
    log_total = score_peak + jnp.log(row_sums)
    return (
        mixed_rows.reshape(row_total, local_width).astype(jnp.bfloat16),
        (query_rows, key_rows, value_rows, log_total),
    )


def local_attend_back(attn_saved, context, grad_mixed):
    query_rows, key_rows, value_rows, log_total = attn_saved
    attn_scale = 1.0 / math.sqrt(HEAD_DIM)
    frames, _, head_count, _ = query_rows.shape
    grad_heads = grad_mixed.reshape(frames, 3, head_count, HEAD_DIM)
    scores = (
        jnp.einsum("fihd,fjhd->fhij", query_rows, key_rows, preferred_element_type=jnp.float32)
        * attn_scale
    )
    prob_rows = jnp.where(context[None, None], jnp.exp(scores - log_total), 0.0)
    grad_values = jnp.einsum(
        "fhij,fihd->fjhd",
        prob_rows.astype(jnp.bfloat16),
        grad_heads,
        preferred_element_type=jnp.float32,
    )
    grad_probs = jnp.einsum(
        "fihd,fjhd->fhij", grad_heads, value_rows, preferred_element_type=jnp.float32
    )
    grad_scores = (
        prob_rows * (grad_probs - jnp.sum(grad_probs * prob_rows, axis=-1, keepdims=True))
    ).astype(jnp.bfloat16)
    grad_query = (
        jnp.einsum("fhij,fjhd->fihd", grad_scores, key_rows, preferred_element_type=jnp.float32)
        * attn_scale
    )
    grad_keys = (
        jnp.einsum("fhij,fihd->fjhd", grad_scores, query_rows, preferred_element_type=jnp.float32)
        * attn_scale
    )
    stacked = jnp.stack([grad_query, grad_keys, grad_values], axis=2)
    return stacked.reshape(frames * 3, 3, head_count * HEAD_DIM).astype(jnp.bfloat16)


def gather_project(normed, weight, form):
    piece_rows = lax.all_gather(normed, "mp", axis=0, tiled=True)
    return (piece_rows, jnp.einsum(form, piece_rows, weight, preferred_element_type=jnp.float32))


def reduce_rows(left, weight, form, row_count):

    def partial_term(first_row, count_rows):
        return jnp.einsum(form, left, weight, preferred_element_type=jnp.float32)

    return lax.psum_scatter(
        partial_term(jnp.int32(0), row_count * lax.axis_size("mp")),
        "mp",
        scatter_dimension=0,
        tiled=True,
    )


def reduce_grads(left, weight, form, row_count):

    def partial_term(first_row, count_rows):
        return jnp.einsum(form, left, weight, preferred_element_type=jnp.float32)

    return lax.psum_scatter(
        partial_term(jnp.int32(0), row_count * lax.axis_size("mp")),
        "mp",
        scatter_dimension=0,
        tiled=True,
    )


def gather_grads(grad_low):
    return lax.all_gather(grad_low, "mp", axis=0, tiled=True)


def layer_forward(frame_rows, weights, attend, context):
    gain_pair, w_qkv, w_out, w_up, w_down = weights
    row_count = frame_rows.shape[0]
    normed = rms_scale(frame_rows, gain_pair[0]).astype(jnp.bfloat16)
    normed_all, projected = gather_project(normed, w_qkv, "nd,dce->nce")
    mixed_rows, attn_saved = attend(projected, context)
    attn_rows = reduce_rows(mixed_rows, w_out, "ne,ed->nd", row_count)
    middle = frame_rows + attn_rows
    normed_mid = rms_scale(middle, gain_pair[1]).astype(jnp.bfloat16)
    normed_mid_all, up_all = gather_project(normed_mid, w_up, "nd,de->ne")
    hidden = jax.nn.gelu(up_all).astype(jnp.bfloat16)
    down_rows = reduce_rows(hidden, w_down, "nf,fd->nd", row_count)
    record = (normed_all, attn_saved, mixed_rows, middle, normed_mid_all, up_all, hidden)
    return (middle + down_rows, attn_rows + down_rows, record)


def layer_backward(frame_rows, weights, attend_back, context, record, grad_result):
    gain_pair, w_qkv, w_out, w_up, w_down = weights
    normed_all, attn_saved, mixed_rows, middle, normed_mid_all, up_all, hidden = record
    row_count = frame_rows.shape[0]
    grad_down_all = gather_grads(grad_result.astype(jnp.bfloat16))
    grad_w_down = jnp.einsum("nf,nd->fd", hidden, grad_down_all, preferred_element_type=jnp.float32)
    grad_hidden = jnp.einsum("nd,fd->nf", grad_down_all, w_down, preferred_element_type=jnp.float32)
    _, gelu_back = jax.vjp(jax.nn.gelu, up_all)
    grad_up = gelu_back(grad_hidden)[0].astype(jnp.bfloat16)
    grad_w_up = jnp.einsum("nd,ne->de", normed_mid_all, grad_up, preferred_element_type=jnp.float32)
    grad_normed_mid = reduce_grads(grad_up, w_up, "ne,de->nd", row_count)
    _, mid_back = jax.vjp(rms_scale, middle, gain_pair[1])
    grad_middle_part, grad_gain_mid = mid_back(grad_normed_mid)
    grad_middle = grad_result + grad_middle_part
    grad_attn_all = gather_grads(grad_middle.astype(jnp.bfloat16))
    grad_w_out = jnp.einsum(
        "ne,nd->ed", mixed_rows, grad_attn_all, preferred_element_type=jnp.float32
    )
    grad_mixed = jnp.einsum(
        "nd,ed->ne", grad_attn_all, w_out, preferred_element_type=jnp.float32
    ).astype(jnp.bfloat16)
    grad_projected = attend_back(attn_saved, context, grad_mixed)
    grad_w_qkv = jnp.einsum(
        "nd,nce->dce", normed_all, grad_projected, preferred_element_type=jnp.float32
    )
    grad_normed = reduce_grads(grad_projected, w_qkv, "nce,dce->nd", row_count)
    _, first_back = jax.vjp(rms_scale, frame_rows, gain_pair[0])
    grad_rows_part, grad_gain_first = first_back(grad_normed)
    grad_frame_rows = grad_middle + grad_rows_part
    layer_grads = (
        jnp.stack([grad_gain_first, grad_gain_mid]),
        grad_w_qkv,
        grad_w_out,
        grad_w_up,
        grad_w_down,
    )
    return (grad_frame_rows, layer_grads)


def on_device(embeds, lengths, norm_gains, w_qkv, w_out, w_up, w_down, cotangent):
    weights = (norm_gains[0], w_qkv[0], w_out[0], w_up[0], w_down[0])
    micro_count = embeds.shape[0]
    shard_rows = embeds.shape[1]
    width = embeds.shape[-1]
    frames = shard_rows * lax.axis_size("mp")
    is_first = lax.axis_index("section") == 0
    local_allowed = jnp.tril(jnp.ones((3, 3), dtype=jnp.bool_))
    gain_total = jnp.zeros(norm_gains.shape[1:], jnp.float32)
    weight_totals = tuple((jnp.zeros(weight.shape, jnp.float32) for weight in weights[1:]))
    totals = (gain_total,) + weight_totals
    y_part = jnp.zeros(embeds.shape, jnp.float32)
    e_part = jnp.zeros(embeds.shape, jnp.float32)
    zero_send = jnp.zeros((shard_rows, width), jnp.bfloat16)

    def add_grads(running, layer_grads):
        run_gain, run_qkv, run_out, run_up, run_down = running
        part_gain, part_qkv, part_out, part_up, part_down = layer_grads
        return (
            run_gain + part_gain,
            run_qkv + part_qkv,
            run_out + part_out,
            run_up + part_up,
            run_down + part_down,
        )

    def global_forward(micro_index):
        context = global_context(lengths[micro_index, 0], frames)
        frame_in = jnp.sum(embeds[micro_index].astype(jnp.float32), axis=1)
        result, _, record = layer_forward(frame_in, weights, global_attend, context)
        return (frame_in, context, result, record)

    def pick(first_value, second_value):
        return jnp.where(is_first, first_value, second_value)

    carry_state = (totals, y_part, e_part)
    forward_recv = zero_send
    backward_recv = zero_send
    for tick_index in range(micro_count + 2):

        def first_section(state_in):
            running, y_state, e_state = state_in
            send_fwd = zero_send
            if tick_index < micro_count:
                _, _, result, _ = global_forward(tick_index)
                send_fwd = result.astype(jnp.bfloat16)
                joined = (
                    embeds[tick_index].astype(jnp.float32)
                    + send_fwd.astype(jnp.float32)[:, None, :]
                )
                y_state = y_state.at[tick_index].set(joined)
            if tick_index >= 2:
                micro_index = tick_index - 2
                frame_in, context, _, record = global_forward(micro_index)
                grad_frame, layer_grads = layer_backward(
                    frame_in,
                    weights,
                    global_attend_back,
                    context,
                    record,
                    backward_recv.astype(jnp.float32),
                )
                running = add_grads(running, layer_grads)
                e_state = e_state.at[micro_index].set(
                    jnp.broadcast_to(grad_frame[:, None, :], e_state.shape[1:])
                )
            return ((running, y_state, e_state), send_fwd, zero_send)

        def second_section(state_in):
            running, y_state, e_state = state_in
            send_back = zero_send
            if 1 <= tick_index <= micro_count:
                micro_index = tick_index - 1
                local_in = (
                    embeds[micro_index].astype(jnp.float32)
                    + forward_recv.astype(jnp.float32)[:, None, :]
                )
                local_in = local_in.reshape(shard_rows * 3, width)
                _, branches, record = layer_forward(local_in, weights, local_attend, local_allowed)
                grad_seed = (
                    cotangent[micro_index].astype(jnp.float32).reshape(shard_rows * 3, width)
                )
                grad_local, layer_grads = layer_backward(
                    local_in, weights, local_attend_back, local_allowed, record, grad_seed
                )
                running = add_grads(running, layer_grads)
                y_state = y_state.at[micro_index].set(branches.reshape(shard_rows, 3, width))
                grad_frames = grad_local.reshape(shard_rows, 3, width)
                e_state = e_state.at[micro_index].set(grad_frames)
                send_back = jnp.sum(grad_frames, axis=1).astype(jnp.bfloat16)
            return ((running, y_state, e_state), zero_send, send_back)

        first_result = first_section(carry_state)
        second_result = second_section(carry_state)
        carry_state, send_fwd, send_back = jax.tree.map(pick, first_result, second_result)
        if tick_index < micro_count:
            forward_recv = passed_along(send_fwd, "section", 1)
        if 1 <= tick_index <= micro_count:
            backward_recv = passed_along(send_back, "section", -1)
    totals, y_part, e_part = carry_state
    gain_total, grad_qkv, grad_out, grad_up, grad_down = totals
    grad_qkv, grad_out, grad_up, grad_down = (
        lax.psum_scatter(grad_qkv, "dp", scatter_dimension=0, tiled=True),
        lax.psum_scatter(grad_out, "dp", scatter_dimension=1, tiled=True),
        lax.psum_scatter(grad_up, "dp", scatter_dimension=0, tiled=True),
        lax.psum_scatter(grad_down, "dp", scatter_dimension=1, tiled=True),
    )
    gain_total = lax.psum(gain_total, ("dp", "mp"))
    y_sum, e_sum = (
        lax.psum(y_part.astype(jnp.bfloat16), "section").astype(jnp.float32),
        lax.psum(e_part.astype(jnp.bfloat16), "section").astype(jnp.float32),
    )
    return (
        y_sum.astype(jnp.bfloat16),
        e_sum.astype(jnp.bfloat16),
        gain_total[None],
        grad_qkv[None],
        grad_out[None],
        grad_up[None],
        grad_down[None],
    )


BF = jnp.bfloat16
F32 = jnp.float32
MESH = pl.DeviceIdType.MESH
SLOTS = 4
CHUNKS = 10
HELPED = 2
ROWS = 256
UNROLL = 4


def dot_nn(left, right):
    return lax.dot_general(left, right, (((1,), (0,)), ((), ())), preferred_element_type=F32)


def dot_nt(left, right):
    return lax.dot_general(left, right, (((1,), (1,)), ((), ())), preferred_element_type=F32)


def dot_tn(left, right):
    return lax.dot_general(left, right, (((0,), (0,)), ((), ())), preferred_element_type=F32)


def gelu_tanh(u):
    c0 = math.sqrt(2.0 / math.pi)
    return jnp.tanh(u * (c0 + (c0 * 0.044715) * (u * u)))


def gelu_slope(u, th):
    c0 = math.sqrt(2.0 / math.pi)
    return 0.5 * (1.0 + th) + 0.5 * u * (1.0 - th * th) * (c0 + (3.0 * 0.044715 * c0) * (u * u))


def loop(lower, upper, step, unroll=1):
    def wrapped(i, carry):
        step(i)
        return carry

    lax.fori_loop(lower, upper, wrapped, 0, unroll=unroll)


def grouped(count, work, store, size=4):
    def group(g):
        done = [work(g * size + t) for t in range(size)]
        for t in range(size):
            store(g * size + t, *done[t])

    loop(0, count // size, group)


def by16(i):
    return pl.ds(pl.multiple_of(i * 16, 16), 16)


def by512(i):
    return pl.ds(pl.multiple_of(i * 512, 512), 512)


def halves16(i):
    return lax.div(i, 8), lax.rem(lax.div(i, 4), 2), pl.ds(pl.multiple_of(lax.rem(i, 4) * 16, 16), 16)


def own16(i, m):
    mb, r = lax.div(i, 4), pl.multiple_of(lax.rem(i, 4) * 16, 16)
    return mb, pl.ds(r, 16), pl.ds(pl.multiple_of(mb * 128 + m * 64 + r, 16), 16)


def swap_halves(v):
    lane = lax.broadcasted_iota(jnp.int32, v.shape, 1)
    return jnp.where(lax.rem(lane, 64) < 32, pltpu.roll(v, 96, 1), pltpu.roll(v, 32, 1))


def body(
    emb, cot, lens, gains, wq_h, wo_h, wu_h, wd_h,
    lo_h, ge_h, g_h, gg_o,
    wq, wo, wu, wd, em, gd, sr, xm, ab, bm, qk, ob, dob, uph, xs, xr, tb,
    cs, tabs, st, gga, ggr, gpart, rg, ryz,
    gsem, wsem, esem, exs, exr, csem, cxs, cxr, mps, mpr, hops, hopr, lol, los, lor, dls, dlr,
    gel, ges, ger, ggs, ggrs, gms, gmr, ysn, yrc, zrs, zrr, zls, zlr,
    has, har, hbs, hbr, hzrs, hzrr, hzls, hzlr, hres, hrer, sts, strc, xas, xar, xms, xmr, das, dar, dms, dmr, ycr, rcr, lcr,
):
    s = lax.axis_index("section")
    d = lax.axis_index("dp")
    m = lax.axis_index("mp")
    y = lax.rem(d, 2)
    z = lax.div(d, 2)
    peer = (s, d, 1 - m)
    across = (1 - s, d, m)
    ypeer = (s, d + 1 - 2 * y, m)
    zup = (s, jnp.minimum(d + 2, 7), m)
    zdown = (s, jnp.maximum(d - 2, 0), m)
    frame = s == 0
    code = s == 1
    scale = 1.0 / math.sqrt(HEAD_DIM)

    def remote(src, dst, ssem, rsem, to):
        return pltpu.make_async_remote_copy(
            src_ref=src, dst_ref=dst, send_sem=ssem, recv_sem=rsem, device_id=to, device_id_type=MESH
        )

    def local(src, dst, sem):
        return pltpu.make_async_copy(src, dst, sem)

    w_copies = [local(a, b, wsem.at[i]) for i, (a, b) in enumerate(((wq_h, wq), (wo_h, wo), (wu_h, wu), (wd_h, wd)))]
    e_local = [local(emb.at[:, c], em.at[c, :, m], esem.at[c]) for c in range(3)]
    c_local = [local(cot.at[:, c], gd.at[c, :, m], csem.at[c]) for c in range(3)]
    for cp in e_local:
        cp.start()
    w_copies[0].start()

    bar = pltpu.get_barrier_semaphore()
    pl.semaphore_signal(bar, 1, device_id=peer, device_id_type=MESH)
    pl.semaphore_signal(bar, 1, device_id=across, device_id_type=MESH)
    for t in range(1, 8):
        pl.semaphore_signal(bar, 1, device_id=(s, lax.rem(d + t, 8), m), device_id_type=MESH)
    with jax.named_scope("barrier"):
        pl.semaphore_wait(bar, 9)

    e_far = [remote(emb.at[:, c], em.at[c, :, m], exs.at[c], exr.at[c], peer) for c in range(3)]
    c_far = [remote(cot.at[:, c], gd.at[c, :, m], cxs.at[c], cxr.at[c], peer) for c in range(3)]
    for cp in e_far:
        cp.start()
    for cp in w_copies[1:]:
        cp.start()

    hop = [remote(sr.at[:, m], sr.at[:, m], hops.at[0], hopr.at[0], across),
           remote(sr.at[:, m], sr.at[:, m], hops.at[1], hopr.at[1], peer)]
    hop2 = [
        remote(sr.at[:, m, :, c * 512 : c * 512 + 512],
               ryz.at[pl.ds(d * 4 + c * 2, 2), pl.ds(pl.multiple_of(m * 64, 64), 64)],
               hops.at[2 + c], hopr.at[2 + c], across)
        for c in range(2)
    ]
    lo_local = [local(em.at[c, :, 1 - m], lo_h.at[:, c], lol.at[c]) for c in range(3)]
    lo_far = [remote(em.at[c, :, 1 - m], lo_h.at[:, c], los.at[c], lor.at[c], across) for c in range(3)]
    dl_far = [remote(em.at[c, :, m], em.at[c, :, 1 - m], dls.at[c], dlr.at[c], across) for c in range(3)]
    ge_local = [local(em.at[c, :, 1 - m], ge_h.at[:, c], gel.at[c]) for c in range(3)]
    ge_far = [remote(em.at[c, :, 1 - m], ge_h.at[:, c], ges.at[c], ger.at[c], across) for c in range(3)]

    grads_out = [local(xm.at[t], g_h.at[t], gsem.at[t]) for t in range(3)]
    gga[...] = jnp.zeros_like(gga)

    def rms(v):
        return lax.rsqrt(jnp.mean(v * v, axis=-1, keepdims=True) + norm_eps)

    def exchange(recv_slot, send_slot, whole):
        mine = slice(None) if whole else 1 - m
        return remote(xs.at[send_slot, :, mine], xr.at[recv_slot, :, mine], mps.at[send_slot], mpr.at[recv_slot], peer)

    def put_xs(slot, cols, t):
        xs[slot, :, :, :, cols] = t.astype(BF).reshape(2, 2, 64, t.shape[-1])

    def summed(recv_slot, send_slot, i):
        mb, mh, r = halves16(i)
        return xs[send_slot, mb, mh, r].astype(F32) + xr[recv_slot, mb, mh, r].astype(F32)

    def summed_own(recv_slot, send_slot, i):
        mb, r, _ = own16(i, m)
        return xs[send_slot, mb, m, r].astype(F32) + xr[recv_slot, mb, m, r].astype(F32)

    def out_block(o, recv_slot, send_slot):
        for n in range(2):
            put_xs(send_slot, slice(n * 512, n * 512 + 512), dot_nn(o, wo[:, n * 512 : n * 512 + 512]))
        exchange(recv_slot, send_slot, True).start()

    def up_block(b_in, put):
        for f in range(4):
            t = dot_nn(b_in, wu[:, f * 512 : f * 512 + 512])
            for g in range(8):
                put(f, slice(g * 32, g * 32 + 32), t[g * 32 : g * 32 + 32])

    def down_block(get_hid, recv_slot, send_slot):
        for n in range(2):
            cols = slice(n * 512, n * 512 + 512)
            t = dot_nn(get_hid(0), wd[0:512, cols])
            for f in range(1, 4):
                t = t + dot_nn(get_hid(f), wd[f * 512 : f * 512 + 512, cols])
            put_xs(send_slot, cols, t)
        exchange(recv_slot, send_slot, False).start()

    def dff_block(g_low, page, put_hid, recv_slot, send_slot):
        for f in range(4):
            t = dot_nt(g_low, wd[f * 512 : f * 512 + 512])
            for g in range(8):
                at = slice(g * 32, g * 32 + 32)
                u = uph[page(f), at].astype(F32)
                th = gelu_tanh(u)
                if put_hid is not None:
                    put_hid(f, at, (0.5 * u * (1.0 + th)).astype(BF))
                uph[page(f), at] = (gelu_slope(u, th) * t[g * 32 : g * 32 + 32]).astype(BF)
        for n in range(2):
            at = slice(n * 512, n * 512 + 512)
            t = dot_nt(uph[page(0)], wu[at, 0:512])
            for f in range(1, 4):
                t = t + dot_nt(uph[page(f)], wu[at, f * 512 : f * 512 + 512])
            put_xs(send_slot, at, t)
        exchange(recv_slot, send_slot, True).start()

    def dqkv_block(page, recv_slot, send_slot):
        for n in range(2):
            at = slice(n * 512, n * 512 + 512)
            t = dot_nt(qk[page(0)], wq[0, at])
            for c in range(1, 3):
                t = t + dot_nt(qk[page(c)], wq[c, at])
            put_xs(send_slot, at, t)
        exchange(recv_slot, send_slot, False).start()

    def norm_back(v, grad, gain):
        sc = rms(v)
        u = grad * gain
        vn = v * sc
        corr = jnp.mean(vn * u, axis=-1, keepdims=True)
        return sc * (u - vn * corr), grad * vn

    def add_gain(row, part):
        gga[row] = gga[row] + (part[0:8] + part[8:16])

    def acc_at(i):
        t = lax.rem(i, 4)
        return lax.div(i, 4), pl.ds(pl.multiple_of(lax.div(t, 2) * 128, 128), 128), by512(lax.rem(t, 2))

    gm = remote(gpart.at[0], gpart.at[1], gms, gmr, peer)

    def gain_first():
        gpart[0] = jnp.broadcast_to(jnp.sum(gga[0], axis=0, keepdims=True), (8, 1024))
        gm.start()

    g_far = []
    for t in range(1, 8):
        o = lax.rem(d + t, 8)
        g_far.append((remote(ggr.at[d], ggr.at[d], ggs.at[t], ggrs.at[d], (s, o, m)),
                      remote(ggr.at[d], ggr.at[o], ggs.at[t], ggrs.at[o], (s, o, m))))

    def gain_second():
        gm.wait()
        own1 = jnp.sum(gga[1], axis=0, keepdims=True)
        ggr[d] = jnp.concatenate([gpart[0, 0:1] + gpart[1, 0:1], own1, jnp.zeros((6, 1024), F32)], axis=0)
        for cp, _ in g_far:
            cp.start()

    def gain_last():
        for cp, back in g_far:
            cp.wait_send()
            back.wait_recv()
        acc = ggr[0]
        for t in range(1, 8):
            acc = acc + ggr[t]
        gg_o[0] = acc[0:2]

    def ha(h, k):
        return 32 + h * 13 + k

    def hz(h, idx):
        return 32 + h * 13 + 8 + idx

    def help_a(h):
        return remote(uph.at[pl.ds(24 + h % 2 * 4, 4), pl.ds(pl.multiple_of(y * 128, 128), 128)],
                      ryz.at[pl.ds(ha(h, 0), 4)], has.at[h], har.at[h], across)

    def help_b(h):
        return remote(uph.at[pl.ds(24 + h % 2 * 4, 4), pl.ds(pl.multiple_of((1 - y) * 128, 128), 128)],
                      ryz.at[pl.ds(ha(h, 4), 4)], hbs.at[h], hbr.at[h], (1 - s, d + 1 - 2 * y, m))

    def help_right(h, k):
        return remote(ryz.at[ha(h, k)], ryz.at[hz(h, k + 1)], hzrs.at[h, k], hzrr.at[h, k], zup)

    def help_left(h, k):
        return remote(ryz.at[ha(h, k)], ryz.at[hz(h, k)], hzls.at[h, k], hzlr.at[h, k], zdown)

    def help_back(h):
        return remote(ryz.at[ha(h, z)], ryz.at[36 + h], hres.at[h], hrer.at[h], across)

    def add_pages(to, page):
        for g in range(4):
            at = slice(g * 32, g * 32 + 32)
            ryz[to, at] = (ryz[to, at].astype(F32) + ryz[page, at].astype(F32)).astype(BF)

    def help_start(h):
        help_a(h).wait_recv()
        help_b(h).wait_recv()

        def each(t):
            k = jnp.where(z < 2, 3 - t, t)
            add_pages(ha(h, k), ha(h, 4 + k))

            @pl.when((z == 0) & (k > 0))
            def _():
                help_right(h, k).start()

            @pl.when((z == 3) & (k < 3))
            def _():
                help_left(h, k).start()

        loop(0, 4, each)

    def help_pass(h, leg):
        def on_right(k):
            help_right(h, k).wait_recv()
            add_pages(ha(h, k), hz(h, k + 1))
            help_right(h, k).start()

        def on_left(k):
            help_left(h, k).wait_recv()
            add_pages(ha(h, k), hz(h, k))
            help_left(h, k).start()

        if leg == 0:
            @pl.when(z == 1)
            def _():
                on_right(3)
                on_right(2)

            @pl.when(z == 2)
            def _():
                on_left(0)
                on_left(1)
        else:
            @pl.when(z == 1)
            def _():
                on_left(0)

            @pl.when(z == 2)
            def _():
                on_right(3)

    def help_finish(h):
        @pl.when(z > 0)
        def _():
            help_right(h, z).wait_recv()
            add_pages(ha(h, z), hz(h, z + 1))

        @pl.when(z < 3)
        def _():
            help_left(h, z).wait_recv()
            add_pages(ha(h, z), hz(h, z))

        help_back(h).start()

    def help_sent(h):
        help_back(h).wait_send()
        for k in range(4):
            @pl.when(k > z)
            def _():
                help_right(h, k).wait_send()

            @pl.when(k < z)
            def _():
                help_left(h, k).wait_send()

    def low_lanes():
        return lax.broadcasted_iota(jnp.int32, (128, 128), 1) < 64

    def stack_heads(v):
        zero = jnp.zeros_like(v)
        return jnp.concatenate([jnp.where(low_lanes(), v, zero), jnp.where(low_lanes(), zero, v)], axis=0)

    def side_by_side(v):
        return jnp.concatenate([v[0:128], v[128:256]], axis=1)

    def frame_allowed(mb):
        pos = lax.broadcasted_iota(jnp.int32, (128, 128), 0)
        lane = lax.broadcasted_iota(jnp.int32, (128, 128), 1)
        one = (lane <= pos) & (lane.astype(F32) >= cs[2, mb * 128 : mb * 128 + 128])
        return jnp.concatenate([one, one], axis=0)

    def frame_probs(places, q2, k):
        allowed = [frame_allowed(mb) for mb in range(2)]
        sc = [dot_nt(a, b) * scale for a, b in zip(q2, k)]
        sc = [jnp.where(allowed[mb], v, masked_fill) for (mb, _, _), v in zip(places, sc)]
        top = [jnp.max(v, axis=-1, keepdims=True) for v in sc]
        e = [jnp.exp(v - t) for v, t in zip(sc, top)]
        inv = [1.0 / jnp.sum(v, axis=-1, keepdims=True) for v in e]
        return [v * t for v, t in zip(e, inv)]

    def frame_places(g):
        return [
            (mb, slice(mb * 128, mb * 128 + 128), pl.ds(pl.multiple_of((g * 2 + t) * 128, 128), 128))
            for mb in range(2) for t in range(2)
        ]

    def frame_attend(b):
        def part(g):
            places = frame_places(g)
            q2 = [stack_heads(qk[b * 3, at, cols]) for _, at, cols in places]
            k = [qk[b * 3 + 1, at, cols] for _, at, cols in places]
            v2 = [stack_heads(qk[b * 3 + 2, at, cols]) for _, at, cols in places]
            p = [side_by_side(v.astype(BF)) for v in frame_probs(places, q2, k)]
            o = [dot_nn(v, w) for v, w in zip(p, v2)]
            for (_, at, cols), v in zip(places, o):
                ob[b, at, cols] = v.astype(BF)

        loop(0, 2, part)

    def frame_attend_back(b, do_slot):
        def part(g):
            places = frame_places(g)
            q2 = [stack_heads(qk[b * 3, at, cols]) for _, at, cols in places]
            k = [qk[b * 3 + 1, at, cols] for _, at, cols in places]
            v = [qk[b * 3 + 2, at, cols] for _, at, cols in places]
            do2 = [stack_heads(dob[do_slot, at, cols]) for _, at, cols in places]
            p = frame_probs(places, q2, k)
            dp = [dot_nt(a, c) for a, c in zip(do2, v)]
            mean = [jnp.sum(a * c, axis=-1, keepdims=True) for a, c in zip(dp, p)]
            ds = [(c * (a - t)).astype(BF) for a, c, t in zip(dp, p, mean)]
            dv = [dot_tn(a.astype(BF), c) for a, c in zip(p, do2)]
            dk = [dot_tn(a, c) for a, c in zip(ds, q2)]
            dq = [dot_nn(side_by_side(a), stack_heads(c)) for a, c in zip(ds, k)]
            for i, (_, at, cols) in enumerate(places):
                co, si = cs[0, at], cs[1, at]
                for c, t in ((0, dq[i] * scale), (1, dk[i] * scale)):
                    qk[b * 3 + c, at, cols] = (t * co - swap_halves(t) * si).astype(BF)
                qk[b * 3 + 2, at, cols] = dv[i].astype(BF)

        loop(0, 2, part)

    def frame_tables(b):
        for mb in range(2):
            at = slice(mb * 128, mb * 128 + 128)
            pos = lax.broadcasted_iota(jnp.int32, (128, 128), 0)
            lane = lax.broadcasted_iota(jnp.int32, (128, 128), 1)
            start = jnp.broadcast_to(st[b, mb : mb + 1], (128, 128)).T
            hot = ((pos.astype(F32) - start) == lane.astype(F32)).astype(BF)
            for c in range(2):
                cs[c, at] = dot_nn(hot, tabs[c, 0]) + dot_nn(hot, tabs[c, 1]) + dot_nn(hot, tabs[c, 2])
            cs[2, at] = start

    def frame_qkv(a_slot, b):
        for c in range(3):
            t = dot_nn(ab[a_slot], wq[c])
            for g in range(4):
                v = t[:, g * 128 : g * 128 + 128]
                if c < 2:
                    v = v * cs[0] + swap_halves(v) * cs[1]
                qk[b * 3 + c, :, g * 128 : g * 128 + 128] = v.astype(BF)

    def px(b, i):
        mb, r = lax.div(i, 8), by16(lax.rem(i, 8))
        q, k = lax.div(b, 2), lax.rem(b, 2) * 2
        return jnp.concatenate([rg[q, k, mb, r], rg[q, k + 1, mb, r]], axis=1).astype(F32)

    def put_px(b, i, v):
        mb, r = lax.div(i, 8), by16(lax.rem(i, 8))
        q, k = lax.div(b, 2), lax.rem(b, 2) * 2
        rg[q, k, mb, r] = v[:, 0:512].astype(BF)
        rg[q, k + 1, mb, r] = v[:, 512:1024].astype(BF)

    def ds_rows(b, i):
        mb, r = lax.div(i, 8), by16(lax.rem(i, 8))
        return jnp.concatenate([ryz[b * 4 + mb, r], ryz[b * 4 + 2 + mb, r]], axis=1).astype(F32)

    def ds_all(b):
        return jnp.concatenate(
            [ryz[pl.ds(b * 4, 2)].reshape(ROWS, 512), ryz[pl.ds(b * 4 + 2, 2)].reshape(ROWS, 512)], axis=1
        )

    mrows = pl.ds(pl.multiple_of(m * 64, 64), 64)

    def px_ref(b):
        return rg.at[lax.div(b, 2), pl.ds(lax.rem(b, 2) * 2, 2), :, mrows]

    def ds_ref(b):
        return ryz.at[pl.ds(b * 4, 4), mrows]

    def block_of(i):
        j = lax.div(i, 2)
        low = jnp.where(j == 0, 1, jnp.where(j == 1, 0, j))
        high = jnp.where(j == 0, 2, jnp.where(j == 1, 3, 3 - j))
        zz = jnp.where(z == 0, j, jnp.where(z == 1, low, jnp.where(z == 2, high, 3 - j)))
        other = lax.rem(i, 2)
        return zz * 2 + jnp.where(other == 0, y, 1 - y), zz, other

    def spread(ref, sems, rsem, ms, mr, i, with_peer):
        b, zz, other = block_of(i)

        def go(direction, to):
            remote(ref(b), ref(b), sems.at[b, direction], rsem.at[b], to).start()

        @pl.when(other == 0)
        def _():
            go(2, ypeer)

            @pl.when((zz <= z) & (z < 3))
            def _():
                go(0, zup)

            @pl.when((zz >= z) & (z > 0))
            def _():
                go(1, zdown)

        if with_peer:
            remote(ref(b), ref(b), ms.at[b], mr.at[b], peer).start()

    def arrive(ref, sems, rsem, ms, mr, i):
        b, _, _ = block_of(i)
        remote(ref(b), ref(b), sems.at[b, 2], rsem.at[b], ypeer).wait_recv()
        spread(ref, sems, rsem, ms, mr, i, True)

    def drained(ref, sems, rsem, ms, mr, i, with_peer):
        b, zz, other = block_of(i)

        @pl.when(other == 0)
        def _():
            remote(ref(b), ref(b), sems.at[b, 2], rsem.at[b], ypeer).wait_send()

            @pl.when((zz <= z) & (z < 3))
            def _():
                remote(ref(b), ref(b), sems.at[b, 0], rsem.at[b], zup).wait_send()

            @pl.when((zz >= z) & (z > 0))
            def _():
                remote(ref(b), ref(b), sems.at[b, 1], rsem.at[b], zdown).wait_send()

        if with_peer:
            remote(ref(b), ref(b), ms.at[b], mr.at[b], peer).wait_send()

    xset = (px_ref, xas, xar, xms, xmr)
    dset = (ds_ref, das, dar, dms, dmr)

    inner = (z == 1) | (z == 2)

    def arrive_early(which):
        arrive(*which, 1)
        arrive(*which, 2)

        @pl.when(inner)
        def _():
            arrive(*which, 4)

    def arrive_at(which, i):
        @pl.when(i == 2)
        def _():
            arrive(*which, jnp.where(inner, 6, 4))

        @pl.when((i > 1) & (i < jnp.where(inner, 5, 6)))
        def _():
            there = jnp.where(i == 2, 3, jnp.where(i == 3, 6, jnp.where(i == 4, 5, 7)))
            here = jnp.where(i == 2, 3, jnp.where(i == 3, 5, 7))
            arrive(*which, jnp.where(inner, here, there))

    def halves_in(which, i):
        ref, _, _, ms, mr = which
        b, _, _ = block_of(i)
        remote(ref(b), ref(b), ms.at[b], mr.at[b], peer).wait_recv()

    def ring(e):
        t = lax.rem(e, 4)
        return jnp.where(t < 2, t + 1, t + 2), 1 + lax.rem(e, 2)

    mine128 = pl.ds(pl.multiple_of(d * 128, 128), 128)

    def lanes(i):
        return pl.ds(pl.multiple_of(i * 128, 128), 128)

    def hid_at(f):
        return slice(f * 256, f * 256 + 256)

    def gd_slice(b):
        page = b * 4 + lax.div(d, 4) * 2
        cols = pl.ds(pl.multiple_of(lax.rem(d, 4) * 128, 128), 128)
        return ryz[pl.ds(page, 2), :, cols].reshape(ROWS, 128).T

    def put_tb(f, at, v):
        tb[f * 256 + at.start : f * 256 + at.stop, 0:512] = v

    def frame_grad(chunk, left, right, first):
        at = acc_at(chunk)
        t = dot_nn(left, right)
        xm[at] = t if first else xm[at] + t

    def frame_grads_down(b, first):
        left = gd_slice(b)
        for f in range(4):
            frame_grad(f, left, tb[hid_at(f), 0:512], first)

    def frame_grads_up(b, bm_slot, bm_cols, first):
        left = bm[bm_slot, :, bm_cols].T
        for f in range(4):
            frame_grad(4 + f, left, uph[f * 8 + b], first)

    def frame_grads_attend(b, ga_slot, a_slot, a_cols, first):
        frame_grad(8, gd[ga_slot, :, :, :, mine128].reshape(ROWS, 128).T, ob[b], first)
        left = ab[a_slot, :, a_cols].T
        for c in range(3):
            frame_grad(9 + c, left, qk[b * 3 + c], first)

    @pl.when(frame)
    def _():
        pos = lax.broadcasted_iota(jnp.int32, (128, 128), 0)
        lane = lax.broadcasted_iota(jnp.int32, (128, 128), 1)
        freq = jnp.exp(lax.rem(lane, 32).astype(F32) * (-2.0 * math.log(rotary_base) / HEAD_DIM))
        angle = pos.astype(F32) * freq
        sine = jnp.sin(angle)
        for c, v in enumerate((jnp.cos(angle), jnp.where(lax.rem(lane, 64) < 32, -sine, sine))):
            for t in range(3):
                term = v.astype(BF)
                tabs[c, t] = term
                v = v - term.astype(F32)
        place = lax.broadcasted_iota(jnp.int32, (8, 128), 1)
        rows = []
        for mb in range(2):
            start = jnp.zeros((8, 128), jnp.int32)
            end = jnp.int32(0)
            for j in range(4):
                size = lens[mb, 0, j]
                end = end + size
                start = start + jnp.where(place >= end, size, 0)
            rows.append(start)
        which = lax.broadcasted_iota(jnp.int32, (8, 128), 0)
        st[d] = jnp.where(which == 0, rows[0], rows[1]).astype(F32)
        for t in range(1, 8):
            o = lax.rem(d + t, 8)
            remote(st.at[d], st.at[d], sts.at[t], strc.at[d], (s, o, m)).start()
        frame_tables(d)

        with jax.named_scope("embeds_wait"):
            for cp in e_local:
                cp.wait()
            for cp in e_far:
                cp.wait()

        gain0 = gains[0, 0:1]
        gain1 = gains[0, 1:2]

        def x_own(i):
            mb, mh, r = halves16(i)
            return em[0, mb, mh, r].astype(F32) + em[1, mb, mh, r].astype(F32) + em[2, mb, mh, r].astype(F32)

        def rows_in(i):
            v = x_own(i)
            xm[2, by16(i)] = v
            ab[0, by16(i)] = (v * rms(v) * gain0).astype(BF)
            put_px(d, i, v)

        with jax.named_scope("own_qkv"):
            loop(0, 16, rows_in, unroll=UNROLL)
            spread(*xset, 0, False)
            w_copies[0].wait()
            frame_qkv(0, d)
        with jax.named_scope("own_attend"):
            frame_attend(d)
        w_copies[1].wait()
        with jax.named_scope("own_out"):
            out_block(ob[d], 0, 0)
            w_copies[2].wait()
            exchange(0, 0, True).wait()

        def rows_mid(i):
            v = xm[2, by16(i)] + summed(0, 0, i)
            return v, (v * rms(v) * gain1).astype(BF)

        def put_mid(i, v, w):
            xm[2, by16(i)] = v
            bm[0, by16(i)] = w

        def put_own(f, at, u):
            uph[f * 8 + d, at] = u.astype(BF)
            put_tb(f, at, (0.5 * u * (1.0 + gelu_tanh(u))).astype(BF))

        with jax.named_scope("own_ff"):
            grouped(16, rows_mid, put_mid)
            up_block(bm[0], put_own)
            w_copies[3].wait()
            down_block(lambda f: tb[hid_at(f), 0:512], 3, 0)
            exchange(3, 0, False).wait()

        def rows_res(i):
            mb, r, row = own16(i, m)
            sr[mb, m, r] = (xm[2, row] + summed_own(3, 0, i)).astype(BF)

        loop(0, 8, rows_res, unroll=UNROLL)
        hop[0].start()

        for t in range(1, 8):
            o = lax.rem(d + t, 8)
            remote(st.at[d], st.at[o], sts.at[t], strc.at[o], (s, o, m)).wait()

        def others_in(i):
            b, _, _ = block_of(i)
            halves_in(xset, i)
            frame_tables(b)

            def rows_norm(t):
                v = px(b, t)
                ab[2, by16(t)] = (v * rms(v) * gain0).astype(BF)

            loop(0, 16, rows_norm, unroll=UNROLL)
            ab[1, :, lanes(i)] = ab[2, :, mine128]
            frame_qkv(2, b)
            frame_attend(b)
            out_block(ob[b], *ring(i))

        def others_ff(i):
            b, _, _ = block_of(i)
            recv_slot, send_slot = ring(i)
            exchange(recv_slot, send_slot, True).wait()
            drained(*xset, i, True)

            def rows_m(t):
                v = px(b, t) + summed(recv_slot, send_slot, t)
                return v, (v * rms(v) * gain1).astype(BF)

            def put_m(t, v, w):
                put_px(b, t, v)
                bm[2, by16(t)] = w

            grouped(16, rows_m, put_m)
            bm[1, :, lanes(i)] = bm[2, :, mine128]

            def put_up(f, at, u):
                uph[f * 8 + b, at] = u.astype(BF)

            up_block(bm[2], put_up)

        with jax.named_scope("oth_arrive"):
            arrive_early(xset)

        def others(i):
            with jax.named_scope("oth_arrive"):
                arrive_at(xset, i)

            @pl.when(i < 8)
            def _():
                with jax.named_scope("oth_in"):
                    others_in(i)

            @pl.when(i > 1)
            def _():
                with jax.named_scope("oth_ff"):
                    others_ff(i - 1)

        loop(1, 9, others)
        drained(*xset, 0, False)
        hop[0].wait_send()

        with jax.named_scope("help_start0"):
            help_start(0)

        with jax.named_scope("d_sent_wait"):
            for cp in hop2:
                cp.wait_recv()
            spread(*dset, 0, True)
            halves_in(dset, 0)
        with jax.named_scope("own_dff"):
            dff_block(ds_all(d), lambda f: f * 8 + d, put_tb, 0, 0)
            frame_grads_down(d, True)
        with jax.named_scope("help_pass0"):
            help_pass(0, 0)
        exchange(0, 0, True).wait()

        def rows_dmid(i):
            add, part = norm_back(xm[2, by16(i)], summed(0, 0, i), gain1)
            return ds_rows(d, i) + add, part

        def put_dmid(i, dm, part):
            mb, mh, r = halves16(i)
            xm[2, by16(i)] = dm
            gd[0, mb, mh, r] = dm.astype(BF)
            add_gain(1, part)

        with jax.named_scope("own_dmid"):
            grouped(16, rows_dmid, put_dmid)
            dob[0] = dot_nt(gd[0].reshape(ROWS, 1024), wo[...]).astype(BF)
        with jax.named_scope("arrive_early"):
            arrive_early(dset)
        frame_tables(d)
        with jax.named_scope("own_attend_back"):
            frame_attend_back(d, 0)
        dqkv_block(lambda c: d * 3 + c, 3, 0)
        with jax.named_scope("own_grads"):
            frame_grads_up(d, 0, mine128, True)
        exchange(3, 0, False).wait()

        def rows_dx(i):
            mb, r, row = own16(i, m)
            v = em[0, mb, m, r].astype(F32) + em[1, mb, m, r].astype(F32) + em[2, mb, m, r].astype(F32)
            add, part = norm_back(v, summed_own(3, 0, i), gain0)
            return xm[2, row] + add, part

        def put_dx(i, dv, part):
            mb, r, _ = own16(i, m)
            top = dv.astype(BF)
            em[0, mb, m, r] = top
            em[1, mb, m, r] = (dv - top.astype(F32)).astype(BF)
            add_gain(0, part)

        grouped(8, rows_dx, put_dx)
        gain_first()

        def rows_ge(i):
            mb, r, _ = own16(i, m)
            dv = em[0, mb, m, r].astype(F32) + em[1, mb, m, r].astype(F32)
            return tuple((em[c, mb, 1 - m, r].astype(F32) + dv).astype(BF) for c in range(3))

        def put_ge(i, *parts):
            mb, r, _ = own16(i, m)
            for c in range(3):
                em[c, mb, 1 - m, r] = parts[c]

        def embed_grads():
            for cp in dl_far:
                cp.wait_recv()
            grouped(8, rows_ge, put_ge)
            for cp in ge_local + ge_far:
                cp.start()

        gain_second()
        with jax.named_scope("help_pass0"):
            help_pass(0, 1)
        frame_grads_attend(d, 0, 0, mine128, True)

        def back_first(i):
            b, _, _ = block_of(i)
            halves_in(dset, i)
            dff_block(ds_all(b), lambda f: f * 8 + b, put_tb, *ring(i + 7))
            frame_grads_down(b, False)

        def back_second(i):
            b, _, _ = block_of(i)
            recv_slot, send_slot = ring(i + 7)
            exchange(recv_slot, send_slot, True).wait()

            def rows_dm(t):
                mb, mh, r = halves16(t)
                add, _ = norm_back(px(b, t), summed(recv_slot, send_slot, t), gain1)
                gd[1, mb, mh, r] = (ds_rows(b, t) + add).astype(BF)

            loop(0, 16, rows_dm, unroll=UNROLL)
            dob[0] = dot_nt(gd[1].reshape(ROWS, 1024), wo[...]).astype(BF)
            frame_tables(b)
            frame_attend_back(b, 0)
            frame_grads_up(b, 1, lanes(i), False)
            frame_grads_attend(b, 1, 1, lanes(i), False)

        def others_back(i):
            @pl.when(i < 8)
            def _():
                with jax.named_scope("oth_dff"):
                    back_first(i)

            with jax.named_scope("oth_arrive_d"):
                arrive_at(dset, i)

            @pl.when(i > 1)
            def _():
                with jax.named_scope("oth_rest"):
                    back_second(i - 1)

            @pl.when(i == 2)
            def _():
                with jax.named_scope("help_finish0"):
                    help_finish(0)

            @pl.when(i == 4)
            def _():
                with jax.named_scope("help_start1"):
                    help_start(1)

            @pl.when(i == 5)
            def _():
                with jax.named_scope("help_pass1"):
                    help_pass(1, 0)

            @pl.when(i == 6)
            def _():
                with jax.named_scope("help_pass1"):
                    help_pass(1, 1)

            @pl.when(i == 7)
            def _():
                with jax.named_scope("help_finish1"):
                    help_finish(1)
                with jax.named_scope("embed_grads"):
                    embed_grads()

        loop(1, 9, others_back)
        for h in range(HELPED):
            help_sent(h)
        loop(0, 8, lambda i: drained(*dset, i, True))
        for cp in grads_out:
            cp.start()
        gain_last()
        for cp in ge_local:
            cp.wait()
        for cp in ge_far:
            cp.wait_send()
        for cp in lo_far:
            cp.wait_recv()
        for cp in grads_out:
            cp.wait()

    def head_sum(prod):
        r0 = lax.broadcasted_iota(jnp.int32, (256, 256), 0)
        r1 = lax.broadcasted_iota(jnp.int32, (256, 256), 1)
        ones = (lax.div(r0, 64) == lax.div(r1, 64)).astype(BF)
        return dot_nn(prod.astype(BF), ones)

    def code_probs(q, k):
        probs = []
        for i in range(3):
            sc = [head_sum(q[i] * k[j]) * scale for j in range(i + 1)]
            top = functools.reduce(jnp.maximum, sc)
            e = [jnp.exp(v - top) for v in sc]
            inv = 1.0 / functools.reduce(jnp.add, e)
            probs.append([v * inv for v in e])
        return probs

    def code_part(i):
        return (pl.ds(pl.multiple_of(lax.div(i, 2) * 64, 64), 64), pl.ds(pl.multiple_of(lax.rem(i, 2) * 256, 256), 256))

    def code_attend(i):
        at, cols = code_part(i)
        q, k, v = ([qk[c * 3 + b, at, cols].astype(F32) for b in range(3)] for c in range(3))
        probs = code_probs(q, k)
        for t in range(3):
            o = functools.reduce(jnp.add, [probs[t][j].astype(BF).astype(F32) * v[j] for j in range(t + 1)])
            ob[t, at, cols] = o.astype(BF)

    def code_attend_back(i):
        at, cols = code_part(i)
        q, k, v = ([qk[c * 3 + b, at, cols].astype(F32) for b in range(3)] for c in range(3))
        do = [ob[3 + b, at, cols].astype(F32) for b in range(3)]
        probs = code_probs(q, k)
        dk = [0.0] * 3
        dv = [0.0] * 3
        for t in range(3):
            dp = [head_sum(do[t] * v[j]) for j in range(t + 1)]
            mean = functools.reduce(jnp.add, [dp[j] * probs[t][j] for j in range(t + 1)])
            dq = 0.0
            for j in range(t + 1):
                ds = (probs[t][j] * (dp[j] - mean)).astype(BF).astype(F32)
                dq = dq + ds * k[j]
                dk[j] = dk[j] + ds * q[t]
                dv[j] = dv[j] + probs[t][j].astype(BF).astype(F32) * do[t]
            qk[t, at, cols] = (dq * scale).astype(BF)
        for j in range(3):
            qk[3 + j, at, cols] = (dk[j] * scale).astype(BF)
            qk[6 + j, at, cols] = dv[j].astype(BF)

    def flip(get):
        def one(b):
            at = pl.ds(pl.multiple_of(b * 256, 256), 256)
            t = get(b)
            for g in range(4):
                tb[g * 256 : g * 256 + 256, at] = t[:, g * 256 : g * 256 + 256].T

        loop(0, 3, one)

    def ry(slot):
        return ryz.at[pl.ds(slot * 4, 4)]

    def rz(slot, idx):
        return SLOTS * 4 + slot * 5 + idx

    def sends(slot):
        return remote(rg.at[slot, :, 1 - y], ry(slot), ysn.at[slot], yrc.at[slot], ypeer)

    def right(slot, k):
        return remote(rg.at[slot, k, y], ryz.at[rz(slot, k + 1)], zrs.at[slot, k], zrr.at[slot, k], zup)

    def left(slot, k):
        return remote(rg.at[slot, k, y], ryz.at[rz(slot, k)], zls.at[slot, k], zlr.at[slot, k], zdown)

    def free_slot(slot, last=False):
        sends(slot).wait_send()
        for k in range(4):
            @pl.when((k > z) & ((z > 0) | (k < 2)) if last else k > z)
            def _():
                right(slot, k).wait_send()

            @pl.when((k < z) & ((z < 3) | (k > 1)) if last else k < z)
            def _():
                left(slot, k).wait_send()

    def make_chunk(i, act, send=True):
        slot = lax.rem(i, SLOTS)

        @pl.when(i >= SLOTS)
        def _():
            free_slot(slot)

        def part(k):
            at = pl.ds(pl.multiple_of(k * 256, 256), 256)
            rg[slot, k] = dot_nn(tb[at, :], act()).astype(BF).reshape(2, 128, 512)

        loop(0, 4, part)

        @pl.when(i >= SLOTS)
        def _():
            pl.semaphore_wait(ycr, 1)

        if send:
            sends(slot).start()

    def make_help(h, act):
        def part(k):
            at = pl.ds(pl.multiple_of(k * 256, 256), 256)
            uph[24 + h % 2 * 4 + k] = dot_nn(tb[at, :], act()).astype(BF)

        loop(0, 4, part)
        help_a(h).start()
        help_b(h).start()

    def add_into(slot, k, page):
        for g in range(4):
            at = slice(g * 32, g * 32 + 32)
            rg[slot, k, y, at] = (rg[slot, k, y, at].astype(F32) + ryz[page, at].astype(F32)).astype(BF)

    def proc_y(i):
        slot = lax.rem(i, SLOTS)
        sends(slot).wait_recv()

        @pl.when(i >= SLOTS)
        def _():
            @pl.when(z < 3)
            def _():
                pl.semaphore_wait(rcr, 1)

            @pl.when(z > 0)
            def _():
                pl.semaphore_wait(lcr, 1)

        def up_first(t):
            k = 3 - t
            add_into(slot, k, slot * 4 + k)

            @pl.when((z == 0) & (k > 0))
            def _():
                right(slot, k).start()

                @pl.when((i == CHUNKS - 1) & (k > 1))
                def _():
                    right(slot, k).wait_send()

        def down_first(t):
            add_into(slot, t, slot * 4 + t)

            @pl.when((z == 3) & (t < 3))
            def _():
                left(slot, t).start()

                @pl.when((i == CHUNKS - 1) & (t < 2))
                def _():
                    left(slot, t).wait_send()

        @pl.when(z < 2)
        def _():
            loop(0, 4, up_first)

        @pl.when(z >= 2)
        def _():
            loop(0, 4, down_first)

        @pl.when(i + SLOTS < CHUNKS)
        def _():
            pl.semaphore_signal(ycr, 1, device_id=ypeer, device_id_type=MESH)

    def pass_right(slot, k):
        right(slot, k).wait_recv()
        add_into(slot, k, rz(slot, k + 1))
        right(slot, k).start()

    def pass_left(slot, k):
        left(slot, k).wait_recv()
        add_into(slot, k, rz(slot, k))
        left(slot, k).start()

    def fwd_z(i):
        slot = lax.rem(i, SLOTS)

        @pl.when(z == 1)
        def _():
            pass_right(slot, 3)
            pass_right(slot, 2)

        @pl.when(z == 2)
        def _():
            pass_left(slot, 0)
            pass_left(slot, 1)

    def fwd_z2(i):
        slot = lax.rem(i, SLOTS)

        @pl.when(z == 1)
        def _():
            pass_left(slot, 0)

        @pl.when(z == 2)
        def _():
            pass_right(slot, 3)

    def finish(i):
        slot = lax.rem(i, SLOTS)

        @pl.when(z > 0)
        def _():
            right(slot, z).wait_recv()
            add_into(slot, z, rz(slot, z + 1))

        @pl.when(z < 3)
        def _():
            left(slot, z).wait_recv()
            add_into(slot, z, rz(slot, z))

        total = rg[slot, z, y].astype(F32)

        xm[acc_at(jnp.where(i < 3, i + 1, i + 2))] = total

        @pl.when(i + SLOTS < CHUNKS)
        def _():
            @pl.when(z > 0)
            def _():
                pl.semaphore_signal(rcr, 1, device_id=zdown, device_id_type=MESH)

            @pl.when(z < 3)
            def _():
                pl.semaphore_signal(lcr, 1, device_id=zup, device_id_type=MESH)

    @pl.when(code)
    def _():
        for cp in c_local:
            cp.start()
        for cp in c_far:
            cp.start()
        for cp in e_local:
            cp.wait()
        for cp in e_far:
            cp.wait()
        gain0 = gains[0, 0:1]
        gain1 = gains[0, 1:2]
        for cp in c_local:
            cp.wait()
        for cp in c_far:
            cp.wait()
        flip(lambda b: gd[b].reshape(ROWS, 1024))
        with jax.named_scope("sent_wait"):
            hop[0].wait_recv()
            hop[1].start()
            hop[1].wait_recv()

        def rows_in(i):
            mb, mh, r = halves16(i)
            came = sr[mb, mh, r].astype(F32)
            for c in range(3):
                v = em[c, mb, mh, r].astype(F32) + came
                xm[c, by16(i)] = v
                ab[c, by16(i)] = (v * rms(v) * gain0).astype(BF)

        with jax.named_scope("code_norm"):
            loop(0, 16, rows_in, unroll=UNROLL)

        def qkv_all(b):
            for c in range(3):
                qk[c * 3 + b] = dot_nn(ab[b], wq[c]).astype(BF)

        w_copies[0].wait()
        with jax.named_scope("code_qkv"):
            loop(0, 3, qkv_all)
        with jax.named_scope("code_attend"):
            loop(0, 8, code_attend)
        w_copies[1].wait()
        with jax.named_scope("code_out"):
            loop(0, 3, lambda b: out_block(ob[b], b, b))
        w_copies[2].wait()
        w_copies[3].wait()

        def ff(b):
            exchange(b, b, True).wait()

            def rows_mid(i):
                v = xm[b, by16(i)] + summed(b, b, i)
                return v, (v * rms(v) * gain1).astype(BF)

            def put_mid(i, v, w):
                xm[b, by16(i)] = v
                bm[b, by16(i)] = w

            grouped(16, rows_mid, put_mid)

            def put(f, at, u):
                uph[f * 3 + b, at] = u.astype(BF)
                uph[12 + f * 3 + b, at] = (0.5 * u * (1.0 + gelu_tanh(u))).astype(BF)

            up_block(bm[b], put)
            down_block(lambda f: uph[12 + f * 3 + b], 3 + b, b)

        with jax.named_scope("code_ff"):
            loop(0, 3, ff)

        def res(b):
            exchange(3 + b, b, False).wait()

            def rows_res(i):
                mb, r, row = own16(i, m)
                em[b, mb, 1 - m, r] = (xm[b, row] + summed_own(3 + b, b, i)).astype(BF)

            loop(0, 8, rows_res, unroll=UNROLL)

        with jax.named_scope("code_grad_down"):
            make_chunk(0, lambda: uph[15:18].reshape(768, 512))
            make_help(0, lambda: uph[12:15].reshape(768, 512))
            loop(1, 3, lambda i: make_chunk(i, lambda: uph[pl.ds(15 + i * 3, 3)].reshape(768, 512), False))
        loop(0, 3, res)
        for cp in lo_local:
            cp.start()

        def dff(b):
            dff_block(gd[b].reshape(ROWS, 1024), lambda f: f * 3 + b, None, b, b)

            @pl.when(b == 1)
            def _():
                sends(1).start()

        with jax.named_scope("code_dff"):
            loop(0, 3, dff)
        def dmid(b):
            exchange(b, b, True).wait()

            def rows_dmid(i):
                mb, mh, r = halves16(i)
                add, part = norm_back(xm[b, by16(i)], summed(b, b, i), gain1)
                return gd[b, mb, mh, r].astype(F32) + add, part

            def put_dmid(i, dm, part):
                mb, mh, r = halves16(i)
                xm[b, by16(i)] = dm
                gd[b, mb, mh, r] = dm.astype(BF)
                add_gain(1, part)

            grouped(16, rows_dmid, put_dmid)
            ob[3 + b] = dot_nt(gd[b].reshape(ROWS, 1024), wo[...]).astype(BF)

        with jax.named_scope("code_dmid"):
            loop(0, 3, dmid)
        sends(2).start()
        with jax.named_scope("code_attend_back"):
            loop(0, 8, code_attend_back)
        with jax.named_scope("code_dqkv"):
            loop(0, 3, lambda b: dqkv_block(lambda c: c * 3 + b, 3 + b, b))

        def dx(b):
            exchange(3 + b, b, False).wait()

            def rows_dx(i):
                mb, r, row = own16(i, m)
                v = em[b, mb, m, r].astype(F32) + sr[mb, m, r].astype(F32)
                add, part = norm_back(v, summed_own(3 + b, b, i), gain0)
                return xm[b, row] + add, part

            def put_dx(i, dv, part):
                mb, r, row = own16(i, m)
                xm[b, row] = dv
                em[b, mb, m, r] = dv.astype(BF)
                add_gain(0, part)

            grouped(8, rows_dx, put_dx)

        with jax.named_scope("code_dx"):
            loop(0, 3, dx)
        hop[1].wait_send()

        def rows_ds(i):
            mb, r, row = own16(i, m)
            sr[mb, m, r] = (xm[0, row] + xm[1, row] + xm[2, row]).astype(BF)

        loop(0, 8, rows_ds, unroll=UNROLL)
        for cp in hop2:
            cp.start()
        gain_first()
        with jax.named_scope("code_y2"):
            flip(lambda b: bm[b])
            make_chunk(3, lambda: uph[3:6].reshape(768, 512))
            proc_y(0)
            proc_y(1)
            fwd_z(0)
            gain_second()
            proc_y(2)
            fwd_z(1)
            fwd_z2(0)

        def tail(i):
            @pl.when(i - 3 < CHUNKS)
            def _():
                with jax.named_scope("tail_z2"):
                    fwd_z2(i - 3)

            with jax.named_scope("tail_finish"):
                finish(i - 4)

            @pl.when(i == 6)
            def _():
                flip(lambda b: gd[b].reshape(ROWS, 1024))

            @pl.when(i == 7)
            def _():
                flip(lambda b: ab[b])

            @pl.when(i < 6)
            def _():
                make_chunk(i, lambda: uph[pl.ds((i - 2) * 3, 3)].reshape(768, 512))

            @pl.when(i == 4)
            def _():
                for cp in hop2:
                    cp.wait_send()
                make_help(1, lambda: uph[0:3].reshape(768, 512))

            @pl.when(i == 6)
            def _():
                make_chunk(i, lambda: ob[0:3].reshape(768, 512))

            @pl.when((i > 6) & (i < CHUNKS))
            def _():
                make_chunk(i, lambda: qk[pl.ds((i - 7) * 3, 3)].reshape(768, 512))

            @pl.when(i == 6)
            def _():
                for h in (0, 1):
                    help_a(h).wait_send()
                    help_b(h).wait_send()
                for cp in dl_far:
                    cp.start()

            @pl.when(i == 8)
            def _():
                for cp in dl_far:
                    cp.wait_send()
                for cp in lo_far:
                    cp.start()

            @pl.when(i - 1 < CHUNKS)
            def _():
                with jax.named_scope("tail_y"):
                    proc_y(i - 1)

            @pl.when(i - 2 < CHUNKS)
            def _():
                with jax.named_scope("tail_z"):
                    fwd_z(i - 2)

            for h in range(HELPED):
                @pl.when(i == 8 + h * 3)
                def _():
                    with jax.named_scope("helped"):
                        help_back(h).wait_recv()
                        xm[acc_at(h * 4)] = ryz[36 + h].astype(F32)
                        grads_out[h].start()

        loop(4, CHUNKS + 4, tail)
        grads_out[2].start()
        for cp in lo_local:
            cp.wait()
        for cp in lo_far:
            cp.wait_send()
        gain_last()
        for cp in ge_far:
            cp.wait_recv()
        for t in range(CHUNKS - SLOTS, CHUNKS):
            free_slot(t % SLOTS, t == CHUNKS - 1)
        for cp in grads_out:
            cp.wait()


def unpack(lo_i, ge_i, g_i, gg_i, lo_o, ge_o, gg_o, gq_o, go_o, gu_o, gd_o, lo, ge, g, gq, go, gu, gdn, sems):
    ins = [pltpu.make_async_copy(g_i.at[t], g.at[t], sems.at[t]) for t in range(3)]
    ins += [pltpu.make_async_copy(lo_i, lo, sems.at[3]), pltpu.make_async_copy(ge_i, ge, sems.at[4])]
    outs = [
        pltpu.make_async_copy(a, b, sems.at[5 + t])
        for t, (a, b) in enumerate(((gdn, gd_o), (gu, gu_o), (go, go_o), (gq, gq_o), (lo, lo_o), (ge, ge_o)))
    ]
    for cp in ins:
        cp.start()
    gg_o[...] = gg_i[...]

    def chunk(i):
        rows, cols = (i % 4) // 2 * 128, i % 2 * 512
        return g[i // 4, rows : rows + 128, cols : cols + 512]

    ins[0].wait()
    for f in range(4):
        gdn[f * 512 : f * 512 + 512] = chunk(f).T
    outs[0].start()
    ins[1].wait()
    for f in range(4):
        gu[:, f * 512 : f * 512 + 512] = chunk(4 + f)
    outs[1].start()
    ins[2].wait()
    go[...] = chunk(8).T
    outs[2].start()
    for c in range(3):
        gq[c] = chunk(9 + c)
    outs[3].start()
    for t in range(2):
        ins[3 + t].wait()
        outs[4 + t].start()
    for cp in outs:
        cp.wait()


def on_device_kernel(embeds, lengths, norm_gains, w_qkv, w_out, w_up, w_down, cotangent):
    anyspec = pl.BlockSpec(memory_space=pl.ANY)
    hbm = pl.BlockSpec(memory_space=pltpu.HBM)
    vm = pl.BlockSpec(memory_space=pltpu.VMEM)
    sd = jax.ShapeDtypeStruct
    V = pltpu.VMEM
    D = pltpu.SemaphoreType.DMA
    R = pltpu.SemaphoreType.REGULAR
    full = (2, 2, 64, 1024)
    scratch = [
        V((3, 1024, 512), BF), V((512, 1024), BF), V((1024, 2048), BF), V((2048, 1024), BF),
        V((3,) + full, BF), V((3,) + full, BF), V(full, BF),
        V((3, ROWS, 1024), F32), V((3, ROWS, 1024), BF), V((3, ROWS, 1024), BF),
        V((24, ROWS, 512), BF), V((8, ROWS, 512), BF), V((1, ROWS, 512), BF), V((32, ROWS, 512), BF),
        V((3,) + full, BF), V((6,) + full, BF), V((1024, 768), BF),
        V((3, ROWS, 128), F32), V((2, 3, 128, 128), BF), V((8, 8, 128), F32),
        V((2, 8, 1024), F32), V((8, 8, 1024), F32), V((2, 8, 1024), F32),
        V((SLOTS, 4, 2, 128, 512), BF), V((32 + HELPED * 13, 128, 512), BF),
        D((3,)), D((4,)), D((3,)), D((3,)), D((3,)), D((3,)), D((3,)), D((3,)), D((3,)), D((6,)), D((4,)), D((4,)),
        D((3,)), D((3,)), D((3,)), D((3,)), D((3,)),
        D((3,)), D((3,)), D((3,)), D((8,)), D((8,)), D, D,
        D((SLOTS,)), D((SLOTS,)), D((SLOTS, 4)), D((SLOTS, 4)), D((SLOTS, 4)), D((SLOTS, 4)),
        D((HELPED,)), D((HELPED,)), D((HELPED,)), D((HELPED,)), D((HELPED, 4)), D((HELPED, 4)), D((HELPED, 4)), D((HELPED, 4)),
        D((HELPED,)), D((HELPED,)), D((8,)), D((8,)), D((8, 3)), D((8,)), D((8,)), D((8,)), D((8, 3)), D((8,)), D((8,)), D((8,)),
        R, R, R,
    ]
    rows, gain = sd((2, 3, 64, 1024), BF), sd((1, 2, 1024), F32)
    grads = (sd((3, 128, 512), F32), sd((512, 128), F32), sd((128, 2048), F32), sd((2048, 128), F32))
    outs = pl.pallas_call(
        body,
        out_shape=(rows, rows, sd((3, ROWS, 1024), F32), gain),
        in_specs=[anyspec, anyspec, pl.BlockSpec(memory_space=pltpu.SMEM), vm, anyspec, anyspec, anyspec, anyspec],
        out_specs=(anyspec, anyspec, anyspec, vm),
        scratch_shapes=scratch,
        compiler_params=pltpu.CompilerParams(
            collective_id=0, has_side_effects=True, vmem_limit_bytes=61 * 2**20 - 2**19
        ),
        name="two_sections",
    )(
        jnp.transpose(embeds, (0, 2, 1, 3)), jnp.transpose(cotangent, (0, 2, 1, 3)), lengths, norm_gains,
        jnp.transpose(w_qkv[0], (1, 0, 2)), w_out[0], w_up[0], w_down[0],
    )
    outs = pl.pallas_call(
        unpack,
        out_shape=(rows, rows, gain) + grads,
        in_specs=[hbm] * 3 + [vm],
        out_specs=(hbm, hbm, vm) + (hbm,) * 4,
        scratch_shapes=[V(rows.shape, BF), V(rows.shape, BF), V((3, ROWS, 1024), F32)]
        + [V(g.shape, F32) for g in (grads[0], grads[1], grads[2], grads[3])] + [D((11,))],
        compiler_params=pltpu.CompilerParams(vmem_limit_bytes=60 * 2**20),
        name="results",
    )(*outs)
    lo, ge, gg, gq, go, gu, gdn = outs
    return (
        jnp.transpose(lo, (0, 2, 1, 3)), jnp.transpose(ge, (0, 2, 1, 3)), gg,
        jnp.transpose(gq, (1, 0, 2))[None], go[None], gu[None], gdn[None],
    )


def solution(mesh):
    fits = tuple(mesh.shape[name] for name in ("section", "dp", "mp")) == (2, 8, 2)
    return jax.shard_map(
        on_device_kernel if fits else on_device,
        mesh=mesh,
        in_specs=(
            P(None, ("dp", "mp"), None, None),
            P(None, "dp", None),
            P("section", None, None),
            P("section", None, None, "mp"),
            P("section", "mp", None),
            P("section", None, "mp"),
            P("section", "mp", None),
            P(None, ("dp", "mp"), None, None),
        ),
        out_specs=(
            P(None, ("dp", "mp"), None, None),
            P(None, ("dp", "mp"), None, None),
            P("section", None, None),
            P("section", "dp", None, "mp"),
            P("section", "mp", "dp"),
            P("section", "dp", "mp"),
            P("section", "mp", "dp"),
        ),
        check_vma=False,
    )
```

```python
import functools
import math

import jax
import jax.numpy as jnp
from jax import lax
from jax.experimental import pallas as pl
from jax.experimental.pallas import tpu as pltpu
from jax.sharding import PartitionSpec as P

HEAD_DIM = 64


norm_eps = 1e-05
masked_fill = -1e30
rotary_base = 10000.0


def passed_along(value, axis, steps):
    count = lax.axis_size(axis)
    leading, last = (max(0, -steps), min(count, count - steps))
    return lax.ppermute(value, axis, [(source, source + steps) for source in range(leading, last)])


def rms_scale(values, gain_row):
    return (
        values * lax.rsqrt(jnp.mean(values * values, axis=-1, keepdims=True) + norm_eps) * gain_row
    )


def rotate(values, cos_tab, sin_tab):
    half_dim = values.shape[-1] // 2
    first_half = values[..., :half_dim]
    second_half = values[..., half_dim:]
    cos_rows = cos_tab[:, None, :]
    sin_rows = sin_tab[:, None, :]
    return jnp.concatenate(
        [
            first_half * cos_rows - second_half * sin_rows,
            second_half * cos_rows + first_half * sin_rows,
        ],
        axis=-1,
    )


def global_context(length_row, frames):
    doc_ends = jnp.cumsum(length_row)
    places = jnp.arange(frames, dtype=jnp.int32)
    passed = (places[:, None] >= doc_ends[None, :]).astype(jnp.int32)
    segment = jnp.sum(passed, axis=1)
    offsets = places - jnp.sum(passed * length_row[None, :], axis=1)
    allowed = (segment[:, None] == segment[None, :]) & (places[None, :] <= places[:, None])
    half_dim = HEAD_DIM // 2
    frequency = jnp.exp(
        jnp.arange(half_dim, dtype=jnp.float32) * (-2.0 * math.log(rotary_base) / HEAD_DIM)
    )
    angles = offsets.astype(jnp.float32)[:, None] * frequency[None, :]
    return (allowed, jnp.cos(angles), jnp.sin(angles))


def global_attend(projected, context):
    allowed, cos_tab, sin_tab = context
    attn_scale = 1.0 / math.sqrt(HEAD_DIM)
    row_total, _, local_width = projected.shape
    head_count = local_width // HEAD_DIM
    query_rows = rotate(
        projected[:, 0].reshape(row_total, head_count, HEAD_DIM), cos_tab, sin_tab
    ).astype(jnp.bfloat16)
    key_rows = rotate(
        projected[:, 1].reshape(row_total, head_count, HEAD_DIM), cos_tab, sin_tab
    ).astype(jnp.bfloat16)
    value_rows = projected[:, 2].reshape(row_total, head_count, HEAD_DIM).astype(jnp.bfloat16)
    scores = (
        jnp.einsum("qhd,khd->hqk", query_rows, key_rows, preferred_element_type=jnp.float32)
        * attn_scale
    )
    scores = jnp.where(allowed[None], scores, masked_fill)
    score_peak = jnp.max(scores, axis=-1, keepdims=True)
    exp_scores = jnp.exp(scores - score_peak)
    row_sums = jnp.sum(exp_scores, axis=-1, keepdims=True)
    weights_low = (exp_scores / row_sums).astype(jnp.bfloat16)
    mixed_rows = jnp.einsum(
        "hqk,khd->qhd", weights_low, value_rows, preferred_element_type=jnp.float32
    )
    log_total = score_peak + jnp.log(row_sums)
    return (
        mixed_rows.reshape(row_total, local_width).astype(jnp.bfloat16),
        (query_rows, key_rows, value_rows, log_total),
    )


def global_attend_back(attn_saved, context, grad_mixed):
    query_rows, key_rows, value_rows, log_total = attn_saved
    allowed, cos_tab, sin_tab = context
    attn_scale = 1.0 / math.sqrt(HEAD_DIM)
    row_total, head_count, _ = query_rows.shape
    grad_heads = grad_mixed.reshape(row_total, head_count, HEAD_DIM)
    scores = (
        jnp.einsum("qhd,khd->hqk", query_rows, key_rows, preferred_element_type=jnp.float32)
        * attn_scale
    )
    prob_rows = jnp.where(allowed[None], jnp.exp(scores - log_total), 0.0)
    grad_values = jnp.einsum(
        "hqk,qhd->khd",
        prob_rows.astype(jnp.bfloat16),
        grad_heads,
        preferred_element_type=jnp.float32,
    )
    grad_probs = jnp.einsum(
        "qhd,khd->hqk", grad_heads, value_rows, preferred_element_type=jnp.float32
    )
    grad_scores = (
        prob_rows * (grad_probs - jnp.sum(grad_probs * prob_rows, axis=-1, keepdims=True))
    ).astype(jnp.bfloat16)
    grad_query = (
        jnp.einsum("hqk,khd->qhd", grad_scores, key_rows, preferred_element_type=jnp.float32)
        * attn_scale
    )
    grad_keys = (
        jnp.einsum("hqk,qhd->khd", grad_scores, query_rows, preferred_element_type=jnp.float32)
        * attn_scale
    )
    grad_query = rotate(grad_query, cos_tab, -sin_tab)
    grad_keys = rotate(grad_keys, cos_tab, -sin_tab)
    stacked = jnp.stack([grad_query, grad_keys, grad_values], axis=1)
    return stacked.reshape(row_total, 3, head_count * HEAD_DIM).astype(jnp.bfloat16)


def local_attend(projected, context):
    attn_scale = 1.0 / math.sqrt(HEAD_DIM)
    row_total, _, local_width = projected.shape
    head_count = local_width // HEAD_DIM
    frames = row_total // 3
    qkv_parts = projected.reshape(frames, 3, 3, head_count, HEAD_DIM).astype(jnp.bfloat16)
    query_rows = qkv_parts[:, :, 0]
    key_rows = qkv_parts[:, :, 1]
    value_rows = qkv_parts[:, :, 2]
    scores = (
        jnp.einsum("fihd,fjhd->fhij", query_rows, key_rows, preferred_element_type=jnp.float32)
        * attn_scale
    )
    scores = jnp.where(context[None, None], scores, masked_fill)
    score_peak = jnp.max(scores, axis=-1, keepdims=True)
    exp_scores = jnp.exp(scores - score_peak)
    row_sums = jnp.sum(exp_scores, axis=-1, keepdims=True)
    weights_low = (exp_scores / row_sums).astype(jnp.bfloat16)
    mixed_rows = jnp.einsum(
        "fhij,fjhd->fihd", weights_low, value_rows, preferred_element_type=jnp.float32
    )
    log_total = score_peak + jnp.log(row_sums)
    return (
        mixed_rows.reshape(row_total, local_width).astype(jnp.bfloat16),
        (query_rows, key_rows, value_rows, log_total),
    )


def local_attend_back(attn_saved, context, grad_mixed):
    query_rows, key_rows, value_rows, log_total = attn_saved
    attn_scale = 1.0 / math.sqrt(HEAD_DIM)
    frames, _, head_count, _ = query_rows.shape
    grad_heads = grad_mixed.reshape(frames, 3, head_count, HEAD_DIM)
    scores = (
        jnp.einsum("fihd,fjhd->fhij", query_rows, key_rows, preferred_element_type=jnp.float32)
        * attn_scale
    )
    prob_rows = jnp.where(context[None, None], jnp.exp(scores - log_total), 0.0)
    grad_values = jnp.einsum(
        "fhij,fihd->fjhd",
        prob_rows.astype(jnp.bfloat16),
        grad_heads,
        preferred_element_type=jnp.float32,
    )
    grad_probs = jnp.einsum(
        "fihd,fjhd->fhij", grad_heads, value_rows, preferred_element_type=jnp.float32
    )
    grad_scores = (
        prob_rows * (grad_probs - jnp.sum(grad_probs * prob_rows, axis=-1, keepdims=True))
    ).astype(jnp.bfloat16)
    grad_query = (
        jnp.einsum("fhij,fjhd->fihd", grad_scores, key_rows, preferred_element_type=jnp.float32)
        * attn_scale
    )
    grad_keys = (
        jnp.einsum("fhij,fihd->fjhd", grad_scores, query_rows, preferred_element_type=jnp.float32)
        * attn_scale
    )
    stacked = jnp.stack([grad_query, grad_keys, grad_values], axis=2)
    return stacked.reshape(frames * 3, 3, head_count * HEAD_DIM).astype(jnp.bfloat16)


def gather_project(normed, weight, form):
    piece_rows = lax.all_gather(normed, "mp", axis=0, tiled=True)
    return (piece_rows, jnp.einsum(form, piece_rows, weight, preferred_element_type=jnp.float32))


def reduce_rows(left, weight, form, row_count):

    def partial_term(first_row, count_rows):
        return jnp.einsum(form, left, weight, preferred_element_type=jnp.float32)

    return lax.psum_scatter(
        partial_term(jnp.int32(0), row_count * lax.axis_size("mp")),
        "mp",
        scatter_dimension=0,
        tiled=True,
    )


def reduce_grads(left, weight, form, row_count):

    def partial_term(first_row, count_rows):
        return jnp.einsum(form, left, weight, preferred_element_type=jnp.float32)

    return lax.psum_scatter(
        partial_term(jnp.int32(0), row_count * lax.axis_size("mp")),
        "mp",
        scatter_dimension=0,
        tiled=True,
    )


def gather_grads(grad_low):
    return lax.all_gather(grad_low, "mp", axis=0, tiled=True)


def layer_forward(frame_rows, weights, attend, context):
    gain_pair, w_qkv, w_out, w_up, w_down = weights
    row_count = frame_rows.shape[0]
    normed = rms_scale(frame_rows, gain_pair[0]).astype(jnp.bfloat16)
    normed_all, projected = gather_project(normed, w_qkv, "nd,dce->nce")
    mixed_rows, attn_saved = attend(projected, context)
    attn_rows = reduce_rows(mixed_rows, w_out, "ne,ed->nd", row_count)
    middle = frame_rows + attn_rows
    normed_mid = rms_scale(middle, gain_pair[1]).astype(jnp.bfloat16)
    normed_mid_all, up_all = gather_project(normed_mid, w_up, "nd,de->ne")
    hidden = jax.nn.gelu(up_all).astype(jnp.bfloat16)
    down_rows = reduce_rows(hidden, w_down, "nf,fd->nd", row_count)
    record = (normed_all, attn_saved, mixed_rows, middle, normed_mid_all, up_all, hidden)
    return (middle + down_rows, attn_rows + down_rows, record)


def layer_backward(frame_rows, weights, attend_back, context, record, grad_result):
    gain_pair, w_qkv, w_out, w_up, w_down = weights
    normed_all, attn_saved, mixed_rows, middle, normed_mid_all, up_all, hidden = record
    row_count = frame_rows.shape[0]
    grad_down_all = gather_grads(grad_result.astype(jnp.bfloat16))
    grad_w_down = jnp.einsum("nf,nd->fd", hidden, grad_down_all, preferred_element_type=jnp.float32)
    grad_hidden = jnp.einsum("nd,fd->nf", grad_down_all, w_down, preferred_element_type=jnp.float32)
    _, gelu_back = jax.vjp(jax.nn.gelu, up_all)
    grad_up = gelu_back(grad_hidden)[0].astype(jnp.bfloat16)
    grad_w_up = jnp.einsum("nd,ne->de", normed_mid_all, grad_up, preferred_element_type=jnp.float32)
    grad_normed_mid = reduce_grads(grad_up, w_up, "ne,de->nd", row_count)
    _, mid_back = jax.vjp(rms_scale, middle, gain_pair[1])
    grad_middle_part, grad_gain_mid = mid_back(grad_normed_mid)
    grad_middle = grad_result + grad_middle_part
    grad_attn_all = gather_grads(grad_middle.astype(jnp.bfloat16))
    grad_w_out = jnp.einsum(
        "ne,nd->ed", mixed_rows, grad_attn_all, preferred_element_type=jnp.float32
    )
    grad_mixed = jnp.einsum(
        "nd,ed->ne", grad_attn_all, w_out, preferred_element_type=jnp.float32
    ).astype(jnp.bfloat16)
    grad_projected = attend_back(attn_saved, context, grad_mixed)
    grad_w_qkv = jnp.einsum(
        "nd,nce->dce", normed_all, grad_projected, preferred_element_type=jnp.float32
    )
    grad_normed = reduce_grads(grad_projected, w_qkv, "nce,dce->nd", row_count)
    _, first_back = jax.vjp(rms_scale, frame_rows, gain_pair[0])
    grad_rows_part, grad_gain_first = first_back(grad_normed)
    grad_frame_rows = grad_middle + grad_rows_part
    layer_grads = (
        jnp.stack([grad_gain_first, grad_gain_mid]),
        grad_w_qkv,
        grad_w_out,
        grad_w_up,
        grad_w_down,
    )
    return (grad_frame_rows, layer_grads)


def on_device(embeds, lengths, norm_gains, w_qkv, w_out, w_up, w_down, cotangent):
    weights = (norm_gains[0], w_qkv[0], w_out[0], w_up[0], w_down[0])
    micro_count = embeds.shape[0]
    shard_rows = embeds.shape[1]
    width = embeds.shape[-1]
    frames = shard_rows * lax.axis_size("mp")
    is_first = lax.axis_index("section") == 0
    local_allowed = jnp.tril(jnp.ones((3, 3), dtype=jnp.bool_))
    gain_total = jnp.zeros(norm_gains.shape[1:], jnp.float32)
    weight_totals = tuple((jnp.zeros(weight.shape, jnp.float32) for weight in weights[1:]))
    totals = (gain_total,) + weight_totals
    y_part = jnp.zeros(embeds.shape, jnp.float32)
    e_part = jnp.zeros(embeds.shape, jnp.float32)
    zero_send = jnp.zeros((shard_rows, width), jnp.bfloat16)

    def add_grads(running, layer_grads):
        run_gain, run_qkv, run_out, run_up, run_down = running
        part_gain, part_qkv, part_out, part_up, part_down = layer_grads
        return (
            run_gain + part_gain,
            run_qkv + part_qkv,
            run_out + part_out,
            run_up + part_up,
            run_down + part_down,
        )

    def global_forward(micro_index):
        context = global_context(lengths[micro_index, 0], frames)
        frame_in = jnp.sum(embeds[micro_index].astype(jnp.float32), axis=1)
        result, _, record = layer_forward(frame_in, weights, global_attend, context)
        return (frame_in, context, result, record)

    def pick(first_value, second_value):
        return jnp.where(is_first, first_value, second_value)

    carry_state = (totals, y_part, e_part)
    forward_recv = zero_send
    backward_recv = zero_send
    for tick_index in range(micro_count + 2):

        def first_section(state_in):
            running, y_state, e_state = state_in
            send_fwd = zero_send
            if tick_index < micro_count:
                _, _, result, _ = global_forward(tick_index)
                send_fwd = result.astype(jnp.bfloat16)
                joined = (
                    embeds[tick_index].astype(jnp.float32)
                    + send_fwd.astype(jnp.float32)[:, None, :]
                )
                y_state = y_state.at[tick_index].set(joined)
            if tick_index >= 2:
                micro_index = tick_index - 2
                frame_in, context, _, record = global_forward(micro_index)
                grad_frame, layer_grads = layer_backward(
                    frame_in,
                    weights,
                    global_attend_back,
                    context,
                    record,
                    backward_recv.astype(jnp.float32),
                )
                running = add_grads(running, layer_grads)
                e_state = e_state.at[micro_index].set(
                    jnp.broadcast_to(grad_frame[:, None, :], e_state.shape[1:])
                )
            return ((running, y_state, e_state), send_fwd, zero_send)

        def second_section(state_in):
            running, y_state, e_state = state_in
            send_back = zero_send
            if 1 <= tick_index <= micro_count:
                micro_index = tick_index - 1
                local_in = (
                    embeds[micro_index].astype(jnp.float32)
                    + forward_recv.astype(jnp.float32)[:, None, :]
                )
                local_in = local_in.reshape(shard_rows * 3, width)
                _, branches, record = layer_forward(local_in, weights, local_attend, local_allowed)
                grad_seed = (
                    cotangent[micro_index].astype(jnp.float32).reshape(shard_rows * 3, width)
                )
                grad_local, layer_grads = layer_backward(
                    local_in, weights, local_attend_back, local_allowed, record, grad_seed
                )
                running = add_grads(running, layer_grads)
                y_state = y_state.at[micro_index].set(branches.reshape(shard_rows, 3, width))
                grad_frames = grad_local.reshape(shard_rows, 3, width)
                e_state = e_state.at[micro_index].set(grad_frames)
                send_back = jnp.sum(grad_frames, axis=1).astype(jnp.bfloat16)
            return ((running, y_state, e_state), zero_send, send_back)

        first_result = first_section(carry_state)
        second_result = second_section(carry_state)
        carry_state, send_fwd, send_back = jax.tree.map(pick, first_result, second_result)
        if tick_index < micro_count:
            forward_recv = passed_along(send_fwd, "section", 1)
        if 1 <= tick_index <= micro_count:
            backward_recv = passed_along(send_back, "section", -1)
    totals, y_part, e_part = carry_state
    gain_total, grad_qkv, grad_out, grad_up, grad_down = totals
    grad_qkv, grad_out, grad_up, grad_down = (
        lax.psum_scatter(grad_qkv, "dp", scatter_dimension=0, tiled=True),
        lax.psum_scatter(grad_out, "dp", scatter_dimension=1, tiled=True),
        lax.psum_scatter(grad_up, "dp", scatter_dimension=0, tiled=True),
        lax.psum_scatter(grad_down, "dp", scatter_dimension=1, tiled=True),
    )
    gain_total = lax.psum(gain_total, ("dp", "mp"))
    y_sum, e_sum = (
        lax.psum(y_part.astype(jnp.bfloat16), "section").astype(jnp.float32),
        lax.psum(e_part.astype(jnp.bfloat16), "section").astype(jnp.float32),
    )
    return (
        y_sum.astype(jnp.bfloat16),
        e_sum.astype(jnp.bfloat16),
        gain_total[None],
        grad_qkv[None],
        grad_out[None],
        grad_up[None],
        grad_down[None],
    )


BF = jnp.bfloat16
F32 = jnp.float32
MESH = pl.DeviceIdType.MESH
SLOTS = 5
CHUNKS = 9
HELPED = 2
ALONG = 1
ROWS = 256
UNROLL = 4


def dot_nn(left, right):
    return lax.dot_general(left, right, (((1,), (0,)), ((), ())), preferred_element_type=F32)


def dot_nt(left, right):
    return lax.dot_general(left, right, (((1,), (1,)), ((), ())), preferred_element_type=F32)


def dot_tn(left, right):
    return lax.dot_general(left, right, (((0,), (0,)), ((), ())), preferred_element_type=F32)


def gelu_tanh(u):
    c0 = math.sqrt(2.0 / math.pi)
    return jnp.tanh(u * (c0 + (c0 * 0.044715) * (u * u)))


def gelu_slope(u, th):
    c0 = math.sqrt(2.0 / math.pi)
    return 0.5 * (1.0 + th) + 0.5 * u * (1.0 - th * th) * (c0 + (3.0 * 0.044715 * c0) * (u * u))


def loop(lower, upper, step, unroll=1):
    def wrapped(i, carry):
        step(i)
        return carry

    lax.fori_loop(lower, upper, wrapped, 0, unroll=unroll)


def grouped(count, work, store, size=4):
    def group(g):
        done = [work(g * size + t) for t in range(size)]
        for t in range(size):
            store(g * size + t, *done[t])

    loop(0, count // size, group)


def by16(i):
    return pl.ds(pl.multiple_of(i * 16, 16), 16)


def by512(i):
    return pl.ds(pl.multiple_of(i * 512, 512), 512)


def halves16(i):
    return lax.div(i, 8), lax.rem(lax.div(i, 4), 2), pl.ds(pl.multiple_of(lax.rem(i, 4) * 16, 16), 16)


def own16(i, m):
    mb, r = lax.div(i, 4), pl.multiple_of(lax.rem(i, 4) * 16, 16)
    return mb, pl.ds(r, 16), pl.ds(pl.multiple_of(mb * 128 + m * 64 + r, 16), 16)


def swap_halves(v):
    lane = lax.broadcasted_iota(jnp.int32, v.shape, 1)
    return jnp.where(lax.rem(lane, 64) < 32, pltpu.roll(v, 96, 1), pltpu.roll(v, 32, 1))


def body(
    emb, cot, lens, gains, wq_h, wo_h, wu_h, wd_h,
    lo_h, ge_h, g_h, gg_o,
    wq, wo, wu, wd, em, gd, sr, xm, ab, bm, qk, ob, dob, uph, xs, xr, tb,
    cs, tabs, st, gga, ggr, gpart, rg, ryz,
    gsem, wsem, esem, exs, exr, csem, cxs, cxr, mps, mpr, hops, hopr, lol, los, lor, dls, dlr,
    gel, ges, ger, ggs, ggrs, gms, gmr, ysn, yrc, zrs, zrr, zls, zlr,
    frs, frr, fls, flr, fys, fyr, has, har, hbs, hbr, hzrs, hzrr, hzls, hzlr, hres, hrer, sts, strc, xas, xar, xms, xmr, das, dar, dms, dmr, ycr, rcr, lcr,
):
    s = lax.axis_index("section")
    d = lax.axis_index("dp")
    m = lax.axis_index("mp")
    y = lax.rem(d, 2)
    z = lax.div(d, 2)
    peer = (s, d, 1 - m)
    across = (1 - s, d, m)
    ypeer = (s, d + 1 - 2 * y, m)
    zup = (s, jnp.minimum(d + 2, 7), m)
    zdown = (s, jnp.maximum(d - 2, 0), m)
    frame = s == 0
    code = s == 1
    scale = 1.0 / math.sqrt(HEAD_DIM)

    def remote(src, dst, ssem, rsem, to):
        return pltpu.make_async_remote_copy(
            src_ref=src, dst_ref=dst, send_sem=ssem, recv_sem=rsem, device_id=to, device_id_type=MESH
        )

    def local(src, dst, sem):
        return pltpu.make_async_copy(src, dst, sem)

    w_copies = [local(a, b, wsem.at[i]) for i, (a, b) in enumerate(((wq_h, wq), (wo_h, wo), (wu_h, wu), (wd_h, wd)))]
    e_local = [local(emb.at[:, c], em.at[c, :, m], esem.at[c]) for c in range(3)]
    c_local = [local(cot.at[:, c], gd.at[c, :, m], csem.at[c]) for c in range(3)]
    for cp in e_local:
        cp.start()
    w_copies[0].start()

    bar = pltpu.get_barrier_semaphore()
    pl.semaphore_signal(bar, 1, device_id=peer, device_id_type=MESH)
    pl.semaphore_signal(bar, 1, device_id=across, device_id_type=MESH)
    for t in range(1, 8):
        pl.semaphore_signal(bar, 1, device_id=(s, lax.rem(d + t, 8), m), device_id_type=MESH)
    with jax.named_scope("barrier"):
        pl.semaphore_wait(bar, 9)

    e_far = [remote(emb.at[:, c], em.at[c, :, m], exs.at[c], exr.at[c], peer) for c in range(3)]
    c_far = [remote(cot.at[:, c], gd.at[c, :, m], cxs.at[c], cxr.at[c], peer) for c in range(3)]
    for cp in e_far:
        cp.start()
    for cp in w_copies[1:]:
        cp.start()

    hop = [remote(sr.at[:, m], sr.at[:, m], hops.at[0], hopr.at[0], across),
           remote(sr.at[:, m], sr.at[:, m], hops.at[1], hopr.at[1], peer)]
    hop2 = [
        remote(sr.at[:, m, :, c * 512 : c * 512 + 512],
               ryz.at[pl.ds(d * 4 + c * 2, 2), pl.ds(pl.multiple_of(m * 64, 64), 64)],
               hops.at[2 + c], hopr.at[2 + c], across)
        for c in range(2)
    ]
    lo_local = [local(em.at[c, :, 1 - m], lo_h.at[:, c], lol.at[c]) for c in range(3)]
    lo_far = [remote(em.at[c, :, 1 - m], lo_h.at[:, c], los.at[c], lor.at[c], across) for c in range(3)]
    dl_far = [remote(em.at[c, :, m], em.at[c, :, 1 - m], dls.at[c], dlr.at[c], across) for c in range(3)]
    ge_local = [local(em.at[c, :, 1 - m], ge_h.at[:, c], gel.at[c]) for c in range(3)]
    ge_far = [remote(em.at[c, :, 1 - m], ge_h.at[:, c], ges.at[c], ger.at[c], across) for c in range(3)]

    grads_out = [local(xm.at[t], g_h.at[t], gsem.at[t]) for t in range(3)]
    gga[...] = jnp.zeros_like(gga)

    def rms(v):
        return lax.rsqrt(jnp.mean(v * v, axis=-1, keepdims=True) + norm_eps)

    def exchange(recv_slot, send_slot, whole):
        mine = slice(None) if whole else 1 - m
        return remote(xs.at[send_slot, :, mine], xr.at[recv_slot, :, mine], mps.at[send_slot], mpr.at[recv_slot], peer)

    def put_xs(slot, cols, t):
        xs[slot, :, :, :, cols] = t.astype(BF).reshape(2, 2, 64, t.shape[-1])

    def summed(recv_slot, send_slot, i):
        mb, mh, r = halves16(i)
        return xs[send_slot, mb, mh, r].astype(F32) + xr[recv_slot, mb, mh, r].astype(F32)

    def summed_own(recv_slot, send_slot, i):
        mb, r, _ = own16(i, m)
        return xs[send_slot, mb, m, r].astype(F32) + xr[recv_slot, mb, m, r].astype(F32)

    def out_block(o, recv_slot, send_slot):
        for n in range(2):
            put_xs(send_slot, slice(n * 512, n * 512 + 512), dot_nn(o, wo[:, n * 512 : n * 512 + 512]))
        exchange(recv_slot, send_slot, True).start()

    def up_block(b_in, put):
        for f in range(4):
            t = dot_nn(b_in, wu[:, f * 512 : f * 512 + 512])
            for g in range(8):
                put(f, slice(g * 32, g * 32 + 32), t[g * 32 : g * 32 + 32])

    def down_block(get_hid, recv_slot, send_slot):
        for n in range(2):
            cols = slice(n * 512, n * 512 + 512)
            t = dot_nn(get_hid(0), wd[0:512, cols])
            for f in range(1, 4):
                t = t + dot_nn(get_hid(f), wd[f * 512 : f * 512 + 512, cols])
            put_xs(send_slot, cols, t)
        exchange(recv_slot, send_slot, False).start()

    def dff_block(g_low, page, put_hid, recv_slot, send_slot):
        for f in range(4):
            t = dot_nt(g_low, wd[f * 512 : f * 512 + 512])
            for g in range(8):
                at = slice(g * 32, g * 32 + 32)
                u = uph[page(f), at].astype(F32)
                th = gelu_tanh(u)
                if put_hid is not None:
                    put_hid(f, at, (0.5 * u * (1.0 + th)).astype(BF))
                uph[page(f), at] = (gelu_slope(u, th) * t[g * 32 : g * 32 + 32]).astype(BF)
        for n in range(2):
            at = slice(n * 512, n * 512 + 512)
            t = dot_nt(uph[page(0)], wu[at, 0:512])
            for f in range(1, 4):
                t = t + dot_nt(uph[page(f)], wu[at, f * 512 : f * 512 + 512])
            put_xs(send_slot, at, t)
        exchange(recv_slot, send_slot, True).start()

    def dqkv_block(page, recv_slot, send_slot):
        for n in range(2):
            at = slice(n * 512, n * 512 + 512)
            t = dot_nt(qk[page(0)], wq[0, at])
            for c in range(1, 3):
                t = t + dot_nt(qk[page(c)], wq[c, at])
            put_xs(send_slot, at, t)
        exchange(recv_slot, send_slot, False).start()

    def norm_back(v, grad, gain):
        sc = rms(v)
        u = grad * gain
        vn = v * sc
        corr = jnp.mean(vn * u, axis=-1, keepdims=True)
        return sc * (u - vn * corr), grad * vn

    def add_gain(row, part):
        gga[row] = gga[row] + (part[0:8] + part[8:16])

    def acc_at(i):
        t = lax.rem(i, 4)
        return lax.div(i, 4), pl.ds(pl.multiple_of(lax.div(t, 2) * 128, 128), 128), by512(lax.rem(t, 2))

    gm = remote(gpart.at[0], gpart.at[1], gms, gmr, peer)

    def gain_first():
        gpart[0] = jnp.broadcast_to(jnp.sum(gga[0], axis=0, keepdims=True), (8, 1024))
        gm.start()

    g_far = []
    for t in range(1, 8):
        o = lax.rem(d + t, 8)
        g_far.append((remote(ggr.at[d], ggr.at[d], ggs.at[t], ggrs.at[d], (s, o, m)),
                      remote(ggr.at[d], ggr.at[o], ggs.at[t], ggrs.at[o], (s, o, m))))

    def gain_second():
        gm.wait()
        own1 = jnp.sum(gga[1], axis=0, keepdims=True)
        ggr[d] = jnp.concatenate([gpart[0, 0:1] + gpart[1, 0:1], own1, jnp.zeros((6, 1024), F32)], axis=0)
        for cp, _ in g_far:
            cp.start()

    def gain_last():
        for cp, back in g_far:
            cp.wait_send()
            back.wait_recv()
        acc = ggr[0]
        for t in range(1, 8):
            acc = acc + ggr[t]
        gg_o[0] = acc[0:2]

    def ha(h, k):
        return 32 + h * 13 + k

    def hz(h, idx):
        return 32 + h * 13 + 8 + idx

    def hg(h):
        return (24, 16)[h]

    def help_a(h):
        return remote(uph.at[pl.ds(hg(h), 4), pl.ds(pl.multiple_of(y * 128, 128), 128)],
                      ryz.at[pl.ds(ha(h, 0), 4)], has.at[h], har.at[h], across)

    def help_b(h):
        return remote(uph.at[pl.ds(hg(h), 4), pl.ds(pl.multiple_of((1 - y) * 128, 128), 128)],
                      ryz.at[pl.ds(ha(h, 4), 4)], hbs.at[h], hbr.at[h], (1 - s, d + 1 - 2 * y, m))

    def help_right(h, k):
        return remote(ryz.at[ha(h, k)], ryz.at[hz(h, k + 1)], hzrs.at[h, k], hzrr.at[h, k], zup)

    def help_left(h, k):
        return remote(ryz.at[ha(h, k)], ryz.at[hz(h, k)], hzls.at[h, k], hzlr.at[h, k], zdown)

    def help_back(h):
        return remote(ryz.at[ha(h, z)], ryz.at[56 + h], hres.at[h], hrer.at[h], across)

    def add_pages(to, page):
        for g in range(4):
            at = slice(g * 32, g * 32 + 32)
            ryz[to, at] = (ryz[to, at].astype(F32) + ryz[page, at].astype(F32)).astype(BF)

    def help_start(h):
        help_a(h).wait_recv()
        help_b(h).wait_recv()

        def each(t):
            k = jnp.where(z < 2, 3 - t, t)
            add_pages(ha(h, k), ha(h, 4 + k))

            @pl.when((z == 0) & (k > 0))
            def _():
                help_right(h, k).start()

            @pl.when((z == 3) & (k < 3))
            def _():
                help_left(h, k).start()

        loop(0, 4, each)

    def help_pass(h, leg):
        def on_right(k):
            help_right(h, k).wait_recv()
            add_pages(ha(h, k), hz(h, k + 1))
            help_right(h, k).start()

        def on_left(k):
            help_left(h, k).wait_recv()
            add_pages(ha(h, k), hz(h, k))
            help_left(h, k).start()

        if leg == 0:
            @pl.when(z == 1)
            def _():
                on_right(3)
                on_right(2)

            @pl.when(z == 2)
            def _():
                on_left(0)
                on_left(1)
        else:
            @pl.when(z == 1)
            def _():
                on_left(0)

            @pl.when(z == 2)
            def _():
                on_right(3)

    def help_finish(h):
        @pl.when(z > 0)
        def _():
            help_right(h, z).wait_recv()
            add_pages(ha(h, z), hz(h, z + 1))

        @pl.when(z < 3)
        def _():
            help_left(h, z).wait_recv()
            add_pages(ha(h, z), hz(h, z))

        help_back(h).start()

    def help_sent(h):
        help_back(h).wait_send()
        for k in range(4):
            @pl.when(k > z)
            def _():
                help_right(h, k).wait_send()

            @pl.when(k < z)
            def _():
                help_left(h, k).wait_send()

    def low_lanes():
        return lax.broadcasted_iota(jnp.int32, (128, 128), 1) < 64

    def stack_heads(v):
        zero = jnp.zeros_like(v)
        return jnp.concatenate([jnp.where(low_lanes(), v, zero), jnp.where(low_lanes(), zero, v)], axis=0)

    def side_by_side(v):
        return jnp.concatenate([v[0:128], v[128:256]], axis=1)

    def frame_allowed(mb):
        pos = lax.broadcasted_iota(jnp.int32, (128, 128), 0)
        lane = lax.broadcasted_iota(jnp.int32, (128, 128), 1)
        one = (lane <= pos) & (lane.astype(F32) >= cs[2, mb * 128 : mb * 128 + 128])
        return jnp.concatenate([one, one], axis=0)

    def frame_probs(places, q2, k):
        allowed = [frame_allowed(mb) for mb in range(2)]
        sc = [dot_nt(a, b) * scale for a, b in zip(q2, k)]
        sc = [jnp.where(allowed[mb], v, masked_fill) for (mb, _, _), v in zip(places, sc)]
        top = [jnp.max(v, axis=-1, keepdims=True) for v in sc]
        e = [jnp.exp(v - t) for v, t in zip(sc, top)]
        inv = [1.0 / jnp.sum(v, axis=-1, keepdims=True) for v in e]
        return [v * t for v, t in zip(e, inv)]

    def frame_places(g):
        return [
            (mb, slice(mb * 128, mb * 128 + 128), pl.ds(pl.multiple_of((g * 2 + t) * 128, 128), 128))
            for mb in range(2) for t in range(2)
        ]

    def frame_attend(b):
        def part(g):
            places = frame_places(g)
            q2 = [stack_heads(qk[b * 3, at, cols]) for _, at, cols in places]
            k = [qk[b * 3 + 1, at, cols] for _, at, cols in places]
            v2 = [stack_heads(qk[b * 3 + 2, at, cols]) for _, at, cols in places]
            p = [side_by_side(v.astype(BF)) for v in frame_probs(places, q2, k)]
            o = [dot_nn(v, w) for v, w in zip(p, v2)]
            for (_, at, cols), v in zip(places, o):
                ob[b, at, cols] = v.astype(BF)

        loop(0, 2, part)

    def frame_attend_back(b, do_slot):
        def part(g):
            places = frame_places(g)
            q2 = [stack_heads(qk[b * 3, at, cols]) for _, at, cols in places]
            k = [qk[b * 3 + 1, at, cols] for _, at, cols in places]
            v = [qk[b * 3 + 2, at, cols] for _, at, cols in places]
            do2 = [stack_heads(dob[do_slot, at, cols]) for _, at, cols in places]
            p = frame_probs(places, q2, k)
            dp = [dot_nt(a, c) for a, c in zip(do2, v)]
            mean = [jnp.sum(a * c, axis=-1, keepdims=True) for a, c in zip(dp, p)]
            ds = [(c * (a - t)).astype(BF) for a, c, t in zip(dp, p, mean)]
            dv = [dot_tn(a.astype(BF), c) for a, c in zip(p, do2)]
            dk = [dot_tn(a, c) for a, c in zip(ds, q2)]
            dq = [dot_nn(side_by_side(a), stack_heads(c)) for a, c in zip(ds, k)]
            for i, (_, at, cols) in enumerate(places):
                co, si = cs[0, at], cs[1, at]
                for c, t in ((0, dq[i] * scale), (1, dk[i] * scale)):
                    qk[b * 3 + c, at, cols] = (t * co - swap_halves(t) * si).astype(BF)
                qk[b * 3 + 2, at, cols] = dv[i].astype(BF)

        loop(0, 2, part)

    def frame_tables(b):
        for mb in range(2):
            at = slice(mb * 128, mb * 128 + 128)
            pos = lax.broadcasted_iota(jnp.int32, (128, 128), 0)
            lane = lax.broadcasted_iota(jnp.int32, (128, 128), 1)
            start = jnp.broadcast_to(st[b, mb : mb + 1], (128, 128)).T
            hot = ((pos.astype(F32) - start) == lane.astype(F32)).astype(BF)
            for c in range(2):
                cs[c, at] = dot_nn(hot, tabs[c, 0]) + dot_nn(hot, tabs[c, 1]) + dot_nn(hot, tabs[c, 2])
            cs[2, at] = start

    def frame_qkv(a_slot, b):
        for c in range(3):
            t = dot_nn(ab[a_slot], wq[c])
            for g in range(4):
                v = t[:, g * 128 : g * 128 + 128]
                if c < 2:
                    v = v * cs[0] + swap_halves(v) * cs[1]
                qk[b * 3 + c, :, g * 128 : g * 128 + 128] = v.astype(BF)

    def px(b, i):
        mb, r = lax.div(i, 8), by16(lax.rem(i, 8))
        q, k = lax.div(b, 2), lax.rem(b, 2) * 2
        return jnp.concatenate([rg[q, k, mb, r], rg[q, k + 1, mb, r]], axis=1).astype(F32)

    def put_px(b, i, v):
        mb, r = lax.div(i, 8), by16(lax.rem(i, 8))
        q, k = lax.div(b, 2), lax.rem(b, 2) * 2
        rg[q, k, mb, r] = v[:, 0:512].astype(BF)
        rg[q, k + 1, mb, r] = v[:, 512:1024].astype(BF)

    def ds_rows(b, i):
        mb, r = lax.div(i, 8), by16(lax.rem(i, 8))
        return jnp.concatenate([ryz[b * 4 + mb, r], ryz[b * 4 + 2 + mb, r]], axis=1).astype(F32)

    def ds_all(b):
        return jnp.concatenate(
            [ryz[pl.ds(b * 4, 2)].reshape(ROWS, 512), ryz[pl.ds(b * 4 + 2, 2)].reshape(ROWS, 512)], axis=1
        )

    mrows = pl.ds(pl.multiple_of(m * 64, 64), 64)

    def px_ref(b):
        return rg.at[lax.div(b, 2), pl.ds(lax.rem(b, 2) * 2, 2), :, mrows]

    def ds_ref(b):
        return ryz.at[pl.ds(b * 4, 4), mrows]

    def block_of(i):
        j = lax.div(i, 2)
        low = jnp.where(j == 0, 1, jnp.where(j == 1, 0, j))
        high = jnp.where(j == 0, 2, jnp.where(j == 1, 3, 3 - j))
        zz = jnp.where(z == 0, j, jnp.where(z == 1, low, jnp.where(z == 2, high, 3 - j)))
        other = lax.rem(i, 2)
        return zz * 2 + jnp.where(other == 0, y, 1 - y), zz, other

    def spread(ref, sems, rsem, ms, mr, i, with_peer):
        b, zz, other = block_of(i)

        def go(direction, to):
            remote(ref(b), ref(b), sems.at[b, direction], rsem.at[b], to).start()

        @pl.when(other == 0)
        def _():
            go(2, ypeer)

            @pl.when((zz <= z) & (z < 3))
            def _():
                go(0, zup)

            @pl.when((zz >= z) & (z > 0))
            def _():
                go(1, zdown)

        if with_peer:
            remote(ref(b), ref(b), ms.at[b], mr.at[b], peer).start()

    def arrive(ref, sems, rsem, ms, mr, i):
        b, _, _ = block_of(i)
        remote(ref(b), ref(b), sems.at[b, 2], rsem.at[b], ypeer).wait_recv()
        spread(ref, sems, rsem, ms, mr, i, True)

    def drained(ref, sems, rsem, ms, mr, i, with_peer):
        b, zz, other = block_of(i)

        @pl.when(other == 0)
        def _():
            remote(ref(b), ref(b), sems.at[b, 2], rsem.at[b], ypeer).wait_send()

            @pl.when((zz <= z) & (z < 3))
            def _():
                remote(ref(b), ref(b), sems.at[b, 0], rsem.at[b], zup).wait_send()

            @pl.when((zz >= z) & (z > 0))
            def _():
                remote(ref(b), ref(b), sems.at[b, 1], rsem.at[b], zdown).wait_send()

        if with_peer:
            remote(ref(b), ref(b), ms.at[b], mr.at[b], peer).wait_send()

    xset = (px_ref, xas, xar, xms, xmr)
    dset = (ds_ref, das, dar, dms, dmr)

    inner = (z == 1) | (z == 2)

    def arrive_early(which):
        arrive(*which, 1)
        arrive(*which, 2)

        @pl.when(inner)
        def _():
            arrive(*which, 4)

    def arrive_at(which, i):
        @pl.when(i == 2)
        def _():
            arrive(*which, jnp.where(inner, 6, 4))

        @pl.when((i > 1) & (i < jnp.where(inner, 5, 6)))
        def _():
            there = jnp.where(i == 2, 3, jnp.where(i == 3, 6, jnp.where(i == 4, 5, 7)))
            here = jnp.where(i == 2, 3, jnp.where(i == 3, 5, 7))
            arrive(*which, jnp.where(inner, here, there))

    def halves_in(which, i):
        ref, _, _, ms, mr = which
        b, _, _ = block_of(i)
        remote(ref(b), ref(b), ms.at[b], mr.at[b], peer).wait_recv()

    def ring(e):
        t = lax.rem(e, 4)
        return jnp.where(t < 2, t + 1, t + 2), 1 + lax.rem(e, 2)

    mine128 = pl.ds(pl.multiple_of(d * 128, 128), 128)

    def lanes(i):
        return pl.ds(pl.multiple_of(i * 128, 128), 128)

    def hid_at(f):
        return slice(f * 256, f * 256 + 256)

    def gd_slice(b):
        page = b * 4 + lax.div(d, 4) * 2
        cols = pl.ds(pl.multiple_of(lax.rem(d, 4) * 128, 128), 128)
        return ryz[pl.ds(page, 2), :, cols].reshape(ROWS, 128).T

    def put_tb(f, at, v):
        tb[f * 256 + at.start : f * 256 + at.stop, 0:512] = v

    def frame_grad(chunk, left, right, first):
        at = acc_at(chunk)
        t = dot_nn(left, right)
        xm[at] = t if first else xm[at] + t

    def frame_grads_down(b, first):
        left = gd_slice(b)
        for f in range(4):
            frame_grad(f, left, tb[hid_at(f), 0:512], first)

    def frame_grads_up(b, bm_slot, bm_cols, first):
        left = bm[bm_slot, :, bm_cols].T
        for f in range(4):
            frame_grad(4 + f, left, uph[f * 8 + b], first)

    def frame_grads_attend(b, ga_slot, a_slot, a_cols, first):
        frame_grad(8, gd[ga_slot, :, :, :, mine128].reshape(ROWS, 128).T, ob[b], first)
        left = ab[a_slot, :, a_cols].T
        for c in range(3):
            frame_grad(9 + c, left, qk[b * 3 + c], first)

    @pl.when(frame)
    def _():
        pos = lax.broadcasted_iota(jnp.int32, (128, 128), 0)
        lane = lax.broadcasted_iota(jnp.int32, (128, 128), 1)
        freq = jnp.exp(lax.rem(lane, 32).astype(F32) * (-2.0 * math.log(rotary_base) / HEAD_DIM))
        angle = pos.astype(F32) * freq
        sine = jnp.sin(angle)
        for c, v in enumerate((jnp.cos(angle), jnp.where(lax.rem(lane, 64) < 32, -sine, sine))):
            for t in range(3):
                term = v.astype(BF)
                tabs[c, t] = term
                v = v - term.astype(F32)
        place = lax.broadcasted_iota(jnp.int32, (8, 128), 1)
        rows = []
        for mb in range(2):
            start = jnp.zeros((8, 128), jnp.int32)
            end = jnp.int32(0)
            for j in range(4):
                size = lens[mb, 0, j]
                end = end + size
                start = start + jnp.where(place >= end, size, 0)
            rows.append(start)
        which = lax.broadcasted_iota(jnp.int32, (8, 128), 0)
        st[d] = jnp.where(which == 0, rows[0], rows[1]).astype(F32)
        for t in range(1, 8):
            o = lax.rem(d + t, 8)
            remote(st.at[d], st.at[d], sts.at[t], strc.at[d], (s, o, m)).start()
        frame_tables(d)

        with jax.named_scope("embeds_wait"):
            for cp in e_local:
                cp.wait()
            for cp in e_far:
                cp.wait()

        gain0 = gains[0, 0:1]
        gain1 = gains[0, 1:2]

        def x_own(i):
            mb, mh, r = halves16(i)
            return em[0, mb, mh, r].astype(F32) + em[1, mb, mh, r].astype(F32) + em[2, mb, mh, r].astype(F32)

        def rows_in(i):
            v = x_own(i)
            xm[2, by16(i)] = v
            ab[0, by16(i)] = (v * rms(v) * gain0).astype(BF)
            put_px(d, i, v)

        with jax.named_scope("own_qkv"):
            loop(0, 16, rows_in, unroll=UNROLL)
            spread(*xset, 0, False)
            w_copies[0].wait()
            frame_qkv(0, d)
        with jax.named_scope("own_attend"):
            frame_attend(d)
        w_copies[1].wait()
        with jax.named_scope("own_out"):
            out_block(ob[d], 0, 0)
            w_copies[2].wait()
            exchange(0, 0, True).wait()

        def rows_mid(i):
            v = xm[2, by16(i)] + summed(0, 0, i)
            return v, (v * rms(v) * gain1).astype(BF)

        def put_mid(i, v, w):
            xm[2, by16(i)] = v
            bm[0, by16(i)] = w

        def put_own(f, at, u):
            uph[f * 8 + d, at] = u.astype(BF)
            put_tb(f, at, (0.5 * u * (1.0 + gelu_tanh(u))).astype(BF))

        with jax.named_scope("own_ff"):
            grouped(16, rows_mid, put_mid)
            up_block(bm[0], put_own)
            w_copies[3].wait()
            down_block(lambda f: tb[hid_at(f), 0:512], 3, 0)
            exchange(3, 0, False).wait()

        def rows_res(i):
            mb, r, row = own16(i, m)
            sr[mb, m, r] = (xm[2, row] + summed_own(3, 0, i)).astype(BF)

        loop(0, 8, rows_res, unroll=UNROLL)
        hop[0].start()

        for t in range(1, 8):
            o = lax.rem(d + t, 8)
            remote(st.at[d], st.at[o], sts.at[t], strc.at[o], (s, o, m)).wait()

        def others_in(i):
            b, _, _ = block_of(i)
            halves_in(xset, i)
            frame_tables(b)

            def rows_norm(t):
                v = px(b, t)
                ab[2, by16(t)] = (v * rms(v) * gain0).astype(BF)

            loop(0, 16, rows_norm, unroll=UNROLL)
            ab[1, :, lanes(i)] = ab[2, :, mine128]
            frame_qkv(2, b)
            frame_attend(b)
            out_block(ob[b], *ring(i))

        def others_ff(i):
            b, _, _ = block_of(i)
            recv_slot, send_slot = ring(i)
            exchange(recv_slot, send_slot, True).wait()
            drained(*xset, i, True)

            def rows_m(t):
                v = px(b, t) + summed(recv_slot, send_slot, t)
                return v, (v * rms(v) * gain1).astype(BF)

            def put_m(t, v, w):
                put_px(b, t, v)
                bm[2, by16(t)] = w

            grouped(16, rows_m, put_m)
            bm[1, :, lanes(i)] = bm[2, :, mine128]

            def put_up(f, at, u):
                uph[f * 8 + b, at] = u.astype(BF)

            up_block(bm[2], put_up)

        with jax.named_scope("oth_arrive"):
            arrive_early(xset)

        def others(i):
            with jax.named_scope("oth_arrive"):
                arrive_at(xset, i)

            @pl.when(i < 8)
            def _():
                with jax.named_scope("oth_in"):
                    others_in(i)

            @pl.when(i > 1)
            def _():
                with jax.named_scope("oth_ff"):
                    others_ff(i - 1)

        loop(1, 9, others)
        drained(*xset, 0, False)
        hop[0].wait_send()

        with jax.named_scope("help_start0"):
            help_start(0)

        with jax.named_scope("d_sent_wait"):
            for cp in hop2:
                cp.wait_recv()
            spread(*dset, 0, True)
            halves_in(dset, 0)
        with jax.named_scope("own_dff"):
            dff_block(ds_all(d), lambda f: f * 8 + d, put_tb, 0, 0)
            frame_grads_down(d, True)
        with jax.named_scope("help_pass0"):
            help_pass(0, 0)
        exchange(0, 0, True).wait()

        def rows_dmid(i):
            add, part = norm_back(xm[2, by16(i)], summed(0, 0, i), gain1)
            return ds_rows(d, i) + add, part

        def put_dmid(i, dm, part):
            mb, mh, r = halves16(i)
            xm[2, by16(i)] = dm
            gd[0, mb, mh, r] = dm.astype(BF)
            add_gain(1, part)

        with jax.named_scope("own_dmid"):
            grouped(16, rows_dmid, put_dmid)
            dob[0] = dot_nt(gd[0].reshape(ROWS, 1024), wo[...]).astype(BF)
        with jax.named_scope("arrive_early"):
            arrive_early(dset)
        frame_tables(d)
        with jax.named_scope("own_attend_back"):
            frame_attend_back(d, 0)
        dqkv_block(lambda c: d * 3 + c, 3, 0)
        with jax.named_scope("own_grads"):
            frame_grads_up(d, 0, mine128, True)
        exchange(3, 0, False).wait()

        def rows_dx(i):
            mb, r, row = own16(i, m)
            v = em[0, mb, m, r].astype(F32) + em[1, mb, m, r].astype(F32) + em[2, mb, m, r].astype(F32)
            add, part = norm_back(v, summed_own(3, 0, i), gain0)
            return xm[2, row] + add, part

        def put_dx(i, dv, part):
            mb, r, _ = own16(i, m)
            top = dv.astype(BF)
            em[0, mb, m, r] = top
            em[1, mb, m, r] = (dv - top.astype(F32)).astype(BF)
            add_gain(0, part)

        grouped(8, rows_dx, put_dx)
        gain_first()

        def rows_ge(i):
            mb, r, _ = own16(i, m)
            dv = em[0, mb, m, r].astype(F32) + em[1, mb, m, r].astype(F32)
            return tuple((em[c, mb, 1 - m, r].astype(F32) + dv).astype(BF) for c in range(3))

        def put_ge(i, *parts):
            mb, r, _ = own16(i, m)
            for c in range(3):
                em[c, mb, 1 - m, r] = parts[c]

        def embed_grads():
            for cp in dl_far:
                cp.wait_recv()
            grouped(8, rows_ge, put_ge)
            for cp in ge_local + ge_far:
                cp.start()

        gain_second()
        with jax.named_scope("help_pass0"):
            help_pass(0, 1)
        frame_grads_attend(d, 0, 0, mine128, True)

        def back_first(i):
            b, _, _ = block_of(i)
            halves_in(dset, i)
            dff_block(ds_all(b), lambda f: f * 8 + b, put_tb, *ring(i + 7))
            frame_grads_down(b, False)

        def back_second(i):
            b, _, _ = block_of(i)
            recv_slot, send_slot = ring(i + 7)
            exchange(recv_slot, send_slot, True).wait()

            def rows_dm(t):
                mb, mh, r = halves16(t)
                add, _ = norm_back(px(b, t), summed(recv_slot, send_slot, t), gain1)
                gd[1, mb, mh, r] = (ds_rows(b, t) + add).astype(BF)

            loop(0, 16, rows_dm, unroll=UNROLL)
            dob[0] = dot_nt(gd[1].reshape(ROWS, 1024), wo[...]).astype(BF)
            frame_tables(b)
            frame_attend_back(b, 0)
            frame_grads_up(b, 1, lanes(i), False)
            frame_grads_attend(b, 1, 1, lanes(i), False)

        def others_back(i):
            @pl.when(i < 8)
            def _():
                with jax.named_scope("oth_dff"):
                    back_first(i)

            with jax.named_scope("oth_arrive_d"):
                arrive_at(dset, i)

            @pl.when(i > 1)
            def _():
                with jax.named_scope("oth_rest"):
                    back_second(i - 1)

            @pl.when(i == 2)
            def _():
                with jax.named_scope("help_finish0"):
                    help_finish(0)

            @pl.when(i == 4)
            def _():
                with jax.named_scope("help_start1"):
                    help_start(1)

            @pl.when(i == 5)
            def _():
                with jax.named_scope("help_pass1"):
                    help_pass(1, 0)
                with jax.named_scope("embed_grads"):
                    embed_grads()

            @pl.when(i == 6)
            def _():
                with jax.named_scope("help_pass1"):
                    help_pass(1, 1)

            @pl.when(i == 7)
            def _():
                with jax.named_scope("help_finish1"):
                    help_finish(1)
        loop(1, 9, others_back)
        for h in range(HELPED):
            help_sent(h)
        loop(0, 8, lambda i: drained(*dset, i, True))
        for cp in grads_out:
            cp.start()
        gain_last()
        for cp in ge_local:
            cp.wait()
        for cp in ge_far:
            cp.wait_send()
        for cp in lo_far:
            cp.wait_recv()
        for cp in grads_out:
            cp.wait()

    def head_sum(prod):
        r0 = lax.broadcasted_iota(jnp.int32, (256, 256), 0)
        r1 = lax.broadcasted_iota(jnp.int32, (256, 256), 1)
        ones = (lax.div(r0, 64) == lax.div(r1, 64)).astype(BF)
        return dot_nn(prod.astype(BF), ones)

    def code_probs(q, k):
        probs = []
        for i in range(3):
            sc = [head_sum(q[i] * k[j]) * scale for j in range(i + 1)]
            top = functools.reduce(jnp.maximum, sc)
            e = [jnp.exp(v - top) for v in sc]
            inv = 1.0 / functools.reduce(jnp.add, e)
            probs.append([v * inv for v in e])
        return probs

    def code_part(i):
        return (pl.ds(pl.multiple_of(lax.div(i, 2) * 64, 64), 64), pl.ds(pl.multiple_of(lax.rem(i, 2) * 256, 256), 256))

    def code_attend(i):
        at, cols = code_part(i)
        q, k, v = ([qk[c * 3 + b, at, cols].astype(F32) for b in range(3)] for c in range(3))
        probs = code_probs(q, k)
        for t in range(3):
            o = functools.reduce(jnp.add, [probs[t][j].astype(BF).astype(F32) * v[j] for j in range(t + 1)])
            ob[t, at, cols] = o.astype(BF)

    def code_attend_back(i):
        at, cols = code_part(i)
        q, k, v = ([qk[c * 3 + b, at, cols].astype(F32) for b in range(3)] for c in range(3))
        do = [ob[3 + b, at, cols].astype(F32) for b in range(3)]
        probs = code_probs(q, k)
        dk = [0.0] * 3
        dv = [0.0] * 3
        for t in range(3):
            dp = [head_sum(do[t] * v[j]) for j in range(t + 1)]
            mean = functools.reduce(jnp.add, [dp[j] * probs[t][j] for j in range(t + 1)])
            dq = 0.0
            for j in range(t + 1):
                ds = (probs[t][j] * (dp[j] - mean)).astype(BF).astype(F32)
                dq = dq + ds * k[j]
                dk[j] = dk[j] + ds * q[t]
                dv[j] = dv[j] + probs[t][j].astype(BF).astype(F32) * do[t]
            qk[t, at, cols] = (dq * scale).astype(BF)
        for j in range(3):
            qk[3 + j, at, cols] = (dk[j] * scale).astype(BF)
            qk[6 + j, at, cols] = dv[j].astype(BF)

    def flip(get):
        def one(b):
            at = pl.ds(pl.multiple_of(b * 256, 256), 256)
            t = get(b)
            for g in range(4):
                tb[g * 256 : g * 256 + 256, at] = t[:, g * 256 : g * 256 + 256].T

        loop(0, 3, one)

    def ry(slot):
        return ryz.at[pl.ds(slot * 4, 4)]

    def rz(slot, idx):
        return SLOTS * 4 + slot * 5 + idx

    def sends(slot):
        return remote(rg.at[slot, :, 1 - y], ry(slot), ysn.at[slot], yrc.at[slot], ypeer)

    def right(slot, k):
        return remote(rg.at[slot, k, y], ryz.at[rz(slot, k + 1)], zrs.at[slot, k], zrr.at[slot, k], zup)

    def left(slot, k):
        return remote(rg.at[slot, k, y], ryz.at[rz(slot, k)], zls.at[slot, k], zlr.at[slot, k], zdown)

    def free_slot(slot, last=False):
        sends(slot).wait_send()
        for k in range(4):
            @pl.when((k > z) & ((z > 0) | (k < 2)) if last else k > z)
            def _():
                right(slot, k).wait_send()

            @pl.when((k < z) & ((z < 3) | (k > 1)) if last else k < z)
            def _():
                left(slot, k).wait_send()

    def make_chunk(i, act, send=True):
        slot = lax.rem(i, SLOTS)

        @pl.when(i >= SLOTS)
        def _():
            free_slot(slot)

        def part(k):
            at = pl.ds(pl.multiple_of(k * 256, 256), 256)
            rg[slot, k] = dot_nn(tb[at, :], act()).astype(BF).reshape(2, 128, 512)

        loop(0, 4, part)

        @pl.when(i >= SLOTS)
        def _():
            pl.semaphore_wait(ycr, 1)

        if send:
            sends(slot).start()

    def make_help(h, act):
        def part(k):
            at = pl.ds(pl.multiple_of(k * 256, 256), 256)
            uph[hg(h) + k] = dot_nn(tb[at, :], act()).astype(BF)

        loop(0, 4, part)
        help_a(h).start()
        help_b(h).start()

    def fg(h):
        return (28, 12)[h]

    def fz(h):
        return (10, 16)[h]

    def along_right(h, k):
        return remote(uph.at[fg(h) + k], qk.at[fz(h) + k + 1], frs.at[h, k], frr.at[h, k], zup)

    def along_left(h, k):
        return remote(uph.at[fg(h) + k], qk.at[fz(h) + k], fls.at[h, k], flr.at[h, k], zdown)

    def along_y(h):
        return remote(uph.at[fg(h) + z, pl.ds(pl.multiple_of((1 - y) * 128, 128), 128)],
                      qk.at[fz(h) + 5, 0:128], fys.at[h], fyr.at[h], ypeer)

    def make_along(h, act):
        def part(k):
            at = pl.ds(pl.multiple_of(k * 256, 256), 256)
            uph[fg(h) + k] = dot_nn(tb[at, :], act()).astype(BF)

            @pl.when((z == 0) & (k > 0))
            def _():
                along_right(h, k).start()

            @pl.when((z == 3) & (k < 3))
            def _():
                along_left(h, k).start()

        loop(0, 4, part)

    def add_half(to, page):
        for g in range(8):
            at = slice(g * 32, g * 32 + 32)
            uph[to, at] = (uph[to, at].astype(F32) + qk[page, at].astype(F32)).astype(BF)

    def along_pass(h, leg):
        def on_right(k):
            along_right(h, k).wait_recv()
            add_half(fg(h) + k, fz(h) + k + 1)
            along_right(h, k).start()

        def on_left(k):
            along_left(h, k).wait_recv()
            add_half(fg(h) + k, fz(h) + k)
            along_left(h, k).start()

        if leg == 0:
            @pl.when(z == 1)
            def _():
                on_right(3)
                on_right(2)

            @pl.when(z == 2)
            def _():
                on_left(0)
                on_left(1)
        else:
            @pl.when(z == 1)
            def _():
                on_left(0)

            @pl.when(z == 2)
            def _():
                on_right(3)

    def along_sum(h):
        @pl.when(z > 0)
        def _():
            along_right(h, z).wait_recv()
            add_half(fg(h) + z, fz(h) + z + 1)

        @pl.when(z < 3)
        def _():
            along_left(h, z).wait_recv()
            add_half(fg(h) + z, fz(h) + z)

        along_y(h).start()

    def along_finish(h, chunk):
        along_y(h).wait()
        rows = pl.ds(pl.multiple_of(y * 128, 128), 128)
        xm[acc_at(chunk)] = uph[fg(h) + z, rows].astype(F32) + qk[fz(h) + 5, 0:128].astype(F32)
        for k in range(4):
            @pl.when(k > z)
            def _():
                along_right(h, k).wait_send()

            @pl.when(k < z)
            def _():
                along_left(h, k).wait_send()

    def add_into(slot, k, page):
        for g in range(4):
            at = slice(g * 32, g * 32 + 32)
            rg[slot, k, y, at] = (rg[slot, k, y, at].astype(F32) + ryz[page, at].astype(F32)).astype(BF)

    def proc_y(i):
        slot = lax.rem(i, SLOTS)
        sends(slot).wait_recv()

        @pl.when(i >= SLOTS)
        def _():
            @pl.when(z < 3)
            def _():
                pl.semaphore_wait(rcr, 1)

            @pl.when(z > 0)
            def _():
                pl.semaphore_wait(lcr, 1)

        def up_first(t):
            k = 3 - t
            add_into(slot, k, slot * 4 + k)

            @pl.when((z == 0) & (k > 0))
            def _():
                right(slot, k).start()

                @pl.when((i == CHUNKS - 1) & (k > 1))
                def _():
                    right(slot, k).wait_send()

        def down_first(t):
            add_into(slot, t, slot * 4 + t)

            @pl.when((z == 3) & (t < 3))
            def _():
                left(slot, t).start()

                @pl.when((i == CHUNKS - 1) & (t < 2))
                def _():
                    left(slot, t).wait_send()

        @pl.when(z < 2)
        def _():
            loop(0, 4, up_first)

        @pl.when(z >= 2)
        def _():
            loop(0, 4, down_first)

        @pl.when(i + SLOTS < CHUNKS)
        def _():
            pl.semaphore_signal(ycr, 1, device_id=ypeer, device_id_type=MESH)

    def pass_right(slot, k):
        right(slot, k).wait_recv()
        add_into(slot, k, rz(slot, k + 1))
        right(slot, k).start()

    def pass_left(slot, k):
        left(slot, k).wait_recv()
        add_into(slot, k, rz(slot, k))
        left(slot, k).start()

    def fwd_z(i):
        slot = lax.rem(i, SLOTS)

        @pl.when(z == 1)
        def _():
            pass_right(slot, 3)
            pass_right(slot, 2)

        @pl.when(z == 2)
        def _():
            pass_left(slot, 0)
            pass_left(slot, 1)

    def fwd_z2(i):
        slot = lax.rem(i, SLOTS)

        @pl.when(z == 1)
        def _():
            pass_left(slot, 0)

        @pl.when(z == 2)
        def _():
            pass_right(slot, 3)

    def finish(i):
        slot = lax.rem(i, SLOTS)

        @pl.when(z > 0)
        def _():
            right(slot, z).wait_recv()
            add_into(slot, z, rz(slot, z + 1))

        @pl.when(z < 3)
        def _():
            left(slot, z).wait_recv()
            add_into(slot, z, rz(slot, z))

        total = rg[slot, z, y].astype(F32)

        xm[acc_at(jnp.where(i < 2, i + 2, i + 3))] = total

        @pl.when(i + SLOTS < CHUNKS)
        def _():
            @pl.when(z > 0)
            def _():
                pl.semaphore_signal(rcr, 1, device_id=zdown, device_id_type=MESH)

            @pl.when(z < 3)
            def _():
                pl.semaphore_signal(lcr, 1, device_id=zup, device_id_type=MESH)

    @pl.when(code)
    def _():
        for cp in c_local:
            cp.start()
        for cp in c_far:
            cp.start()
        for cp in e_local:
            cp.wait()
        for cp in e_far:
            cp.wait()
        gain0 = gains[0, 0:1]
        gain1 = gains[0, 1:2]
        for cp in c_local:
            cp.wait()
        for cp in c_far:
            cp.wait()
        flip(lambda b: gd[b].reshape(ROWS, 1024))
        with jax.named_scope("sent_wait"):
            hop[0].wait_recv()
            hop[1].start()
            hop[1].wait_recv()

        def rows_in(i):
            mb, mh, r = halves16(i)
            came = sr[mb, mh, r].astype(F32)
            for c in range(3):
                v = em[c, mb, mh, r].astype(F32) + came
                xm[c, by16(i)] = v
                ab[c, by16(i)] = (v * rms(v) * gain0).astype(BF)

        with jax.named_scope("code_norm"):
            loop(0, 16, rows_in, unroll=UNROLL)

        def qkv_all(b):
            for c in range(3):
                qk[c * 3 + b] = dot_nn(ab[b], wq[c]).astype(BF)

        w_copies[0].wait()
        with jax.named_scope("code_qkv"):
            loop(0, 3, qkv_all)
        with jax.named_scope("code_attend"):
            loop(0, 8, code_attend)
        w_copies[1].wait()
        with jax.named_scope("code_out"):
            loop(0, 3, lambda b: out_block(ob[b], b, b))
        w_copies[2].wait()
        w_copies[3].wait()

        def ff(b):
            exchange(b, b, True).wait()

            def rows_mid(i):
                v = xm[b, by16(i)] + summed(b, b, i)
                return v, (v * rms(v) * gain1).astype(BF)

            def put_mid(i, v, w):
                xm[b, by16(i)] = v
                bm[b, by16(i)] = w

            grouped(16, rows_mid, put_mid)

            def put(f, at, u):
                uph[f * 3 + b, at] = u.astype(BF)
                uph[12 + f * 3 + b, at] = (0.5 * u * (1.0 + gelu_tanh(u))).astype(BF)

            up_block(bm[b], put)
            down_block(lambda f: uph[12 + f * 3 + b], 3 + b, b)

        with jax.named_scope("code_ff"):
            loop(0, 3, ff)

        def res(b):
            exchange(3 + b, b, False).wait()

            def rows_res(i):
                mb, r, row = own16(i, m)
                em[b, mb, 1 - m, r] = (xm[b, row] + summed_own(3 + b, b, i)).astype(BF)

            loop(0, 8, rows_res, unroll=UNROLL)

        with jax.named_scope("code_grad_down"):
            make_chunk(0, lambda: uph[18:21].reshape(768, 512))
            make_along(0, lambda: uph[15:18].reshape(768, 512))
            make_help(0, lambda: uph[12:15].reshape(768, 512))
            make_chunk(1, lambda: uph[21:24].reshape(768, 512), False)
        loop(0, 3, res)
        for cp in lo_local:
            cp.start()

        def dff(b):
            dff_block(gd[b].reshape(ROWS, 1024), lambda f: f * 3 + b, None, b, b)

            @pl.when(b == 1)
            def _():
                sends(1).start()

        with jax.named_scope("code_dff"):
            loop(0, 3, dff)
        def dmid(b):
            exchange(b, b, True).wait()

            def rows_dmid(i):
                mb, mh, r = halves16(i)
                add, part = norm_back(xm[b, by16(i)], summed(b, b, i), gain1)
                return gd[b, mb, mh, r].astype(F32) + add, part

            def put_dmid(i, dm, part):
                mb, mh, r = halves16(i)
                xm[b, by16(i)] = dm
                gd[b, mb, mh, r] = dm.astype(BF)
                add_gain(1, part)

            grouped(16, rows_dmid, put_dmid)
            ob[3 + b] = dot_nt(gd[b].reshape(ROWS, 1024), wo[...]).astype(BF)

        with jax.named_scope("code_dmid"):
            loop(0, 3, dmid)
        with jax.named_scope("code_early"):
            proc_y(0)
            flip(lambda b: bm[b])
            make_chunk(2, lambda: uph[3:6].reshape(768, 512))
            along_pass(0, 0)
        with jax.named_scope("code_attend_back"):
            loop(0, 8, code_attend_back)
        with jax.named_scope("code_dqkv"):
            loop(0, 3, lambda b: dqkv_block(lambda c: c * 3 + b, 3 + b, b))

        def dx(b):
            exchange(3 + b, b, False).wait()

            def rows_dx(i):
                mb, r, row = own16(i, m)
                v = em[b, mb, m, r].astype(F32) + sr[mb, m, r].astype(F32)
                add, part = norm_back(v, summed_own(3 + b, b, i), gain0)
                return xm[b, row] + add, part

            def put_dx(i, dv, part):
                mb, r, row = own16(i, m)
                xm[b, row] = dv
                em[b, mb, m, r] = dv.astype(BF)
                add_gain(0, part)

            grouped(8, rows_dx, put_dx)

        with jax.named_scope("code_dx"):
            loop(0, 3, dx)
        hop[1].wait_send()

        def rows_ds(i):
            mb, r, row = own16(i, m)
            sr[mb, m, r] = (xm[0, row] + xm[1, row] + xm[2, row]).astype(BF)

        loop(0, 8, rows_ds, unroll=UNROLL)
        for cp in hop2:
            cp.start()
        gain_first()
        with jax.named_scope("code_y2"):
            make_chunk(3, lambda: uph[6:9].reshape(768, 512))
            proc_y(1)
            gain_second()
            along_pass(0, 1)
            fwd_z(0)

        def tail(i):
            @pl.when(i - 3 < CHUNKS)
            def _():
                with jax.named_scope("tail_z2"):
                    fwd_z2(i - 3)

            @pl.when(i > 3)
            def _():
                with jax.named_scope("tail_finish"):
                    finish(i - 4)

            @pl.when(i == 4)
            def _():
                make_chunk(i, lambda: uph[9:12].reshape(768, 512))
                for cp in hop2:
                    cp.wait_send()
                make_help(1, lambda: uph[0:3].reshape(768, 512))

            @pl.when(i == 5)
            def _():
                flip(lambda b: gd[b].reshape(ROWS, 1024))
                make_chunk(i, lambda: ob[0:3].reshape(768, 512))

            @pl.when(i == 6)
            def _():
                flip(lambda b: ab[b])

            @pl.when((i > 5) & (i < CHUNKS))
            def _():
                make_chunk(i, lambda: qk[pl.ds((i - 6) * 3, 3)].reshape(768, 512))

            @pl.when(i == 6)
            def _():
                for h in (0, 1):
                    help_a(h).wait_send()
                    help_b(h).wait_send()
                for cp in dl_far:
                    cp.start()

            @pl.when(i == 8)
            def _():
                for cp in dl_far:
                    cp.wait_send()
                for cp in lo_far:
                    cp.start()

            @pl.when(i - 1 < CHUNKS)
            def _():
                with jax.named_scope("tail_y"):
                    proc_y(i - 1)

            @pl.when(i - 2 < CHUNKS)
            def _():
                with jax.named_scope("tail_z"):
                    fwd_z(i - 2)

            with jax.named_scope("tail_along"):
                pl.when(i == 4)(lambda: along_sum(0))
                pl.when(i == 5)(lambda: along_finish(0, 1))

            for h in range(HELPED):
                @pl.when(i == 7 + h * 4)
                def _():
                    with jax.named_scope("helped"):
                        help_back(h).wait_recv()
                        xm[acc_at(h * 4)] = ryz[56 + h].astype(F32)
                        grads_out[h].start()

        loop(3, CHUNKS + 4, tail)
        grads_out[2].start()
        for cp in lo_local:
            cp.wait()
        for cp in lo_far:
            cp.wait_send()
        gain_last()
        for cp in ge_far:
            cp.wait_recv()
        for t in range(CHUNKS - SLOTS, CHUNKS):
            free_slot(t % SLOTS, t == CHUNKS - 1)
        for cp in grads_out:
            cp.wait()


def unpack(lo_i, ge_i, g_i, gg_i, lo_o, ge_o, gg_o, gq_o, go_o, gu_o, gd_o, lo, ge, g, gq, go, gu, gdn, sems):
    ins = [pltpu.make_async_copy(g_i.at[t], g.at[t], sems.at[t]) for t in range(3)]
    ins += [pltpu.make_async_copy(lo_i, lo, sems.at[3]), pltpu.make_async_copy(ge_i, ge, sems.at[4])]
    outs = [
        pltpu.make_async_copy(a, b, sems.at[5 + t])
        for t, (a, b) in enumerate(((gdn, gd_o), (gu, gu_o), (go, go_o), (gq, gq_o), (lo, lo_o), (ge, ge_o)))
    ]
    for cp in ins:
        cp.start()
    gg_o[...] = gg_i[...]

    def chunk(i):
        rows, cols = (i % 4) // 2 * 128, i % 2 * 512
        return g[i // 4, rows : rows + 128, cols : cols + 512]

    ins[0].wait()
    for f in range(4):
        gdn[f * 512 : f * 512 + 512] = chunk(f).T
    outs[0].start()
    ins[1].wait()
    for f in range(4):
        gu[:, f * 512 : f * 512 + 512] = chunk(4 + f)
    outs[1].start()
    ins[2].wait()
    go[...] = chunk(8).T
    outs[2].start()
    for c in range(3):
        gq[c] = chunk(9 + c)
    outs[3].start()
    for t in range(2):
        ins[3 + t].wait()
        outs[4 + t].start()
    for cp in outs:
        cp.wait()


def on_device_kernel(embeds, lengths, norm_gains, w_qkv, w_out, w_up, w_down, cotangent):
    anyspec = pl.BlockSpec(memory_space=pl.ANY)
    hbm = pl.BlockSpec(memory_space=pltpu.HBM)
    vm = pl.BlockSpec(memory_space=pltpu.VMEM)
    sd = jax.ShapeDtypeStruct
    V = pltpu.VMEM
    D = pltpu.SemaphoreType.DMA
    R = pltpu.SemaphoreType.REGULAR
    full = (2, 2, 64, 1024)
    scratch = [
        V((3, 1024, 512), BF), V((512, 1024), BF), V((1024, 2048), BF), V((2048, 1024), BF),
        V((3,) + full, BF), V((3,) + full, BF), V(full, BF),
        V((3, ROWS, 1024), F32), V((3, ROWS, 1024), BF), V((3, ROWS, 1024), BF),
        V((24, ROWS, 512), BF), V((8, ROWS, 512), BF), V((1, ROWS, 512), BF), V((32, ROWS, 512), BF),
        V((3,) + full, BF), V((6,) + full, BF), V((1024, 768), BF),
        V((3, ROWS, 128), F32), V((2, 3, 128, 128), BF), V((8, 8, 128), F32),
        V((2, 8, 1024), F32), V((8, 8, 1024), F32), V((2, 8, 1024), F32),
        V((SLOTS, 4, 2, 128, 512), BF), V((32 + HELPED * 13, 128, 512), BF),
        D((3,)), D((4,)), D((3,)), D((3,)), D((3,)), D((3,)), D((3,)), D((3,)), D((3,)), D((6,)), D((4,)), D((4,)),
        D((3,)), D((3,)), D((3,)), D((3,)), D((3,)),
        D((3,)), D((3,)), D((3,)), D((8,)), D((8,)), D, D,
        D((SLOTS,)), D((SLOTS,)), D((SLOTS, 4)), D((SLOTS, 4)), D((SLOTS, 4)), D((SLOTS, 4)),
        D((ALONG, 4)), D((ALONG, 4)), D((ALONG, 4)), D((ALONG, 4)), D((ALONG,)), D((ALONG,)),
        D((HELPED,)), D((HELPED,)), D((HELPED,)), D((HELPED,)), D((HELPED, 4)), D((HELPED, 4)), D((HELPED, 4)), D((HELPED, 4)),
        D((HELPED,)), D((HELPED,)), D((8,)), D((8,)), D((8, 3)), D((8,)), D((8,)), D((8,)), D((8, 3)), D((8,)), D((8,)), D((8,)),
        R, R, R,
    ]
    rows, gain = sd((2, 3, 64, 1024), BF), sd((1, 2, 1024), F32)
    grads = (sd((3, 128, 512), F32), sd((512, 128), F32), sd((128, 2048), F32), sd((2048, 128), F32))
    outs = pl.pallas_call(
        body,
        out_shape=(rows, rows, sd((3, ROWS, 1024), F32), gain),
        in_specs=[anyspec, anyspec, pl.BlockSpec(memory_space=pltpu.SMEM), vm, anyspec, anyspec, anyspec, anyspec],
        out_specs=(anyspec, anyspec, anyspec, vm),
        scratch_shapes=scratch,
        compiler_params=pltpu.CompilerParams(
            collective_id=0, has_side_effects=True, vmem_limit_bytes=61 * 2**20 - 2**19
        ),
        name="two_sections",
    )(
        jnp.transpose(embeds, (0, 2, 1, 3)), jnp.transpose(cotangent, (0, 2, 1, 3)), lengths, norm_gains,
        jnp.transpose(w_qkv[0], (1, 0, 2)), w_out[0], w_up[0], w_down[0],
    )
    outs = pl.pallas_call(
        unpack,
        out_shape=(rows, rows, gain) + grads,
        in_specs=[hbm] * 3 + [vm],
        out_specs=(hbm, hbm, vm) + (hbm,) * 4,
        scratch_shapes=[V(rows.shape, BF), V(rows.shape, BF), V((3, ROWS, 1024), F32)]
        + [V(g.shape, F32) for g in (grads[0], grads[1], grads[2], grads[3])] + [D((11,))],
        compiler_params=pltpu.CompilerParams(vmem_limit_bytes=60 * 2**20),
        name="results",
    )(*outs)
    lo, ge, gg, gq, go, gu, gdn = outs
    return (
        jnp.transpose(lo, (0, 2, 1, 3)), jnp.transpose(ge, (0, 2, 1, 3)), gg,
        jnp.transpose(gq, (1, 0, 2))[None], go[None], gu[None], gdn[None],
    )


def solution(mesh):
    fits = tuple(mesh.shape[name] for name in ("section", "dp", "mp")) == (2, 8, 2)
    return jax.shard_map(
        on_device_kernel if fits else on_device,
        mesh=mesh,
        in_specs=(
            P(None, ("dp", "mp"), None, None),
            P(None, "dp", None),
            P("section", None, None),
            P("section", None, None, "mp"),
            P("section", "mp", None),
            P("section", None, "mp"),
            P("section", "mp", None),
            P(None, ("dp", "mp"), None, None),
        ),
        out_specs=(
            P(None, ("dp", "mp"), None, None),
            P(None, ("dp", "mp"), None, None),
            P("section", None, None),
            P("section", "dp", None, "mp"),
            P("section", "mp", "dp"),
            P("section", "dp", "mp"),
            P("section", "mp", "dp"),
        ),
        check_vma=False,
    )
```

```python
import functools
import math

import jax
import jax.numpy as jnp
from jax import lax
from jax.experimental import pallas as pl
from jax.experimental.pallas import tpu as pltpu
from jax.sharding import PartitionSpec as P

HEAD_DIM = 64


norm_eps = 1e-05
masked_fill = -1e30
rotary_base = 10000.0


def passed_along(value, axis, steps):
    count = lax.axis_size(axis)
    leading, last = (max(0, -steps), min(count, count - steps))
    return lax.ppermute(value, axis, [(source, source + steps) for source in range(leading, last)])


def rms_scale(values, gain_row):
    return (
        values * lax.rsqrt(jnp.mean(values * values, axis=-1, keepdims=True) + norm_eps) * gain_row
    )


def rotate(values, cos_tab, sin_tab):
    half_dim = values.shape[-1] // 2
    first_half = values[..., :half_dim]
    second_half = values[..., half_dim:]
    cos_rows = cos_tab[:, None, :]
    sin_rows = sin_tab[:, None, :]
    return jnp.concatenate(
        [
            first_half * cos_rows - second_half * sin_rows,
            second_half * cos_rows + first_half * sin_rows,
        ],
        axis=-1,
    )


def global_context(length_row, frames):
    doc_ends = jnp.cumsum(length_row)
    places = jnp.arange(frames, dtype=jnp.int32)
    passed = (places[:, None] >= doc_ends[None, :]).astype(jnp.int32)
    segment = jnp.sum(passed, axis=1)
    offsets = places - jnp.sum(passed * length_row[None, :], axis=1)
    allowed = (segment[:, None] == segment[None, :]) & (places[None, :] <= places[:, None])
    half_dim = HEAD_DIM // 2
    frequency = jnp.exp(
        jnp.arange(half_dim, dtype=jnp.float32) * (-2.0 * math.log(rotary_base) / HEAD_DIM)
    )
    angles = offsets.astype(jnp.float32)[:, None] * frequency[None, :]
    return (allowed, jnp.cos(angles), jnp.sin(angles))


def global_attend(projected, context):
    allowed, cos_tab, sin_tab = context
    attn_scale = 1.0 / math.sqrt(HEAD_DIM)
    row_total, _, local_width = projected.shape
    head_count = local_width // HEAD_DIM
    query_rows = rotate(
        projected[:, 0].reshape(row_total, head_count, HEAD_DIM), cos_tab, sin_tab
    ).astype(jnp.bfloat16)
    key_rows = rotate(
        projected[:, 1].reshape(row_total, head_count, HEAD_DIM), cos_tab, sin_tab
    ).astype(jnp.bfloat16)
    value_rows = projected[:, 2].reshape(row_total, head_count, HEAD_DIM).astype(jnp.bfloat16)
    scores = (
        jnp.einsum("qhd,khd->hqk", query_rows, key_rows, preferred_element_type=jnp.float32)
        * attn_scale
    )
    scores = jnp.where(allowed[None], scores, masked_fill)
    score_peak = jnp.max(scores, axis=-1, keepdims=True)
    exp_scores = jnp.exp(scores - score_peak)
    row_sums = jnp.sum(exp_scores, axis=-1, keepdims=True)
    weights_low = (exp_scores / row_sums).astype(jnp.bfloat16)
    mixed_rows = jnp.einsum(
        "hqk,khd->qhd", weights_low, value_rows, preferred_element_type=jnp.float32
    )
    log_total = score_peak + jnp.log(row_sums)
    return (
        mixed_rows.reshape(row_total, local_width).astype(jnp.bfloat16),
        (query_rows, key_rows, value_rows, log_total),
    )


def global_attend_back(attn_saved, context, grad_mixed):
    query_rows, key_rows, value_rows, log_total = attn_saved
    allowed, cos_tab, sin_tab = context
    attn_scale = 1.0 / math.sqrt(HEAD_DIM)
    row_total, head_count, _ = query_rows.shape
    grad_heads = grad_mixed.reshape(row_total, head_count, HEAD_DIM)
    scores = (
        jnp.einsum("qhd,khd->hqk", query_rows, key_rows, preferred_element_type=jnp.float32)
        * attn_scale
    )
    prob_rows = jnp.where(allowed[None], jnp.exp(scores - log_total), 0.0)
    grad_values = jnp.einsum(
        "hqk,qhd->khd",
        prob_rows.astype(jnp.bfloat16),
        grad_heads,
        preferred_element_type=jnp.float32,
    )
    grad_probs = jnp.einsum(
        "qhd,khd->hqk", grad_heads, value_rows, preferred_element_type=jnp.float32
    )
    grad_scores = (
        prob_rows * (grad_probs - jnp.sum(grad_probs * prob_rows, axis=-1, keepdims=True))
    ).astype(jnp.bfloat16)
    grad_query = (
        jnp.einsum("hqk,khd->qhd", grad_scores, key_rows, preferred_element_type=jnp.float32)
        * attn_scale
    )
    grad_keys = (
        jnp.einsum("hqk,qhd->khd", grad_scores, query_rows, preferred_element_type=jnp.float32)
        * attn_scale
    )
    grad_query = rotate(grad_query, cos_tab, -sin_tab)
    grad_keys = rotate(grad_keys, cos_tab, -sin_tab)
    stacked = jnp.stack([grad_query, grad_keys, grad_values], axis=1)
    return stacked.reshape(row_total, 3, head_count * HEAD_DIM).astype(jnp.bfloat16)


def local_attend(projected, context):
    attn_scale = 1.0 / math.sqrt(HEAD_DIM)
    row_total, _, local_width = projected.shape
    head_count = local_width // HEAD_DIM
    frames = row_total // 3
    qkv_parts = projected.reshape(frames, 3, 3, head_count, HEAD_DIM).astype(jnp.bfloat16)
    query_rows = qkv_parts[:, :, 0]
    key_rows = qkv_parts[:, :, 1]
    value_rows = qkv_parts[:, :, 2]
    scores = (
        jnp.einsum("fihd,fjhd->fhij", query_rows, key_rows, preferred_element_type=jnp.float32)
        * attn_scale
    )
    scores = jnp.where(context[None, None], scores, masked_fill)
    score_peak = jnp.max(scores, axis=-1, keepdims=True)
    exp_scores = jnp.exp(scores - score_peak)
    row_sums = jnp.sum(exp_scores, axis=-1, keepdims=True)
    weights_low = (exp_scores / row_sums).astype(jnp.bfloat16)
    mixed_rows = jnp.einsum(
        "fhij,fjhd->fihd", weights_low, value_rows, preferred_element_type=jnp.float32
    )
    log_total = score_peak + jnp.log(row_sums)
    return (
        mixed_rows.reshape(row_total, local_width).astype(jnp.bfloat16),
        (query_rows, key_rows, value_rows, log_total),
    )


def local_attend_back(attn_saved, context, grad_mixed):
    query_rows, key_rows, value_rows, log_total = attn_saved
    attn_scale = 1.0 / math.sqrt(HEAD_DIM)
    frames, _, head_count, _ = query_rows.shape
    grad_heads = grad_mixed.reshape(frames, 3, head_count, HEAD_DIM)
    scores = (
        jnp.einsum("fihd,fjhd->fhij", query_rows, key_rows, preferred_element_type=jnp.float32)
        * attn_scale
    )
    prob_rows = jnp.where(context[None, None], jnp.exp(scores - log_total), 0.0)
    grad_values = jnp.einsum(
        "fhij,fihd->fjhd",
        prob_rows.astype(jnp.bfloat16),
        grad_heads,
        preferred_element_type=jnp.float32,
    )
    grad_probs = jnp.einsum(
        "fihd,fjhd->fhij", grad_heads, value_rows, preferred_element_type=jnp.float32
    )
    grad_scores = (
        prob_rows * (grad_probs - jnp.sum(grad_probs * prob_rows, axis=-1, keepdims=True))
    ).astype(jnp.bfloat16)
    grad_query = (
        jnp.einsum("fhij,fjhd->fihd", grad_scores, key_rows, preferred_element_type=jnp.float32)
        * attn_scale
    )
    grad_keys = (
        jnp.einsum("fhij,fihd->fjhd", grad_scores, query_rows, preferred_element_type=jnp.float32)
        * attn_scale
    )
    stacked = jnp.stack([grad_query, grad_keys, grad_values], axis=2)
    return stacked.reshape(frames * 3, 3, head_count * HEAD_DIM).astype(jnp.bfloat16)


def gather_project(normed, weight, form):
    piece_rows = lax.all_gather(normed, "mp", axis=0, tiled=True)
    return (piece_rows, jnp.einsum(form, piece_rows, weight, preferred_element_type=jnp.float32))


def reduce_rows(left, weight, form, row_count):

    def partial_term(first_row, count_rows):
        return jnp.einsum(form, left, weight, preferred_element_type=jnp.float32)

    return lax.psum_scatter(
        partial_term(jnp.int32(0), row_count * lax.axis_size("mp")),
        "mp",
        scatter_dimension=0,
        tiled=True,
    )


def reduce_grads(left, weight, form, row_count):

    def partial_term(first_row, count_rows):
        return jnp.einsum(form, left, weight, preferred_element_type=jnp.float32)

    return lax.psum_scatter(
        partial_term(jnp.int32(0), row_count * lax.axis_size("mp")),
        "mp",
        scatter_dimension=0,
        tiled=True,
    )


def gather_grads(grad_low):
    return lax.all_gather(grad_low, "mp", axis=0, tiled=True)


def layer_forward(frame_rows, weights, attend, context):
    gain_pair, w_qkv, w_out, w_up, w_down = weights
    row_count = frame_rows.shape[0]
    normed = rms_scale(frame_rows, gain_pair[0]).astype(jnp.bfloat16)
    normed_all, projected = gather_project(normed, w_qkv, "nd,dce->nce")
    mixed_rows, attn_saved = attend(projected, context)
    attn_rows = reduce_rows(mixed_rows, w_out, "ne,ed->nd", row_count)
    middle = frame_rows + attn_rows
    normed_mid = rms_scale(middle, gain_pair[1]).astype(jnp.bfloat16)
    normed_mid_all, up_all = gather_project(normed_mid, w_up, "nd,de->ne")
    hidden = jax.nn.gelu(up_all).astype(jnp.bfloat16)
    down_rows = reduce_rows(hidden, w_down, "nf,fd->nd", row_count)
    record = (normed_all, attn_saved, mixed_rows, middle, normed_mid_all, up_all, hidden)
    return (middle + down_rows, attn_rows + down_rows, record)


def layer_backward(frame_rows, weights, attend_back, context, record, grad_result):
    gain_pair, w_qkv, w_out, w_up, w_down = weights
    normed_all, attn_saved, mixed_rows, middle, normed_mid_all, up_all, hidden = record
    row_count = frame_rows.shape[0]
    grad_down_all = gather_grads(grad_result.astype(jnp.bfloat16))
    grad_w_down = jnp.einsum("nf,nd->fd", hidden, grad_down_all, preferred_element_type=jnp.float32)
    grad_hidden = jnp.einsum("nd,fd->nf", grad_down_all, w_down, preferred_element_type=jnp.float32)
    _, gelu_back = jax.vjp(jax.nn.gelu, up_all)
    grad_up = gelu_back(grad_hidden)[0].astype(jnp.bfloat16)
    grad_w_up = jnp.einsum("nd,ne->de", normed_mid_all, grad_up, preferred_element_type=jnp.float32)
    grad_normed_mid = reduce_grads(grad_up, w_up, "ne,de->nd", row_count)
    _, mid_back = jax.vjp(rms_scale, middle, gain_pair[1])
    grad_middle_part, grad_gain_mid = mid_back(grad_normed_mid)
    grad_middle = grad_result + grad_middle_part
    grad_attn_all = gather_grads(grad_middle.astype(jnp.bfloat16))
    grad_w_out = jnp.einsum(
        "ne,nd->ed", mixed_rows, grad_attn_all, preferred_element_type=jnp.float32
    )
    grad_mixed = jnp.einsum(
        "nd,ed->ne", grad_attn_all, w_out, preferred_element_type=jnp.float32
    ).astype(jnp.bfloat16)
    grad_projected = attend_back(attn_saved, context, grad_mixed)
    grad_w_qkv = jnp.einsum(
        "nd,nce->dce", normed_all, grad_projected, preferred_element_type=jnp.float32
    )
    grad_normed = reduce_grads(grad_projected, w_qkv, "nce,dce->nd", row_count)
    _, first_back = jax.vjp(rms_scale, frame_rows, gain_pair[0])
    grad_rows_part, grad_gain_first = first_back(grad_normed)
    grad_frame_rows = grad_middle + grad_rows_part
    layer_grads = (
        jnp.stack([grad_gain_first, grad_gain_mid]),
        grad_w_qkv,
        grad_w_out,
        grad_w_up,
        grad_w_down,
    )
    return (grad_frame_rows, layer_grads)


def on_device(embeds, lengths, norm_gains, w_qkv, w_out, w_up, w_down, cotangent):
    weights = (norm_gains[0], w_qkv[0], w_out[0], w_up[0], w_down[0])
    micro_count = embeds.shape[0]
    shard_rows = embeds.shape[1]
    width = embeds.shape[-1]
    frames = shard_rows * lax.axis_size("mp")
    is_first = lax.axis_index("section") == 0
    local_allowed = jnp.tril(jnp.ones((3, 3), dtype=jnp.bool_))
    gain_total = jnp.zeros(norm_gains.shape[1:], jnp.float32)
    weight_totals = tuple((jnp.zeros(weight.shape, jnp.float32) for weight in weights[1:]))
    totals = (gain_total,) + weight_totals
    y_part = jnp.zeros(embeds.shape, jnp.float32)
    e_part = jnp.zeros(embeds.shape, jnp.float32)
    zero_send = jnp.zeros((shard_rows, width), jnp.bfloat16)

    def add_grads(running, layer_grads):
        run_gain, run_qkv, run_out, run_up, run_down = running
        part_gain, part_qkv, part_out, part_up, part_down = layer_grads
        return (
            run_gain + part_gain,
            run_qkv + part_qkv,
            run_out + part_out,
            run_up + part_up,
            run_down + part_down,
        )

    def global_forward(micro_index):
        context = global_context(lengths[micro_index, 0], frames)
        frame_in = jnp.sum(embeds[micro_index].astype(jnp.float32), axis=1)
        result, _, record = layer_forward(frame_in, weights, global_attend, context)
        return (frame_in, context, result, record)

    def pick(first_value, second_value):
        return jnp.where(is_first, first_value, second_value)

    carry_state = (totals, y_part, e_part)
    forward_recv = zero_send
    backward_recv = zero_send
    for tick_index in range(micro_count + 2):

        def first_section(state_in):
            running, y_state, e_state = state_in
            send_fwd = zero_send
            if tick_index < micro_count:
                _, _, result, _ = global_forward(tick_index)
                send_fwd = result.astype(jnp.bfloat16)
                joined = (
                    embeds[tick_index].astype(jnp.float32)
                    + send_fwd.astype(jnp.float32)[:, None, :]
                )
                y_state = y_state.at[tick_index].set(joined)
            if tick_index >= 2:
                micro_index = tick_index - 2
                frame_in, context, _, record = global_forward(micro_index)
                grad_frame, layer_grads = layer_backward(
                    frame_in,
                    weights,
                    global_attend_back,
                    context,
                    record,
                    backward_recv.astype(jnp.float32),
                )
                running = add_grads(running, layer_grads)
                e_state = e_state.at[micro_index].set(
                    jnp.broadcast_to(grad_frame[:, None, :], e_state.shape[1:])
                )
            return ((running, y_state, e_state), send_fwd, zero_send)

        def second_section(state_in):
            running, y_state, e_state = state_in
            send_back = zero_send
            if 1 <= tick_index <= micro_count:
                micro_index = tick_index - 1
                local_in = (
                    embeds[micro_index].astype(jnp.float32)
                    + forward_recv.astype(jnp.float32)[:, None, :]
                )
                local_in = local_in.reshape(shard_rows * 3, width)
                _, branches, record = layer_forward(local_in, weights, local_attend, local_allowed)
                grad_seed = (
                    cotangent[micro_index].astype(jnp.float32).reshape(shard_rows * 3, width)
                )
                grad_local, layer_grads = layer_backward(
                    local_in, weights, local_attend_back, local_allowed, record, grad_seed
                )
                running = add_grads(running, layer_grads)
                y_state = y_state.at[micro_index].set(branches.reshape(shard_rows, 3, width))
                grad_frames = grad_local.reshape(shard_rows, 3, width)
                e_state = e_state.at[micro_index].set(grad_frames)
                send_back = jnp.sum(grad_frames, axis=1).astype(jnp.bfloat16)
            return ((running, y_state, e_state), zero_send, send_back)

        first_result = first_section(carry_state)
        second_result = second_section(carry_state)
        carry_state, send_fwd, send_back = jax.tree.map(pick, first_result, second_result)
        if tick_index < micro_count:
            forward_recv = passed_along(send_fwd, "section", 1)
        if 1 <= tick_index <= micro_count:
            backward_recv = passed_along(send_back, "section", -1)
    totals, y_part, e_part = carry_state
    gain_total, grad_qkv, grad_out, grad_up, grad_down = totals
    grad_qkv, grad_out, grad_up, grad_down = (
        lax.psum_scatter(grad_qkv, "dp", scatter_dimension=0, tiled=True),
        lax.psum_scatter(grad_out, "dp", scatter_dimension=1, tiled=True),
        lax.psum_scatter(grad_up, "dp", scatter_dimension=0, tiled=True),
        lax.psum_scatter(grad_down, "dp", scatter_dimension=1, tiled=True),
    )
    gain_total = lax.psum(gain_total, ("dp", "mp"))
    y_sum, e_sum = (
        lax.psum(y_part.astype(jnp.bfloat16), "section").astype(jnp.float32),
        lax.psum(e_part.astype(jnp.bfloat16), "section").astype(jnp.float32),
    )
    return (
        y_sum.astype(jnp.bfloat16),
        e_sum.astype(jnp.bfloat16),
        gain_total[None],
        grad_qkv[None],
        grad_out[None],
        grad_up[None],
        grad_down[None],
    )


BF = jnp.bfloat16
F32 = jnp.float32
MESH = pl.DeviceIdType.MESH
SLOTS = 5
CHUNKS = 9
HELPED = 2
ALONG = 1
ROWS = 256
UNROLL = 4


def dot_nn(left, right):
    return lax.dot_general(left, right, (((1,), (0,)), ((), ())), preferred_element_type=F32)


def dot_nt(left, right):
    return lax.dot_general(left, right, (((1,), (1,)), ((), ())), preferred_element_type=F32)


def dot_tn(left, right):
    return lax.dot_general(left, right, (((0,), (0,)), ((), ())), preferred_element_type=F32)


def gelu_tanh(u):
    c0 = math.sqrt(2.0 / math.pi)
    return jnp.tanh(u * (c0 + (c0 * 0.044715) * (u * u)))


def gelu_slope(u, th):
    c0 = math.sqrt(2.0 / math.pi)
    return 0.5 * (1.0 + th) + 0.5 * u * (1.0 - th * th) * (c0 + (3.0 * 0.044715 * c0) * (u * u))


def loop(lower, upper, step, unroll=1):
    def wrapped(i, carry):
        step(i)
        return carry

    lax.fori_loop(lower, upper, wrapped, 0, unroll=unroll)


def grouped(count, work, store, size=4):
    def group(g):
        done = [work(g * size + t) for t in range(size)]
        for t in range(size):
            store(g * size + t, *done[t])

    loop(0, count // size, group)


def by16(i):
    return pl.ds(pl.multiple_of(i * 16, 16), 16)


def by512(i):
    return pl.ds(pl.multiple_of(i * 512, 512), 512)


def halves16(i):
    return lax.div(i, 8), lax.rem(lax.div(i, 4), 2), pl.ds(pl.multiple_of(lax.rem(i, 4) * 16, 16), 16)


def own16(i, m):
    mb, r = lax.div(i, 4), pl.multiple_of(lax.rem(i, 4) * 16, 16)
    return mb, pl.ds(r, 16), pl.ds(pl.multiple_of(mb * 128 + m * 64 + r, 16), 16)


def swap_halves(v):
    lane = lax.broadcasted_iota(jnp.int32, v.shape, 1)
    return jnp.where(lax.rem(lane, 64) < 32, pltpu.roll(v, 96, 1), pltpu.roll(v, 32, 1))


def body(
    emb, cot, lens, gains, wq_h, wo_h, wu_h, wd_h,
    lo_h, ge_h, g_h, gg_o,
    wq, wo, wu, wd, em, gd, sr, xm, ab, bm, qk, ob, dob, uph, xs, xr, tb,
    cs, tabs, st, gga, ggr, gpart, rg, ryz,
    gsem, wsem, esem, exs, exr, csem, cxs, cxr, mps, mpr, hops, hopr, lol, los, lor, dls, dlr,
    gel, ges, ger, ggs, ggrs, gms, gmr, ysn, yrc, zrs, zrr, zls, zlr,
    lys, lyr, frs, frr, fls, flr, fys, fyr, has, har, hbs, hbr, hzrs, hzrr, hzls, hzlr, hres, hrer, sts, strc, xas, xar, xms, xmr, das, dar, dms, dmr, ycr, rcr, lcr,
):
    s = lax.axis_index("section")
    d = lax.axis_index("dp")
    m = lax.axis_index("mp")
    y = lax.rem(d, 2)
    z = lax.div(d, 2)
    peer = (s, d, 1 - m)
    across = (1 - s, d, m)
    ypeer = (s, d + 1 - 2 * y, m)
    zup = (s, jnp.minimum(d + 2, 7), m)
    zdown = (s, jnp.maximum(d - 2, 0), m)
    frame = s == 0
    code = s == 1
    scale = 1.0 / math.sqrt(HEAD_DIM)

    def remote(src, dst, ssem, rsem, to):
        return pltpu.make_async_remote_copy(
            src_ref=src, dst_ref=dst, send_sem=ssem, recv_sem=rsem, device_id=to, device_id_type=MESH
        )

    def local(src, dst, sem):
        return pltpu.make_async_copy(src, dst, sem)

    w_copies = [local(a, b, wsem.at[i]) for i, (a, b) in enumerate(((wq_h, wq), (wo_h, wo), (wu_h, wu), (wd_h, wd)))]
    e_local = [local(emb.at[:, c], em.at[c, :, m], esem.at[c]) for c in range(3)]
    c_local = [local(cot.at[:, c], gd.at[c, :, m], csem.at[c]) for c in range(3)]
    for cp in e_local:
        cp.start()
    w_copies[0].start()

    bar = pltpu.get_barrier_semaphore()
    pl.semaphore_signal(bar, 1, device_id=peer, device_id_type=MESH)
    pl.semaphore_signal(bar, 1, device_id=across, device_id_type=MESH)
    for t in range(1, 8):
        pl.semaphore_signal(bar, 1, device_id=(s, lax.rem(d + t, 8), m), device_id_type=MESH)
    with jax.named_scope("barrier"):
        pl.semaphore_wait(bar, 9)

    e_far = [remote(emb.at[:, c], em.at[c, :, m], exs.at[c], exr.at[c], peer) for c in range(3)]
    c_far = [remote(cot.at[:, c], gd.at[c, :, m], cxs.at[c], cxr.at[c], peer) for c in range(3)]
    for cp in e_far:
        cp.start()
    for cp in w_copies[1:]:
        cp.start()

    hop = [remote(sr.at[:, m], sr.at[:, m], hops.at[0], hopr.at[0], across),
           remote(sr.at[:, m], sr.at[:, m], hops.at[1], hopr.at[1], peer)]
    hop2 = [
        remote(sr.at[:, m, :, c * 512 : c * 512 + 512],
               ryz.at[pl.ds(d * 4 + c * 2, 2), pl.ds(pl.multiple_of(m * 64, 64), 64)],
               hops.at[2 + c], hopr.at[2 + c], across)
        for c in range(2)
    ]
    lo_local = [local(em.at[c, :, 1 - m], lo_h.at[:, c], lol.at[c]) for c in range(3)]
    lo_far = [remote(em.at[c, :, 1 - m], lo_h.at[:, c], los.at[c], lor.at[c], across) for c in range(3)]
    dl_far = [remote(em.at[c, :, m], em.at[c, :, 1 - m], dls.at[c], dlr.at[c], across) for c in range(3)]
    ge_local = [local(em.at[c, :, 1 - m], ge_h.at[:, c], gel.at[c]) for c in range(3)]
    ge_far = [remote(em.at[c, :, 1 - m], ge_h.at[:, c], ges.at[c], ger.at[c], across) for c in range(3)]

    grads_out = [local(xm.at[t], g_h.at[t], gsem.at[t]) for t in range(3)]
    gga[...] = jnp.zeros_like(gga)

    def rms(v):
        return lax.rsqrt(jnp.mean(v * v, axis=-1, keepdims=True) + norm_eps)

    def exchange(recv_slot, send_slot, whole):
        mine = slice(None) if whole else 1 - m
        return remote(xs.at[send_slot, :, mine], xr.at[recv_slot, :, mine], mps.at[send_slot], mpr.at[recv_slot], peer)

    def put_xs(slot, cols, t):
        xs[slot, :, :, :, cols] = t.astype(BF).reshape(2, 2, 64, t.shape[-1])

    def summed(recv_slot, send_slot, i):
        mb, mh, r = halves16(i)
        return xs[send_slot, mb, mh, r].astype(F32) + xr[recv_slot, mb, mh, r].astype(F32)

    def summed_own(recv_slot, send_slot, i):
        mb, r, _ = own16(i, m)
        return xs[send_slot, mb, m, r].astype(F32) + xr[recv_slot, mb, m, r].astype(F32)

    def out_block(o, recv_slot, send_slot):
        for n in range(2):
            put_xs(send_slot, slice(n * 512, n * 512 + 512), dot_nn(o, wo[:, n * 512 : n * 512 + 512]))
        exchange(recv_slot, send_slot, True).start()

    def up_block(b_in, put):
        for f in range(4):
            t = dot_nn(b_in, wu[:, f * 512 : f * 512 + 512])
            for g in range(8):
                put(f, slice(g * 32, g * 32 + 32), t[g * 32 : g * 32 + 32])

    def down_block(get_hid, recv_slot, send_slot):
        for n in range(2):
            cols = slice(n * 512, n * 512 + 512)
            t = dot_nn(get_hid(0), wd[0:512, cols])
            for f in range(1, 4):
                t = t + dot_nn(get_hid(f), wd[f * 512 : f * 512 + 512, cols])
            put_xs(send_slot, cols, t)
        exchange(recv_slot, send_slot, False).start()

    def dff_block(g_low, page, put_hid, recv_slot, send_slot):
        for f in range(4):
            t = dot_nt(g_low, wd[f * 512 : f * 512 + 512])
            for g in range(8):
                at = slice(g * 32, g * 32 + 32)
                u = uph[page(f), at]
                th = gelu_tanh(u)
                if put_hid is not None:
                    put_hid(f, at, 0.5 * u * (1.0 + th))
                uph[page(f), at] = gelu_slope(u, th) * t[g * 32 : g * 32 + 32].astype(BF)
        for n in range(2):
            at = slice(n * 512, n * 512 + 512)
            t = dot_nt(uph[page(0)], wu[at, 0:512])
            for f in range(1, 4):
                t = t + dot_nt(uph[page(f)], wu[at, f * 512 : f * 512 + 512])
            put_xs(send_slot, at, t)
        exchange(recv_slot, send_slot, True).start()

    def dqkv_block(page, recv_slot, send_slot):
        for n in range(2):
            at = slice(n * 512, n * 512 + 512)
            t = dot_nt(qk[page(0)], wq[0, at])
            for c in range(1, 3):
                t = t + dot_nt(qk[page(c)], wq[c, at])
            put_xs(send_slot, at, t)
        exchange(recv_slot, send_slot, False).start()

    def norm_back(v, grad, gain):
        sc = rms(v)
        u = grad * gain
        vn = v * sc
        corr = jnp.mean(vn * u, axis=-1, keepdims=True)
        return sc * (u - vn * corr), grad * vn

    def add_gain(row, part):
        gga[row] = gga[row] + (part[0:8] + part[8:16])

    def acc_at(i):
        t = lax.rem(i, 4)
        return lax.div(i, 4), pl.ds(pl.multiple_of(lax.div(t, 2) * 128, 128), 128), by512(lax.rem(t, 2))

    gm = remote(gpart.at[0], gpart.at[1], gms, gmr, peer)

    def gain_first():
        gpart[0] = jnp.broadcast_to(jnp.sum(gga[0], axis=0, keepdims=True), (8, 1024))
        gm.start()

    g_far = []
    for t in range(1, 8):
        o = lax.rem(d + t, 8)
        g_far.append((remote(ggr.at[d], ggr.at[d], ggs.at[t], ggrs.at[d], (s, o, m)),
                      remote(ggr.at[d], ggr.at[o], ggs.at[t], ggrs.at[o], (s, o, m))))

    def gain_second():
        gm.wait()
        own1 = jnp.sum(gga[1], axis=0, keepdims=True)
        ggr[d] = jnp.concatenate([gpart[0, 0:1] + gpart[1, 0:1], own1, jnp.zeros((6, 1024), F32)], axis=0)
        for cp, _ in g_far:
            cp.start()

    def gain_last():
        for cp, back in g_far:
            cp.wait_send()
            back.wait_recv()
        acc = ggr[0]
        for t in range(1, 8):
            acc = acc + ggr[t]
        gg_o[0] = acc[0:2]

    def ha(h, k):
        return 32 + h * 13 + k

    def hz(h, idx):
        return 32 + h * 13 + 8 + idx

    def hg(h):
        return (24, 16)[h]

    def help_a(h):
        return remote(uph.at[pl.ds(hg(h), 4), pl.ds(pl.multiple_of(y * 128, 128), 128)],
                      ryz.at[pl.ds(ha(h, 0), 4)], has.at[h], har.at[h], across)

    def help_b(h):
        return remote(uph.at[pl.ds(hg(h), 4), pl.ds(pl.multiple_of((1 - y) * 128, 128), 128)],
                      ryz.at[pl.ds(ha(h, 4), 4)], hbs.at[h], hbr.at[h], (1 - s, d + 1 - 2 * y, m))

    def help_right(h, k):
        return remote(ryz.at[ha(h, k)], ryz.at[hz(h, k + 1)], hzrs.at[h, k], hzrr.at[h, k], zup)

    def help_left(h, k):
        return remote(ryz.at[ha(h, k)], ryz.at[hz(h, k)], hzls.at[h, k], hzlr.at[h, k], zdown)

    def help_back(h):
        return remote(ryz.at[ha(h, z)], ryz.at[56 + h], hres.at[h], hrer.at[h], across)

    def add_pages(to, page):
        for g in range(4):
            at = slice(g * 32, g * 32 + 32)
            ryz[to, at] = (ryz[to, at].astype(F32) + ryz[page, at].astype(F32)).astype(BF)

    def help_start(h):
        help_a(h).wait_recv()
        help_b(h).wait_recv()

        def each(t):
            k = jnp.where(z < 2, 3 - t, t)
            add_pages(ha(h, k), ha(h, 4 + k))

            @pl.when((z == 0) & (k > 0))
            def _():
                help_right(h, k).start()

            @pl.when((z == 3) & (k < 3))
            def _():
                help_left(h, k).start()

        loop(0, 4, each)

    def help_pass(h, leg):
        def on_right(k):
            help_right(h, k).wait_recv()
            add_pages(ha(h, k), hz(h, k + 1))
            help_right(h, k).start()

        def on_left(k):
            help_left(h, k).wait_recv()
            add_pages(ha(h, k), hz(h, k))
            help_left(h, k).start()

        if leg == 0:
            @pl.when(z == 1)
            def _():
                on_right(3)
                on_right(2)

            @pl.when(z == 2)
            def _():
                on_left(0)
                on_left(1)
        else:
            @pl.when(z == 1)
            def _():
                on_left(0)

            @pl.when(z == 2)
            def _():
                on_right(3)

    def help_finish(h):
        @pl.when(z > 0)
        def _():
            help_right(h, z).wait_recv()
            add_pages(ha(h, z), hz(h, z + 1))

        @pl.when(z < 3)
        def _():
            help_left(h, z).wait_recv()
            add_pages(ha(h, z), hz(h, z))

        help_back(h).start()

    def help_sent(h):
        help_back(h).wait_send()
        for k in range(4):
            @pl.when(k > z)
            def _():
                help_right(h, k).wait_send()

            @pl.when(k < z)
            def _():
                help_left(h, k).wait_send()

    def low_lanes():
        return lax.broadcasted_iota(jnp.int32, (128, 128), 1) < 64

    def stack_heads(v):
        zero = jnp.zeros_like(v)
        return jnp.concatenate([jnp.where(low_lanes(), v, zero), jnp.where(low_lanes(), zero, v)], axis=0)

    def side_by_side(v):
        return jnp.concatenate([v[0:128], v[128:256]], axis=1)

    def frame_allowed(mb):
        pos = lax.broadcasted_iota(jnp.int32, (128, 128), 0)
        lane = lax.broadcasted_iota(jnp.int32, (128, 128), 1)
        one = (lane <= pos) & (lane.astype(F32) >= cs[2, mb * 128 : mb * 128 + 128])
        return jnp.concatenate([one, one], axis=0)

    def frame_probs(places, q2, k):
        allowed = [frame_allowed(mb) for mb in range(2)]
        sc = [dot_nt(a, b) * scale for a, b in zip(q2, k)]
        sc = [jnp.where(allowed[mb], v, masked_fill) for (mb, _, _), v in zip(places, sc)]
        top = [jnp.max(v, axis=-1, keepdims=True) for v in sc]
        e = [jnp.exp(v - t) for v, t in zip(sc, top)]
        inv = [1.0 / jnp.sum(v, axis=-1, keepdims=True) for v in e]
        return [v * t for v, t in zip(e, inv)]

    def frame_places(g):
        return [
            (mb, slice(mb * 128, mb * 128 + 128), pl.ds(pl.multiple_of((g * 2 + t) * 128, 128), 128))
            for mb in range(2) for t in range(2)
        ]

    def frame_attend(b):
        def part(g):
            places = frame_places(g)
            q2 = [stack_heads(qk[b * 3, at, cols]) for _, at, cols in places]
            k = [qk[b * 3 + 1, at, cols] for _, at, cols in places]
            v2 = [stack_heads(qk[b * 3 + 2, at, cols]) for _, at, cols in places]
            p = [side_by_side(v.astype(BF)) for v in frame_probs(places, q2, k)]
            o = [dot_nn(v, w) for v, w in zip(p, v2)]
            for (_, at, cols), v in zip(places, o):
                ob[b, at, cols] = v.astype(BF)

        loop(0, 2, part)

    def frame_attend_back(b, do_slot):
        def part(g):
            places = frame_places(g)
            q2 = [stack_heads(qk[b * 3, at, cols]) for _, at, cols in places]
            k = [qk[b * 3 + 1, at, cols] for _, at, cols in places]
            v = [qk[b * 3 + 2, at, cols] for _, at, cols in places]
            do2 = [stack_heads(dob[do_slot, at, cols]) for _, at, cols in places]
            p = frame_probs(places, q2, k)
            dp = [dot_nt(a, c) for a, c in zip(do2, v)]
            mean = [jnp.sum(a * c, axis=-1, keepdims=True) for a, c in zip(dp, p)]
            ds = [(c * (a - t)).astype(BF) for a, c, t in zip(dp, p, mean)]
            dv = [dot_tn(a.astype(BF), c) for a, c in zip(p, do2)]
            dk = [dot_tn(a, c) for a, c in zip(ds, q2)]
            dq = [dot_nn(side_by_side(a), stack_heads(c)) for a, c in zip(ds, k)]
            for i, (_, at, cols) in enumerate(places):
                co, si = cs[0, at], cs[1, at]
                for c, t in ((0, dq[i] * scale), (1, dk[i] * scale)):
                    qk[b * 3 + c, at, cols] = (t * co - swap_halves(t) * si).astype(BF)
                qk[b * 3 + 2, at, cols] = dv[i].astype(BF)

        loop(0, 2, part)

    def frame_tables(b):
        for mb in range(2):
            at = slice(mb * 128, mb * 128 + 128)
            pos = lax.broadcasted_iota(jnp.int32, (128, 128), 0)
            lane = lax.broadcasted_iota(jnp.int32, (128, 128), 1)
            start = jnp.broadcast_to(st[b, mb : mb + 1], (128, 128)).T
            hot = ((pos.astype(F32) - start) == lane.astype(F32)).astype(BF)
            for c in range(2):
                cs[c, at] = dot_nn(hot, tabs[c, 0]) + dot_nn(hot, tabs[c, 1]) + dot_nn(hot, tabs[c, 2])
            cs[2, at] = start

    def frame_qkv(a_slot, b):
        for c in range(3):
            t = dot_nn(ab[a_slot], wq[c])
            for g in range(4):
                v = t[:, g * 128 : g * 128 + 128]
                if c < 2:
                    v = v * cs[0] + swap_halves(v) * cs[1]
                qk[b * 3 + c, :, g * 128 : g * 128 + 128] = v.astype(BF)

    def px(b, i):
        mb, r = lax.div(i, 8), by16(lax.rem(i, 8))
        q, k = lax.div(b, 2), lax.rem(b, 2) * 2
        return jnp.concatenate([rg[q, k, mb, r], rg[q, k + 1, mb, r]], axis=1).astype(F32)

    def put_px(b, i, v):
        mb, r = lax.div(i, 8), by16(lax.rem(i, 8))
        q, k = lax.div(b, 2), lax.rem(b, 2) * 2
        rg[q, k, mb, r] = v[:, 0:512].astype(BF)
        rg[q, k + 1, mb, r] = v[:, 512:1024].astype(BF)

    def ds_rows(b, i):
        mb, r = lax.div(i, 8), by16(lax.rem(i, 8))
        return jnp.concatenate([ryz[b * 4 + mb, r], ryz[b * 4 + 2 + mb, r]], axis=1).astype(F32)

    def ds_all(b):
        return jnp.concatenate(
            [ryz[pl.ds(b * 4, 2)].reshape(ROWS, 512), ryz[pl.ds(b * 4 + 2, 2)].reshape(ROWS, 512)], axis=1
        )

    mrows = pl.ds(pl.multiple_of(m * 64, 64), 64)

    def px_ref(b):
        return rg.at[lax.div(b, 2), pl.ds(lax.rem(b, 2) * 2, 2), :, mrows]

    def ds_ref(b):
        return ryz.at[pl.ds(b * 4, 4), mrows]

    def block_of(i):
        j = lax.div(i, 2)
        low = jnp.where(j == 0, 1, jnp.where(j == 1, 0, j))
        high = jnp.where(j == 0, 2, jnp.where(j == 1, 3, 3 - j))
        zz = jnp.where(z == 0, j, jnp.where(z == 1, low, jnp.where(z == 2, high, 3 - j)))
        other = lax.rem(i, 2)
        return zz * 2 + jnp.where(other == 0, y, 1 - y), zz, other

    def spread(ref, sems, rsem, ms, mr, i, with_peer):
        b, zz, other = block_of(i)

        def go(direction, to):
            remote(ref(b), ref(b), sems.at[b, direction], rsem.at[b], to).start()

        @pl.when(other == 0)
        def _():
            go(2, ypeer)

            @pl.when((zz <= z) & (z < 3))
            def _():
                go(0, zup)

            @pl.when((zz >= z) & (z > 0))
            def _():
                go(1, zdown)

        if with_peer:
            remote(ref(b), ref(b), ms.at[b], mr.at[b], peer).start()

    def arrive(ref, sems, rsem, ms, mr, i):
        b, _, _ = block_of(i)
        remote(ref(b), ref(b), sems.at[b, 2], rsem.at[b], ypeer).wait_recv()
        spread(ref, sems, rsem, ms, mr, i, True)

    def drained(ref, sems, rsem, ms, mr, i, with_peer):
        b, zz, other = block_of(i)

        @pl.when(other == 0)
        def _():
            remote(ref(b), ref(b), sems.at[b, 2], rsem.at[b], ypeer).wait_send()

            @pl.when((zz <= z) & (z < 3))
            def _():
                remote(ref(b), ref(b), sems.at[b, 0], rsem.at[b], zup).wait_send()

            @pl.when((zz >= z) & (z > 0))
            def _():
                remote(ref(b), ref(b), sems.at[b, 1], rsem.at[b], zdown).wait_send()

        if with_peer:
            remote(ref(b), ref(b), ms.at[b], mr.at[b], peer).wait_send()

    xset = (px_ref, xas, xar, xms, xmr)
    dset = (ds_ref, das, dar, dms, dmr)

    inner = (z == 1) | (z == 2)

    def arrive_early(which):
        arrive(*which, 1)
        arrive(*which, 2)

        @pl.when(inner)
        def _():
            arrive(*which, 4)

    def arrive_at(which, i):
        @pl.when(i == 2)
        def _():
            arrive(*which, jnp.where(inner, 6, 4))

        @pl.when((i > 1) & (i < jnp.where(inner, 5, 6)))
        def _():
            there = jnp.where(i == 2, 3, jnp.where(i == 3, 6, jnp.where(i == 4, 5, 7)))
            here = jnp.where(i == 2, 3, jnp.where(i == 3, 5, 7))
            arrive(*which, jnp.where(inner, here, there))

    def halves_in(which, i):
        ref, _, _, ms, mr = which
        b, _, _ = block_of(i)
        remote(ref(b), ref(b), ms.at[b], mr.at[b], peer).wait_recv()

    def ring(e):
        t = lax.rem(e, 4)
        return jnp.where(t < 2, t + 1, t + 2), 1 + lax.rem(e, 2)

    mine128 = pl.ds(pl.multiple_of(d * 128, 128), 128)

    def lanes(i):
        return pl.ds(pl.multiple_of(i * 128, 128), 128)

    def hid_at(f):
        return slice(f * 256, f * 256 + 256)

    def gd_slice(b):
        page = b * 4 + lax.div(d, 4) * 2
        cols = pl.ds(pl.multiple_of(lax.rem(d, 4) * 128, 128), 128)
        return ryz[pl.ds(page, 2), :, cols].reshape(ROWS, 128).T

    def put_tb(f, at, v):
        tb[f * 256 + at.start : f * 256 + at.stop, 0:512] = v

    def frame_grad(chunk, left, right, first):
        at = acc_at(chunk)
        t = dot_nn(left, right)
        xm[at] = t if first else xm[at] + t

    def frame_grads_down(b, first):
        left = gd_slice(b)
        for f in range(4):
            frame_grad(f, left, tb[hid_at(f), 0:512], first)

    def frame_grads_up(b, bm_slot, bm_cols, first):
        left = bm[bm_slot, :, bm_cols].T
        for f in range(4):
            frame_grad(4 + f, left, uph[f * 8 + b], first)

    def frame_grads_attend(b, ga_slot, a_slot, a_cols, first):
        frame_grad(8, gd[ga_slot, :, :, :, mine128].reshape(ROWS, 128).T, ob[b], first)
        left = ab[a_slot, :, a_cols].T
        for c in range(3):
            frame_grad(9 + c, left, qk[b * 3 + c], first)

    @pl.when(frame)
    def _():
        pos = lax.broadcasted_iota(jnp.int32, (128, 128), 0)
        lane = lax.broadcasted_iota(jnp.int32, (128, 128), 1)
        freq = jnp.exp(lax.rem(lane, 32).astype(F32) * (-2.0 * math.log(rotary_base) / HEAD_DIM))
        angle = pos.astype(F32) * freq
        sine = jnp.sin(angle)
        for c, v in enumerate((jnp.cos(angle), jnp.where(lax.rem(lane, 64) < 32, -sine, sine))):
            for t in range(3):
                term = v.astype(BF)
                tabs[c, t] = term
                v = v - term.astype(F32)
        place = lax.broadcasted_iota(jnp.int32, (8, 128), 1)
        rows = []
        for mb in range(2):
            start = jnp.zeros((8, 128), jnp.int32)
            end = jnp.int32(0)
            for j in range(4):
                size = lens[mb, 0, j]
                end = end + size
                start = start + jnp.where(place >= end, size, 0)
            rows.append(start)
        which = lax.broadcasted_iota(jnp.int32, (8, 128), 0)
        st[d] = jnp.where(which == 0, rows[0], rows[1]).astype(F32)
        for t in range(1, 8):
            o = lax.rem(d + t, 8)
            remote(st.at[d], st.at[d], sts.at[t], strc.at[d], (s, o, m)).start()
        frame_tables(d)

        with jax.named_scope("embeds_wait"):
            for cp in e_local:
                cp.wait()
            for cp in e_far:
                cp.wait()

        gain0 = gains[0, 0:1]
        gain1 = gains[0, 1:2]

        def x_own(i):
            mb, mh, r = halves16(i)
            return em[0, mb, mh, r].astype(F32) + em[1, mb, mh, r].astype(F32) + em[2, mb, mh, r].astype(F32)

        def rows_in(i):
            v = x_own(i)
            xm[2, by16(i)] = v
            ab[0, by16(i)] = (v * rms(v) * gain0).astype(BF)
            put_px(d, i, v)

        with jax.named_scope("own_qkv"):
            loop(0, 16, rows_in, unroll=UNROLL)
            spread(*xset, 0, False)
            w_copies[0].wait()
            frame_qkv(0, d)
        with jax.named_scope("own_attend"):
            frame_attend(d)
        w_copies[1].wait()
        with jax.named_scope("own_out"):
            out_block(ob[d], 0, 0)
            w_copies[2].wait()
            exchange(0, 0, True).wait()

        def rows_mid(i):
            v = xm[2, by16(i)] + summed(0, 0, i)
            return v, (v * rms(v) * gain1).astype(BF)

        def put_mid(i, v, w):
            xm[2, by16(i)] = v
            bm[0, by16(i)] = w

        def put_own(f, at, u):
            uph[f * 8 + d, at] = u.astype(BF)
            u = u.astype(BF)
            put_tb(f, at, 0.5 * u * (1.0 + gelu_tanh(u)))

        with jax.named_scope("own_ff"):
            grouped(16, rows_mid, put_mid)
            up_block(bm[0], put_own)
            w_copies[3].wait()
            down_block(lambda f: tb[hid_at(f), 0:512], 3, 0)
            exchange(3, 0, False).wait()

        def rows_res(i):
            mb, r, row = own16(i, m)
            sr[mb, m, r] = (xm[2, row] + summed_own(3, 0, i)).astype(BF)

        loop(0, 8, rows_res, unroll=UNROLL)
        hop[0].start()

        for t in range(1, 8):
            o = lax.rem(d + t, 8)
            remote(st.at[d], st.at[o], sts.at[t], strc.at[o], (s, o, m)).wait()

        def others_in(i):
            b, _, _ = block_of(i)
            halves_in(xset, i)
            frame_tables(b)

            def rows_norm(t):
                v = px(b, t)
                ab[2, by16(t)] = (v * rms(v) * gain0).astype(BF)

            loop(0, 16, rows_norm, unroll=UNROLL)
            ab[1, :, lanes(i)] = ab[2, :, mine128]
            frame_qkv(2, b)
            frame_attend(b)
            out_block(ob[b], *ring(i))

        def others_ff(i):
            b, _, _ = block_of(i)
            recv_slot, send_slot = ring(i)
            exchange(recv_slot, send_slot, True).wait()
            drained(*xset, i, True)

            def rows_m(t):
                v = px(b, t) + summed(recv_slot, send_slot, t)
                return v, (v * rms(v) * gain1).astype(BF)

            def put_m(t, v, w):
                put_px(b, t, v)
                bm[2, by16(t)] = w

            grouped(16, rows_m, put_m)
            bm[1, :, lanes(i)] = bm[2, :, mine128]

            def put_up(f, at, u):
                uph[f * 8 + b, at] = u.astype(BF)

            up_block(bm[2], put_up)

        with jax.named_scope("oth_arrive"):
            arrive_early(xset)

        def others(i):
            with jax.named_scope("oth_arrive"):
                arrive_at(xset, i)

            @pl.when(i < 8)
            def _():
                with jax.named_scope("oth_in"):
                    others_in(i)

            @pl.when(i > 1)
            def _():
                with jax.named_scope("oth_ff"):
                    others_ff(i - 1)

        loop(1, 9, others)
        drained(*xset, 0, False)
        hop[0].wait_send()

        with jax.named_scope("help_start0"):
            help_start(0)

        with jax.named_scope("d_sent_wait"):
            for cp in hop2:
                cp.wait_recv()
            spread(*dset, 0, True)
            halves_in(dset, 0)
        with jax.named_scope("own_dff"):
            dff_block(ds_all(d), lambda f: f * 8 + d, put_tb, 0, 0)
            frame_grads_down(d, True)
        with jax.named_scope("help_pass0"):
            help_pass(0, 0)
        exchange(0, 0, True).wait()

        def rows_dmid(i):
            add, part = norm_back(xm[2, by16(i)], summed(0, 0, i), gain1)
            return ds_rows(d, i) + add, part

        def put_dmid(i, dm, part):
            mb, mh, r = halves16(i)
            xm[2, by16(i)] = dm
            gd[0, mb, mh, r] = dm.astype(BF)
            add_gain(1, part)

        with jax.named_scope("own_dmid"):
            grouped(16, rows_dmid, put_dmid)
            dob[0] = dot_nt(gd[0].reshape(ROWS, 1024), wo[...]).astype(BF)
        with jax.named_scope("arrive_early"):
            arrive_early(dset)
        frame_tables(d)
        with jax.named_scope("own_attend_back"):
            frame_attend_back(d, 0)
        dqkv_block(lambda c: d * 3 + c, 3, 0)
        with jax.named_scope("own_grads"):
            frame_grads_up(d, 0, mine128, True)
        exchange(3, 0, False).wait()

        def rows_dx(i):
            mb, r, row = own16(i, m)
            v = em[0, mb, m, r].astype(F32) + em[1, mb, m, r].astype(F32) + em[2, mb, m, r].astype(F32)
            add, part = norm_back(v, summed_own(3, 0, i), gain0)
            return xm[2, row] + add, part

        def put_dx(i, dv, part):
            mb, r, _ = own16(i, m)
            top = dv.astype(BF)
            em[0, mb, m, r] = top
            em[1, mb, m, r] = (dv - top.astype(F32)).astype(BF)
            add_gain(0, part)

        grouped(8, rows_dx, put_dx)
        gain_first()

        def rows_ge(i):
            mb, r, _ = own16(i, m)
            dv = em[0, mb, m, r].astype(F32) + em[1, mb, m, r].astype(F32)
            return tuple((em[c, mb, 1 - m, r].astype(F32) + dv).astype(BF) for c in range(3))

        def put_ge(i, *parts):
            mb, r, _ = own16(i, m)
            for c in range(3):
                em[c, mb, 1 - m, r] = parts[c]

        def embed_grads():
            for cp in dl_far:
                cp.wait_recv()
            grouped(8, rows_ge, put_ge)
            for cp in ge_local + ge_far:
                cp.start()

        gain_second()
        with jax.named_scope("help_pass0"):
            help_pass(0, 1)
        frame_grads_attend(d, 0, 0, mine128, True)

        def back_first(i):
            b, _, _ = block_of(i)
            halves_in(dset, i)
            dff_block(ds_all(b), lambda f: f * 8 + b, put_tb, *ring(i + 7))
            frame_grads_down(b, False)

        def back_second(i):
            b, _, _ = block_of(i)
            recv_slot, send_slot = ring(i + 7)
            exchange(recv_slot, send_slot, True).wait()

            def rows_dm(t):
                mb, mh, r = halves16(t)
                add, _ = norm_back(px(b, t), summed(recv_slot, send_slot, t), gain1)
                gd[1, mb, mh, r] = (ds_rows(b, t) + add).astype(BF)

            loop(0, 16, rows_dm, unroll=UNROLL)
            dob[0] = dot_nt(gd[1].reshape(ROWS, 1024), wo[...]).astype(BF)
            frame_tables(b)
            frame_attend_back(b, 0)
            frame_grads_up(b, 1, lanes(i), False)
            frame_grads_attend(b, 1, 1, lanes(i), False)

        def others_back(i):
            @pl.when(i < 8)
            def _():
                with jax.named_scope("oth_dff"):
                    back_first(i)

            with jax.named_scope("oth_arrive_d"):
                arrive_at(dset, i)

            @pl.when(i > 1)
            def _():
                with jax.named_scope("oth_rest"):
                    back_second(i - 1)

            @pl.when(i == 2)
            def _():
                with jax.named_scope("help_finish0"):
                    help_finish(0)

            @pl.when(i == 4)
            def _():
                with jax.named_scope("help_start1"):
                    help_start(1)

            @pl.when(i == 5)
            def _():
                with jax.named_scope("help_pass1"):
                    help_pass(1, 0)
                with jax.named_scope("embed_grads"):
                    embed_grads()

            @pl.when(i == 6)
            def _():
                with jax.named_scope("help_pass1"):
                    help_pass(1, 1)

            @pl.when(i == 7)
            def _():
                with jax.named_scope("help_finish1"):
                    help_finish(1)
        loop(1, 9, others_back)
        for h in range(HELPED):
            help_sent(h)
        loop(0, 8, lambda i: drained(*dset, i, True))
        for cp in grads_out:
            cp.start()
        gain_last()
        for cp in ge_local:
            cp.wait()
        for cp in ge_far:
            cp.wait_send()
        for cp in lo_far:
            cp.wait_recv()
        for cp in grads_out:
            cp.wait()

    def head_sum(prod):
        r0 = lax.broadcasted_iota(jnp.int32, (256, 256), 0)
        r1 = lax.broadcasted_iota(jnp.int32, (256, 256), 1)
        ones = (lax.div(r0, 64) == lax.div(r1, 64)).astype(BF)
        return dot_nn(prod, ones)

    def code_probs(q, k):
        probs = []
        for i in range(3):
            sc = [head_sum(q[i] * k[j]) * scale for j in range(i + 1)]
            top = functools.reduce(jnp.maximum, sc)
            e = [jnp.exp(v - top) for v in sc]
            inv = 1.0 / functools.reduce(jnp.add, e)
            probs.append([v * inv for v in e])
        return probs

    def code_part(i):
        return (pl.ds(pl.multiple_of(lax.div(i, 2) * 64, 64), 64), pl.ds(pl.multiple_of(lax.rem(i, 2) * 256, 256), 256))

    def code_attend(i):
        at, cols = code_part(i)
        q, k, v = ([qk[c * 3 + b, at, cols] for b in range(3)] for c in range(3))
        probs = code_probs(q, k)
        v = [w.astype(F32) for w in v]
        for t in range(3):
            o = functools.reduce(jnp.add, [probs[t][j].astype(BF).astype(F32) * v[j] for j in range(t + 1)])
            ob[t, at, cols] = o.astype(BF)

    def code_attend_back(i):
        at, cols = code_part(i)
        q, k, v = ([qk[c * 3 + b, at, cols] for b in range(3)] for c in range(3))
        do = [ob[3 + b, at, cols] for b in range(3)]
        probs = code_probs(q, k)
        all_dp = [[head_sum(do[t] * v[j]) for j in range(t + 1)] for t in range(3)]
        q, k, do = ([w.astype(F32) for w in x] for x in (q, k, do))
        dk = [0.0] * 3
        dv = [0.0] * 3
        for t in range(3):
            dp = all_dp[t]
            mean = functools.reduce(jnp.add, [dp[j] * probs[t][j] for j in range(t + 1)])
            dq = 0.0
            for j in range(t + 1):
                ds = (probs[t][j] * (dp[j] - mean)).astype(BF).astype(F32)
                dq = dq + ds * k[j]
                dk[j] = dk[j] + ds * q[t]
                dv[j] = dv[j] + probs[t][j].astype(BF).astype(F32) * do[t]
            qk[t, at, cols] = (dq * scale).astype(BF)
        for j in range(3):
            qk[3 + j, at, cols] = (dk[j] * scale).astype(BF)
            qk[6 + j, at, cols] = dv[j].astype(BF)

    def flip(get):
        def one(b):
            at = pl.ds(pl.multiple_of(b * 256, 256), 256)
            t = get(b)
            for g in range(4):
                tb[g * 256 : g * 256 + 256, at] = t[:, g * 256 : g * 256 + 256].T

        loop(0, 3, one)

    def ry(slot):
        return ryz.at[pl.ds(slot * 4, 4)]

    def rz(slot, idx):
        return SLOTS * 4 + slot * 5 + idx

    def sends(slot):
        return remote(rg.at[slot, :, 1 - y], ry(slot), ysn.at[slot], yrc.at[slot], ypeer)

    def right(slot, k):
        return remote(rg.at[slot, k, y], ryz.at[rz(slot, k + 1)], zrs.at[slot, k], zrr.at[slot, k], zup)

    def left(slot, k):
        return remote(rg.at[slot, k, y], ryz.at[rz(slot, k)], zls.at[slot, k], zlr.at[slot, k], zdown)

    def free_slot(slot, last=False):
        if not last:
            sends(slot).wait_send()
        for k in range(4):
            @pl.when(k > z)
            def _():
                right(slot, k).wait_send()

            @pl.when(k < z)
            def _():
                left(slot, k).wait_send()

    def make_chunk(i, act, send=True):
        slot = lax.rem(i, SLOTS)

        @pl.when(i >= SLOTS)
        def _():
            free_slot(slot)

        def part(k):
            at = pl.ds(pl.multiple_of(k * 256, 256), 256)
            rg[slot, k] = dot_nn(tb[at, :], act()).astype(BF).reshape(2, 128, 512)

        loop(0, 4, part)

        @pl.when(i >= SLOTS)
        def _():
            pl.semaphore_wait(ycr, 1)

        if send:
            sends(slot).start()

    def make_help(h, act):
        def part(k):
            at = pl.ds(pl.multiple_of(k * 256, 256), 256)
            uph[hg(h) + k] = dot_nn(tb[at, :], act()).astype(BF)

        loop(0, 4, part)
        help_a(h).start()
        help_b(h).start()

    def fg(h):
        return (28, 12)[h]

    def fz(h):
        return (10, 16)[h]

    def along_right(h, k):
        return remote(uph.at[fg(h) + k], qk.at[fz(h) + k + 1], frs.at[h, k], frr.at[h, k], zup)

    def along_left(h, k):
        return remote(uph.at[fg(h) + k], qk.at[fz(h) + k], fls.at[h, k], flr.at[h, k], zdown)

    def along_y(h):
        return remote(uph.at[fg(h) + z, pl.ds(pl.multiple_of((1 - y) * 128, 128), 128)],
                      qk.at[fz(h) + 5, 0:128], fys.at[h], fyr.at[h], ypeer)

    def make_along(h, act):
        def part(k):
            at = pl.ds(pl.multiple_of(k * 256, 256), 256)
            uph[fg(h) + k] = dot_nn(tb[at, :], act()).astype(BF)

            @pl.when((z == 0) & (k > 0))
            def _():
                along_right(h, k).start()

            @pl.when((z == 3) & (k < 3))
            def _():
                along_left(h, k).start()

        loop(0, 4, part)

    def add_half(to, page):
        for g in range(8):
            at = slice(g * 32, g * 32 + 32)
            uph[to, at] = (uph[to, at].astype(F32) + qk[page, at].astype(F32)).astype(BF)

    def along_pass(h, leg):
        def on_right(k):
            along_right(h, k).wait_recv()
            add_half(fg(h) + k, fz(h) + k + 1)
            along_right(h, k).start()

        def on_left(k):
            along_left(h, k).wait_recv()
            add_half(fg(h) + k, fz(h) + k)
            along_left(h, k).start()

        if leg == 0:
            @pl.when(z == 1)
            def _():
                on_right(3)
                on_right(2)

            @pl.when(z == 2)
            def _():
                on_left(0)
                on_left(1)
        else:
            @pl.when(z == 1)
            def _():
                on_left(0)

            @pl.when(z == 2)
            def _():
                on_right(3)

    def along_sum(h):
        @pl.when(z > 0)
        def _():
            along_right(h, z).wait_recv()
            add_half(fg(h) + z, fz(h) + z + 1)

        @pl.when(z < 3)
        def _():
            along_left(h, z).wait_recv()
            add_half(fg(h) + z, fz(h) + z)

        along_y(h).start()

    def along_finish(h, chunk):
        along_y(h).wait()
        rows = pl.ds(pl.multiple_of(y * 128, 128), 128)
        xm[acc_at(chunk)] = uph[fg(h) + z, rows].astype(F32) + qk[fz(h) + 5, 0:128].astype(F32)
        for k in range(4):
            @pl.when(k > z)
            def _():
                along_right(h, k).wait_send()

            @pl.when(k < z)
            def _():
                along_left(h, k).wait_send()

    def add_into(slot, k, page):
        for g in range(4):
            at = slice(g * 32, g * 32 + 32)
            rg[slot, k, y, at] = (rg[slot, k, y, at].astype(F32) + ryz[page, at].astype(F32)).astype(BF)

    def z_credit():
        @pl.when(z < 3)
        def _():
            pl.semaphore_wait(rcr, 1)

        @pl.when(z > 0)
        def _():
            pl.semaphore_wait(lcr, 1)

    last_slot = (CHUNKS - 1) % SLOTS

    def last_k(t):
        low = (3, 0, 2, 1)[t]
        return jnp.where(z == 0, 3 - t, jnp.where(z == 1, low, jnp.where(z == 2, 3 - low, t)))

    def last_y(t):
        k = last_k(t)
        return remote(rg.at[last_slot, k, 1 - y], ryz.at[last_slot * 4 + k], lys.at[t], lyr.at[t], ypeer)

    def last_step(t):
        k = last_k(t)
        last_y(t).wait_send()
        if t < 2:
            last_y(t + 2).start()
        last_y(t).wait_recv()
        add_into(last_slot, k, last_slot * 4 + k)

        @pl.when((z == 0) & (k > 0))
        def _():
            right(last_slot, k).start()

        @pl.when((z == 3) & (k < 3))
        def _():
            left(last_slot, k).start()

    def proc_y(i):
        slot = lax.rem(i, SLOTS)
        sends(slot).wait_recv()
        pl.when(i >= SLOTS)(z_credit)

        def up_first(t):
            k = 3 - t
            add_into(slot, k, slot * 4 + k)

            @pl.when((z == 0) & (k > 0))
            def _():
                right(slot, k).start()

        def down_first(t):
            add_into(slot, t, slot * 4 + t)

            @pl.when((z == 3) & (t < 3))
            def _():
                left(slot, t).start()

        @pl.when(z < 2)
        def _():
            loop(0, 4, up_first)

        @pl.when(z >= 2)
        def _():
            loop(0, 4, down_first)

        @pl.when(i + SLOTS < CHUNKS)
        def _():
            pl.semaphore_signal(ycr, 1, device_id=ypeer, device_id_type=MESH)

    def pass_right(slot, k):
        right(slot, k).wait_recv()
        add_into(slot, k, rz(slot, k + 1))
        right(slot, k).start()

    def pass_left(slot, k):
        left(slot, k).wait_recv()
        add_into(slot, k, rz(slot, k))
        left(slot, k).start()

    def fwd_z(i):
        slot = lax.rem(i, SLOTS)

        @pl.when(z == 1)
        def _():
            pass_right(slot, 3)
            pass_right(slot, 2)

        @pl.when(z == 2)
        def _():
            pass_left(slot, 0)
            pass_left(slot, 1)

    def fwd_z2(i):
        slot = lax.rem(i, SLOTS)

        @pl.when(z == 1)
        def _():
            pass_left(slot, 0)

        @pl.when(z == 2)
        def _():
            pass_right(slot, 3)

    def finish(i):
        slot = lax.rem(i, SLOTS)

        @pl.when(z > 0)
        def _():
            right(slot, z).wait_recv()
            add_into(slot, z, rz(slot, z + 1))

        @pl.when(z < 3)
        def _():
            left(slot, z).wait_recv()
            add_into(slot, z, rz(slot, z))

        total = rg[slot, z, y].astype(F32)

        xm[acc_at(jnp.where(i < 2, i + 2, i + 3))] = total

        @pl.when(i + SLOTS < CHUNKS)
        def _():
            @pl.when(z > 0)
            def _():
                pl.semaphore_signal(rcr, 1, device_id=zdown, device_id_type=MESH)

            @pl.when(z < 3)
            def _():
                pl.semaphore_signal(lcr, 1, device_id=zup, device_id_type=MESH)

    @pl.when(code)
    def _():
        for cp in c_local:
            cp.start()
        for cp in c_far:
            cp.start()
        for cp in e_local:
            cp.wait()
        for cp in e_far:
            cp.wait()
        gain0 = gains[0, 0:1]
        gain1 = gains[0, 1:2]
        for cp in c_local:
            cp.wait()
        for cp in c_far:
            cp.wait()
        flip(lambda b: gd[b].reshape(ROWS, 1024))
        with jax.named_scope("sent_wait"):
            hop[0].wait_recv()
            hop[1].start()
            hop[1].wait_recv()

        def rows_in(i):
            mb, mh, r = halves16(i)
            came = sr[mb, mh, r].astype(F32)
            for c in range(3):
                v = em[c, mb, mh, r].astype(F32) + came
                xm[c, by16(i)] = v
                ab[c, by16(i)] = (v * rms(v) * gain0).astype(BF)

        with jax.named_scope("code_norm"):
            loop(0, 16, rows_in, unroll=UNROLL)

        def qkv_all(b):
            for c in range(3):
                qk[c * 3 + b] = dot_nn(ab[b], wq[c]).astype(BF)

        w_copies[0].wait()
        with jax.named_scope("code_qkv"):
            loop(0, 3, qkv_all)
        with jax.named_scope("code_attend"):
            loop(0, 8, code_attend)
        w_copies[1].wait()
        with jax.named_scope("code_out"):
            loop(0, 3, lambda b: out_block(ob[b], b, b))
        w_copies[2].wait()
        w_copies[3].wait()

        def ff(b):
            exchange(b, b, True).wait()

            def rows_mid(i):
                v = xm[b, by16(i)] + summed(b, b, i)
                return v, (v * rms(v) * gain1).astype(BF)

            def put_mid(i, v, w):
                mb, mh, r = halves16(i)
                xm[b, by16(i)] = v
                bm[b, by16(i)] = w

                @pl.when(mh == m)
                def _():
                    em[b, mb, 1 - m, r] = v.astype(BF)

            grouped(16, rows_mid, put_mid)

            def put(f, at, u):
                u = u.astype(BF)
                uph[f * 3 + b, at] = u
                uph[12 + f * 3 + b, at] = 0.5 * u * (1.0 + gelu_tanh(u))

            up_block(bm[b], put)

        with jax.named_scope("code_ff"):
            loop(0, 3, ff)

        def res(b):
            exchange(3 + b, b, False).wait()

            def rows_res(i):
                mb, r, _ = own16(i, m)
                return (em[b, mb, 1 - m, r].astype(F32) + summed_own(3 + b, b, i)).astype(BF)

            def put_res(i, v):
                mb, r, _ = own16(i, m)
                em[b, mb, 1 - m, r] = v

            grouped(8, lambda i: (rows_res(i),), put_res)

        with jax.named_scope("code_grad_down"):
            make_chunk(0, lambda: uph[18:21].reshape(768, 512))
            make_along(0, lambda: uph[15:18].reshape(768, 512))
            make_help(0, lambda: uph[12:15].reshape(768, 512))
            make_chunk(1, lambda: uph[21:24].reshape(768, 512), False)
        def dff(b):
            dff_block(gd[b].reshape(ROWS, 1024), lambda f: f * 3 + b, None, 3 + b, b)

            @pl.when(b == 1)
            def _():
                sends(1).start()

        with jax.named_scope("code_dff"):
            loop(0, 3, dff)

        def dmid(b):
            exchange(3 + b, b, True).wait()

            def rows_dmid(i):
                mb, mh, r = halves16(i)
                add, part = norm_back(xm[b, by16(i)], summed(3 + b, b, i), gain1)
                return gd[b, mb, mh, r].astype(F32) + add, part

            def put_dmid(i, dm, part):
                mb, mh, r = halves16(i)
                xm[b, by16(i)] = dm
                gd[b, mb, mh, r] = dm.astype(BF)
                add_gain(1, part)

            grouped(16, rows_dmid, put_dmid)
            ob[3 + b] = dot_nt(gd[b].reshape(ROWS, 1024), wo[...]).astype(BF)

        with jax.named_scope("code_dmid"):
            loop(0, 3, dmid)
        with jax.named_scope("code_early"):
            proc_y(0)
            flip(lambda b: bm[b])
            make_chunk(2, lambda: uph[3:6].reshape(768, 512))
            along_pass(0, 0)
        with jax.named_scope("code_attend_back"):
            loop(0, 8, code_attend_back)
        with jax.named_scope("code_dqkv"):
            loop(0, 3, lambda b: dqkv_block(lambda c: c * 3 + b, b, b))

        def dx(b):
            exchange(b, b, False).wait()

            def rows_dx(i):
                mb, r, row = own16(i, m)
                v = em[b, mb, m, r].astype(F32) + sr[mb, m, r].astype(F32)
                add, part = norm_back(v, summed_own(b, b, i), gain0)
                return xm[b, row] + add, part

            def put_dx(i, dv, part):
                mb, r, row = own16(i, m)
                xm[b, row] = dv
                em[b, mb, m, r] = dv.astype(BF)
                add_gain(0, part)

            grouped(8, rows_dx, put_dx)

        with jax.named_scope("code_dx"):
            loop(0, 3, dx)
        hop[1].wait_send()

        def rows_ds(i):
            mb, r, row = own16(i, m)
            sr[mb, m, r] = (xm[0, row] + xm[1, row] + xm[2, row]).astype(BF)

        loop(0, 8, rows_ds, unroll=UNROLL)
        for cp in hop2:
            cp.start()
        gain_first()
        with jax.named_scope("code_y2"):
            make_chunk(3, lambda: uph[6:9].reshape(768, 512))
            proc_y(1)
            gain_second()
            along_pass(0, 1)
            fwd_z(0)

        with jax.named_scope("code_down"):
            loop(0, 3, lambda b: down_block(lambda f: uph[12 + f * 3 + b], 3 + b, b))
            loop(0, 3, res)
        for cp in lo_local:
            cp.start()

        def tail(i):
            with jax.named_scope("tail_z2"):
                fwd_z2(i - 3)

            @pl.when(i > 3)
            def _():
                with jax.named_scope("tail_finish"):
                    finish(i - 4)

            @pl.when(i == 4)
            def _():
                make_chunk(i, lambda: uph[9:12].reshape(768, 512))
                for cp in hop2:
                    cp.wait_send()
                make_help(1, lambda: uph[0:3].reshape(768, 512))

            @pl.when(i == 5)
            def _():
                flip(lambda b: gd[b].reshape(ROWS, 1024))
                make_chunk(i, lambda: ob[0:3].reshape(768, 512))

            @pl.when(i == 6)
            def _():
                flip(lambda b: ab[b])

            @pl.when((i > 5) & (i < CHUNKS - 1))
            def _():
                make_chunk(i, lambda: qk[pl.ds((i - 6) * 3, 3)].reshape(768, 512))

            @pl.when(i == CHUNKS - 1)
            def _():
                make_chunk(i, lambda: qk[6:9].reshape(768, 512), False)

            @pl.when(i == 6)
            def _():
                for h in (0, 1):
                    help_a(h).wait_send()
                    help_b(h).wait_send()
                for cp in dl_far:
                    cp.start()

            @pl.when(i == 8)
            def _():
                for cp in dl_far:
                    cp.wait_send()
                for cp in lo_far:
                    cp.start()

            with jax.named_scope("tail_y"):
                proc_y(i - 1)

            @pl.when(i == CHUNKS - 1)
            def _():
                last_y(0).start()
                last_y(1).start()

            with jax.named_scope("tail_z"):
                fwd_z(i - 2)

            with jax.named_scope("tail_along"):
                pl.when(i == 4)(lambda: along_sum(0))
                pl.when(i == 5)(lambda: along_finish(0, 1))

            @pl.when(i == 7)
            def _():
                helped(0)

        def helped(h):
            with jax.named_scope("helped"):
                help_back(h).wait_recv()
                xm[acc_at(h * 4)] = ryz[56 + h].astype(F32)
                grads_out[h].start()

        loop(3, CHUNKS, tail)
        n = CHUNKS - 1
        with jax.named_scope("last_0"):
            z_credit()
            last_step(0)
        with jax.named_scope("last_1"):
            fwd_z2(n - 2)
            last_step(1)
            finish(n - 3)
        with jax.named_scope("last_2"):
            fwd_z(n - 1)
            last_step(2)
            finish(n - 2)
        with jax.named_scope("last_3"):
            fwd_z2(n - 1)
            last_step(3)
        with jax.named_scope("last_4"):
            fwd_z(n)
            finish(n - 1)
        with jax.named_scope("helped"):
            helped(1)
        with jax.named_scope("last_5"):
            fwd_z2(n)
            finish(n)
        grads_out[2].start()
        for cp in lo_local:
            cp.wait()
        for cp in lo_far:
            cp.wait_send()
        gain_last()
        for cp in ge_far:
            cp.wait_recv()
        for t in range(CHUNKS - SLOTS, CHUNKS):
            free_slot(t % SLOTS, t == CHUNKS - 1)
        for cp in grads_out:
            cp.wait()


def unpack(lo_i, ge_i, g_i, gg_i, lo_o, ge_o, gg_o, gq_o, go_o, gu_o, gd_o, lo, ge, g, gq, go, gu, gdn, sems):
    ins = [pltpu.make_async_copy(g_i.at[t], g.at[t], sems.at[t]) for t in range(3)]
    ins += [pltpu.make_async_copy(lo_i, lo, sems.at[3]), pltpu.make_async_copy(ge_i, ge, sems.at[4])]
    outs = [
        pltpu.make_async_copy(a, b, sems.at[5 + t])
        for t, (a, b) in enumerate(((gdn, gd_o), (gu, gu_o), (go, go_o), (gq, gq_o), (lo, lo_o), (ge, ge_o)))
    ]
    for cp in ins:
        cp.start()
    gg_o[...] = gg_i[...]

    def chunk(i):
        rows, cols = (i % 4) // 2 * 128, i % 2 * 512
        return g[i // 4, rows : rows + 128, cols : cols + 512]

    ins[0].wait()
    for f in range(4):
        gdn[f * 512 : f * 512 + 512] = chunk(f).T
    outs[0].start()
    ins[1].wait()
    for f in range(4):
        gu[:, f * 512 : f * 512 + 512] = chunk(4 + f)
    outs[1].start()
    ins[2].wait()
    go[...] = chunk(8).T
    outs[2].start()
    for c in range(3):
        gq[c] = chunk(9 + c)
    outs[3].start()
    for t in range(2):
        ins[3 + t].wait()
        outs[4 + t].start()
    for cp in outs:
        cp.wait()


def on_device_kernel(embeds, lengths, norm_gains, w_qkv, w_out, w_up, w_down, cotangent):
    anyspec = pl.BlockSpec(memory_space=pl.ANY)
    hbm = pl.BlockSpec(memory_space=pltpu.HBM)
    vm = pl.BlockSpec(memory_space=pltpu.VMEM)
    sd = jax.ShapeDtypeStruct
    V = pltpu.VMEM
    D = pltpu.SemaphoreType.DMA
    R = pltpu.SemaphoreType.REGULAR
    full = (2, 2, 64, 1024)
    scratch = [
        V((3, 1024, 512), BF), V((512, 1024), BF), V((1024, 2048), BF), V((2048, 1024), BF),
        V((3,) + full, BF), V((3,) + full, BF), V(full, BF),
        V((3, ROWS, 1024), F32), V((3, ROWS, 1024), BF), V((3, ROWS, 1024), BF),
        V((24, ROWS, 512), BF), V((8, ROWS, 512), BF), V((1, ROWS, 512), BF), V((32, ROWS, 512), BF),
        V((3,) + full, BF), V((6,) + full, BF), V((1024, 768), BF),
        V((3, ROWS, 128), F32), V((2, 3, 128, 128), BF), V((8, 8, 128), F32),
        V((2, 8, 1024), F32), V((8, 8, 1024), F32), V((2, 8, 1024), F32),
        V((SLOTS, 4, 2, 128, 512), BF), V((32 + HELPED * 13, 128, 512), BF),
        D((3,)), D((4,)), D((3,)), D((3,)), D((3,)), D((3,)), D((3,)), D((3,)), D((3,)), D((6,)), D((4,)), D((4,)),
        D((3,)), D((3,)), D((3,)), D((3,)), D((3,)),
        D((3,)), D((3,)), D((3,)), D((8,)), D((8,)), D, D,
        D((SLOTS,)), D((SLOTS,)), D((SLOTS, 4)), D((SLOTS, 4)), D((SLOTS, 4)), D((SLOTS, 4)),
        D((4,)), D((4,)),
        D((ALONG, 4)), D((ALONG, 4)), D((ALONG, 4)), D((ALONG, 4)), D((ALONG,)), D((ALONG,)),
        D((HELPED,)), D((HELPED,)), D((HELPED,)), D((HELPED,)), D((HELPED, 4)), D((HELPED, 4)), D((HELPED, 4)), D((HELPED, 4)),
        D((HELPED,)), D((HELPED,)), D((8,)), D((8,)), D((8, 3)), D((8,)), D((8,)), D((8,)), D((8, 3)), D((8,)), D((8,)), D((8,)),
        R, R, R,
    ]
    rows, gain = sd((2, 3, 64, 1024), BF), sd((1, 2, 1024), F32)
    grads = (sd((3, 128, 512), F32), sd((512, 128), F32), sd((128, 2048), F32), sd((2048, 128), F32))
    outs = pl.pallas_call(
        body,
        out_shape=(rows, rows, sd((3, ROWS, 1024), F32), gain),
        in_specs=[anyspec, anyspec, pl.BlockSpec(memory_space=pltpu.SMEM), vm, anyspec, anyspec, anyspec, anyspec],
        out_specs=(anyspec, anyspec, anyspec, vm),
        scratch_shapes=scratch,
        compiler_params=pltpu.CompilerParams(
            collective_id=0, has_side_effects=True, vmem_limit_bytes=61 * 2**20 - 2**19
        ),
        name="two_sections",
    )(
        jnp.transpose(embeds, (0, 2, 1, 3)), jnp.transpose(cotangent, (0, 2, 1, 3)), lengths, norm_gains,
        jnp.transpose(w_qkv[0], (1, 0, 2)), w_out[0], w_up[0], w_down[0],
    )
    outs = pl.pallas_call(
        unpack,
        out_shape=(rows, rows, gain) + grads,
        in_specs=[hbm] * 3 + [vm],
        out_specs=(hbm, hbm, vm) + (hbm,) * 4,
        scratch_shapes=[V(rows.shape, BF), V(rows.shape, BF), V((3, ROWS, 1024), F32)]
        + [V(g.shape, F32) for g in (grads[0], grads[1], grads[2], grads[3])] + [D((11,))],
        compiler_params=pltpu.CompilerParams(vmem_limit_bytes=60 * 2**20),
        name="results",
    )(*outs)
    lo, ge, gg, gq, go, gu, gdn = outs
    return (
        jnp.transpose(lo, (0, 2, 1, 3)), jnp.transpose(ge, (0, 2, 1, 3)), gg,
        jnp.transpose(gq, (1, 0, 2))[None], go[None], gu[None], gdn[None],
    )


def solution(mesh):
    fits = tuple(mesh.shape[name] for name in ("section", "dp", "mp")) == (2, 8, 2)
    return jax.shard_map(
        on_device_kernel if fits else on_device,
        mesh=mesh,
        in_specs=(
            P(None, ("dp", "mp"), None, None),
            P(None, "dp", None),
            P("section", None, None),
            P("section", None, None, "mp"),
            P("section", "mp", None),
            P("section", None, "mp"),
            P("section", "mp", None),
            P(None, ("dp", "mp"), None, None),
        ),
        out_specs=(
            P(None, ("dp", "mp"), None, None),
            P(None, ("dp", "mp"), None, None),
            P("section", None, None),
            P("section", "dp", None, "mp"),
            P("section", "mp", "dp"),
            P("section", "dp", "mp"),
            P("section", "mp", "dp"),
        ),
        check_vma=False,
    )
```

```python
import functools
import math

import jax
import jax.numpy as jnp
from jax import lax
from jax.experimental import pallas as pl
from jax.experimental.pallas import tpu as pltpu
from jax.sharding import PartitionSpec as P

HEAD_DIM = 64


norm_eps = 1e-05
masked_fill = -1e30
rotary_base = 10000.0


def passed_along(value, axis, steps):
    count = lax.axis_size(axis)
    leading, last = (max(0, -steps), min(count, count - steps))
    return lax.ppermute(value, axis, [(source, source + steps) for source in range(leading, last)])


def rms_scale(values, gain_row):
    return (
        values * lax.rsqrt(jnp.mean(values * values, axis=-1, keepdims=True) + norm_eps) * gain_row
    )


def rotate(values, cos_tab, sin_tab):
    half_dim = values.shape[-1] // 2
    first_half = values[..., :half_dim]
    second_half = values[..., half_dim:]
    cos_rows = cos_tab[:, None, :]
    sin_rows = sin_tab[:, None, :]
    return jnp.concatenate(
        [
            first_half * cos_rows - second_half * sin_rows,
            second_half * cos_rows + first_half * sin_rows,
        ],
        axis=-1,
    )


def global_context(length_row, frames):
    doc_ends = jnp.cumsum(length_row)
    places = jnp.arange(frames, dtype=jnp.int32)
    passed = (places[:, None] >= doc_ends[None, :]).astype(jnp.int32)
    segment = jnp.sum(passed, axis=1)
    offsets = places - jnp.sum(passed * length_row[None, :], axis=1)
    allowed = (segment[:, None] == segment[None, :]) & (places[None, :] <= places[:, None])
    half_dim = HEAD_DIM // 2
    frequency = jnp.exp(
        jnp.arange(half_dim, dtype=jnp.float32) * (-2.0 * math.log(rotary_base) / HEAD_DIM)
    )
    angles = offsets.astype(jnp.float32)[:, None] * frequency[None, :]
    return (allowed, jnp.cos(angles), jnp.sin(angles))


def global_attend(projected, context):
    allowed, cos_tab, sin_tab = context
    attn_scale = 1.0 / math.sqrt(HEAD_DIM)
    row_total, _, local_width = projected.shape
    head_count = local_width // HEAD_DIM
    query_rows = rotate(
        projected[:, 0].reshape(row_total, head_count, HEAD_DIM), cos_tab, sin_tab
    ).astype(jnp.bfloat16)
    key_rows = rotate(
        projected[:, 1].reshape(row_total, head_count, HEAD_DIM), cos_tab, sin_tab
    ).astype(jnp.bfloat16)
    value_rows = projected[:, 2].reshape(row_total, head_count, HEAD_DIM).astype(jnp.bfloat16)
    scores = (
        jnp.einsum("qhd,khd->hqk", query_rows, key_rows, preferred_element_type=jnp.float32)
        * attn_scale
    )
    scores = jnp.where(allowed[None], scores, masked_fill)
    score_peak = jnp.max(scores, axis=-1, keepdims=True)
    exp_scores = jnp.exp(scores - score_peak)
    row_sums = jnp.sum(exp_scores, axis=-1, keepdims=True)
    weights_low = (exp_scores / row_sums).astype(jnp.bfloat16)
    mixed_rows = jnp.einsum(
        "hqk,khd->qhd", weights_low, value_rows, preferred_element_type=jnp.float32
    )
    log_total = score_peak + jnp.log(row_sums)
    return (
        mixed_rows.reshape(row_total, local_width).astype(jnp.bfloat16),
        (query_rows, key_rows, value_rows, log_total),
    )


def global_attend_back(attn_saved, context, grad_mixed):
    query_rows, key_rows, value_rows, log_total = attn_saved
    allowed, cos_tab, sin_tab = context
    attn_scale = 1.0 / math.sqrt(HEAD_DIM)
    row_total, head_count, _ = query_rows.shape
    grad_heads = grad_mixed.reshape(row_total, head_count, HEAD_DIM)
    scores = (
        jnp.einsum("qhd,khd->hqk", query_rows, key_rows, preferred_element_type=jnp.float32)
        * attn_scale
    )
    prob_rows = jnp.where(allowed[None], jnp.exp(scores - log_total), 0.0)
    grad_values = jnp.einsum(
        "hqk,qhd->khd",
        prob_rows.astype(jnp.bfloat16),
        grad_heads,
        preferred_element_type=jnp.float32,
    )
    grad_probs = jnp.einsum(
        "qhd,khd->hqk", grad_heads, value_rows, preferred_element_type=jnp.float32
    )
    grad_scores = (
        prob_rows * (grad_probs - jnp.sum(grad_probs * prob_rows, axis=-1, keepdims=True))
    ).astype(jnp.bfloat16)
    grad_query = (
        jnp.einsum("hqk,khd->qhd", grad_scores, key_rows, preferred_element_type=jnp.float32)
        * attn_scale
    )
    grad_keys = (
        jnp.einsum("hqk,qhd->khd", grad_scores, query_rows, preferred_element_type=jnp.float32)
        * attn_scale
    )
    grad_query = rotate(grad_query, cos_tab, -sin_tab)
    grad_keys = rotate(grad_keys, cos_tab, -sin_tab)
    stacked = jnp.stack([grad_query, grad_keys, grad_values], axis=1)
    return stacked.reshape(row_total, 3, head_count * HEAD_DIM).astype(jnp.bfloat16)


def local_attend(projected, context):
    attn_scale = 1.0 / math.sqrt(HEAD_DIM)
    row_total, _, local_width = projected.shape
    head_count = local_width // HEAD_DIM
    frames = row_total // 3
    qkv_parts = projected.reshape(frames, 3, 3, head_count, HEAD_DIM).astype(jnp.bfloat16)
    query_rows = qkv_parts[:, :, 0]
    key_rows = qkv_parts[:, :, 1]
    value_rows = qkv_parts[:, :, 2]
    scores = (
        jnp.einsum("fihd,fjhd->fhij", query_rows, key_rows, preferred_element_type=jnp.float32)
        * attn_scale
    )
    scores = jnp.where(context[None, None], scores, masked_fill)
    score_peak = jnp.max(scores, axis=-1, keepdims=True)
    exp_scores = jnp.exp(scores - score_peak)
    row_sums = jnp.sum(exp_scores, axis=-1, keepdims=True)
    weights_low = (exp_scores / row_sums).astype(jnp.bfloat16)
    mixed_rows = jnp.einsum(
        "fhij,fjhd->fihd", weights_low, value_rows, preferred_element_type=jnp.float32
    )
    log_total = score_peak + jnp.log(row_sums)
    return (
        mixed_rows.reshape(row_total, local_width).astype(jnp.bfloat16),
        (query_rows, key_rows, value_rows, log_total),
    )


def local_attend_back(attn_saved, context, grad_mixed):
    query_rows, key_rows, value_rows, log_total = attn_saved
    attn_scale = 1.0 / math.sqrt(HEAD_DIM)
    frames, _, head_count, _ = query_rows.shape
    grad_heads = grad_mixed.reshape(frames, 3, head_count, HEAD_DIM)
    scores = (
        jnp.einsum("fihd,fjhd->fhij", query_rows, key_rows, preferred_element_type=jnp.float32)
        * attn_scale
    )
    prob_rows = jnp.where(context[None, None], jnp.exp(scores - log_total), 0.0)
    grad_values = jnp.einsum(
        "fhij,fihd->fjhd",
        prob_rows.astype(jnp.bfloat16),
        grad_heads,
        preferred_element_type=jnp.float32,
    )
    grad_probs = jnp.einsum(
        "fihd,fjhd->fhij", grad_heads, value_rows, preferred_element_type=jnp.float32
    )
    grad_scores = (
        prob_rows * (grad_probs - jnp.sum(grad_probs * prob_rows, axis=-1, keepdims=True))
    ).astype(jnp.bfloat16)
    grad_query = (
        jnp.einsum("fhij,fjhd->fihd", grad_scores, key_rows, preferred_element_type=jnp.float32)
        * attn_scale
    )
    grad_keys = (
        jnp.einsum("fhij,fihd->fjhd", grad_scores, query_rows, preferred_element_type=jnp.float32)
        * attn_scale
    )
    stacked = jnp.stack([grad_query, grad_keys, grad_values], axis=2)
    return stacked.reshape(frames * 3, 3, head_count * HEAD_DIM).astype(jnp.bfloat16)


def gather_project(normed, weight, form):
    piece_rows = lax.all_gather(normed, "mp", axis=0, tiled=True)
    return (piece_rows, jnp.einsum(form, piece_rows, weight, preferred_element_type=jnp.float32))


def reduce_rows(left, weight, form, row_count):

    def partial_term(first_row, count_rows):
        return jnp.einsum(form, left, weight, preferred_element_type=jnp.float32)

    return lax.psum_scatter(
        partial_term(jnp.int32(0), row_count * lax.axis_size("mp")),
        "mp",
        scatter_dimension=0,
        tiled=True,
    )


def reduce_grads(left, weight, form, row_count):

    def partial_term(first_row, count_rows):
        return jnp.einsum(form, left, weight, preferred_element_type=jnp.float32)

    return lax.psum_scatter(
        partial_term(jnp.int32(0), row_count * lax.axis_size("mp")),
        "mp",
        scatter_dimension=0,
        tiled=True,
    )


def gather_grads(grad_low):
    return lax.all_gather(grad_low, "mp", axis=0, tiled=True)


def layer_forward(frame_rows, weights, attend, context):
    gain_pair, w_qkv, w_out, w_up, w_down = weights
    row_count = frame_rows.shape[0]
    normed = rms_scale(frame_rows, gain_pair[0]).astype(jnp.bfloat16)
    normed_all, projected = gather_project(normed, w_qkv, "nd,dce->nce")
    mixed_rows, attn_saved = attend(projected, context)
    attn_rows = reduce_rows(mixed_rows, w_out, "ne,ed->nd", row_count)
    middle = frame_rows + attn_rows
    normed_mid = rms_scale(middle, gain_pair[1]).astype(jnp.bfloat16)
    normed_mid_all, up_all = gather_project(normed_mid, w_up, "nd,de->ne")
    hidden = jax.nn.gelu(up_all).astype(jnp.bfloat16)
    down_rows = reduce_rows(hidden, w_down, "nf,fd->nd", row_count)
    record = (normed_all, attn_saved, mixed_rows, middle, normed_mid_all, up_all, hidden)
    return (middle + down_rows, attn_rows + down_rows, record)


def layer_backward(frame_rows, weights, attend_back, context, record, grad_result):
    gain_pair, w_qkv, w_out, w_up, w_down = weights
    normed_all, attn_saved, mixed_rows, middle, normed_mid_all, up_all, hidden = record
    row_count = frame_rows.shape[0]
    grad_down_all = gather_grads(grad_result.astype(jnp.bfloat16))
    grad_w_down = jnp.einsum("nf,nd->fd", hidden, grad_down_all, preferred_element_type=jnp.float32)
    grad_hidden = jnp.einsum("nd,fd->nf", grad_down_all, w_down, preferred_element_type=jnp.float32)
    _, gelu_back = jax.vjp(jax.nn.gelu, up_all)
    grad_up = gelu_back(grad_hidden)[0].astype(jnp.bfloat16)
    grad_w_up = jnp.einsum("nd,ne->de", normed_mid_all, grad_up, preferred_element_type=jnp.float32)
    grad_normed_mid = reduce_grads(grad_up, w_up, "ne,de->nd", row_count)
    _, mid_back = jax.vjp(rms_scale, middle, gain_pair[1])
    grad_middle_part, grad_gain_mid = mid_back(grad_normed_mid)
    grad_middle = grad_result + grad_middle_part
    grad_attn_all = gather_grads(grad_middle.astype(jnp.bfloat16))
    grad_w_out = jnp.einsum(
        "ne,nd->ed", mixed_rows, grad_attn_all, preferred_element_type=jnp.float32
    )
    grad_mixed = jnp.einsum(
        "nd,ed->ne", grad_attn_all, w_out, preferred_element_type=jnp.float32
    ).astype(jnp.bfloat16)
    grad_projected = attend_back(attn_saved, context, grad_mixed)
    grad_w_qkv = jnp.einsum(
        "nd,nce->dce", normed_all, grad_projected, preferred_element_type=jnp.float32
    )
    grad_normed = reduce_grads(grad_projected, w_qkv, "nce,dce->nd", row_count)
    _, first_back = jax.vjp(rms_scale, frame_rows, gain_pair[0])
    grad_rows_part, grad_gain_first = first_back(grad_normed)
    grad_frame_rows = grad_middle + grad_rows_part
    layer_grads = (
        jnp.stack([grad_gain_first, grad_gain_mid]),
        grad_w_qkv,
        grad_w_out,
        grad_w_up,
        grad_w_down,
    )
    return (grad_frame_rows, layer_grads)


def on_device(embeds, lengths, norm_gains, w_qkv, w_out, w_up, w_down, cotangent):
    weights = (norm_gains[0], w_qkv[0], w_out[0], w_up[0], w_down[0])
    micro_count = embeds.shape[0]
    shard_rows = embeds.shape[1]
    width = embeds.shape[-1]
    frames = shard_rows * lax.axis_size("mp")
    is_first = lax.axis_index("section") == 0
    local_allowed = jnp.tril(jnp.ones((3, 3), dtype=jnp.bool_))
    gain_total = jnp.zeros(norm_gains.shape[1:], jnp.float32)
    weight_totals = tuple((jnp.zeros(weight.shape, jnp.float32) for weight in weights[1:]))
    totals = (gain_total,) + weight_totals
    y_part = jnp.zeros(embeds.shape, jnp.float32)
    e_part = jnp.zeros(embeds.shape, jnp.float32)
    zero_send = jnp.zeros((shard_rows, width), jnp.bfloat16)

    def add_grads(running, layer_grads):
        run_gain, run_qkv, run_out, run_up, run_down = running
        part_gain, part_qkv, part_out, part_up, part_down = layer_grads
        return (
            run_gain + part_gain,
            run_qkv + part_qkv,
            run_out + part_out,
            run_up + part_up,
            run_down + part_down,
        )

    def global_forward(micro_index):
        context = global_context(lengths[micro_index, 0], frames)
        frame_in = jnp.sum(embeds[micro_index].astype(jnp.float32), axis=1)
        result, _, record = layer_forward(frame_in, weights, global_attend, context)
        return (frame_in, context, result, record)

    def pick(first_value, second_value):
        return jnp.where(is_first, first_value, second_value)

    carry_state = (totals, y_part, e_part)
    forward_recv = zero_send
    backward_recv = zero_send
    for tick_index in range(micro_count + 2):

        def first_section(state_in):
            running, y_state, e_state = state_in
            send_fwd = zero_send
            if tick_index < micro_count:
                _, _, result, _ = global_forward(tick_index)
                send_fwd = result.astype(jnp.bfloat16)
                joined = (
                    embeds[tick_index].astype(jnp.float32)
                    + send_fwd.astype(jnp.float32)[:, None, :]
                )
                y_state = y_state.at[tick_index].set(joined)
            if tick_index >= 2:
                micro_index = tick_index - 2
                frame_in, context, _, record = global_forward(micro_index)
                grad_frame, layer_grads = layer_backward(
                    frame_in,
                    weights,
                    global_attend_back,
                    context,
                    record,
                    backward_recv.astype(jnp.float32),
                )
                running = add_grads(running, layer_grads)
                e_state = e_state.at[micro_index].set(
                    jnp.broadcast_to(grad_frame[:, None, :], e_state.shape[1:])
                )
            return ((running, y_state, e_state), send_fwd, zero_send)

        def second_section(state_in):
            running, y_state, e_state = state_in
            send_back = zero_send
            if 1 <= tick_index <= micro_count:
                micro_index = tick_index - 1
                local_in = (
                    embeds[micro_index].astype(jnp.float32)
                    + forward_recv.astype(jnp.float32)[:, None, :]
                )
                local_in = local_in.reshape(shard_rows * 3, width)
                _, branches, record = layer_forward(local_in, weights, local_attend, local_allowed)
                grad_seed = (
                    cotangent[micro_index].astype(jnp.float32).reshape(shard_rows * 3, width)
                )
                grad_local, layer_grads = layer_backward(
                    local_in, weights, local_attend_back, local_allowed, record, grad_seed
                )
                running = add_grads(running, layer_grads)
                y_state = y_state.at[micro_index].set(branches.reshape(shard_rows, 3, width))
                grad_frames = grad_local.reshape(shard_rows, 3, width)
                e_state = e_state.at[micro_index].set(grad_frames)
                send_back = jnp.sum(grad_frames, axis=1).astype(jnp.bfloat16)
            return ((running, y_state, e_state), zero_send, send_back)

        first_result = first_section(carry_state)
        second_result = second_section(carry_state)
        carry_state, send_fwd, send_back = jax.tree.map(pick, first_result, second_result)
        if tick_index < micro_count:
            forward_recv = passed_along(send_fwd, "section", 1)
        if 1 <= tick_index <= micro_count:
            backward_recv = passed_along(send_back, "section", -1)
    totals, y_part, e_part = carry_state
    gain_total, grad_qkv, grad_out, grad_up, grad_down = totals
    grad_qkv, grad_out, grad_up, grad_down = (
        lax.psum_scatter(grad_qkv, "dp", scatter_dimension=0, tiled=True),
        lax.psum_scatter(grad_out, "dp", scatter_dimension=1, tiled=True),
        lax.psum_scatter(grad_up, "dp", scatter_dimension=0, tiled=True),
        lax.psum_scatter(grad_down, "dp", scatter_dimension=1, tiled=True),
    )
    gain_total = lax.psum(gain_total, ("dp", "mp"))
    y_sum, e_sum = (
        lax.psum(y_part.astype(jnp.bfloat16), "section").astype(jnp.float32),
        lax.psum(e_part.astype(jnp.bfloat16), "section").astype(jnp.float32),
    )
    return (
        y_sum.astype(jnp.bfloat16),
        e_sum.astype(jnp.bfloat16),
        gain_total[None],
        grad_qkv[None],
        grad_out[None],
        grad_up[None],
        grad_down[None],
    )


BF = jnp.bfloat16
F32 = jnp.float32
MESH = pl.DeviceIdType.MESH
SLOTS = 5
CHUNKS = 9
HELPED = 2
ALONG = 1
ROWS = 256
UNROLL = 4


def dot_nn(left, right):
    return lax.dot_general(left, right, (((1,), (0,)), ((), ())), preferred_element_type=F32)


def dot_nt(left, right):
    return lax.dot_general(left, right, (((1,), (1,)), ((), ())), preferred_element_type=F32)


def dot_tn(left, right):
    return lax.dot_general(left, right, (((0,), (0,)), ((), ())), preferred_element_type=F32)


def gelu_tanh(u):
    c0 = math.sqrt(2.0 / math.pi)
    return jnp.tanh(u * (c0 + (c0 * 0.044715) * (u * u)))


def gelu_slope(u, th):
    c0 = math.sqrt(2.0 / math.pi)
    return 0.5 * (1.0 + th) + 0.5 * u * (1.0 - th * th) * (c0 + (3.0 * 0.044715 * c0) * (u * u))


def loop(lower, upper, step, unroll=1):
    def wrapped(i, carry):
        step(i)
        return carry

    lax.fori_loop(lower, upper, wrapped, 0, unroll=unroll)


def grouped(count, work, store, size=4):
    def group(g):
        done = [work(g * size + t) for t in range(size)]
        for t in range(size):
            store(g * size + t, *done[t])

    loop(0, count // size, group)


def by16(i):
    return pl.ds(pl.multiple_of(i * 16, 16), 16)


def by512(i):
    return pl.ds(pl.multiple_of(i * 512, 512), 512)


def halves16(i):
    return lax.div(i, 8), lax.rem(lax.div(i, 4), 2), pl.ds(pl.multiple_of(lax.rem(i, 4) * 16, 16), 16)


def own16(i, m):
    mb, r = lax.div(i, 4), pl.multiple_of(lax.rem(i, 4) * 16, 16)
    return mb, pl.ds(r, 16), pl.ds(pl.multiple_of(mb * 128 + m * 64 + r, 16), 16)


def swap_halves(v):
    lane = lax.broadcasted_iota(jnp.int32, v.shape, 1)
    return jnp.where(lax.rem(lane, 64) < 32, pltpu.roll(v, 96, 1), pltpu.roll(v, 32, 1))


def body(
    emb, cot, lens, gains, wq_h, wo_h, wu_h, wd_h,
    lo_h, ge_h, g_h, gg_o,
    wq, wo, wu, wd, em, gd, sr, xm, ab, bm, qk, ob, dob, uph, xs, xr, tb,
    cs, tabs, st, gga, ggr, gpart, rg, ryz,
    gsem, wsem, esem, exs, exr, csem, cxs, cxr, mps, mpr, hops, hopr, lol, los, lor, dls, dlr,
    gel, ges, ger, ggs, ggrs, gms, gmr, ysn, yrc, zrs, zrr, zls, zlr,
    lys, lyr, frs, frr, fls, flr, fys, fyr, has, har, hbs, hbr, hzrs, hzrr, hzls, hzlr, hres, hrer, sts, strc, xas, xar, xms, xmr, das, dar, dms, dmr, ycr, rcr, lcr,
):
    s = lax.axis_index("section")
    d = lax.axis_index("dp")
    m = lax.axis_index("mp")
    y = lax.rem(d, 2)
    z = lax.div(d, 2)
    peer = (s, d, 1 - m)
    across = (1 - s, d, m)
    ypeer = (s, d + 1 - 2 * y, m)
    zup = (s, jnp.minimum(d + 2, 7), m)
    zdown = (s, jnp.maximum(d - 2, 0), m)
    frame = s == 0
    code = s == 1
    scale = 1.0 / math.sqrt(HEAD_DIM)

    def remote(src, dst, ssem, rsem, to):
        return pltpu.make_async_remote_copy(
            src_ref=src, dst_ref=dst, send_sem=ssem, recv_sem=rsem, device_id=to, device_id_type=MESH
        )

    def local(src, dst, sem):
        return pltpu.make_async_copy(src, dst, sem)

    w_copies = [local(a, b, wsem.at[i]) for i, (a, b) in enumerate(((wq_h, wq), (wo_h, wo), (wu_h, wu), (wd_h, wd)))]
    e_local = [local(emb, em.at[:, :, m], esem)]
    c_local = [local(cot.at[:, c], gd.at[c, :, m], csem.at[c]) for c in range(3)]
    for cp in e_local:
        cp.start()
    w_copies[0].start()

    bar = pltpu.get_barrier_semaphore()
    pl.semaphore_signal(bar, 1, device_id=peer, device_id_type=MESH)
    pl.semaphore_signal(bar, 1, device_id=across, device_id_type=MESH)
    for t in range(1, 8):
        pl.semaphore_signal(bar, 1, device_id=(s, lax.rem(d + t, 8), m), device_id_type=MESH)
    with jax.named_scope("barrier"):
        pl.semaphore_wait(bar, 9)

    e_far = [remote(emb, em.at[:, :, m], exs, exr, peer)]
    c_far = [remote(cot.at[:, c], gd.at[c, :, m], cxs.at[c], cxr.at[c], peer) for c in range(3)]
    for cp in e_far:
        cp.start()
    for cp in w_copies[1:]:
        cp.start()

    hop = [remote(sr.at[:, m], sr.at[:, m], hops.at[0], hopr.at[0], across),
           remote(sr.at[:, m], sr.at[:, m], hops.at[1], hopr.at[1], peer)]
    hop2 = [
        remote(sr.at[:, m, :, c * 512 : c * 512 + 512],
               ryz.at[pl.ds(d * 4 + c * 2, 2), pl.ds(pl.multiple_of(m * 64, 64), 64)],
               hops.at[2 + c], hopr.at[2 + c], across)
        for c in range(2)
    ]
    lo_local = [local(em.at[:, :, 1 - m], lo_h, lol)]
    lo_far = [remote(em.at[:, :, 1 - m], lo_h, los, lor, across)]
    dl_far = [remote(em.at[:, :, m], em.at[:, :, 1 - m], dls, dlr, across)]
    ge_local = [local(em.at[:, :, 1 - m], ge_h, gel)]
    ge_far = [remote(em.at[:, :, 1 - m], ge_h, ges, ger, across)]

    grads_out = [local(xm.at[t], g_h.at[t], gsem.at[t]) for t in range(3)]
    gga[...] = jnp.zeros_like(gga)

    def rms(v):
        return lax.rsqrt(jnp.mean(v * v, axis=-1, keepdims=True) + norm_eps)

    def exchange(recv_slot, send_slot, whole):
        mine = slice(None) if whole else 1 - m
        return remote(xs.at[send_slot, :, mine], xr.at[recv_slot, :, mine], mps.at[send_slot], mpr.at[recv_slot], peer)

    def put_xs(slot, cols, t):
        xs[slot, :, :, :, cols] = t.astype(BF).reshape(2, 2, 64, t.shape[-1])

    def summed(recv_slot, send_slot, i):
        mb, mh, r = halves16(i)
        return xs[send_slot, mb, mh, r].astype(F32) + xr[recv_slot, mb, mh, r].astype(F32)

    def summed_own(recv_slot, send_slot, i):
        mb, r, _ = own16(i, m)
        return xs[send_slot, mb, m, r].astype(F32) + xr[recv_slot, mb, m, r].astype(F32)

    def out_block(o, recv_slot, send_slot):
        for n in range(2):
            put_xs(send_slot, slice(n * 512, n * 512 + 512), dot_nn(o, wo[:, n * 512 : n * 512 + 512]))
        exchange(recv_slot, send_slot, True).start()

    def up_block(b_in, put):
        for f in range(4):
            t = dot_nn(b_in, wu[:, f * 512 : f * 512 + 512])
            for g in range(8):
                put(f, slice(g * 32, g * 32 + 32), t[g * 32 : g * 32 + 32])

    def down_block(get_hid, recv_slot, send_slot):
        for n in range(2):
            cols = slice(n * 512, n * 512 + 512)
            t = dot_nn(get_hid(0), wd[0:512, cols])
            for f in range(1, 4):
                t = t + dot_nn(get_hid(f), wd[f * 512 : f * 512 + 512, cols])
            put_xs(send_slot, cols, t)
        exchange(recv_slot, send_slot, False).start()

    def dff_block(g_low, page, put_hid, recv_slot, send_slot):
        for f in range(4):
            t = dot_nt(g_low, wd[f * 512 : f * 512 + 512])
            for g in range(8):
                at = slice(g * 32, g * 32 + 32)
                u = uph[page(f), at]
                th = gelu_tanh(u)
                if put_hid is not None:
                    put_hid(f, at, 0.5 * u * (1.0 + th))
                uph[page(f), at] = gelu_slope(u, th) * t[g * 32 : g * 32 + 32].astype(BF)
        for n in range(2):
            at = slice(n * 512, n * 512 + 512)
            t = dot_nt(uph[page(0)], wu[at, 0:512])
            for f in range(1, 4):
                t = t + dot_nt(uph[page(f)], wu[at, f * 512 : f * 512 + 512])
            put_xs(send_slot, at, t)
        exchange(recv_slot, send_slot, True).start()

    def dqkv_block(page, recv_slot, send_slot):
        for n in range(2):
            at = slice(n * 512, n * 512 + 512)
            t = dot_nt(qk[page(0)], wq[0, at])
            for c in range(1, 3):
                t = t + dot_nt(qk[page(c)], wq[c, at])
            put_xs(send_slot, at, t)
        exchange(recv_slot, send_slot, False).start()

    def norm_back(v, grad, gain):
        sc = rms(v)
        u = grad * gain
        vn = v * sc
        corr = jnp.mean(vn * u, axis=-1, keepdims=True)
        return sc * (u - vn * corr), grad * vn

    def add_gain(row, part):
        gga[row] = gga[row] + (part[0:8] + part[8:16])

    def acc_at(i):
        t = lax.rem(i, 4)
        return lax.div(i, 4), pl.ds(pl.multiple_of(lax.div(t, 2) * 128, 128), 128), by512(lax.rem(t, 2))

    gm = remote(gpart.at[0], gpart.at[1], gms, gmr, peer)

    def gain_first():
        gpart[0] = jnp.broadcast_to(jnp.sum(gga[0], axis=0, keepdims=True), (8, 1024))
        gm.start()

    g_far = []
    for t in range(1, 8):
        o = lax.rem(d + t, 8)
        g_far.append((remote(ggr.at[d], ggr.at[d], ggs.at[t], ggrs.at[d], (s, o, m)),
                      remote(ggr.at[d], ggr.at[o], ggs.at[t], ggrs.at[o], (s, o, m))))

    def gain_second():
        gm.wait()
        own1 = jnp.sum(gga[1], axis=0, keepdims=True)
        ggr[d] = jnp.concatenate([gpart[0, 0:1] + gpart[1, 0:1], own1, jnp.zeros((6, 1024), F32)], axis=0)
        for cp, _ in g_far:
            cp.start()

    def gain_last():
        for cp, back in g_far:
            cp.wait_send()
            back.wait_recv()
        acc = ggr[0]
        for t in range(1, 8):
            acc = acc + ggr[t]
        gg_o[0] = acc[0:2]

    def ha(h, k):
        return 32 + h * 13 + k

    def hz(h, idx):
        return 32 + h * 13 + 8 + idx

    def hg(h):
        return (24, 16)[h]

    def help_a(h):
        return remote(uph.at[pl.ds(hg(h), 4), pl.ds(pl.multiple_of(y * 128, 128), 128)],
                      ryz.at[pl.ds(ha(h, 0), 4)], has.at[h], har.at[h], across)

    def help_b(h):
        return remote(uph.at[pl.ds(hg(h), 4), pl.ds(pl.multiple_of((1 - y) * 128, 128), 128)],
                      ryz.at[pl.ds(ha(h, 4), 4)], hbs.at[h], hbr.at[h], (1 - s, d + 1 - 2 * y, m))

    def help_right(h, k):
        return remote(ryz.at[ha(h, k)], ryz.at[hz(h, k + 1)], hzrs.at[h, k - 1], hzrr.at[h, k - 1], zup)

    def help_left(h, k):
        return remote(ryz.at[ha(h, k)], ryz.at[hz(h, k)], hzls.at[h, k], hzlr.at[h, k], zdown)

    def help_back(h):
        return remote(ryz.at[ha(h, z)], ryz.at[56 + h], hres.at[h], hrer.at[h], across)

    def add_pages(to, page):
        for g in range(4):
            at = slice(g * 32, g * 32 + 32)
            ryz[to, at] = (ryz[to, at].astype(F32) + ryz[page, at].astype(F32)).astype(BF)

    def help_start(h):
        help_a(h).wait_recv()
        help_b(h).wait_recv()

        def each(t):
            k = jnp.where(z < 2, 3 - t, t)
            add_pages(ha(h, k), ha(h, 4 + k))

            @pl.when((z == 0) & (k > 0))
            def _():
                help_right(h, k).start()

            @pl.when((z == 3) & (k < 3))
            def _():
                help_left(h, k).start()

        loop(0, 4, each)

    def help_pass(h, leg):
        def on_right(k):
            help_right(h, k).wait_recv()
            add_pages(ha(h, k), hz(h, k + 1))
            help_right(h, k).start()

        def on_left(k):
            help_left(h, k).wait_recv()
            add_pages(ha(h, k), hz(h, k))
            help_left(h, k).start()

        if leg == 0:
            @pl.when(z == 1)
            def _():
                on_right(3)
                on_right(2)

            @pl.when(z == 2)
            def _():
                on_left(0)
                on_left(1)
        else:
            @pl.when(z == 1)
            def _():
                on_left(0)

            @pl.when(z == 2)
            def _():
                on_right(3)

    def help_finish(h):
        @pl.when(z > 0)
        def _():
            help_right(h, z).wait_recv()
            add_pages(ha(h, z), hz(h, z + 1))

        @pl.when(z < 3)
        def _():
            help_left(h, z).wait_recv()
            add_pages(ha(h, z), hz(h, z))

        help_back(h).start()

    def help_sent(h):
        help_back(h).wait_send()
        for k in range(3):
            @pl.when(k + 1 > z)
            def _():
                help_right(h, k + 1).wait_send()

            @pl.when(k < z)
            def _():
                help_left(h, k).wait_send()

    def low_lanes():
        return lax.broadcasted_iota(jnp.int32, (128, 128), 1) < 64

    def stack_heads(v):
        zero = jnp.zeros_like(v)
        return jnp.concatenate([jnp.where(low_lanes(), v, zero), jnp.where(low_lanes(), zero, v)], axis=0)

    def side_by_side(v):
        return jnp.concatenate([v[0:128], v[128:256]], axis=1)

    def frame_allowed(mb):
        pos = lax.broadcasted_iota(jnp.int32, (128, 128), 0)
        lane = lax.broadcasted_iota(jnp.int32, (128, 128), 1)
        one = (lane <= pos) & (lane.astype(F32) >= cs[2, mb * 128 : mb * 128 + 128])
        return jnp.concatenate([one, one], axis=0)

    def frame_probs(places, q2, k):
        allowed = [frame_allowed(mb) for mb in range(2)]
        sc = [dot_nt(a, b) * scale for a, b in zip(q2, k)]
        sc = [jnp.where(allowed[mb], v, masked_fill) for (mb, _, _), v in zip(places, sc)]
        top = [jnp.max(v, axis=-1, keepdims=True) for v in sc]
        e = [jnp.exp(v - t) for v, t in zip(sc, top)]
        inv = [1.0 / jnp.sum(v, axis=-1, keepdims=True) for v in e]
        return [v * t for v, t in zip(e, inv)]

    def frame_places(g):
        return [
            (mb, slice(mb * 128, mb * 128 + 128), pl.ds(pl.multiple_of((g * 2 + t) * 128, 128), 128))
            for mb in range(2) for t in range(2)
        ]

    def frame_attend(b):
        def part(g):
            places = frame_places(g)
            q2 = [stack_heads(qk[b * 3, at, cols]) for _, at, cols in places]
            k = [qk[b * 3 + 1, at, cols] for _, at, cols in places]
            v2 = [stack_heads(qk[b * 3 + 2, at, cols]) for _, at, cols in places]
            p = [side_by_side(v.astype(BF)) for v in frame_probs(places, q2, k)]
            o = [dot_nn(v, w) for v, w in zip(p, v2)]
            for (_, at, cols), v in zip(places, o):
                ob[b, at, cols] = v.astype(BF)

        loop(0, 2, part)

    def frame_attend_back(b, do_slot):
        def part(g):
            places = frame_places(g)
            q2 = [stack_heads(qk[b * 3, at, cols]) for _, at, cols in places]
            k = [qk[b * 3 + 1, at, cols] for _, at, cols in places]
            v = [qk[b * 3 + 2, at, cols] for _, at, cols in places]
            do2 = [stack_heads(dob[do_slot, at, cols]) for _, at, cols in places]
            p = frame_probs(places, q2, k)
            dp = [dot_nt(a, c) for a, c in zip(do2, v)]
            mean = [jnp.sum(a * c, axis=-1, keepdims=True) for a, c in zip(dp, p)]
            ds = [(c * (a - t)).astype(BF) for a, c, t in zip(dp, p, mean)]
            dv = [dot_tn(a.astype(BF), c) for a, c in zip(p, do2)]
            dk = [dot_tn(a, c) for a, c in zip(ds, q2)]
            dq = [dot_nn(side_by_side(a), stack_heads(c)) for a, c in zip(ds, k)]
            for i, (_, at, cols) in enumerate(places):
                co, si = cs[0, at], cs[1, at]
                for c, t in ((0, dq[i] * scale), (1, dk[i] * scale)):
                    qk[b * 3 + c, at, cols] = (t * co - swap_halves(t) * si).astype(BF)
                qk[b * 3 + 2, at, cols] = dv[i].astype(BF)

        loop(0, 2, part)

    def frame_tables(b):
        for mb in range(2):
            at = slice(mb * 128, mb * 128 + 128)
            pos = lax.broadcasted_iota(jnp.int32, (128, 128), 0)
            lane = lax.broadcasted_iota(jnp.int32, (128, 128), 1)
            start = jnp.broadcast_to(st[b, mb : mb + 1], (128, 128)).T
            hot = ((pos.astype(F32) - start) == lane.astype(F32)).astype(BF)
            for c in range(2):
                cs[c, at] = dot_nn(hot, tabs[c, 0]) + dot_nn(hot, tabs[c, 1]) + dot_nn(hot, tabs[c, 2])
            cs[2, at] = start

    def frame_qkv(a_slot, b):
        for c in range(3):
            t = dot_nn(ab[a_slot], wq[c])
            for g in range(4):
                v = t[:, g * 128 : g * 128 + 128]
                if c < 2:
                    v = v * cs[0] + swap_halves(v) * cs[1]
                qk[b * 3 + c, :, g * 128 : g * 128 + 128] = v.astype(BF)

    def px(b, i):
        mb, r = lax.div(i, 8), by16(lax.rem(i, 8))
        q, k = lax.div(b, 2), lax.rem(b, 2) * 2
        return jnp.concatenate([rg[q, k, mb, r], rg[q, k + 1, mb, r]], axis=1).astype(F32)

    def put_px(b, i, v):
        mb, r = lax.div(i, 8), by16(lax.rem(i, 8))
        q, k = lax.div(b, 2), lax.rem(b, 2) * 2
        rg[q, k, mb, r] = v[:, 0:512].astype(BF)
        rg[q, k + 1, mb, r] = v[:, 512:1024].astype(BF)

    def ds_rows(b, i):
        mb, r = lax.div(i, 8), by16(lax.rem(i, 8))
        return jnp.concatenate([ryz[b * 4 + mb, r], ryz[b * 4 + 2 + mb, r]], axis=1).astype(F32)

    def ds_all(b):
        return jnp.concatenate(
            [ryz[pl.ds(b * 4, 2)].reshape(ROWS, 512), ryz[pl.ds(b * 4 + 2, 2)].reshape(ROWS, 512)], axis=1
        )

    mrows = pl.ds(pl.multiple_of(m * 64, 64), 64)

    def px_ref(b):
        return rg.at[lax.div(b, 2), pl.ds(lax.rem(b, 2) * 2, 2), :, mrows]

    def ds_ref(b):
        return ryz.at[pl.ds(b * 4, 4), mrows]

    def block_of(i):
        j = lax.div(i, 2)
        low = jnp.where(j == 0, 1, jnp.where(j == 1, 0, j))
        high = jnp.where(j == 0, 2, jnp.where(j == 1, 3, 3 - j))
        zz = jnp.where(z == 0, j, jnp.where(z == 1, low, jnp.where(z == 2, high, 3 - j)))
        other = lax.rem(i, 2)
        return zz * 2 + jnp.where(other == 0, y, 1 - y), zz, other

    def spread(ref, sems, rsem, ms, mr, i, with_peer):
        b, zz, other = block_of(i)

        def go(direction, to):
            remote(ref(b), ref(b), sems.at[zz, direction], rsem.at[b], to).start()

        @pl.when(other == 0)
        def _():
            go(2, ypeer)

            @pl.when((zz <= z) & (z < 3))
            def _():
                go(0, zup)

            @pl.when((zz >= z) & (z > 0))
            def _():
                go(1, zdown)

        if with_peer:
            remote(ref(b), ref(b), ms.at[b], mr.at[b], peer).start()

    def arrive(ref, sems, rsem, ms, mr, i):
        b, zz, _ = block_of(i)
        remote(ref(b), ref(b), sems.at[zz, 2], rsem.at[b], ypeer).wait_recv()
        spread(ref, sems, rsem, ms, mr, i, True)

    def drained(ref, sems, rsem, ms, mr, i, with_peer):
        b, zz, other = block_of(i)

        @pl.when(other == 0)
        def _():
            remote(ref(b), ref(b), sems.at[zz, 2], rsem.at[b], ypeer).wait_send()

            @pl.when((zz <= z) & (z < 3))
            def _():
                remote(ref(b), ref(b), sems.at[zz, 0], rsem.at[b], zup).wait_send()

            @pl.when((zz >= z) & (z > 0))
            def _():
                remote(ref(b), ref(b), sems.at[zz, 1], rsem.at[b], zdown).wait_send()

        if with_peer:
            remote(ref(b), ref(b), ms.at[b], mr.at[b], peer).wait_send()

    xset = (px_ref, xas, xar, xms, xmr)
    dset = (ds_ref, das, dar, dms, dmr)

    inner = (z == 1) | (z == 2)

    def arrive_early(which):
        arrive(*which, 1)
        arrive(*which, 2)

        @pl.when(inner)
        def _():
            arrive(*which, 4)

    def arrive_at(which, i):
        @pl.when((i == 3) & inner | (i == 4) & ~inner)
        def _():
            arrive(*which, 6)

        @pl.when((i == 2) & ~inner)
        def _():
            arrive(*which, 4)

        @pl.when((i == 2) | (i == 4) | (i == 6))
        def _():
            arrive(*which, i + 1)

    def halves_in(which, i):
        ref, _, _, ms, mr = which
        b, _, _ = block_of(i)
        remote(ref(b), ref(b), ms.at[b], mr.at[b], peer).wait_recv()

    def ring(e):
        t = lax.rem(e, 4)
        return jnp.where(t < 2, t + 1, t + 2), 1 + lax.rem(e, 2)

    mine128 = pl.ds(pl.multiple_of(d * 128, 128), 128)

    def lanes(i):
        return pl.ds(pl.multiple_of(i * 128, 128), 128)

    def hid_at(f):
        return slice(f * 256, f * 256 + 256)

    def gd_slice(b):
        page = b * 4 + lax.div(d, 4) * 2
        cols = pl.ds(pl.multiple_of(lax.rem(d, 4) * 128, 128), 128)
        return ryz[pl.ds(page, 2), :, cols].reshape(ROWS, 128).T

    def put_tb(f, at, v):
        tb[f * 256 + at.start : f * 256 + at.stop, 0:512] = v

    def frame_grad(chunk, left, right, first):
        at = acc_at(chunk)
        t = dot_nn(left, right)
        xm[at] = t if first else xm[at] + t

    def frame_grads_down(b, first):
        left = gd_slice(b)
        for f in range(4):
            frame_grad(f, left, tb[hid_at(f), 0:512], first)

    def frame_grads_up(b, bm_slot, bm_cols, first):
        left = bm[bm_slot, :, bm_cols].T
        for f in range(4):
            frame_grad(4 + f, left, uph[f * 8 + b], first)

    def frame_grads_attend(b, ga_slot, a_slot, a_cols, first):
        frame_grad(8, gd[ga_slot, :, :, :, mine128].reshape(ROWS, 128).T, ob[b], first)
        left = ab[a_slot, :, a_cols].T
        for c in range(3):
            frame_grad(9 + c, left, qk[b * 3 + c], first)

    @pl.when(frame)
    def _():
        pos = lax.broadcasted_iota(jnp.int32, (128, 128), 0)
        lane = lax.broadcasted_iota(jnp.int32, (128, 128), 1)
        freq = jnp.exp(lax.rem(lane, 32).astype(F32) * (-2.0 * math.log(rotary_base) / HEAD_DIM))
        angle = pos.astype(F32) * freq
        sine = jnp.sin(angle)
        for c, v in enumerate((jnp.cos(angle), jnp.where(lax.rem(lane, 64) < 32, -sine, sine))):
            for t in range(3):
                term = v.astype(BF)
                tabs[c, t] = term
                v = v - term.astype(F32)
        place = lax.broadcasted_iota(jnp.int32, (8, 128), 1)
        rows = []
        for mb in range(2):
            start = jnp.zeros((8, 128), jnp.int32)
            end = jnp.int32(0)
            for j in range(4):
                size = lens[mb, 0, j]
                end = end + size
                start = start + jnp.where(place >= end, size, 0)
            rows.append(start)
        which = lax.broadcasted_iota(jnp.int32, (8, 128), 0)
        st[d] = jnp.where(which == 0, rows[0], rows[1]).astype(F32)
        for t in range(1, 8):
            o = lax.rem(d + t, 8)
            remote(st.at[d], st.at[d], sts.at[t], strc.at[d], (s, o, m)).start()
        frame_tables(d)

        with jax.named_scope("embeds_wait"):
            for cp in e_local:
                cp.wait()
            for cp in e_far:
                cp.wait()

        gain0 = gains[0, 0:1]
        gain1 = gains[0, 1:2]

        def x_own(i):
            mb, mh, r = halves16(i)
            return em[mb, 0, mh, r].astype(F32) + em[mb, 1, mh, r].astype(F32) + em[mb, 2, mh, r].astype(F32)

        def rows_in(i):
            v = x_own(i)
            xm[2, by16(i)] = v
            ab[0, by16(i)] = (v * rms(v) * gain0).astype(BF)
            put_px(d, i, v)

        with jax.named_scope("own_qkv"):
            loop(0, 16, rows_in, unroll=UNROLL)
            spread(*xset, 0, False)
            w_copies[0].wait()
            frame_qkv(0, d)
        with jax.named_scope("own_attend"):
            frame_attend(d)
        w_copies[1].wait()
        with jax.named_scope("own_out"):
            out_block(ob[d], 0, 0)
            w_copies[2].wait()
            exchange(0, 0, True).wait()

        def rows_mid(i):
            v = xm[2, by16(i)] + summed(0, 0, i)
            return v, (v * rms(v) * gain1).astype(BF)

        def put_mid(i, v, w):
            xm[2, by16(i)] = v
            bm[0, by16(i)] = w

        def put_own(f, at, u):
            uph[f * 8 + d, at] = u.astype(BF)
            u = u.astype(BF)
            put_tb(f, at, 0.5 * u * (1.0 + gelu_tanh(u)))

        with jax.named_scope("own_ff"):
            grouped(16, rows_mid, put_mid)
            up_block(bm[0], put_own)
            w_copies[3].wait()
            down_block(lambda f: tb[hid_at(f), 0:512], 3, 0)
            exchange(3, 0, False).wait()

        def rows_res(i):
            mb, r, row = own16(i, m)
            sr[mb, m, r] = (xm[2, row] + summed_own(3, 0, i)).astype(BF)

        loop(0, 8, rows_res, unroll=UNROLL)
        hop[0].start()

        for t in range(1, 8):
            o = lax.rem(d + t, 8)
            remote(st.at[d], st.at[o], sts.at[t], strc.at[o], (s, o, m)).wait()

        def others_in(i):
            b, _, _ = block_of(i)
            halves_in(xset, i)
            frame_tables(b)

            def rows_norm(t):
                v = px(b, t)
                ab[2, by16(t)] = (v * rms(v) * gain0).astype(BF)

            loop(0, 16, rows_norm, unroll=UNROLL)
            ab[1, :, lanes(i)] = ab[2, :, mine128]
            frame_qkv(2, b)
            frame_attend(b)
            out_block(ob[b], *ring(i))

        def others_ff(i):
            b, _, _ = block_of(i)
            recv_slot, send_slot = ring(i)
            exchange(recv_slot, send_slot, True).wait()
            drained(*xset, i, True)

            def rows_m(t):
                v = px(b, t) + summed(recv_slot, send_slot, t)
                return v, (v * rms(v) * gain1).astype(BF)

            def put_m(t, v, w):
                put_px(b, t, v)
                bm[2, by16(t)] = w

            grouped(16, rows_m, put_m)
            bm[1, :, lanes(i)] = bm[2, :, mine128]

            def put_up(f, at, u):
                uph[f * 8 + b, at] = u.astype(BF)

            up_block(bm[2], put_up)

        with jax.named_scope("oth_arrive"):
            arrive_early(xset)

        def others(i):
            with jax.named_scope("oth_arrive"):
                arrive_at(xset, i)

            @pl.when(i < 8)
            def _():
                with jax.named_scope("oth_in"):
                    others_in(i)

            @pl.when(i > 1)
            def _():
                with jax.named_scope("oth_ff"):
                    others_ff(i - 1)

        loop(1, 9, others)
        drained(*xset, 0, False)
        hop[0].wait_send()

        with jax.named_scope("help_start0"):
            help_start(0)

        with jax.named_scope("d_sent_wait"):
            for cp in hop2:
                cp.wait_recv()
            spread(*dset, 0, True)
            halves_in(dset, 0)
        with jax.named_scope("own_dff"):
            dff_block(ds_all(d), lambda f: f * 8 + d, put_tb, 0, 0)
            frame_grads_down(d, True)
        with jax.named_scope("help_pass0"):
            help_pass(0, 0)
        exchange(0, 0, True).wait()

        def rows_dmid(i):
            add, part = norm_back(xm[2, by16(i)], summed(0, 0, i), gain1)
            return ds_rows(d, i) + add, part

        def put_dmid(i, dm, part):
            mb, mh, r = halves16(i)
            xm[2, by16(i)] = dm
            gd[0, mb, mh, r] = dm.astype(BF)
            add_gain(1, part)

        with jax.named_scope("own_dmid"):
            grouped(16, rows_dmid, put_dmid)
            dob[0] = dot_nt(gd[0].reshape(ROWS, 1024), wo[...]).astype(BF)
        with jax.named_scope("arrive_early"):
            arrive_early(dset)
        frame_tables(d)
        with jax.named_scope("own_attend_back"):
            frame_attend_back(d, 0)
        dqkv_block(lambda c: d * 3 + c, 3, 0)
        with jax.named_scope("own_grads"):
            frame_grads_up(d, 0, mine128, True)
        exchange(3, 0, False).wait()

        def rows_dx(i):
            mb, r, row = own16(i, m)
            v = em[mb, 0, m, r].astype(F32) + em[mb, 1, m, r].astype(F32) + em[mb, 2, m, r].astype(F32)
            add, part = norm_back(v, summed_own(3, 0, i), gain0)
            return xm[2, row] + add, part

        def put_dx(i, dv, part):
            mb, r, _ = own16(i, m)
            top = dv.astype(BF)
            em[mb, 0, m, r] = top
            em[mb, 1, m, r] = (dv - top.astype(F32)).astype(BF)
            add_gain(0, part)

        grouped(8, rows_dx, put_dx)
        gain_first()

        def rows_ge(i):
            mb, r, _ = own16(i, m)
            dv = em[mb, 0, m, r].astype(F32) + em[mb, 1, m, r].astype(F32)
            return tuple((em[mb, c, 1 - m, r].astype(F32) + dv).astype(BF) for c in range(3))

        def put_ge(i, *parts):
            mb, r, _ = own16(i, m)
            for c in range(3):
                em[mb, c, 1 - m, r] = parts[c]

        def embed_grads():
            for cp in dl_far:
                cp.wait_recv()
            grouped(8, rows_ge, put_ge)
            for cp in ge_local + ge_far:
                cp.start()

        gain_second()
        with jax.named_scope("help_pass0"):
            help_pass(0, 1)
        frame_grads_attend(d, 0, 0, mine128, True)

        def back_first(i):
            b, _, _ = block_of(i)
            halves_in(dset, i)
            dff_block(ds_all(b), lambda f: f * 8 + b, put_tb, *ring(i + 7))
            frame_grads_down(b, False)

        def back_second(i):
            b, _, _ = block_of(i)
            recv_slot, send_slot = ring(i + 7)
            exchange(recv_slot, send_slot, True).wait()

            def rows_dm(t):
                mb, mh, r = halves16(t)
                add, _ = norm_back(px(b, t), summed(recv_slot, send_slot, t), gain1)
                gd[1, mb, mh, r] = (ds_rows(b, t) + add).astype(BF)

            loop(0, 16, rows_dm, unroll=UNROLL)
            dob[0] = dot_nt(gd[1].reshape(ROWS, 1024), wo[...]).astype(BF)
            frame_tables(b)
            frame_attend_back(b, 0)
            frame_grads_up(b, 1, lanes(i), False)
            frame_grads_attend(b, 1, 1, lanes(i), False)

        def others_back(i):
            @pl.when(i < 8)
            def _():
                with jax.named_scope("oth_dff"):
                    back_first(i)

            with jax.named_scope("oth_arrive_d"):
                arrive_at(dset, i)

            @pl.when(i > 1)
            def _():
                with jax.named_scope("oth_rest"):
                    back_second(i - 1)

            @pl.when(i == 2)
            def _():
                with jax.named_scope("help_finish0"):
                    help_finish(0)

            @pl.when(i == 4)
            def _():
                with jax.named_scope("help_start1"):
                    help_start(1)

            @pl.when(i == 5)
            def _():
                with jax.named_scope("help_pass1"):
                    help_pass(1, 0)
                with jax.named_scope("embed_grads"):
                    embed_grads()

            @pl.when(i == 6)
            def _():
                with jax.named_scope("help_pass1"):
                    help_pass(1, 1)

            @pl.when(i == 7)
            def _():
                with jax.named_scope("help_finish1"):
                    help_finish(1)
        loop(1, 9, others_back)
        for h in range(HELPED):
            help_sent(h)
        loop(0, 8, lambda i: drained(*dset, i, True))
        for cp in grads_out:
            cp.start()
        gain_last()
        for cp in ge_local:
            cp.wait()
        for cp in ge_far:
            cp.wait_send()
        for cp in lo_far:
            cp.wait_recv()
        for cp in grads_out:
            cp.wait()

    def head_sum(prod):
        r0 = lax.broadcasted_iota(jnp.int32, (256, 256), 0)
        r1 = lax.broadcasted_iota(jnp.int32, (256, 256), 1)
        ones = (lax.div(r0, 64) == lax.div(r1, 64)).astype(BF)
        return dot_nn(prod, ones)

    def code_probs(q, k):
        probs = []
        for i in range(3):
            sc = [head_sum(q[i] * k[j]) * scale for j in range(i + 1)]
            top = functools.reduce(jnp.maximum, sc)
            e = [jnp.exp(v - top) for v in sc]
            inv = 1.0 / functools.reduce(jnp.add, e)
            probs.append([v * inv for v in e])
        return probs

    def code_part(i):
        return (pl.ds(pl.multiple_of(lax.div(i, 2) * 64, 64), 64), pl.ds(pl.multiple_of(lax.rem(i, 2) * 256, 256), 256))

    def code_attend(i):
        at, cols = code_part(i)
        q, k, v = ([qk[c * 3 + b, at, cols] for b in range(3)] for c in range(3))
        probs = code_probs(q, k)
        v = [w.astype(F32) for w in v]
        for t in range(3):
            o = functools.reduce(jnp.add, [probs[t][j].astype(BF).astype(F32) * v[j] for j in range(t + 1)])
            ob[t, at, cols] = o.astype(BF)

    def code_attend_back(i):
        at, cols = code_part(i)
        q, k, v = ([qk[c * 3 + b, at, cols] for b in range(3)] for c in range(3))
        do = [ob[3 + b, at, cols] for b in range(3)]
        probs = code_probs(q, k)
        all_dp = [[head_sum(do[t] * v[j]) for j in range(t + 1)] for t in range(3)]
        q, k, do = ([w.astype(F32) for w in x] for x in (q, k, do))
        dk = [0.0] * 3
        dv = [0.0] * 3
        for t in range(3):
            dp = all_dp[t]
            mean = functools.reduce(jnp.add, [dp[j] * probs[t][j] for j in range(t + 1)])
            dq = 0.0
            for j in range(t + 1):
                ds = (probs[t][j] * (dp[j] - mean)).astype(BF).astype(F32)
                dq = dq + ds * k[j]
                dk[j] = dk[j] + ds * q[t]
                dv[j] = dv[j] + probs[t][j].astype(BF).astype(F32) * do[t]
            qk[t, at, cols] = (dq * scale).astype(BF)
        for j in range(3):
            qk[3 + j, at, cols] = (dk[j] * scale).astype(BF)
            qk[6 + j, at, cols] = dv[j].astype(BF)

    def flip(get):
        def one(b):
            at = pl.ds(pl.multiple_of(b * 256, 256), 256)
            t = get(b)
            for g in range(4):
                tb[g * 256 : g * 256 + 256, at] = t[:, g * 256 : g * 256 + 256].T

        loop(0, 3, one)

    def ry(slot):
        return ryz.at[pl.ds(slot * 4, 4)]

    def rz(slot, idx):
        return SLOTS * 4 + slot * 5 + idx

    def sends(slot):
        return remote(rg.at[slot, :, 1 - y], ry(slot), ysn.at[slot], yrc.at[slot], ypeer)

    def right(slot, k):
        return remote(rg.at[slot, k, y], ryz.at[rz(slot, k + 1)], zrs.at[slot, k - 1], zrr.at[slot, k - 1], zup)

    def left(slot, k):
        return remote(rg.at[slot, k, y], ryz.at[rz(slot, k)], zls.at[slot, k], zlr.at[slot, k], zdown)

    def free_slot(slot, last=False):
        if not last:
            sends(slot).wait_send()
        for k in range(3):
            @pl.when(k + 1 > z)
            def _():
                right(slot, k + 1).wait_send()

            @pl.when(k < z)
            def _():
                left(slot, k).wait_send()

    def make_chunk(i, act, send=True):
        slot = lax.rem(i, SLOTS)

        @pl.when(i >= SLOTS)
        def _():
            free_slot(slot)

        def part(k):
            at = pl.ds(pl.multiple_of(k * 256, 256), 256)
            rg[slot, k] = dot_nn(tb[at, :], act()).astype(BF).reshape(2, 128, 512)

        loop(0, 4, part)

        @pl.when(i >= SLOTS)
        def _():
            pl.semaphore_wait(ycr, 1)

        if send:
            sends(slot).start()

    def make_help(h, act):
        def part(k):
            at = pl.ds(pl.multiple_of(k * 256, 256), 256)
            uph[hg(h) + k] = dot_nn(tb[at, :], act()).astype(BF)

        loop(0, 4, part)
        help_a(h).start()
        help_b(h).start()

    def fg(h):
        return (28, 12)[h]

    def fz(h):
        return (10, 16)[h]

    def along_right(h, k):
        return remote(uph.at[fg(h) + k], qk.at[fz(h) + k + 1], frs.at[h, k - 1], frr.at[h, k - 1], zup)

    def along_left(h, k):
        return remote(uph.at[fg(h) + k], qk.at[fz(h) + k], fls.at[h, k], flr.at[h, k], zdown)

    def along_y(h):
        return remote(uph.at[fg(h) + z, pl.ds(pl.multiple_of((1 - y) * 128, 128), 128)],
                      qk.at[fz(h) + 5, 0:128], fys.at[h], fyr.at[h], ypeer)

    def make_along(h, act):
        def part(k):
            at = pl.ds(pl.multiple_of(k * 256, 256), 256)
            uph[fg(h) + k] = dot_nn(tb[at, :], act()).astype(BF)

            @pl.when((z == 0) & (k > 0))
            def _():
                along_right(h, k).start()

            @pl.when((z == 3) & (k < 3))
            def _():
                along_left(h, k).start()

        loop(0, 4, part)

    def add_half(to, page):
        for g in range(8):
            at = slice(g * 32, g * 32 + 32)
            uph[to, at] = (uph[to, at].astype(F32) + qk[page, at].astype(F32)).astype(BF)

    def along_pass(h, leg):
        def on_right(k):
            along_right(h, k).wait_recv()
            add_half(fg(h) + k, fz(h) + k + 1)
            along_right(h, k).start()

        def on_left(k):
            along_left(h, k).wait_recv()
            add_half(fg(h) + k, fz(h) + k)
            along_left(h, k).start()

        if leg == 0:
            @pl.when(z == 1)
            def _():
                on_right(3)
                on_right(2)

            @pl.when(z == 2)
            def _():
                on_left(0)
                on_left(1)
        else:
            @pl.when(z == 1)
            def _():
                on_left(0)

            @pl.when(z == 2)
            def _():
                on_right(3)

    def along_sum(h):
        @pl.when(z > 0)
        def _():
            along_right(h, z).wait_recv()
            add_half(fg(h) + z, fz(h) + z + 1)

        @pl.when(z < 3)
        def _():
            along_left(h, z).wait_recv()
            add_half(fg(h) + z, fz(h) + z)

        along_y(h).start()

    def along_finish(h, chunk):
        along_y(h).wait()
        rows = pl.ds(pl.multiple_of(y * 128, 128), 128)
        xm[acc_at(chunk)] = uph[fg(h) + z, rows].astype(F32) + qk[fz(h) + 5, 0:128].astype(F32)
        for k in range(3):
            @pl.when(k + 1 > z)
            def _():
                along_right(h, k + 1).wait_send()

            @pl.when(k < z)
            def _():
                along_left(h, k).wait_send()

    def add_into(slot, k, page):
        for g in range(4):
            at = slice(g * 32, g * 32 + 32)
            rg[slot, k, y, at] = (rg[slot, k, y, at].astype(F32) + ryz[page, at].astype(F32)).astype(BF)

    def z_credit():
        @pl.when(z < 3)
        def _():
            pl.semaphore_wait(rcr, 1)

        @pl.when(z > 0)
        def _():
            pl.semaphore_wait(lcr, 1)

    last_slot = (CHUNKS - 1) % SLOTS

    def last_k(t):
        low = (3, 0, 2, 1)[t]
        return jnp.where(z == 0, 3 - t, jnp.where(z == 1, low, jnp.where(z == 2, 3 - low, t)))

    def last_y(t):
        k = last_k(t)
        return remote(rg.at[last_slot, k, 1 - y], ryz.at[last_slot * 4 + k], lys.at[t], lyr.at[t], ypeer)

    def last_step(t):
        k = last_k(t)
        last_y(t).wait_send()
        if t < 2:
            last_y(t + 2).start()
        last_y(t).wait_recv()
        add_into(last_slot, k, last_slot * 4 + k)

        @pl.when((z == 0) & (k > 0))
        def _():
            right(last_slot, k).start()

        @pl.when((z == 3) & (k < 3))
        def _():
            left(last_slot, k).start()

    def proc_y(i):
        slot = lax.rem(i, SLOTS)
        sends(slot).wait_recv()
        pl.when(i >= SLOTS)(z_credit)

        def up_first(t):
            k = 3 - t
            add_into(slot, k, slot * 4 + k)

            @pl.when((z == 0) & (k > 0))
            def _():
                right(slot, k).start()

        def down_first(t):
            add_into(slot, t, slot * 4 + t)

            @pl.when((z == 3) & (t < 3))
            def _():
                left(slot, t).start()

        @pl.when(z < 2)
        def _():
            loop(0, 4, up_first)

        @pl.when(z >= 2)
        def _():
            loop(0, 4, down_first)

        @pl.when(i + SLOTS < CHUNKS)
        def _():
            pl.semaphore_signal(ycr, 1, device_id=ypeer, device_id_type=MESH)

    def pass_right(slot, k):
        right(slot, k).wait_recv()
        add_into(slot, k, rz(slot, k + 1))
        right(slot, k).start()

    def pass_left(slot, k):
        left(slot, k).wait_recv()
        add_into(slot, k, rz(slot, k))
        left(slot, k).start()

    def fwd_z(i):
        slot = lax.rem(i, SLOTS)

        @pl.when(z == 1)
        def _():
            pass_right(slot, 3)
            pass_right(slot, 2)

        @pl.when(z == 2)
        def _():
            pass_left(slot, 0)
            pass_left(slot, 1)

    def pass_last(leg):
        @pl.when(z == 1)
        def _():
            pass_right(last_slot, 3 - leg)

        @pl.when(z == 2)
        def _():
            pass_left(last_slot, leg)

    def fwd_z2(i):
        slot = lax.rem(i, SLOTS)

        @pl.when(z == 1)
        def _():
            pass_left(slot, 0)

        @pl.when(z == 2)
        def _():
            pass_right(slot, 3)

    def finish(i):
        slot = lax.rem(i, SLOTS)

        @pl.when(z > 0)
        def _():
            right(slot, z).wait_recv()
            add_into(slot, z, rz(slot, z + 1))

        @pl.when(z < 3)
        def _():
            left(slot, z).wait_recv()
            add_into(slot, z, rz(slot, z))

        total = rg[slot, z, y].astype(F32)

        xm[acc_at(jnp.where(i < 2, i + 2, i + 3))] = total

        @pl.when(i + SLOTS < CHUNKS)
        def _():
            @pl.when(z > 0)
            def _():
                pl.semaphore_signal(rcr, 1, device_id=zdown, device_id_type=MESH)

            @pl.when(z < 3)
            def _():
                pl.semaphore_signal(lcr, 1, device_id=zup, device_id_type=MESH)

    @pl.when(code)
    def _():
        for cp in c_local:
            cp.start()
        for cp in c_far:
            cp.start()
        for cp in e_local:
            cp.wait()
        for cp in e_far:
            cp.wait()
        gain0 = gains[0, 0:1]
        gain1 = gains[0, 1:2]
        for cp in c_local:
            cp.wait()
        for cp in c_far:
            cp.wait()
        flip(lambda b: gd[b].reshape(ROWS, 1024))
        with jax.named_scope("sent_wait"):
            hop[0].wait_recv()
            hop[1].start()
            hop[1].wait_recv()

        def rows_in(i):
            mb, mh, r = halves16(i)
            came = sr[mb, mh, r].astype(F32)
            for c in range(3):
                v = em[mb, c, mh, r].astype(F32) + came
                xm[c, by16(i)] = v
                ab[c, by16(i)] = (v * rms(v) * gain0).astype(BF)

        with jax.named_scope("code_norm"):
            loop(0, 16, rows_in, unroll=UNROLL)

        def qkv_all(b):
            for c in range(3):
                qk[c * 3 + b] = dot_nn(ab[b], wq[c]).astype(BF)

        w_copies[0].wait()
        with jax.named_scope("code_qkv"):
            loop(0, 3, qkv_all)
        with jax.named_scope("code_attend"):
            loop(0, 8, code_attend)
        w_copies[1].wait()
        with jax.named_scope("code_out"):
            loop(0, 3, lambda b: out_block(ob[b], b, b))
        w_copies[2].wait()
        w_copies[3].wait()

        def ff(b):
            exchange(b, b, True).wait()

            def rows_mid(i):
                v = xm[b, by16(i)] + summed(b, b, i)
                return v, (v * rms(v) * gain1).astype(BF)

            def put_mid(i, v, w):
                xm[b, by16(i)] = v
                bm[b, by16(i)] = w

            grouped(16, rows_mid, put_mid)

        def up_tile(f, b):
            t = dot_nn(bm[b], wu[:, f * 512 : f * 512 + 512])
            for g in range(8):
                at = slice(g * 32, g * 32 + 32)
                u = t[at].astype(BF)
                uph[f * 3 + b, at] = u
                uph[12 + f * 3 + b, at] = 0.5 * u * (1.0 + gelu_tanh(u))

        with jax.named_scope("code_ff"):
            loop(0, 3, ff)

        def res(b):
            exchange(3 + b, b, False).wait()

            def rows_res(i):
                mb, r, _ = own16(i, m)
                return (em[mb, b, 1 - m, r].astype(F32) + summed_own(3 + b, b, i)).astype(BF)

            def put_res(i, v):
                mb, r, _ = own16(i, m)
                em[mb, b, 1 - m, r] = v

            grouped(8, lambda i: (rows_res(i),), put_res)

        with jax.named_scope("code_grad_down"):
            for f in (2, 1, 0, 3):
                loop(0, 3, functools.partial(up_tile, f))
                hidden = functools.partial(lambda f: uph[12 + f * 3 : 15 + f * 3].reshape(768, 512), f)
                if f == 2:
                    make_chunk(0, hidden)
                elif f == 1:
                    make_along(0, hidden)
                elif f == 0:
                    make_help(0, hidden)
                else:
                    make_chunk(1, hidden)

        def keep(b):
            def rows_keep(i):
                mb, r, row = own16(i, m)
                em[mb, b, 1 - m, r] = xm[b, row].astype(BF)

            loop(0, 8, rows_keep, unroll=UNROLL)

        loop(0, 3, keep)
        def dff(b):
            dff_block(gd[b].reshape(ROWS, 1024), lambda f: f * 3 + b, None, 3 + b, b)

        with jax.named_scope("code_dff"):
            loop(0, 3, dff)

        def dmid(b):
            exchange(3 + b, b, True).wait()

            def rows_dmid(i):
                mb, mh, r = halves16(i)
                add, part = norm_back(xm[b, by16(i)], summed(3 + b, b, i), gain1)
                return gd[b, mb, mh, r].astype(F32) + add, part

            def put_dmid(i, dm, part):
                mb, mh, r = halves16(i)
                xm[b, by16(i)] = dm
                gd[b, mb, mh, r] = dm.astype(BF)
                add_gain(1, part)

            grouped(16, rows_dmid, put_dmid)
            ob[3 + b] = dot_nt(gd[b].reshape(ROWS, 1024), wo[...]).astype(BF)

        with jax.named_scope("code_dmid"):
            loop(0, 3, dmid)
        with jax.named_scope("code_early"):
            proc_y(0)
            flip(lambda b: bm[b])
            make_chunk(2, lambda: uph[3:6].reshape(768, 512))
            along_pass(0, 0)
        with jax.named_scope("code_attend_back"):
            loop(0, 8, code_attend_back)
        with jax.named_scope("code_dqkv"):
            loop(0, 3, lambda b: dqkv_block(lambda c: c * 3 + b, b, b))

        def dx(b):
            exchange(b, b, False).wait()

            def rows_dx(i):
                mb, r, row = own16(i, m)
                v = em[mb, b, m, r].astype(F32) + sr[mb, m, r].astype(F32)
                add, part = norm_back(v, summed_own(b, b, i), gain0)
                return xm[b, row] + add, part

            def put_dx(i, dv, part):
                mb, r, row = own16(i, m)
                xm[b, row] = dv
                em[mb, b, m, r] = dv.astype(BF)
                add_gain(0, part)

            grouped(8, rows_dx, put_dx)

        with jax.named_scope("code_dx"):
            loop(0, 3, dx)
        hop[1].wait_send()

        def rows_ds(i):
            mb, r, row = own16(i, m)
            sr[mb, m, r] = (xm[0, row] + xm[1, row] + xm[2, row]).astype(BF)

        loop(0, 8, rows_ds, unroll=UNROLL)
        for cp in hop2:
            cp.start()
        gain_first()
        with jax.named_scope("code_y2"):
            make_chunk(3, lambda: uph[6:9].reshape(768, 512))
            proc_y(1)
            gain_second()
            along_pass(0, 1)
            fwd_z(0)

        with jax.named_scope("code_down"):
            loop(0, 3, lambda b: down_block(lambda f: uph[12 + f * 3 + b], 3 + b, b))
            loop(0, 3, res)
        for cp in lo_local:
            cp.start()
        make_chunk(4, lambda: uph[9:12].reshape(768, 512))

        def tail(i):
            @pl.when(i == 4)
            def _():
                for cp in hop2:
                    cp.wait_send()
                make_help(1, lambda: uph[0:3].reshape(768, 512))

            @pl.when(i == 5)
            def _():
                flip(lambda b: gd[b].reshape(ROWS, 1024))
                make_chunk(i, lambda: ob[0:3].reshape(768, 512))

            @pl.when(i == 6)
            def _():
                flip(lambda b: ab[b])

            @pl.when((i > 5) & (i < CHUNKS - 1))
            def _():
                make_chunk(i, lambda: qk[pl.ds((i - 6) * 3, 3)].reshape(768, 512))

            @pl.when(i == CHUNKS - 1)
            def _():
                make_chunk(i, lambda: qk[6:9].reshape(768, 512), False)

            @pl.when(i == 6)
            def _():
                for h in (0, 1):
                    help_a(h).wait_send()
                    help_b(h).wait_send()
                for cp in dl_far:
                    cp.start()

            @pl.when(i == 8)
            def _():
                for cp in dl_far:
                    cp.wait_send()
                for cp in lo_far:
                    cp.start()

            with jax.named_scope("tail_z2"):
                fwd_z2(i - 3)

            @pl.when(i > 3)
            def _():
                with jax.named_scope("tail_finish"):
                    finish(i - 4)

            with jax.named_scope("tail_y"):
                proc_y(i - 1)

            @pl.when(i == CHUNKS - 1)
            def _():
                last_y(0).start()
                last_y(1).start()

            with jax.named_scope("tail_z"):
                fwd_z(i - 2)

            with jax.named_scope("tail_along"):
                pl.when(i == 4)(lambda: along_sum(0))
                pl.when(i == 5)(lambda: along_finish(0, 1))

            @pl.when(i == 7)
            def _():
                helped(0)

        def helped(h):
            with jax.named_scope("helped"):
                help_back(h).wait_recv()
                xm[acc_at(h * 4)] = ryz[56 + h].astype(F32)
                grads_out[h].start()

        loop(3, CHUNKS, tail)
        n = CHUNKS - 1
        with jax.named_scope("last_0"):
            z_credit()
            last_step(0)
        with jax.named_scope("last_1"):
            fwd_z2(n - 2)
            last_step(1)
            finish(n - 3)
        with jax.named_scope("last_2"):
            fwd_z(n - 1)
            last_step(2)
            pass_last(0)
            finish(n - 2)
        with jax.named_scope("last_3"):
            fwd_z2(n - 1)
            last_step(3)
            pass_last(1)
        with jax.named_scope("last_4"):
            fwd_z2(n)
            finish(n - 1)
        helped(1)
        with jax.named_scope("last_5"):
            finish(n)
        grads_out[2].start()
        for cp in lo_local:
            cp.wait()
        for cp in lo_far:
            cp.wait_send()
        gain_last()
        for cp in ge_far:
            cp.wait_recv()
        for t in range(CHUNKS - SLOTS, CHUNKS):
            free_slot(t % SLOTS, t == CHUNKS - 1)
        for cp in grads_out:
            cp.wait()


def unpack(lo_i, ge_i, g_i, gg_i, lo_o, ge_o, gg_o, gq_o, go_o, gu_o, gd_o, lo, ge, g, gq, go, gu, gdn, sems):
    ins = [pltpu.make_async_copy(g_i.at[t], g.at[t], sems.at[t]) for t in range(3)]
    ins += [pltpu.make_async_copy(lo_i, lo, sems.at[3]), pltpu.make_async_copy(ge_i, ge, sems.at[4])]
    outs = [
        pltpu.make_async_copy(a, b, sems.at[5 + t])
        for t, (a, b) in enumerate(((gdn, gd_o), (gu, gu_o), (go, go_o), (gq, gq_o), (lo, lo_o), (ge, ge_o)))
    ]
    for cp in ins:
        cp.start()
    gg_o[...] = gg_i[...]

    def chunk(i):
        rows, cols = (i % 4) // 2 * 128, i % 2 * 512
        return g[i // 4, rows : rows + 128, cols : cols + 512]

    ins[0].wait()
    for f in range(4):
        gdn[f * 512 : f * 512 + 512] = chunk(f).T
    outs[0].start()
    ins[1].wait()
    for f in range(4):
        gu[:, f * 512 : f * 512 + 512] = chunk(4 + f)
    outs[1].start()
    ins[2].wait()
    go[...] = chunk(8).T
    outs[2].start()
    for c in range(3):
        gq[c] = chunk(9 + c)
    outs[3].start()
    for t in range(2):
        ins[3 + t].wait()
        outs[4 + t].start()
    for cp in outs:
        cp.wait()


def on_device_kernel(embeds, lengths, norm_gains, w_qkv, w_out, w_up, w_down, cotangent):
    anyspec = pl.BlockSpec(memory_space=pl.ANY)
    hbm = pl.BlockSpec(memory_space=pltpu.HBM)
    vm = pl.BlockSpec(memory_space=pltpu.VMEM)
    sd = jax.ShapeDtypeStruct
    V = pltpu.VMEM
    D = pltpu.SemaphoreType.DMA
    R = pltpu.SemaphoreType.REGULAR
    full = (2, 2, 64, 1024)
    scratch = [
        V((3, 1024, 512), BF), V((512, 1024), BF), V((1024, 2048), BF), V((2048, 1024), BF),
        V((2, 3, 2, 64, 1024), BF), V((3,) + full, BF), V(full, BF),
        V((3, ROWS, 1024), F32), V((3, ROWS, 1024), BF), V((3, ROWS, 1024), BF),
        V((24, ROWS, 512), BF), V((8, ROWS, 512), BF), V((1, ROWS, 512), BF), V((32, ROWS, 512), BF),
        V((3,) + full, BF), V((6,) + full, BF), V((1024, 768), BF),
        V((3, ROWS, 128), F32), V((2, 3, 128, 128), BF), V((8, 8, 128), F32),
        V((2, 8, 1024), F32), V((8, 8, 1024), F32), V((2, 8, 1024), F32),
        V((SLOTS, 4, 2, 128, 512), BF), V((32 + HELPED * 13, 128, 512), BF),
        D((3,)), D((4,)), D, D, D, D((3,)), D((3,)), D((3,)), D((3,)), D((6,)), D((4,)), D((4,)),
        D, D, D, D, D,
        D, D, D, D((8,)), D((8,)), D, D,
        D((SLOTS,)), D((SLOTS,)), D((SLOTS, 3)), D((SLOTS, 3)), D((SLOTS, 3)), D((SLOTS, 3)),
        D((4,)), D((4,)),
        D((ALONG, 3)), D((ALONG, 3)), D((ALONG, 3)), D((ALONG, 3)), D((ALONG,)), D((ALONG,)),
        D((HELPED,)), D((HELPED,)), D((HELPED,)), D((HELPED,)),
        D((HELPED, 3)), D((HELPED, 3)), D((HELPED, 3)), D((HELPED, 3)), D((HELPED,)), D((HELPED,)),
        D((8,)), D((8,)), D((4, 3)), D((8,)), D((8,)), D((8,)), D((4, 3)), D((8,)), D((8,)), D((8,)),
        R, R, R,
    ]
    rows, gain = sd((2, 3, 64, 1024), BF), sd((1, 2, 1024), F32)
    grads = (sd((3, 128, 512), F32), sd((512, 128), F32), sd((128, 2048), F32), sd((2048, 128), F32))
    outs = pl.pallas_call(
        body,
        out_shape=(rows, rows, sd((3, ROWS, 1024), F32), gain),
        in_specs=[anyspec, anyspec, pl.BlockSpec(memory_space=pltpu.SMEM), vm, anyspec, anyspec, anyspec, anyspec],
        out_specs=(anyspec, anyspec, anyspec, vm),
        scratch_shapes=scratch,
        compiler_params=pltpu.CompilerParams(
            collective_id=0, has_side_effects=True, vmem_limit_bytes=61 * 2**20 - 2**19
        ),
        name="two_sections",
    )(
        jnp.transpose(embeds, (0, 2, 1, 3)), jnp.transpose(cotangent, (0, 2, 1, 3)), lengths, norm_gains,
        jnp.transpose(w_qkv[0], (1, 0, 2)), w_out[0], w_up[0], w_down[0],
    )
    outs = pl.pallas_call(
        unpack,
        out_shape=(rows, rows, gain) + grads,
        in_specs=[hbm] * 3 + [vm],
        out_specs=(hbm, hbm, vm) + (hbm,) * 4,
        scratch_shapes=[V(rows.shape, BF), V(rows.shape, BF), V((3, ROWS, 1024), F32)]
        + [V(g.shape, F32) for g in (grads[0], grads[1], grads[2], grads[3])] + [D((11,))],
        compiler_params=pltpu.CompilerParams(vmem_limit_bytes=60 * 2**20),
        name="results",
    )(*outs)
    lo, ge, gg, gq, go, gu, gdn = outs
    return (
        jnp.transpose(lo, (0, 2, 1, 3)), jnp.transpose(ge, (0, 2, 1, 3)), gg,
        jnp.transpose(gq, (1, 0, 2))[None], go[None], gu[None], gdn[None],
    )


def solution(mesh):
    fits = tuple(mesh.shape[name] for name in ("section", "dp", "mp")) == (2, 8, 2)
    return jax.shard_map(
        on_device_kernel if fits else on_device,
        mesh=mesh,
        in_specs=(
            P(None, ("dp", "mp"), None, None),
            P(None, "dp", None),
            P("section", None, None),
            P("section", None, None, "mp"),
            P("section", "mp", None),
            P("section", None, "mp"),
            P("section", "mp", None),
            P(None, ("dp", "mp"), None, None),
        ),
        out_specs=(
            P(None, ("dp", "mp"), None, None),
            P(None, ("dp", "mp"), None, None),
            P("section", None, None),
            P("section", "dp", None, "mp"),
            P("section", "mp", "dp"),
            P("section", "dp", "mp"),
            P("section", "mp", "dp"),
        ),
        check_vma=False,
    )
```

```python
import functools
import math

import jax
import jax.numpy as jnp
from jax import lax
from jax.experimental import pallas as pl
from jax.experimental.pallas import tpu as pltpu
from jax.sharding import PartitionSpec as P

HEAD_DIM = 64


norm_eps = 1e-05
masked_fill = -1e30
rotary_base = 10000.0


def passed_along(value, axis, steps):
    count = lax.axis_size(axis)
    leading, last = (max(0, -steps), min(count, count - steps))
    return lax.ppermute(value, axis, [(source, source + steps) for source in range(leading, last)])


def rms_scale(values, gain_row):
    return (
        values * lax.rsqrt(jnp.mean(values * values, axis=-1, keepdims=True) + norm_eps) * gain_row
    )


def rotate(values, cos_tab, sin_tab):
    half_dim = values.shape[-1] // 2
    first_half = values[..., :half_dim]
    second_half = values[..., half_dim:]
    cos_rows = cos_tab[:, None, :]
    sin_rows = sin_tab[:, None, :]
    return jnp.concatenate(
        [
            first_half * cos_rows - second_half * sin_rows,
            second_half * cos_rows + first_half * sin_rows,
        ],
        axis=-1,
    )


def global_context(length_row, frames):
    doc_ends = jnp.cumsum(length_row)
    places = jnp.arange(frames, dtype=jnp.int32)
    passed = (places[:, None] >= doc_ends[None, :]).astype(jnp.int32)
    segment = jnp.sum(passed, axis=1)
    offsets = places - jnp.sum(passed * length_row[None, :], axis=1)
    allowed = (segment[:, None] == segment[None, :]) & (places[None, :] <= places[:, None])
    half_dim = HEAD_DIM // 2
    frequency = jnp.exp(
        jnp.arange(half_dim, dtype=jnp.float32) * (-2.0 * math.log(rotary_base) / HEAD_DIM)
    )
    angles = offsets.astype(jnp.float32)[:, None] * frequency[None, :]
    return (allowed, jnp.cos(angles), jnp.sin(angles))


def global_attend(projected, context):
    allowed, cos_tab, sin_tab = context
    attn_scale = 1.0 / math.sqrt(HEAD_DIM)
    row_total, _, local_width = projected.shape
    head_count = local_width // HEAD_DIM
    query_rows = rotate(
        projected[:, 0].reshape(row_total, head_count, HEAD_DIM), cos_tab, sin_tab
    ).astype(jnp.bfloat16)
    key_rows = rotate(
        projected[:, 1].reshape(row_total, head_count, HEAD_DIM), cos_tab, sin_tab
    ).astype(jnp.bfloat16)
    value_rows = projected[:, 2].reshape(row_total, head_count, HEAD_DIM).astype(jnp.bfloat16)
    scores = (
        jnp.einsum("qhd,khd->hqk", query_rows, key_rows, preferred_element_type=jnp.float32)
        * attn_scale
    )
    scores = jnp.where(allowed[None], scores, masked_fill)
    score_peak = jnp.max(scores, axis=-1, keepdims=True)
    exp_scores = jnp.exp(scores - score_peak)
    row_sums = jnp.sum(exp_scores, axis=-1, keepdims=True)
    weights_low = (exp_scores / row_sums).astype(jnp.bfloat16)
    mixed_rows = jnp.einsum(
        "hqk,khd->qhd", weights_low, value_rows, preferred_element_type=jnp.float32
    )
    log_total = score_peak + jnp.log(row_sums)
    return (
        mixed_rows.reshape(row_total, local_width).astype(jnp.bfloat16),
        (query_rows, key_rows, value_rows, log_total),
    )


def global_attend_back(attn_saved, context, grad_mixed):
    query_rows, key_rows, value_rows, log_total = attn_saved
    allowed, cos_tab, sin_tab = context
    attn_scale = 1.0 / math.sqrt(HEAD_DIM)
    row_total, head_count, _ = query_rows.shape
    grad_heads = grad_mixed.reshape(row_total, head_count, HEAD_DIM)
    scores = (
        jnp.einsum("qhd,khd->hqk", query_rows, key_rows, preferred_element_type=jnp.float32)
        * attn_scale
    )
    prob_rows = jnp.where(allowed[None], jnp.exp(scores - log_total), 0.0)
    grad_values = jnp.einsum(
        "hqk,qhd->khd",
        prob_rows.astype(jnp.bfloat16),
        grad_heads,
        preferred_element_type=jnp.float32,
    )
    grad_probs = jnp.einsum(
        "qhd,khd->hqk", grad_heads, value_rows, preferred_element_type=jnp.float32
    )
    grad_scores = (
        prob_rows * (grad_probs - jnp.sum(grad_probs * prob_rows, axis=-1, keepdims=True))
    ).astype(jnp.bfloat16)
    grad_query = (
        jnp.einsum("hqk,khd->qhd", grad_scores, key_rows, preferred_element_type=jnp.float32)
        * attn_scale
    )
    grad_keys = (
        jnp.einsum("hqk,qhd->khd", grad_scores, query_rows, preferred_element_type=jnp.float32)
        * attn_scale
    )
    grad_query = rotate(grad_query, cos_tab, -sin_tab)
    grad_keys = rotate(grad_keys, cos_tab, -sin_tab)
    stacked = jnp.stack([grad_query, grad_keys, grad_values], axis=1)
    return stacked.reshape(row_total, 3, head_count * HEAD_DIM).astype(jnp.bfloat16)


def local_attend(projected, context):
    attn_scale = 1.0 / math.sqrt(HEAD_DIM)
    row_total, _, local_width = projected.shape
    head_count = local_width // HEAD_DIM
    frames = row_total // 3
    qkv_parts = projected.reshape(frames, 3, 3, head_count, HEAD_DIM).astype(jnp.bfloat16)
    query_rows = qkv_parts[:, :, 0]
    key_rows = qkv_parts[:, :, 1]
    value_rows = qkv_parts[:, :, 2]
    scores = (
        jnp.einsum("fihd,fjhd->fhij", query_rows, key_rows, preferred_element_type=jnp.float32)
        * attn_scale
    )
    scores = jnp.where(context[None, None], scores, masked_fill)
    score_peak = jnp.max(scores, axis=-1, keepdims=True)
    exp_scores = jnp.exp(scores - score_peak)
    row_sums = jnp.sum(exp_scores, axis=-1, keepdims=True)
    weights_low = (exp_scores / row_sums).astype(jnp.bfloat16)
    mixed_rows = jnp.einsum(
        "fhij,fjhd->fihd", weights_low, value_rows, preferred_element_type=jnp.float32
    )
    log_total = score_peak + jnp.log(row_sums)
    return (
        mixed_rows.reshape(row_total, local_width).astype(jnp.bfloat16),
        (query_rows, key_rows, value_rows, log_total),
    )


def local_attend_back(attn_saved, context, grad_mixed):
    query_rows, key_rows, value_rows, log_total = attn_saved
    attn_scale = 1.0 / math.sqrt(HEAD_DIM)
    frames, _, head_count, _ = query_rows.shape
    grad_heads = grad_mixed.reshape(frames, 3, head_count, HEAD_DIM)
    scores = (
        jnp.einsum("fihd,fjhd->fhij", query_rows, key_rows, preferred_element_type=jnp.float32)
        * attn_scale
    )
    prob_rows = jnp.where(context[None, None], jnp.exp(scores - log_total), 0.0)
    grad_values = jnp.einsum(
        "fhij,fihd->fjhd",
        prob_rows.astype(jnp.bfloat16),
        grad_heads,
        preferred_element_type=jnp.float32,
    )
    grad_probs = jnp.einsum(
        "fihd,fjhd->fhij", grad_heads, value_rows, preferred_element_type=jnp.float32
    )
    grad_scores = (
        prob_rows * (grad_probs - jnp.sum(grad_probs * prob_rows, axis=-1, keepdims=True))
    ).astype(jnp.bfloat16)
    grad_query = (
        jnp.einsum("fhij,fjhd->fihd", grad_scores, key_rows, preferred_element_type=jnp.float32)
        * attn_scale
    )
    grad_keys = (
        jnp.einsum("fhij,fihd->fjhd", grad_scores, query_rows, preferred_element_type=jnp.float32)
        * attn_scale
    )
    stacked = jnp.stack([grad_query, grad_keys, grad_values], axis=2)
    return stacked.reshape(frames * 3, 3, head_count * HEAD_DIM).astype(jnp.bfloat16)


def gather_project(normed, weight, form):
    piece_rows = lax.all_gather(normed, "mp", axis=0, tiled=True)
    return (piece_rows, jnp.einsum(form, piece_rows, weight, preferred_element_type=jnp.float32))


def reduce_rows(left, weight, form, row_count):

    def partial_term(first_row, count_rows):
        return jnp.einsum(form, left, weight, preferred_element_type=jnp.float32)

    return lax.psum_scatter(
        partial_term(jnp.int32(0), row_count * lax.axis_size("mp")),
        "mp",
        scatter_dimension=0,
        tiled=True,
    )


def reduce_grads(left, weight, form, row_count):

    def partial_term(first_row, count_rows):
        return jnp.einsum(form, left, weight, preferred_element_type=jnp.float32)

    return lax.psum_scatter(
        partial_term(jnp.int32(0), row_count * lax.axis_size("mp")),
        "mp",
        scatter_dimension=0,
        tiled=True,
    )


def gather_grads(grad_low):
    return lax.all_gather(grad_low, "mp", axis=0, tiled=True)


def layer_forward(frame_rows, weights, attend, context):
    gain_pair, w_qkv, w_out, w_up, w_down = weights
    row_count = frame_rows.shape[0]
    normed = rms_scale(frame_rows, gain_pair[0]).astype(jnp.bfloat16)
    normed_all, projected = gather_project(normed, w_qkv, "nd,dce->nce")
    mixed_rows, attn_saved = attend(projected, context)
    attn_rows = reduce_rows(mixed_rows, w_out, "ne,ed->nd", row_count)
    middle = frame_rows + attn_rows
    normed_mid = rms_scale(middle, gain_pair[1]).astype(jnp.bfloat16)
    normed_mid_all, up_all = gather_project(normed_mid, w_up, "nd,de->ne")
    hidden = jax.nn.gelu(up_all).astype(jnp.bfloat16)
    down_rows = reduce_rows(hidden, w_down, "nf,fd->nd", row_count)
    record = (normed_all, attn_saved, mixed_rows, middle, normed_mid_all, up_all, hidden)
    return (middle + down_rows, attn_rows + down_rows, record)


def layer_backward(frame_rows, weights, attend_back, context, record, grad_result):
    gain_pair, w_qkv, w_out, w_up, w_down = weights
    normed_all, attn_saved, mixed_rows, middle, normed_mid_all, up_all, hidden = record
    row_count = frame_rows.shape[0]
    grad_down_all = gather_grads(grad_result.astype(jnp.bfloat16))
    grad_w_down = jnp.einsum("nf,nd->fd", hidden, grad_down_all, preferred_element_type=jnp.float32)
    grad_hidden = jnp.einsum("nd,fd->nf", grad_down_all, w_down, preferred_element_type=jnp.float32)
    _, gelu_back = jax.vjp(jax.nn.gelu, up_all)
    grad_up = gelu_back(grad_hidden)[0].astype(jnp.bfloat16)
    grad_w_up = jnp.einsum("nd,ne->de", normed_mid_all, grad_up, preferred_element_type=jnp.float32)
    grad_normed_mid = reduce_grads(grad_up, w_up, "ne,de->nd", row_count)
    _, mid_back = jax.vjp(rms_scale, middle, gain_pair[1])
    grad_middle_part, grad_gain_mid = mid_back(grad_normed_mid)
    grad_middle = grad_result + grad_middle_part
    grad_attn_all = gather_grads(grad_middle.astype(jnp.bfloat16))
    grad_w_out = jnp.einsum(
        "ne,nd->ed", mixed_rows, grad_attn_all, preferred_element_type=jnp.float32
    )
    grad_mixed = jnp.einsum(
        "nd,ed->ne", grad_attn_all, w_out, preferred_element_type=jnp.float32
    ).astype(jnp.bfloat16)
    grad_projected = attend_back(attn_saved, context, grad_mixed)
    grad_w_qkv = jnp.einsum(
        "nd,nce->dce", normed_all, grad_projected, preferred_element_type=jnp.float32
    )
    grad_normed = reduce_grads(grad_projected, w_qkv, "nce,dce->nd", row_count)
    _, first_back = jax.vjp(rms_scale, frame_rows, gain_pair[0])
    grad_rows_part, grad_gain_first = first_back(grad_normed)
    grad_frame_rows = grad_middle + grad_rows_part
    layer_grads = (
        jnp.stack([grad_gain_first, grad_gain_mid]),
        grad_w_qkv,
        grad_w_out,
        grad_w_up,
        grad_w_down,
    )
    return (grad_frame_rows, layer_grads)


def on_device(embeds, lengths, norm_gains, w_qkv, w_out, w_up, w_down, cotangent):
    weights = (norm_gains[0], w_qkv[0], w_out[0], w_up[0], w_down[0])
    micro_count = embeds.shape[0]
    shard_rows = embeds.shape[1]
    width = embeds.shape[-1]
    frames = shard_rows * lax.axis_size("mp")
    is_first = lax.axis_index("section") == 0
    local_allowed = jnp.tril(jnp.ones((3, 3), dtype=jnp.bool_))
    gain_total = jnp.zeros(norm_gains.shape[1:], jnp.float32)
    weight_totals = tuple((jnp.zeros(weight.shape, jnp.float32) for weight in weights[1:]))
    totals = (gain_total,) + weight_totals
    y_part = jnp.zeros(embeds.shape, jnp.float32)
    e_part = jnp.zeros(embeds.shape, jnp.float32)
    zero_send = jnp.zeros((shard_rows, width), jnp.bfloat16)

    def add_grads(running, layer_grads):
        run_gain, run_qkv, run_out, run_up, run_down = running
        part_gain, part_qkv, part_out, part_up, part_down = layer_grads
        return (
            run_gain + part_gain,
            run_qkv + part_qkv,
            run_out + part_out,
            run_up + part_up,
            run_down + part_down,
        )

    def global_forward(micro_index):
        context = global_context(lengths[micro_index, 0], frames)
        frame_in = jnp.sum(embeds[micro_index].astype(jnp.float32), axis=1)
        result, _, record = layer_forward(frame_in, weights, global_attend, context)
        return (frame_in, context, result, record)

    def pick(first_value, second_value):
        return jnp.where(is_first, first_value, second_value)

    carry_state = (totals, y_part, e_part)
    forward_recv = zero_send
    backward_recv = zero_send
    for tick_index in range(micro_count + 2):

        def first_section(state_in):
            running, y_state, e_state = state_in
            send_fwd = zero_send
            if tick_index < micro_count:
                _, _, result, _ = global_forward(tick_index)
                send_fwd = result.astype(jnp.bfloat16)
                joined = (
                    embeds[tick_index].astype(jnp.float32)
                    + send_fwd.astype(jnp.float32)[:, None, :]
                )
                y_state = y_state.at[tick_index].set(joined)
            if tick_index >= 2:
                micro_index = tick_index - 2
                frame_in, context, _, record = global_forward(micro_index)
                grad_frame, layer_grads = layer_backward(
                    frame_in,
                    weights,
                    global_attend_back,
                    context,
                    record,
                    backward_recv.astype(jnp.float32),
                )
                running = add_grads(running, layer_grads)
                e_state = e_state.at[micro_index].set(
                    jnp.broadcast_to(grad_frame[:, None, :], e_state.shape[1:])
                )
            return ((running, y_state, e_state), send_fwd, zero_send)

        def second_section(state_in):
            running, y_state, e_state = state_in
            send_back = zero_send
            if 1 <= tick_index <= micro_count:
                micro_index = tick_index - 1
                local_in = (
                    embeds[micro_index].astype(jnp.float32)
                    + forward_recv.astype(jnp.float32)[:, None, :]
                )
                local_in = local_in.reshape(shard_rows * 3, width)
                _, branches, record = layer_forward(local_in, weights, local_attend, local_allowed)
                grad_seed = (
                    cotangent[micro_index].astype(jnp.float32).reshape(shard_rows * 3, width)
                )
                grad_local, layer_grads = layer_backward(
                    local_in, weights, local_attend_back, local_allowed, record, grad_seed
                )
                running = add_grads(running, layer_grads)
                y_state = y_state.at[micro_index].set(branches.reshape(shard_rows, 3, width))
                grad_frames = grad_local.reshape(shard_rows, 3, width)
                e_state = e_state.at[micro_index].set(grad_frames)
                send_back = jnp.sum(grad_frames, axis=1).astype(jnp.bfloat16)
            return ((running, y_state, e_state), zero_send, send_back)

        first_result = first_section(carry_state)
        second_result = second_section(carry_state)
        carry_state, send_fwd, send_back = jax.tree.map(pick, first_result, second_result)
        if tick_index < micro_count:
            forward_recv = passed_along(send_fwd, "section", 1)
        if 1 <= tick_index <= micro_count:
            backward_recv = passed_along(send_back, "section", -1)
    totals, y_part, e_part = carry_state
    gain_total, grad_qkv, grad_out, grad_up, grad_down = totals
    grad_qkv, grad_out, grad_up, grad_down = (
        lax.psum_scatter(grad_qkv, "dp", scatter_dimension=0, tiled=True),
        lax.psum_scatter(grad_out, "dp", scatter_dimension=1, tiled=True),
        lax.psum_scatter(grad_up, "dp", scatter_dimension=0, tiled=True),
        lax.psum_scatter(grad_down, "dp", scatter_dimension=1, tiled=True),
    )
    gain_total = lax.psum(gain_total, ("dp", "mp"))
    y_sum, e_sum = (
        lax.psum(y_part.astype(jnp.bfloat16), "section").astype(jnp.float32),
        lax.psum(e_part.astype(jnp.bfloat16), "section").astype(jnp.float32),
    )
    return (
        y_sum.astype(jnp.bfloat16),
        e_sum.astype(jnp.bfloat16),
        gain_total[None],
        grad_qkv[None],
        grad_out[None],
        grad_up[None],
        grad_down[None],
    )


BF = jnp.bfloat16
F32 = jnp.float32
MESH = pl.DeviceIdType.MESH
SLOTS = 5
CHUNKS = 9
HELPED = 2
ALONG = 1
ROWS = 256
UNROLL = 4


def dot_nn(left, right):
    return lax.dot_general(left, right, (((1,), (0,)), ((), ())), preferred_element_type=F32)


def dot_nt(left, right):
    return lax.dot_general(left, right, (((1,), (1,)), ((), ())), preferred_element_type=F32)


def dot_tn(left, right):
    return lax.dot_general(left, right, (((0,), (0,)), ((), ())), preferred_element_type=F32)


def gelu_tanh(u):
    c0 = math.sqrt(2.0 / math.pi)
    return jnp.tanh(u * (c0 + (c0 * 0.044715) * (u * u)))


def gelu_slope(u, th):
    c0 = math.sqrt(2.0 / math.pi)
    return 0.5 * (1.0 + th) + 0.5 * u * (1.0 - th * th) * (c0 + (3.0 * 0.044715 * c0) * (u * u))


def loop(lower, upper, step, unroll=1):
    def wrapped(i, carry):
        step(i)
        return carry

    lax.fori_loop(lower, upper, wrapped, 0, unroll=unroll)


def grouped(count, work, store, size=4):
    def group(g):
        done = [work(g * size + t) for t in range(size)]
        for t in range(size):
            store(g * size + t, *done[t])

    loop(0, count // size, group)


def by16(i):
    return pl.ds(pl.multiple_of(i * 16, 16), 16)


def by512(i):
    return pl.ds(pl.multiple_of(i * 512, 512), 512)


def halves16(i):
    return lax.div(i, 8), lax.rem(lax.div(i, 4), 2), pl.ds(pl.multiple_of(lax.rem(i, 4) * 16, 16), 16)


def own16(i, m):
    mb, r = lax.div(i, 4), pl.multiple_of(lax.rem(i, 4) * 16, 16)
    return mb, pl.ds(r, 16), pl.ds(pl.multiple_of(mb * 128 + m * 64 + r, 16), 16)


def swap_halves(v):
    lane = lax.broadcasted_iota(jnp.int32, v.shape, 1)
    return jnp.where(lax.rem(lane, 64) < 32, pltpu.roll(v, 96, 1), pltpu.roll(v, 32, 1))


def body(
    emb, cot, lens, gains, wq_h, wo_h, wu_h, wd_h,
    lo_h, ge_h, g_h, gg_o,
    wq, wo, wu, wd, em, gd, sr, xm, ab, bm, qk, ob, dob, uph, xs, xr, tb,
    cs, tabs, st, gga, ggr, gpart, rg, ryz,
    gsem, wsem, esem, exs, exr, csem, cxs, cxr, mps, mpr, hops, hopr, lol, los, lor, dls, dlr,
    gel, ges, ger, ggs, ggrs, gms, gmr, ysn, yrc, zrs, zrr, zls, zlr,
    lys, lyr, frs, frr, fls, flr, fys, fyr, has, har, hbs, hbr, hzrs, hzrr, hzls, hzlr, hres, hrer, sts, strc, xas, xar, xms, xmr, das, dar, dms, dmr, ycr, rcr, lcr,
):
    s = lax.axis_index("section")
    d = lax.axis_index("dp")
    m = lax.axis_index("mp")
    y = lax.rem(d, 2)
    z = lax.div(d, 2)
    peer = (s, d, 1 - m)
    across = (1 - s, d, m)
    ypeer = (s, d + 1 - 2 * y, m)
    zup = (s, jnp.minimum(d + 2, 7), m)
    zdown = (s, jnp.maximum(d - 2, 0), m)
    frame = s == 0
    code = s == 1
    scale = 1.0 / math.sqrt(HEAD_DIM)

    def remote(src, dst, ssem, rsem, to):
        return pltpu.make_async_remote_copy(
            src_ref=src, dst_ref=dst, send_sem=ssem, recv_sem=rsem, device_id=to, device_id_type=MESH
        )

    def local(src, dst, sem):
        return pltpu.make_async_copy(src, dst, sem)

    w_copies = [local(a, b, wsem.at[i]) for i, (a, b) in enumerate(((wq_h, wq), (wo_h, wo), (wu_h, wu), (wd_h, wd)))]
    e_local = [local(emb, em.at[:, :, m], esem)]
    c_local = [local(cot.at[:, c], gd.at[c, :, m], csem.at[c]) for c in range(3)]
    for cp in e_local:
        cp.start()
    w_copies[0].start()

    bar = pltpu.get_barrier_semaphore()
    pl.semaphore_signal(bar, 1, device_id=peer, device_id_type=MESH)
    pl.semaphore_signal(bar, 1, device_id=across, device_id_type=MESH)
    for t in range(1, 8):
        pl.semaphore_signal(bar, 1, device_id=(s, lax.rem(d + t, 8), m), device_id_type=MESH)
    with jax.named_scope("barrier"):
        pl.semaphore_wait(bar, 9)

    e_far = [remote(emb, em.at[:, :, m], exs, exr, peer)]
    c_far = [remote(cot.at[:, c], gd.at[c, :, m], cxs.at[c], cxr.at[c], peer) for c in range(3)]
    for cp in e_far:
        cp.start()
    for cp in w_copies[1:]:
        cp.start()

    hop = [remote(sr.at[:, m], sr.at[:, m], hops.at[0], hopr.at[0], across),
           remote(sr.at[:, m], sr.at[:, m], hops.at[1], hopr.at[1], peer)]
    hop2 = [
        remote(sr.at[:, m, :, c * 512 : c * 512 + 512],
               ryz.at[pl.ds(d * 4 + c * 2, 2), pl.ds(pl.multiple_of(m * 64, 64), 64)],
               hops.at[2 + c], hopr.at[2 + c], across)
        for c in range(2)
    ]
    lo_local = [local(em.at[:, :, 1 - m], lo_h, lol)]
    lo_far = [remote(em.at[:, :, 1 - m], lo_h, los, lor, across)]
    dl_far = [remote(em.at[:, :, m], em.at[:, :, 1 - m], dls, dlr, across)]
    ge_local = [local(em.at[:, :, 1 - m], ge_h, gel)]
    ge_far = [remote(em.at[:, :, 1 - m], ge_h, ges, ger, across)]

    grads_out = [local(xm.at[t], g_h.at[t], gsem.at[t]) for t in range(3)]
    gga[...] = jnp.zeros_like(gga)

    def rms(v):
        return lax.rsqrt(jnp.mean(v * v, axis=-1, keepdims=True) + norm_eps)

    def exchange(recv_slot, send_slot, whole):
        mine = slice(None) if whole else 1 - m
        return remote(xs.at[send_slot, :, mine], xr.at[recv_slot, :, mine], mps.at[send_slot], mpr.at[recv_slot], peer)

    def put_xs(slot, cols, t):
        xs[slot, :, :, :, cols] = t.astype(BF).reshape(2, 2, 64, t.shape[-1])

    def summed(recv_slot, send_slot, i):
        mb, mh, r = halves16(i)
        return xs[send_slot, mb, mh, r].astype(F32) + xr[recv_slot, mb, mh, r].astype(F32)

    def summed_own(recv_slot, send_slot, i):
        mb, r, _ = own16(i, m)
        return xs[send_slot, mb, m, r].astype(F32) + xr[recv_slot, mb, m, r].astype(F32)

    def out_block(o, recv_slot, send_slot):
        for n in range(2):
            put_xs(send_slot, slice(n * 512, n * 512 + 512), dot_nn(o, wo[:, n * 512 : n * 512 + 512]))
        exchange(recv_slot, send_slot, True).start()

    def up_block(b_in, put):
        for f in range(4):
            t = dot_nn(b_in, wu[:, f * 512 : f * 512 + 512])
            for g in range(8):
                put(f, slice(g * 32, g * 32 + 32), t[g * 32 : g * 32 + 32])

    def down_block(get_hid, recv_slot, send_slot):
        for n in range(2):
            cols = slice(n * 512, n * 512 + 512)
            t = dot_nn(get_hid(0), wd[0:512, cols])
            for f in range(1, 4):
                t = t + dot_nn(get_hid(f), wd[f * 512 : f * 512 + 512, cols])
            put_xs(send_slot, cols, t)
        exchange(recv_slot, send_slot, False).start()

    def dff_block(g_low, page, put_hid, recv_slot, send_slot):
        for f in range(4):
            t = dot_nt(g_low, wd[f * 512 : f * 512 + 512])
            for g in range(8):
                at = slice(g * 32, g * 32 + 32)
                u = uph[page(f), at]
                th = gelu_tanh(u)
                if put_hid is not None:
                    put_hid(f, at, 0.5 * u * (1.0 + th))
                uph[page(f), at] = gelu_slope(u, th) * t[g * 32 : g * 32 + 32].astype(BF)
        for n in range(2):
            at = slice(n * 512, n * 512 + 512)
            t = dot_nt(uph[page(0)], wu[at, 0:512])
            for f in range(1, 4):
                t = t + dot_nt(uph[page(f)], wu[at, f * 512 : f * 512 + 512])
            put_xs(send_slot, at, t)
        exchange(recv_slot, send_slot, True).start()

    def dqkv_block(page, recv_slot, send_slot):
        for n in range(2):
            at = slice(n * 512, n * 512 + 512)
            t = dot_nt(qk[page(0)], wq[0, at])
            for c in range(1, 3):
                t = t + dot_nt(qk[page(c)], wq[c, at])
            put_xs(send_slot, at, t)
        exchange(recv_slot, send_slot, False).start()

    def norm_back(v, grad, gain):
        sc = rms(v)
        u = grad * gain
        vn = v * sc
        corr = jnp.mean(vn * u, axis=-1, keepdims=True)
        return sc * (u - vn * corr), grad * vn

    def add_gain(row, part):
        gga[row] = gga[row] + (part[0:8] + part[8:16])

    def acc_at(i):
        t = lax.rem(i, 4)
        return lax.div(i, 4), pl.ds(pl.multiple_of(lax.div(t, 2) * 128, 128), 128), by512(lax.rem(t, 2))

    gm = remote(gpart.at[0], gpart.at[1], gms, gmr, peer)

    def gain_first():
        gpart[0] = jnp.broadcast_to(jnp.sum(gga[0], axis=0, keepdims=True), (8, 1024))
        gm.start()

    g_far = []
    for t in range(1, 8):
        o = lax.rem(d + t, 8)
        g_far.append((remote(ggr.at[d], ggr.at[d], ggs.at[t], ggrs.at[d], (s, o, m)),
                      remote(ggr.at[d], ggr.at[o], ggs.at[t], ggrs.at[o], (s, o, m))))

    def gain_second():
        gm.wait()
        own1 = jnp.sum(gga[1], axis=0, keepdims=True)
        ggr[d] = jnp.concatenate([gpart[0, 0:1] + gpart[1, 0:1], own1, jnp.zeros((6, 1024), F32)], axis=0)
        for cp, _ in g_far:
            cp.start()

    def gain_last():
        for cp, back in g_far:
            cp.wait_send()
            back.wait_recv()
        acc = ggr[0]
        for t in range(1, 8):
            acc = acc + ggr[t]
        gg_o[0] = acc[0:2]

    def ha(h, k):
        return 32 + h * 13 + k

    def hz(h, idx):
        return 32 + h * 13 + 8 + idx

    def hg(h):
        return (24, 16)[h]

    def help_a(h):
        return remote(uph.at[pl.ds(hg(h), 4), pl.ds(pl.multiple_of(y * 128, 128), 128)],
                      ryz.at[pl.ds(ha(h, 0), 4)], has.at[h], har.at[h], across)

    def help_b(h):
        return remote(uph.at[pl.ds(hg(h), 4), pl.ds(pl.multiple_of((1 - y) * 128, 128), 128)],
                      ryz.at[pl.ds(ha(h, 4), 4)], hbs.at[h], hbr.at[h], (1 - s, d + 1 - 2 * y, m))

    def help_right(h, k):
        return remote(ryz.at[ha(h, k)], ryz.at[hz(h, k + 1)], hzrs.at[h, k - 1], hzrr.at[h, k - 1], zup)

    def help_left(h, k):
        return remote(ryz.at[ha(h, k)], ryz.at[hz(h, k)], hzls.at[h, k], hzlr.at[h, k], zdown)

    def help_back(h):
        return remote(ryz.at[ha(h, z)], ryz.at[56 + h], hres.at[h], hrer.at[h], across)

    def add_pages(to, page):
        for g in range(4):
            at = slice(g * 32, g * 32 + 32)
            ryz[to, at] = (ryz[to, at].astype(F32) + ryz[page, at].astype(F32)).astype(BF)

    def help_start(h):
        help_a(h).wait_recv()
        help_b(h).wait_recv()

        def each(t):
            k = jnp.where(z < 2, 3 - t, t)
            add_pages(ha(h, k), ha(h, 4 + k))

            @pl.when((z == 0) & (k > 0))
            def _():
                help_right(h, k).start()

            @pl.when((z == 3) & (k < 3))
            def _():
                help_left(h, k).start()

        loop(0, 4, each)

    def help_pass(h, leg):
        def on_right(k):
            help_right(h, k).wait_recv()
            add_pages(ha(h, k), hz(h, k + 1))
            help_right(h, k).start()

        def on_left(k):
            help_left(h, k).wait_recv()
            add_pages(ha(h, k), hz(h, k))
            help_left(h, k).start()

        if leg == 0:
            @pl.when(z == 1)
            def _():
                on_right(3)
                on_right(2)

            @pl.when(z == 2)
            def _():
                on_left(0)
                on_left(1)
        else:
            @pl.when(z == 1)
            def _():
                on_left(0)

            @pl.when(z == 2)
            def _():
                on_right(3)

    def help_finish(h):
        @pl.when(z > 0)
        def _():
            help_right(h, z).wait_recv()
            add_pages(ha(h, z), hz(h, z + 1))

        @pl.when(z < 3)
        def _():
            help_left(h, z).wait_recv()
            add_pages(ha(h, z), hz(h, z))

        help_back(h).start()

    def help_sent(h):
        help_back(h).wait_send()
        for k in range(3):
            @pl.when(k + 1 > z)
            def _():
                help_right(h, k + 1).wait_send()

            @pl.when(k < z)
            def _():
                help_left(h, k).wait_send()

    def low_lanes():
        return lax.broadcasted_iota(jnp.int32, (128, 128), 1) < 64

    def stack_heads(v):
        zero = jnp.zeros_like(v)
        return jnp.concatenate([jnp.where(low_lanes(), v, zero), jnp.where(low_lanes(), zero, v)], axis=0)

    def side_by_side(v):
        return jnp.concatenate([v[0:128], v[128:256]], axis=1)

    def frame_allowed(mb):
        pos = lax.broadcasted_iota(jnp.int32, (128, 128), 0)
        lane = lax.broadcasted_iota(jnp.int32, (128, 128), 1)
        one = (lane <= pos) & (lane.astype(F32) >= cs[2, mb * 128 : mb * 128 + 128])
        return jnp.concatenate([one, one], axis=0)

    def frame_probs(places, q2, k):
        allowed = [frame_allowed(mb) for mb in range(2)]
        sc = [dot_nt(a, b) * scale for a, b in zip(q2, k)]
        sc = [jnp.where(allowed[mb], v, masked_fill) for (mb, _, _), v in zip(places, sc)]
        top = [jnp.max(v, axis=-1, keepdims=True) for v in sc]
        e = [jnp.exp(v - t) for v, t in zip(sc, top)]
        inv = [1.0 / jnp.sum(v, axis=-1, keepdims=True) for v in e]
        return [v * t for v, t in zip(e, inv)]

    def frame_places(g):
        return [
            (mb, slice(mb * 128, mb * 128 + 128), pl.ds(pl.multiple_of((g * 2 + t) * 128, 128), 128))
            for mb in range(2) for t in range(2)
        ]

    def frame_attend(b):
        def part(g):
            places = frame_places(g)
            q2 = [stack_heads(qk[b * 3, at, cols]) for _, at, cols in places]
            k = [qk[b * 3 + 1, at, cols] for _, at, cols in places]
            v2 = [stack_heads(qk[b * 3 + 2, at, cols]) for _, at, cols in places]
            p = [side_by_side(v.astype(BF)) for v in frame_probs(places, q2, k)]
            o = [dot_nn(v, w) for v, w in zip(p, v2)]
            for (_, at, cols), v in zip(places, o):
                ob[b, at, cols] = v.astype(BF)

        loop(0, 2, part)

    def frame_attend_back(b, do_slot):
        def part(g):
            places = frame_places(g)
            q2 = [stack_heads(qk[b * 3, at, cols]) for _, at, cols in places]
            k = [qk[b * 3 + 1, at, cols] for _, at, cols in places]
            v = [qk[b * 3 + 2, at, cols] for _, at, cols in places]
            do2 = [stack_heads(dob[do_slot, at, cols]) for _, at, cols in places]
            p = frame_probs(places, q2, k)
            dp = [dot_nt(a, c) for a, c in zip(do2, v)]
            mean = [jnp.sum(a * c, axis=-1, keepdims=True) for a, c in zip(dp, p)]
            ds = [(c * (a - t)).astype(BF) for a, c, t in zip(dp, p, mean)]
            dv = [dot_tn(a.astype(BF), c) for a, c in zip(p, do2)]
            dk = [dot_tn(a, c) for a, c in zip(ds, q2)]
            dq = [dot_nn(side_by_side(a), stack_heads(c)) for a, c in zip(ds, k)]
            for i, (_, at, cols) in enumerate(places):
                co, si = cs[0, at], cs[1, at]
                for c, t in ((0, dq[i] * scale), (1, dk[i] * scale)):
                    qk[b * 3 + c, at, cols] = (t * co - swap_halves(t) * si).astype(BF)
                qk[b * 3 + 2, at, cols] = dv[i].astype(BF)

        loop(0, 2, part)

    def frame_tables(b):
        for mb in range(2):
            at = slice(mb * 128, mb * 128 + 128)
            pos = lax.broadcasted_iota(jnp.int32, (128, 128), 0)
            lane = lax.broadcasted_iota(jnp.int32, (128, 128), 1)
            start = jnp.broadcast_to(st[b, mb : mb + 1], (128, 128)).T
            hot = ((pos.astype(F32) - start) == lane.astype(F32)).astype(BF)
            for c in range(2):
                cs[c, at] = dot_nn(hot, tabs[c, 0]) + dot_nn(hot, tabs[c, 1]) + dot_nn(hot, tabs[c, 2])
            cs[2, at] = start

    def frame_qkv(a_slot, b):
        for c in range(3):
            t = dot_nn(ab[a_slot], wq[c])
            for g in range(4):
                v = t[:, g * 128 : g * 128 + 128]
                if c < 2:
                    v = v * cs[0] + swap_halves(v) * cs[1]
                qk[b * 3 + c, :, g * 128 : g * 128 + 128] = v.astype(BF)

    def px(b, i):
        mb, r = lax.div(i, 8), by16(lax.rem(i, 8))
        q, k = lax.div(b, 2), lax.rem(b, 2) * 2
        return jnp.concatenate([rg[q, k, mb, r], rg[q, k + 1, mb, r]], axis=1).astype(F32)

    def put_px(b, i, v):
        mb, r = lax.div(i, 8), by16(lax.rem(i, 8))
        q, k = lax.div(b, 2), lax.rem(b, 2) * 2
        rg[q, k, mb, r] = v[:, 0:512].astype(BF)
        rg[q, k + 1, mb, r] = v[:, 512:1024].astype(BF)

    def ds_rows(b, i):
        mb, r = lax.div(i, 8), by16(lax.rem(i, 8))
        return jnp.concatenate([ryz[b * 4 + mb, r], ryz[b * 4 + 2 + mb, r]], axis=1).astype(F32)

    def ds_all(b):
        return jnp.concatenate(
            [ryz[pl.ds(b * 4, 2)].reshape(ROWS, 512), ryz[pl.ds(b * 4 + 2, 2)].reshape(ROWS, 512)], axis=1
        )

    mrows = pl.ds(pl.multiple_of(m * 64, 64), 64)

    def px_ref(b):
        return rg.at[lax.div(b, 2), pl.ds(lax.rem(b, 2) * 2, 2), :, mrows]

    def ds_ref(b):
        return ryz.at[pl.ds(b * 4, 4), mrows]

    def block_of(i):
        j = lax.div(i, 2)
        low = jnp.where(j == 0, 1, jnp.where(j == 1, 0, j))
        high = jnp.where(j == 0, 2, jnp.where(j == 1, 3, 3 - j))
        zz = jnp.where(z == 0, j, jnp.where(z == 1, low, jnp.where(z == 2, high, 3 - j)))
        other = lax.rem(i, 2)
        return zz * 2 + jnp.where(other == 0, y, 1 - y), zz, other

    def spread(ref, sems, rsem, ms, mr, i, with_peer):
        b, zz, other = block_of(i)

        def go(direction, to):
            remote(ref(b), ref(b), sems.at[zz, direction], rsem.at[b], to).start()

        @pl.when(other == 0)
        def _():
            go(2, ypeer)

            @pl.when((zz <= z) & (z < 3))
            def _():
                go(0, zup)

            @pl.when((zz >= z) & (z > 0))
            def _():
                go(1, zdown)

        if with_peer:
            remote(ref(b), ref(b), ms.at[b], mr.at[b], peer).start()

    def arrive(ref, sems, rsem, ms, mr, i):
        b, zz, _ = block_of(i)
        remote(ref(b), ref(b), sems.at[zz, 2], rsem.at[b], ypeer).wait_recv()
        spread(ref, sems, rsem, ms, mr, i, True)

    def drained(ref, sems, rsem, ms, mr, i, with_peer):
        b, zz, other = block_of(i)

        @pl.when(other == 0)
        def _():
            remote(ref(b), ref(b), sems.at[zz, 2], rsem.at[b], ypeer).wait_send()

            @pl.when((zz <= z) & (z < 3))
            def _():
                remote(ref(b), ref(b), sems.at[zz, 0], rsem.at[b], zup).wait_send()

            @pl.when((zz >= z) & (z > 0))
            def _():
                remote(ref(b), ref(b), sems.at[zz, 1], rsem.at[b], zdown).wait_send()

        if with_peer:
            remote(ref(b), ref(b), ms.at[b], mr.at[b], peer).wait_send()

    xset = (px_ref, xas, xar, xms, xmr)
    dset = (ds_ref, das, dar, dms, dmr)

    inner = (z == 1) | (z == 2)

    def arrive_early(which):
        arrive(*which, 1)
        arrive(*which, 2)

        @pl.when(inner)
        def _():
            arrive(*which, 4)

    def arrive_at(which, i):
        @pl.when((i == 3) & inner | (i == 4) & ~inner)
        def _():
            arrive(*which, 6)

        @pl.when((i == 2) & ~inner)
        def _():
            arrive(*which, 4)

        @pl.when((i == 2) | (i == 4) | (i == 6))
        def _():
            arrive(*which, i + 1)

    def halves_in(which, i):
        ref, _, _, ms, mr = which
        b, _, _ = block_of(i)
        remote(ref(b), ref(b), ms.at[b], mr.at[b], peer).wait_recv()

    def ring(e):
        t = lax.rem(e, 4)
        return jnp.where(t < 2, t + 1, t + 2), 1 + lax.rem(e, 2)

    mine128 = pl.ds(pl.multiple_of(d * 128, 128), 128)

    def lanes(i):
        return pl.ds(pl.multiple_of(i * 128, 128), 128)

    def hid_at(f):
        return slice(f * 256, f * 256 + 256)

    def gd_slice(b):
        page = b * 4 + lax.div(d, 4) * 2
        cols = pl.ds(pl.multiple_of(lax.rem(d, 4) * 128, 128), 128)
        return ryz[pl.ds(page, 2), :, cols].reshape(ROWS, 128).T

    def put_tb(f, at, v):
        tb[f * 256 + at.start : f * 256 + at.stop, 0:512] = v

    def frame_grad(chunk, left, right, first):
        at = acc_at(chunk)
        t = dot_nn(left, right)
        xm[at] = t if first else xm[at] + t

    def frame_grads_down(b, first):
        left = gd_slice(b)
        for f in range(4):
            frame_grad(f, left, tb[hid_at(f), 0:512], first)

    def frame_grads_up(b, bm_slot, bm_cols, first):
        left = bm[bm_slot, :, bm_cols].T
        for f in range(4):
            frame_grad(4 + f, left, uph[f * 8 + b], first)

    def frame_grads_attend(b, ga_slot, a_slot, a_cols, first):
        frame_grad(8, gd[ga_slot, :, :, :, mine128].reshape(ROWS, 128).T, ob[b], first)
        left = ab[a_slot, :, a_cols].T
        for c in range(3):
            frame_grad(9 + c, left, qk[b * 3 + c], first)

    @pl.when(frame)
    def _():
        pos = lax.broadcasted_iota(jnp.int32, (128, 128), 0)
        lane = lax.broadcasted_iota(jnp.int32, (128, 128), 1)
        freq = jnp.exp(lax.rem(lane, 32).astype(F32) * (-2.0 * math.log(rotary_base) / HEAD_DIM))
        angle = pos.astype(F32) * freq
        sine = jnp.sin(angle)
        for c, v in enumerate((jnp.cos(angle), jnp.where(lax.rem(lane, 64) < 32, -sine, sine))):
            for t in range(3):
                term = v.astype(BF)
                tabs[c, t] = term
                v = v - term.astype(F32)
        place = lax.broadcasted_iota(jnp.int32, (8, 128), 1)
        rows = []
        for mb in range(2):
            start = jnp.zeros((8, 128), jnp.int32)
            end = jnp.int32(0)
            for j in range(4):
                size = lens[mb, 0, j]
                end = end + size
                start = start + jnp.where(place >= end, size, 0)
            rows.append(start)
        which = lax.broadcasted_iota(jnp.int32, (8, 128), 0)
        st[d] = jnp.where(which == 0, rows[0], rows[1]).astype(F32)
        for t in range(1, 8):
            o = lax.rem(d + t, 8)
            remote(st.at[d], st.at[d], sts.at[t], strc.at[d], (s, o, m)).start()
        frame_tables(d)

        with jax.named_scope("embeds_wait"):
            for cp in e_local:
                cp.wait()
            for cp in e_far:
                cp.wait()

        gain0 = gains[0, 0:1]
        gain1 = gains[0, 1:2]

        def x_own(i):
            mb, mh, r = halves16(i)
            return em[mb, 0, mh, r].astype(F32) + em[mb, 1, mh, r].astype(F32) + em[mb, 2, mh, r].astype(F32)

        def rows_in(i):
            v = x_own(i)
            xm[2, by16(i)] = v
            ab[0, by16(i)] = (v * rms(v) * gain0).astype(BF)
            put_px(d, i, v)

        with jax.named_scope("own_qkv"):
            loop(0, 16, rows_in, unroll=UNROLL)
            spread(*xset, 0, False)
            w_copies[0].wait()
            frame_qkv(0, d)
        with jax.named_scope("own_attend"):
            frame_attend(d)
        w_copies[1].wait()
        with jax.named_scope("own_out"):
            out_block(ob[d], 0, 0)
            w_copies[2].wait()
            exchange(0, 0, True).wait()

        def rows_mid(i):
            v = xm[2, by16(i)] + summed(0, 0, i)
            return v, (v * rms(v) * gain1).astype(BF)

        def put_mid(i, v, w):
            xm[2, by16(i)] = v
            bm[0, by16(i)] = w

        def put_own(f, at, u):
            uph[f * 8 + d, at] = u.astype(BF)
            u = u.astype(BF)
            put_tb(f, at, 0.5 * u * (1.0 + gelu_tanh(u)))

        with jax.named_scope("own_ff"):
            grouped(16, rows_mid, put_mid)
            up_block(bm[0], put_own)
            w_copies[3].wait()
            down_block(lambda f: tb[hid_at(f), 0:512], 3, 0)
            exchange(3, 0, False).wait()

        def rows_res(i):
            mb, r, row = own16(i, m)
            sr[mb, m, r] = (xm[2, row] + summed_own(3, 0, i)).astype(BF)

        loop(0, 8, rows_res, unroll=UNROLL)
        hop[0].start()

        for t in range(1, 8):
            o = lax.rem(d + t, 8)
            remote(st.at[d], st.at[o], sts.at[t], strc.at[o], (s, o, m)).wait()

        def others_in(i):
            b, _, _ = block_of(i)
            halves_in(xset, i)
            frame_tables(b)

            def rows_norm(t):
                v = px(b, t)
                ab[2, by16(t)] = (v * rms(v) * gain0).astype(BF)

            loop(0, 16, rows_norm, unroll=UNROLL)
            ab[1, :, lanes(i)] = ab[2, :, mine128]
            frame_qkv(2, b)
            frame_attend(b)
            out_block(ob[b], *ring(i))

        def others_ff(i):
            b, _, _ = block_of(i)
            recv_slot, send_slot = ring(i)
            exchange(recv_slot, send_slot, True).wait()
            drained(*xset, i, True)

            def rows_m(t):
                v = px(b, t) + summed(recv_slot, send_slot, t)
                return v, (v * rms(v) * gain1).astype(BF)

            def put_m(t, v, w):
                put_px(b, t, v)
                bm[2, by16(t)] = w

            grouped(16, rows_m, put_m)
            bm[1, :, lanes(i)] = bm[2, :, mine128]

            def put_up(f, at, u):
                uph[f * 8 + b, at] = u.astype(BF)

            up_block(bm[2], put_up)

        with jax.named_scope("oth_arrive"):
            arrive_early(xset)

        def others(i):
            with jax.named_scope("oth_arrive"):
                arrive_at(xset, i)

            @pl.when(i < 8)
            def _():
                with jax.named_scope("oth_in"):
                    others_in(i)

            @pl.when(i > 1)
            def _():
                with jax.named_scope("oth_ff"):
                    others_ff(i - 1)

        loop(1, 9, others)
        drained(*xset, 0, False)
        hop[0].wait_send()

        with jax.named_scope("help_start0"):
            help_start(0)

        with jax.named_scope("d_sent_wait"):
            for cp in hop2:
                cp.wait_recv()
            spread(*dset, 0, True)
            halves_in(dset, 0)
        with jax.named_scope("own_dff"):
            dff_block(ds_all(d), lambda f: f * 8 + d, put_tb, 0, 0)
            frame_grads_down(d, True)
        with jax.named_scope("help_pass0"):
            help_pass(0, 0)
        exchange(0, 0, True).wait()

        def rows_dmid(i):
            add, part = norm_back(xm[2, by16(i)], summed(0, 0, i), gain1)
            return ds_rows(d, i) + add, part

        def put_dmid(i, dm, part):
            mb, mh, r = halves16(i)
            xm[2, by16(i)] = dm
            gd[0, mb, mh, r] = dm.astype(BF)
            add_gain(1, part)

        with jax.named_scope("own_dmid"):
            grouped(16, rows_dmid, put_dmid)
            dob[0] = dot_nt(gd[0].reshape(ROWS, 1024), wo[...]).astype(BF)
        with jax.named_scope("arrive_early"):
            arrive_early(dset)
        frame_tables(d)
        with jax.named_scope("own_attend_back"):
            frame_attend_back(d, 0)
        dqkv_block(lambda c: d * 3 + c, 3, 0)
        with jax.named_scope("own_grads"):
            frame_grads_up(d, 0, mine128, True)
        exchange(3, 0, False).wait()

        def rows_dx(i):
            mb, r, row = own16(i, m)
            v = em[mb, 0, m, r].astype(F32) + em[mb, 1, m, r].astype(F32) + em[mb, 2, m, r].astype(F32)
            add, part = norm_back(v, summed_own(3, 0, i), gain0)
            return xm[2, row] + add, part

        def put_dx(i, dv, part):
            mb, r, _ = own16(i, m)
            top = dv.astype(BF)
            em[mb, 0, m, r] = top
            em[mb, 1, m, r] = (dv - top.astype(F32)).astype(BF)
            add_gain(0, part)

        grouped(8, rows_dx, put_dx)
        gain_first()

        def rows_ge(i):
            mb, r, _ = own16(i, m)
            dv = em[mb, 0, m, r].astype(F32) + em[mb, 1, m, r].astype(F32)
            return tuple((em[mb, c, 1 - m, r].astype(F32) + dv).astype(BF) for c in range(3))

        def put_ge(i, *parts):
            mb, r, _ = own16(i, m)
            for c in range(3):
                em[mb, c, 1 - m, r] = parts[c]

        def embed_grads():
            for cp in dl_far:
                cp.wait_recv()
            grouped(8, rows_ge, put_ge)
            for cp in ge_local + ge_far:
                cp.start()

        gain_second()
        with jax.named_scope("help_pass0"):
            help_pass(0, 1)
        frame_grads_attend(d, 0, 0, mine128, True)

        def back_first(i):
            b, _, _ = block_of(i)
            halves_in(dset, i)
            dff_block(ds_all(b), lambda f: f * 8 + b, put_tb, *ring(i + 7))
            frame_grads_down(b, False)

        def back_second(i):
            b, _, _ = block_of(i)
            recv_slot, send_slot = ring(i + 7)
            exchange(recv_slot, send_slot, True).wait()

            def rows_dm(t):
                mb, mh, r = halves16(t)
                add, _ = norm_back(px(b, t), summed(recv_slot, send_slot, t), gain1)
                gd[1, mb, mh, r] = (ds_rows(b, t) + add).astype(BF)

            loop(0, 16, rows_dm, unroll=UNROLL)
            dob[0] = dot_nt(gd[1].reshape(ROWS, 1024), wo[...]).astype(BF)
            frame_tables(b)
            frame_attend_back(b, 0)
            frame_grads_up(b, 1, lanes(i), False)
            frame_grads_attend(b, 1, 1, lanes(i), False)

        def others_back(i):
            @pl.when(i < 8)
            def _():
                with jax.named_scope("oth_dff"):
                    back_first(i)

            with jax.named_scope("oth_arrive_d"):
                arrive_at(dset, i)

            @pl.when(i > 1)
            def _():
                with jax.named_scope("oth_rest"):
                    back_second(i - 1)

            @pl.when(i == 2)
            def _():
                with jax.named_scope("help_finish0"):
                    help_finish(0)

            @pl.when(i == 4)
            def _():
                with jax.named_scope("help_start1"):
                    help_start(1)

            @pl.when(i == 5)
            def _():
                with jax.named_scope("help_pass1"):
                    help_pass(1, 0)
                with jax.named_scope("embed_grads"):
                    embed_grads()

            @pl.when(i == 6)
            def _():
                with jax.named_scope("help_pass1"):
                    help_pass(1, 1)

            @pl.when(i == 7)
            def _():
                with jax.named_scope("help_finish1"):
                    help_finish(1)
        loop(1, 9, others_back)
        for h in range(HELPED):
            help_sent(h)
        loop(0, 8, lambda i: drained(*dset, i, True))
        for cp in grads_out:
            cp.start()
        gain_last()
        for cp in ge_local:
            cp.wait()
        for cp in ge_far:
            cp.wait_send()
        for cp in lo_far:
            cp.wait_recv()
        for cp in grads_out:
            cp.wait()

    def head_sum(prod):
        r0 = lax.broadcasted_iota(jnp.int32, (256, 256), 0)
        r1 = lax.broadcasted_iota(jnp.int32, (256, 256), 1)
        ones = (lax.div(r0, 64) == lax.div(r1, 64)).astype(BF)
        return dot_nn(prod, ones)

    def code_probs(q, k):
        probs = []
        for i in range(3):
            sc = [head_sum(q[i] * k[j]) * scale for j in range(i + 1)]
            top = functools.reduce(jnp.maximum, sc)
            e = [jnp.exp(v - top) for v in sc]
            inv = 1.0 / functools.reduce(jnp.add, e)
            probs.append([v * inv for v in e])
        return probs

    def code_part(i):
        return (pl.ds(pl.multiple_of(lax.div(i, 2) * 64, 64), 64), pl.ds(pl.multiple_of(lax.rem(i, 2) * 256, 256), 256))

    def code_attend(i):
        at, cols = code_part(i)
        q, k, v = ([qk[c * 3 + b, at, cols] for b in range(3)] for c in range(3))
        probs = code_probs(q, k)
        v = [w.astype(F32) for w in v]
        for t in range(3):
            o = functools.reduce(jnp.add, [probs[t][j].astype(BF).astype(F32) * v[j] for j in range(t + 1)])
            ob[t, at, cols] = o.astype(BF)

    def code_attend_back(i):
        at, cols = code_part(i)
        q, k, v = ([qk[c * 3 + b, at, cols] for b in range(3)] for c in range(3))
        do = [ob[3 + b, at, cols] for b in range(3)]
        probs = code_probs(q, k)
        all_dp = [[head_sum(do[t] * v[j]) for j in range(t + 1)] for t in range(3)]
        q, k, do = ([w.astype(F32) for w in x] for x in (q, k, do))
        dk = [0.0] * 3
        dv = [0.0] * 3
        for t in range(3):
            dp = all_dp[t]
            mean = functools.reduce(jnp.add, [dp[j] * probs[t][j] for j in range(t + 1)])
            dq = 0.0
            for j in range(t + 1):
                ds = (probs[t][j] * (dp[j] - mean)).astype(BF).astype(F32)
                dq = dq + ds * k[j]
                dk[j] = dk[j] + ds * q[t]
                dv[j] = dv[j] + probs[t][j].astype(BF).astype(F32) * do[t]
            qk[t, at, cols] = (dq * scale).astype(BF)
        for j in range(3):
            qk[3 + j, at, cols] = (dk[j] * scale).astype(BF)
            qk[6 + j, at, cols] = dv[j].astype(BF)

    def flip(get):
        def one(b):
            at = pl.ds(pl.multiple_of(b * 256, 256), 256)
            t = get(b)
            for g in range(4):
                tb[g * 256 : g * 256 + 256, at] = t[:, g * 256 : g * 256 + 256].T

        loop(0, 3, one)

    def ry(slot):
        return ryz.at[pl.ds(slot * 4, 4)]

    def rz(slot, idx):
        return SLOTS * 4 + slot * 5 + idx

    def sends(slot):
        return remote(rg.at[slot, :, 1 - y], ry(slot), ysn.at[slot], yrc.at[slot], ypeer)

    def right(slot, k):
        return remote(rg.at[slot, k, y], ryz.at[rz(slot, k + 1)], zrs.at[slot, k - 1], zrr.at[slot, k - 1], zup)

    def left(slot, k):
        return remote(rg.at[slot, k, y], ryz.at[rz(slot, k)], zls.at[slot, k], zlr.at[slot, k], zdown)

    def free_slot(slot, last=False):
        if not last:
            sends(slot).wait_send()
        for k in range(3):
            @pl.when(k + 1 > z)
            def _():
                right(slot, k + 1).wait_send()

            @pl.when(k < z)
            def _():
                left(slot, k).wait_send()

    def make_chunk(i, act, send=True):
        slot = lax.rem(i, SLOTS)

        @pl.when(i >= SLOTS)
        def _():
            free_slot(slot)

        def part(k):
            at = pl.ds(pl.multiple_of(k * 256, 256), 256)
            rg[slot, k] = dot_nn(tb[at, :], act()).astype(BF).reshape(2, 128, 512)

        loop(0, 4, part)

        @pl.when(i >= SLOTS)
        def _():
            pl.semaphore_wait(ycr, 1)

        if send:
            sends(slot).start()

    def make_help(h, act):
        def part(k):
            at = pl.ds(pl.multiple_of(k * 256, 256), 256)
            uph[hg(h) + k] = dot_nn(tb[at, :], act()).astype(BF)

        loop(0, 4, part)
        help_a(h).start()
        help_b(h).start()

    def fg(h):
        return (28, 12)[h]

    def fz(h):
        return (10, 16)[h]

    def along_right(h, k):
        return remote(uph.at[fg(h) + k], qk.at[fz(h) + k + 1], frs.at[h, k - 1], frr.at[h, k - 1], zup)

    def along_left(h, k):
        return remote(uph.at[fg(h) + k], qk.at[fz(h) + k], fls.at[h, k], flr.at[h, k], zdown)

    def along_y(h):
        return remote(uph.at[fg(h) + z, pl.ds(pl.multiple_of((1 - y) * 128, 128), 128)],
                      qk.at[fz(h) + 5, 0:128], fys.at[h], fyr.at[h], ypeer)

    def make_along(h, act):
        def part(k):
            at = pl.ds(pl.multiple_of(k * 256, 256), 256)
            uph[fg(h) + k] = dot_nn(tb[at, :], act()).astype(BF)

            @pl.when((z == 0) & (k > 0))
            def _():
                along_right(h, k).start()

            @pl.when((z == 3) & (k < 3))
            def _():
                along_left(h, k).start()

        loop(0, 4, part)

    def add_half(to, page):
        for g in range(8):
            at = slice(g * 32, g * 32 + 32)
            uph[to, at] = (uph[to, at].astype(F32) + qk[page, at].astype(F32)).astype(BF)

    def along_pass(h, leg):
        def on_right(k):
            along_right(h, k).wait_recv()
            add_half(fg(h) + k, fz(h) + k + 1)
            along_right(h, k).start()

        def on_left(k):
            along_left(h, k).wait_recv()
            add_half(fg(h) + k, fz(h) + k)
            along_left(h, k).start()

        if leg == 0:
            @pl.when(z == 1)
            def _():
                on_right(3)
                on_right(2)

            @pl.when(z == 2)
            def _():
                on_left(0)
                on_left(1)
        else:
            @pl.when(z == 1)
            def _():
                on_left(0)

            @pl.when(z == 2)
            def _():
                on_right(3)

    def along_sum(h):
        @pl.when(z > 0)
        def _():
            along_right(h, z).wait_recv()
            add_half(fg(h) + z, fz(h) + z + 1)

        @pl.when(z < 3)
        def _():
            along_left(h, z).wait_recv()
            add_half(fg(h) + z, fz(h) + z)

        along_y(h).start()

    def along_finish(h, chunk):
        along_y(h).wait()
        rows = pl.ds(pl.multiple_of(y * 128, 128), 128)
        xm[acc_at(chunk)] = uph[fg(h) + z, rows].astype(F32) + qk[fz(h) + 5, 0:128].astype(F32)
        for k in range(3):
            @pl.when(k + 1 > z)
            def _():
                along_right(h, k + 1).wait_send()

            @pl.when(k < z)
            def _():
                along_left(h, k).wait_send()

    def add_into(slot, k, page):
        for g in range(4):
            at = slice(g * 32, g * 32 + 32)
            rg[slot, k, y, at] = (rg[slot, k, y, at].astype(F32) + ryz[page, at].astype(F32)).astype(BF)

    def z_credit():
        @pl.when(z < 3)
        def _():
            pl.semaphore_wait(rcr, 1)

        @pl.when(z > 0)
        def _():
            pl.semaphore_wait(lcr, 1)

    last_slot = (CHUNKS - 1) % SLOTS

    def last_k(t):
        low = (3, 0, 2, 1)[t]
        return jnp.where(z == 0, 3 - t, jnp.where(z == 1, low, jnp.where(z == 2, 3 - low, t)))

    def last_y(t):
        k = last_k(t)
        return remote(rg.at[last_slot, k, 1 - y], ryz.at[last_slot * 4 + k], lys.at[t], lyr.at[t], ypeer)

    def last_step(t):
        k = last_k(t)
        last_y(t).wait_send()
        if t < 2:
            last_y(t + 2).start()
        last_y(t).wait_recv()
        add_into(last_slot, k, last_slot * 4 + k)

        @pl.when((z == 0) & (k > 0))
        def _():
            right(last_slot, k).start()

        @pl.when((z == 3) & (k < 3))
        def _():
            left(last_slot, k).start()

    def proc_y(i):
        slot = lax.rem(i, SLOTS)
        sends(slot).wait_recv()
        pl.when(i >= SLOTS)(z_credit)

        def up_first(t):
            k = 3 - t
            add_into(slot, k, slot * 4 + k)

            @pl.when((z == 0) & (k > 0))
            def _():
                right(slot, k).start()

        def down_first(t):
            add_into(slot, t, slot * 4 + t)

            @pl.when((z == 3) & (t < 3))
            def _():
                left(slot, t).start()

        @pl.when(z < 2)
        def _():
            loop(0, 4, up_first)

        @pl.when(z >= 2)
        def _():
            loop(0, 4, down_first)

        @pl.when(i + SLOTS < CHUNKS)
        def _():
            pl.semaphore_signal(ycr, 1, device_id=ypeer, device_id_type=MESH)

    def pass_right(slot, k):
        right(slot, k).wait_recv()
        add_into(slot, k, rz(slot, k + 1))
        right(slot, k).start()

    def pass_left(slot, k):
        left(slot, k).wait_recv()
        add_into(slot, k, rz(slot, k))
        left(slot, k).start()

    def fwd_z(i):
        slot = lax.rem(i, SLOTS)

        @pl.when(z == 1)
        def _():
            pass_right(slot, 3)
            pass_right(slot, 2)

        @pl.when(z == 2)
        def _():
            pass_left(slot, 0)
            pass_left(slot, 1)

    def pass_last(leg):
        @pl.when(z == 1)
        def _():
            pass_right(last_slot, 3 - leg)

        @pl.when(z == 2)
        def _():
            pass_left(last_slot, leg)

    def fwd_z2(i):
        slot = lax.rem(i, SLOTS)

        @pl.when(z == 1)
        def _():
            pass_left(slot, 0)

        @pl.when(z == 2)
        def _():
            pass_right(slot, 3)

    def finish(i):
        slot = lax.rem(i, SLOTS)

        @pl.when(z > 0)
        def _():
            right(slot, z).wait_recv()
            add_into(slot, z, rz(slot, z + 1))

        @pl.when(z < 3)
        def _():
            left(slot, z).wait_recv()
            add_into(slot, z, rz(slot, z))

        total = rg[slot, z, y].astype(F32)

        xm[acc_at(jnp.where(i < 2, i + 2, i + 3))] = total

        @pl.when(i + SLOTS < CHUNKS)
        def _():
            @pl.when(z > 0)
            def _():
                pl.semaphore_signal(rcr, 1, device_id=zdown, device_id_type=MESH)

            @pl.when(z < 3)
            def _():
                pl.semaphore_signal(lcr, 1, device_id=zup, device_id_type=MESH)

    @pl.when(code)
    def _():
        for cp in c_local:
            cp.start()
        for cp in c_far:
            cp.start()
        for cp in e_local:
            cp.wait()
        for cp in e_far:
            cp.wait()
        gain0 = gains[0, 0:1]
        gain1 = gains[0, 1:2]
        for cp in c_local:
            cp.wait()
        for cp in c_far:
            cp.wait()
        flip(lambda b: gd[b].reshape(ROWS, 1024))
        with jax.named_scope("sent_wait"):
            hop[0].wait_recv()
            hop[1].start()
            hop[1].wait_recv()

        def rows_in(i):
            mb, mh, r = halves16(i)
            came = sr[mb, mh, r].astype(F32)
            for c in range(3):
                v = em[mb, c, mh, r].astype(F32) + came
                xm[c, by16(i)] = v
                ab[c, by16(i)] = (v * rms(v) * gain0).astype(BF)

        with jax.named_scope("code_norm"):
            loop(0, 16, rows_in, unroll=UNROLL)

        def qkv_all(b):
            for c in range(3):
                qk[c * 3 + b] = dot_nn(ab[b], wq[c]).astype(BF)

        w_copies[0].wait()
        with jax.named_scope("code_qkv"):
            loop(0, 3, qkv_all)
        with jax.named_scope("code_attend"):
            loop(0, 8, code_attend)
        w_copies[1].wait()
        with jax.named_scope("code_out"):
            loop(0, 3, lambda b: out_block(ob[b], b, b))
        w_copies[2].wait()
        w_copies[3].wait()

        def ff(b):
            exchange(b, b, True).wait()

            def rows_mid(i):
                v = xm[b, by16(i)] + summed(b, b, i)
                return v, (v * rms(v) * gain1).astype(BF)

            def put_mid(i, v, w):
                xm[b, by16(i)] = v
                bm[b, by16(i)] = w

            grouped(16, rows_mid, put_mid)

        def up_tile(f, b):
            t = dot_nn(bm[b], wu[:, f * 512 : f * 512 + 512])
            for g in range(8):
                at = slice(g * 32, g * 32 + 32)
                u = t[at].astype(BF)
                uph[f * 3 + b, at] = u
                uph[12 + f * 3 + b, at] = 0.5 * u * (1.0 + gelu_tanh(u))

        with jax.named_scope("code_ff"):
            loop(0, 3, ff)

        def res(b):
            exchange(3 + b, b, False).wait()

            def rows_res(i):
                mb, r, _ = own16(i, m)
                return (em[mb, b, 1 - m, r].astype(F32) + summed_own(3 + b, b, i)).astype(BF)

            def put_res(i, v):
                mb, r, _ = own16(i, m)
                em[mb, b, 1 - m, r] = v

            grouped(8, lambda i: (rows_res(i),), put_res)

        with jax.named_scope("code_grad_down"):
            for f in (2, 1, 0, 3):
                loop(0, 3, functools.partial(up_tile, f))
                hidden = functools.partial(lambda f: uph[12 + f * 3 : 15 + f * 3].reshape(768, 512), f)
                if f == 2:
                    make_chunk(0, hidden)
                elif f == 1:
                    make_along(0, hidden)
                elif f == 0:
                    make_help(0, hidden)
                else:
                    make_chunk(1, hidden)

        def keep(b):
            def rows_keep(i):
                mb, r, row = own16(i, m)
                em[mb, b, 1 - m, r] = xm[b, row].astype(BF)

            loop(0, 8, rows_keep, unroll=UNROLL)

        loop(0, 3, keep)
        def dff(b):
            dff_block(gd[b].reshape(ROWS, 1024), lambda f: f * 3 + b, None, 3 + b, b)

        with jax.named_scope("code_dff"):
            loop(0, 3, dff)
        with jax.named_scope("code_early"):
            flip(lambda b: bm[b])
            make_chunk(2, lambda: uph[3:6].reshape(768, 512))
            proc_y(0)

        def dmid(b):
            exchange(3 + b, b, True).wait()

            def rows_dmid(i):
                mb, mh, r = halves16(i)
                add, part = norm_back(xm[b, by16(i)], summed(3 + b, b, i), gain1)
                return gd[b, mb, mh, r].astype(F32) + add, part

            def put_dmid(i, dm, part):
                mb, mh, r = halves16(i)
                xm[b, by16(i)] = dm
                gd[b, mb, mh, r] = dm.astype(BF)
                add_gain(1, part)

            grouped(16, rows_dmid, put_dmid)
            ob[3 + b] = dot_nt(gd[b].reshape(ROWS, 1024), wo[...]).astype(BF)

        with jax.named_scope("code_dmid"):
            loop(0, 3, dmid)
        along_pass(0, 0)
        with jax.named_scope("code_attend_back"):
            loop(0, 8, code_attend_back)
        with jax.named_scope("code_dqkv"):
            loop(0, 3, lambda b: dqkv_block(lambda c: c * 3 + b, b, b))

        def dx(b):
            exchange(b, b, False).wait()

            def rows_dx(i):
                mb, r, row = own16(i, m)
                v = em[mb, b, m, r].astype(F32) + sr[mb, m, r].astype(F32)
                add, part = norm_back(v, summed_own(b, b, i), gain0)
                return xm[b, row] + add, part

            def put_dx(i, dv, part):
                mb, r, row = own16(i, m)
                xm[b, row] = dv
                em[mb, b, m, r] = dv.astype(BF)
                add_gain(0, part)

            grouped(8, rows_dx, put_dx)

        with jax.named_scope("code_dx"):
            loop(0, 3, dx)
        hop[1].wait_send()

        def rows_ds(i):
            mb, r, row = own16(i, m)
            sr[mb, m, r] = (xm[0, row] + xm[1, row] + xm[2, row]).astype(BF)

        loop(0, 8, rows_ds, unroll=UNROLL)
        for cp in hop2:
            cp.start()
        gain_first()
        with jax.named_scope("code_y2"):
            make_chunk(3, lambda: uph[6:9].reshape(768, 512))
            proc_y(1)
            gain_second()
            along_pass(0, 1)
            fwd_z(0)

        with jax.named_scope("code_down"):
            loop(0, 3, lambda b: down_block(lambda f: uph[12 + f * 3 + b], 3 + b, b))
            loop(0, 3, res)
        for cp in lo_local:
            cp.start()
        make_chunk(4, lambda: uph[9:12].reshape(768, 512))

        def tail(i):
            @pl.when(i == 4)
            def _():
                for cp in hop2:
                    cp.wait_send()
                make_help(1, lambda: uph[0:3].reshape(768, 512))

            @pl.when(i == 5)
            def _():
                flip(lambda b: gd[b].reshape(ROWS, 1024))
                make_chunk(i, lambda: ob[0:3].reshape(768, 512))

            @pl.when(i == 6)
            def _():
                flip(lambda b: ab[b])

            @pl.when((i > 5) & (i < CHUNKS - 1))
            def _():
                make_chunk(i, lambda: qk[pl.ds((i - 6) * 3, 3)].reshape(768, 512))

            @pl.when(i == CHUNKS - 1)
            def _():
                make_chunk(i, lambda: qk[6:9].reshape(768, 512), False)

            @pl.when(i == 6)
            def _():
                for h in (0, 1):
                    help_a(h).wait_send()
                    help_b(h).wait_send()
                for cp in dl_far:
                    cp.start()

            @pl.when(i == 8)
            def _():
                for cp in dl_far:
                    cp.wait_send()
                for cp in lo_far:
                    cp.start()

            with jax.named_scope("tail_z2"):
                fwd_z2(i - 3)

            @pl.when(i > 3)
            def _():
                with jax.named_scope("tail_finish"):
                    finish(i - 4)

            with jax.named_scope("tail_y"):
                proc_y(i - 1)

            @pl.when(i == CHUNKS - 1)
            def _():
                last_y(0).start()
                last_y(1).start()

            with jax.named_scope("tail_z"):
                fwd_z(i - 2)

            with jax.named_scope("tail_along"):
                pl.when(i == 4)(lambda: along_sum(0))
                pl.when(i == 5)(lambda: along_finish(0, 1))

            @pl.when(i == 7)
            def _():
                helped(0)

        def helped(h):
            with jax.named_scope("helped"):
                help_back(h).wait_recv()
                xm[acc_at(h * 4)] = ryz[56 + h].astype(F32)
                grads_out[h].start()

        loop(3, CHUNKS, tail)
        n = CHUNKS - 1
        with jax.named_scope("last_0"):
            z_credit()
            last_step(0)
        with jax.named_scope("last_1"):
            fwd_z2(n - 2)
            last_step(1)
            finish(n - 3)
        with jax.named_scope("last_2"):
            fwd_z(n - 1)
            last_step(2)
            pass_last(0)
            finish(n - 2)
        with jax.named_scope("last_3"):
            fwd_z2(n - 1)
            last_step(3)
            pass_last(1)
        with jax.named_scope("last_4"):
            fwd_z2(n)
            finish(n - 1)
        helped(1)
        with jax.named_scope("last_5"):
            finish(n)
        grads_out[2].start()
        for cp in lo_local:
            cp.wait()
        for cp in lo_far:
            cp.wait_send()
        gain_last()
        for cp in ge_far:
            cp.wait_recv()
        for t in range(CHUNKS - SLOTS, CHUNKS):
            free_slot(t % SLOTS, t == CHUNKS - 1)
        for cp in grads_out:
            cp.wait()


def unpack(lo_i, ge_i, g_i, gg_i, lo_o, ge_o, gg_o, gq_o, go_o, gu_o, gd_o, lo, ge, g, gq, go, gu, gdn, sems):
    ins = [pltpu.make_async_copy(g_i.at[t], g.at[t], sems.at[t]) for t in range(3)]
    ins += [pltpu.make_async_copy(lo_i, lo, sems.at[3]), pltpu.make_async_copy(ge_i, ge, sems.at[4])]
    outs = [
        pltpu.make_async_copy(a, b, sems.at[5 + t])
        for t, (a, b) in enumerate(((gdn, gd_o), (gu, gu_o), (go, go_o), (gq, gq_o), (lo, lo_o), (ge, ge_o)))
    ]
    for cp in ins:
        cp.start()
    gg_o[...] = gg_i[...]

    def chunk(i):
        rows, cols = (i % 4) // 2 * 128, i % 2 * 512
        return g[i // 4, rows : rows + 128, cols : cols + 512]

    ins[0].wait()
    for f in range(4):
        gdn[f * 512 : f * 512 + 512] = chunk(f).T
    outs[0].start()
    ins[1].wait()
    for f in range(4):
        gu[:, f * 512 : f * 512 + 512] = chunk(4 + f)
    outs[1].start()
    ins[2].wait()
    go[...] = chunk(8).T
    outs[2].start()
    for c in range(3):
        gq[c] = chunk(9 + c)
    outs[3].start()
    for t in range(2):
        ins[3 + t].wait()
        outs[4 + t].start()
    for cp in outs:
        cp.wait()


def on_device_kernel(embeds, lengths, norm_gains, w_qkv, w_out, w_up, w_down, cotangent):
    anyspec = pl.BlockSpec(memory_space=pl.ANY)
    hbm = pl.BlockSpec(memory_space=pltpu.HBM)
    vm = pl.BlockSpec(memory_space=pltpu.VMEM)
    sd = jax.ShapeDtypeStruct
    V = pltpu.VMEM
    D = pltpu.SemaphoreType.DMA
    R = pltpu.SemaphoreType.REGULAR
    full = (2, 2, 64, 1024)
    scratch = [
        V((3, 1024, 512), BF), V((512, 1024), BF), V((1024, 2048), BF), V((2048, 1024), BF),
        V((2, 3, 2, 64, 1024), BF), V((3,) + full, BF), V(full, BF),
        V((3, ROWS, 1024), F32), V((3, ROWS, 1024), BF), V((3, ROWS, 1024), BF),
        V((24, ROWS, 512), BF), V((8, ROWS, 512), BF), V((1, ROWS, 512), BF), V((32, ROWS, 512), BF),
        V((3,) + full, BF), V((6,) + full, BF), V((1024, 768), BF),
        V((3, ROWS, 128), F32), V((2, 3, 128, 128), BF), V((8, 8, 128), F32),
        V((2, 8, 1024), F32), V((8, 8, 1024), F32), V((2, 8, 1024), F32),
        V((SLOTS, 4, 2, 128, 512), BF), V((32 + HELPED * 13, 128, 512), BF),
        D((3,)), D((4,)), D, D, D, D((3,)), D((3,)), D((3,)), D((3,)), D((6,)), D((4,)), D((4,)),
        D, D, D, D, D,
        D, D, D, D((8,)), D((8,)), D, D,
        D((SLOTS,)), D((SLOTS,)), D((SLOTS, 3)), D((SLOTS, 3)), D((SLOTS, 3)), D((SLOTS, 3)),
        D((4,)), D((4,)),
        D((ALONG, 3)), D((ALONG, 3)), D((ALONG, 3)), D((ALONG, 3)), D((ALONG,)), D((ALONG,)),
        D((HELPED,)), D((HELPED,)), D((HELPED,)), D((HELPED,)),
        D((HELPED, 3)), D((HELPED, 3)), D((HELPED, 3)), D((HELPED, 3)), D((HELPED,)), D((HELPED,)),
        D((8,)), D((8,)), D((4, 3)), D((8,)), D((8,)), D((8,)), D((4, 3)), D((8,)), D((8,)), D((8,)),
        R, R, R,
    ]
    rows, gain = sd((2, 3, 64, 1024), BF), sd((1, 2, 1024), F32)
    grads = (sd((3, 128, 512), F32), sd((512, 128), F32), sd((128, 2048), F32), sd((2048, 128), F32))
    outs = pl.pallas_call(
        body,
        out_shape=(rows, rows, sd((3, ROWS, 1024), F32), gain),
        in_specs=[anyspec, anyspec, pl.BlockSpec(memory_space=pltpu.SMEM), vm, anyspec, anyspec, anyspec, anyspec],
        out_specs=(anyspec, anyspec, anyspec, vm),
        scratch_shapes=scratch,
        compiler_params=pltpu.CompilerParams(
            collective_id=0, has_side_effects=True, vmem_limit_bytes=61 * 2**20 - 2**19
        ),
        name="two_sections",
    )(
        jnp.transpose(embeds, (0, 2, 1, 3)), jnp.transpose(cotangent, (0, 2, 1, 3)), lengths, norm_gains,
        jnp.transpose(w_qkv[0], (1, 0, 2)), w_out[0], w_up[0], w_down[0],
    )
    outs = pl.pallas_call(
        unpack,
        out_shape=(rows, rows, gain) + grads,
        in_specs=[hbm] * 3 + [vm],
        out_specs=(hbm, hbm, vm) + (hbm,) * 4,
        scratch_shapes=[V(rows.shape, BF), V(rows.shape, BF), V((3, ROWS, 1024), F32)]
        + [V(g.shape, F32) for g in (grads[0], grads[1], grads[2], grads[3])] + [D((11,))],
        compiler_params=pltpu.CompilerParams(vmem_limit_bytes=60 * 2**20),
        name="results",
    )(*outs)
    lo, ge, gg, gq, go, gu, gdn = outs
    return (
        jnp.transpose(lo, (0, 2, 1, 3)), jnp.transpose(ge, (0, 2, 1, 3)), gg,
        jnp.transpose(gq, (1, 0, 2))[None], go[None], gu[None], gdn[None],
    )


def solution(mesh):
    fits = tuple(mesh.shape[name] for name in ("section", "dp", "mp")) == (2, 8, 2)
    return jax.shard_map(
        on_device_kernel if fits else on_device,
        mesh=mesh,
        in_specs=(
            P(None, ("dp", "mp"), None, None),
            P(None, "dp", None),
            P("section", None, None),
            P("section", None, None, "mp"),
            P("section", "mp", None),
            P("section", None, "mp"),
            P("section", "mp", None),
            P(None, ("dp", "mp"), None, None),
        ),
        out_specs=(
            P(None, ("dp", "mp"), None, None),
            P(None, ("dp", "mp"), None, None),
            P("section", None, None),
            P("section", "dp", None, "mp"),
            P("section", "mp", "dp"),
            P("section", "dp", "mp"),
            P("section", "mp", "dp"),
        ),
        check_vma=False,
    )
```
